32 devices in a mesh: section: 2 (over x), dp: 8 (over z, core), mp: 2 (over y).
Axes of the slice: x: 2, y: 2, z: 4, core: 2. Of those that a mesh axis runs over, the one named last changes fastest.
Arguments:
- block_input: bfloat16 [2, 2, 8, 1024, 768], P('section', None, 'dp', 'mp'), may hold values from -6 to 6
- out_cotangent: bfloat16 [2, 2, 8, 1024, 768], P('section', None, 'dp', 'mp'), may hold values from -6 to 6
- doc_lengths: int32 [2, 8], P(None, 'dp'), may hold values from 204 to 1024, as said below
- question_lengths: int32 [2, 8, 2], P(None, 'dp'), may hold values from 64 to 512, as said below
- coordinates: int32 [2, 8, 2, 1024], P(None, 'dp'), may hold values from 0 to 999
- gains: float32 [5, 768], replicated, may hold values from 0.5 to 1.5
- bias_tables: float32 [4, 32, 12], replicated, may hold values from -4 to 4
- self_qkv: bfloat16 [2, 768, 3, 768], P('section', None, None, 'mp'), may hold values from -0.078125 to 0.078125
- self_out: bfloat16 [2, 768, 768], P('section', 'mp'), may hold values from -6 to 6
- ffn_in: bfloat16 [2, 768, 3072], P('section', None, 'mp'), may hold values from -0.21875 to 0.21875
- ffn_out: bfloat16 [2, 3072, 768], P('section', 'mp'), may hold values from -0.109375 to 0.109375
- cross_q: bfloat16 [768, 768], P(None, 'mp'), may hold values from -0.078125 to 0.078125
- cross_kv: bfloat16 [768, 2, 768], P(None, None, 'mp'), may hold values from -0.078125 to 0.078125
- cross_out: bfloat16 [768, 768], P('mp'), may hold values from -6 to 6
Outputs:
- block_output: bfloat16 [2, 2, 8, 1024, 768], P('section', None, 'dp', 'mp')
- input_grad: float32 [2, 2, 8, 1024, 768], P('section', None, 'dp', 'mp')
- gains_grad: float32 [4, 768], replicated
- last_gain_grad: float32 [768], replicated
- tables_grad: float32 [4, 32, 12], replicated
- self_qkv_grad: float32 [2, 768, 3, 768], P('section', 'dp', None, 'mp')
- self_out_grad: float32 [2, 768, 768], P('section', 'mp', 'dp')
- ffn_in_grad: float32 [2, 768, 3072], P('section', 'dp', 'mp')
- ffn_out_grad: float32 [2, 3072, 768], P('section', 'mp', 'dp')
- cross_q_grad: float32 [768, 768], P(('section', 'dp'), 'mp')
- cross_kv_grad: float32 [768, 2, 768], P(('section', 'dp'), None, 'mp')
- cross_out_grad: float32 [768, 768], P('mp', ('section', 'dp'))
The draws below stay inside these ranges and needn't reach their ends.
Inputs may be any that keep to these rules, and one draw needn't show every extreme that they name: `doc_lengths`: tokens past a document's length are padding; at every document index one of the 2 micro-batches has a document of all 1024 positions. `question_lengths`: tokens past a question's length are padding; at every document index some question has all 512 positions.
All inputs are finite; a program needn't handle non-finite values.
Results may differ from the reference program's by a relative error of at most 0.03.
Values may be sent and summed in bfloat16 or wider, within the bound.
A program may use at most 832 MiB of HBM per device.

```python
import math
from functools import partial
import jax
import jax.numpy as jnp
from jax import lax

D = 768
HEADS = 12
HEAD = 64
FF = 3072
BUCKETS = 32
MICRO = 2
ENC_LEN = 1024
QUEST = 2
DEC_LEN = 512
DOCS = 8


def draw_doc_lengths(key, part):
    key = jax.random.fold_in(key, 5)
    first_key, row_key = jax.random.split(key, 2)
    values = jax.random.randint(first_key, (MICRO, DOCS), ENC_LEN // 5, ENC_LEN + 1)
    row_pick = jax.random.randint(row_key, (DOCS,), 0, MICRO)
    chosen = lax_rows(MICRO, DOCS) == row_pick[None, :]
    return jnp.where(chosen, ENC_LEN, values).astype(jnp.int32)


def lax_rows(count, width):
    return jnp.arange(count, dtype=jnp.int32)[:, None] + jnp.zeros((1, width), jnp.int32)


def draw_question_lengths(key, part):
    key = jax.random.fold_in(key, 9)
    first_key, row_key, slot_key = jax.random.split(key, 3)
    values = jax.random.randint(first_key, (MICRO, DOCS, QUEST), max(1, DEC_LEN // 8), DEC_LEN + 1)
    row_pick = jax.random.randint(row_key, (DOCS,), 0, MICRO)
    slot_pick = jax.random.randint(slot_key, (DOCS,), 0, QUEST)
    row_hit = lax_rows(MICRO, DOCS) == row_pick[None, :]
    slot_hit = jnp.arange(QUEST, dtype=jnp.int32)[None, :] == slot_pick[:, None]
    chosen = row_hit[:, :, None] & slot_hit[None, :, :]
    return jnp.where(chosen, DEC_LEN, values).astype(jnp.int32)


def touch_ends(values, key, least, largest):
    shape = values.shape
    place = [jax.random.randint(jax.random.fold_in(key, axis), (), 0, shape[axis]) for axis in range(len(shape))]
    values = values.at[tuple(place)].set(least)
    longest = shape.index(max(shape))
    place[longest] = (place[longest] + 1) % shape[longest]
    return values.at[tuple(place)].set(largest)


def block_scale(own_key, dims, shards, least, largest):
    factor_of, own = 1.0, jax.random.fold_in(own_key, 6)
    for dim, blocks in shards:
        draws = jnp.exp(jax.random.uniform(jax.random.fold_in(own, dim), (blocks,), jnp.float32, least / len(shards), largest / len(shards)))
        factor_of = factor_of * jnp.repeat(draws, dims[dim] // blocks).reshape([-1 if axis == dim else 1 for axis in range(len(dims))])
    return factor_of


def noise(rng, extent, deviation, bound, cuts=(), held_as=jnp.bfloat16):
    result = jax.random.normal(rng, extent, jnp.float32) * deviation
    if len(cuts) > 0:
        result = block_scale(rng, extent, cuts, -0.22, 0.18) * result
    return jnp.clip(result, min=-bound, max=bound).astype(held_as)


def setup_inputs(seed: int = 0) -> dict:
    key_list = jax.random.split(jax.random.key(seed), 15)
    return {
        "block_input": noise(key_list[0], (2, MICRO, DOCS, ENC_LEN, D), 1.0, 6.0, ((0, 2), (2, 8), (3, 2))),
        "out_cotangent": noise(key_list[1], (2, MICRO, DOCS, ENC_LEN, D), 1.0, 6.0, ((0, 2), (2, 8), (3, 2))),
        "doc_lengths": draw_doc_lengths(jax.random.fold_in(key_list[14], 71), 0),
        "question_lengths": draw_question_lengths(jax.random.fold_in(key_list[14], 71), 0),
        "coordinates": touch_ends(jax.random.randint(key_list[4], (MICRO, DOCS, 2, ENC_LEN), 0, 1000), jax.random.fold_in(key_list[4], 1), 0, 999).astype(jnp.int32),
        "gains": jnp.clip(1.0 + 0.1 * jax.random.normal(key_list[5], (5, D), jnp.float32), 0.5, 1.5),
        "bias_tables": noise(key_list[6], (4, BUCKETS, HEADS), 0.7, 4.0, (), jnp.float32),
        "self_qkv": noise(key_list[7], (2, D, 3, HEADS * HEAD), (8 * D) ** -0.5, 0.078125, ((0, 2), (3, 2))),
        "self_out": noise(key_list[8], (2, HEADS * HEAD, D), 1 ** -0.5, 6.0, ((0, 2), (1, 2))),
        "ffn_in": noise(key_list[9], (2, D, FF), D ** -0.5, 0.21875, ((0, 2), (2, 2))),
        "ffn_out": noise(key_list[10], (2, FF, D), FF ** -0.5, 0.109375, ((0, 2), (1, 2))),
        "cross_q": noise(key_list[11], (D, HEADS * HEAD), (8 * D) ** -0.5, 0.078125, ((1, 2),)),
        "cross_kv": noise(key_list[12], (D, 2, HEADS * HEAD), (8 * D) ** -0.5, 0.078125, ((2, 2),)),
        "cross_out": noise(key_list[13], (HEADS * HEAD, D), 1 ** -0.5, 6.0, ((0, 2),)),
    }


NEGATIVE = -1e+30
EPSILON = 1e-06
HIGHEST = lax.Precision.HIGHEST

@jax.custom_vjp
def low(v):
    return lax.optimization_barrier(v.astype(jnp.bfloat16)).astype(jnp.float32)

@jax.custom_vjp
def low_back(v):
    return v

def low_keep(v):
    return (low(v), None)

def low_pass(kept, grad):
    return (grad,)

def back_keep(v):
    return (v, None)

def back_low(kept, grad):
    return (low(grad),)
low.defvjp(low_keep, low_pass)
low_back.defvjp(back_keep, back_low)

def edge_list(exact_span, bucket_count, far_reach):
    log_edges = [int(math.ceil(exact_span * (far_reach / exact_span) ** (power_index / (bucket_count - exact_span)))) for power_index in range(1, bucket_count - exact_span)]
    return list(range(1, exact_span + 1)) + log_edges

def magnitude(distance, thresholds):
    bucket_sum = jnp.zeros(distance.shape, jnp.int32)
    for threshold in thresholds:
        bucket_sum = bucket_sum + (distance >= threshold).astype(jnp.int32)
    return bucket_sum

def two_sided(relative, far_reach):
    return magnitude(jnp.abs(relative), edge_list(8, 16, far_reach)) + 16 * (relative > 0).astype(jnp.int32)

def one_sided(relative):
    return magnitude(jnp.maximum(-relative, 0), edge_list(16, 32, 128))

def lookup(bias_table, buckets):
    one_hot = (buckets[..., None] == lax.iota(jnp.int32, bias_table.shape[0])).astype(bias_table.dtype)
    return jnp.einsum('qkb,bh->hqk', one_hot, bias_table, precision=HIGHEST)

def rms_norm(inputs, gain_row):
    return inputs * lax.rsqrt(lax.optimization_barrier(jnp.mean(inputs * inputs, axis=-1, keepdims=True)) + EPSILON) * gain_row

def encoder_bias(coords, offset, block_rows, tables):
    span_len = coords.shape[1]
    query_pos = offset + lax.iota(jnp.int32, block_rows)
    key_pos = lax.iota(jnp.int32, span_len)
    nearby = two_sided(key_pos[None, :] - query_pos[:, None], 128)
    across = two_sided(coords[0][None, :] - coords[0, offset:offset + block_rows][:, None], 500)
    upward = two_sided(coords[1][None, :] - coords[1, offset:offset + block_rows][:, None], 500)
    return lookup(tables[0], nearby) + lookup(tables[1], across) + lookup(tables[2], upward)

def decoder_bias(block_rows, tables):
    position = lax.iota(jnp.int32, block_rows)
    return lookup(tables[3], one_sided(position[None, :] - position[:, None]))

def encoder_blocks(doc_len, coords, span_len, base_row):
    block_rows = min(512, span_len)
    key_mask = (lax.iota(jnp.int32, span_len) < doc_len)[None, :]
    return [(base_row + offset, base_row + offset + block_rows, base_row, base_row + span_len, partial(encoder_bias, coords, offset, block_rows), key_mask) for offset in range(0, span_len, block_rows)]

def decoder_blocks(quest_lens, span_len, base_row):
    quest_rows = span_len // quest_lens.shape[0]
    position = lax.iota(jnp.int32, quest_rows)
    causal = position[None, :] <= position[:, None]
    block_list = []
    for question in range(quest_lens.shape[0]):
        first_row = base_row + question * quest_rows
        block_list.append((first_row, first_row + quest_rows, first_row, first_row + quest_rows, partial(decoder_bias, quest_rows), causal & (position[None, :] < quest_lens[question])))
    return block_list

def cross_blocks(doc_len, quest_total, span_len, base_row):
    quest_rows = span_len // quest_total
    key_mask = (lax.iota(jnp.int32, span_len) < doc_len)[None, :]
    return [(base_row + question * quest_rows, base_row + (question + 1) * quest_rows, base_row, base_row + span_len, None, key_mask) for question in range(quest_total)]

def block_attend(queries, key_rows, value_rows, bias_block, key_mask):
    scores = low_back(jnp.einsum('qhd,khd->hqk', queries, key_rows, precision=HIGHEST)) + bias_block
    scores = jnp.where(key_mask[None], scores, NEGATIVE)
    probability = low(jax.nn.softmax(scores, axis=-1))
    return jnp.einsum('hqk,khd->qhd', probability, value_rows, precision=HIGHEST)

def attend(queries, key_rows, value_rows, tables, blocks):
    pieces = []
    for first_row, last_row, key_first, key_last, bias_fn, key_mask in blocks:
        bias_block = bias_fn(tables) if bias_fn is not None else jnp.zeros((), queries.dtype)
        pieces.append(jax.checkpoint(block_attend)(queries[first_row:last_row], key_rows[key_first:key_last], value_rows[key_first:key_last], bias_block, key_mask))
    return jnp.concatenate(pieces, axis=0)

def attention_branch(inputs, gain_row, w_qkv, w_out, tables, blocks):
    row_total = inputs.shape[0]
    normed = low(rms_norm(inputs, gain_row))
    projected = low(low_back(jnp.einsum('rd,dtc->rtc', normed, w_qkv, precision=HIGHEST)))
    heads_view = projected.reshape(row_total, 3, HEADS, HEAD)
    attended = attend(heads_view[:, 0], heads_view[:, 1], heads_view[:, 2], tables, blocks)
    merged = low(low_back(attended.reshape(row_total, HEADS * HEAD)))
    return low_back(jnp.dot(merged, w_out, precision=HIGHEST, preferred_element_type=jnp.float32))

def cross_branch(inputs, memory_low, gain_row, w_query, w_pair, w_out, blocks):
    row_total = inputs.shape[0]
    normed = low(rms_norm(inputs, gain_row))
    queries = low(low_back(jnp.dot(normed, w_query, precision=HIGHEST, preferred_element_type=jnp.float32))).reshape(row_total, HEADS, HEAD)
    pair_rows = low(low_back(jnp.einsum('rd,dtc->rtc', memory_low, w_pair, precision=HIGHEST))).reshape(memory_low.shape[0], 2, HEADS, HEAD)
    attended = attend(queries, pair_rows[:, 0], pair_rows[:, 1], None, blocks)
    merged = low(low_back(attended.reshape(row_total, HEADS * HEAD)))
    return low_back(jnp.dot(merged, w_out, precision=HIGHEST, preferred_element_type=jnp.float32))

def feed_forward(inputs, gain_row, w_in, w_down):
    normed = low(rms_norm(inputs, gain_row))
    hidden = low_back(jnp.dot(normed, w_in, precision=HIGHEST, preferred_element_type=jnp.float32))
    activated = low(jax.nn.gelu(hidden))
    return low_back(jnp.dot(activated, w_down, precision=HIGHEST, preferred_element_type=jnp.float32))

def layers(enc_x, dec_x, weights, doc_len, quest_lens, coords):
    gains, tables, self_qkv, self_out, ffn_in, ffn_out, cross_q, cross_kv, cross_out = weights
    span_len = enc_x.shape[0]
    middle = enc_x + attention_branch(enc_x, gains[0], self_qkv[0], self_out[0], tables, encoder_blocks(doc_len, coords, span_len, 0))
    memory = middle + feed_forward(middle, gains[1], ffn_in[0], ffn_out[0])
    memory_low = low(memory)
    first_mid = dec_x + attention_branch(dec_x, gains[2], self_qkv[1], self_out[1], tables, decoder_blocks(quest_lens, span_len, 0))
    second = first_mid + cross_branch(first_mid, memory_low, gains[3], cross_q, cross_kv, cross_out, cross_blocks(doc_len, quest_lens.shape[0], span_len, 0))
    output = second + feed_forward(second, gains[4], ffn_in[1], ffn_out[1])
    return (memory, output)

def reference(block_input, out_cotangent, doc_lengths, question_lengths, coordinates, gains, bias_tables, self_qkv, self_out, ffn_in, ffn_out, cross_q, cross_kv, cross_out):
    params = tuple((weight.astype(jnp.float32) for weight in (gains, bias_tables, self_qkv, self_out, ffn_in, ffn_out, cross_q, cross_kv, cross_out)))
    total_docs = MICRO * DOCS
    records = (block_input[0].reshape(total_docs, ENC_LEN, D), block_input[1].reshape(total_docs, ENC_LEN, D), out_cotangent[0].reshape(total_docs, ENC_LEN, D), out_cotangent[1].reshape(total_docs, ENC_LEN, D), doc_lengths.reshape(total_docs), question_lengths.reshape(total_docs, QUEST), coordinates.reshape(total_docs, 2, ENC_LEN))

    def document_step(totals, record):
        enc_in, dec_in, enc_cot, dec_cot, doc_len, quest_lens, coords = record

        def forward(enc_x, dec_x, *weights):
            return layers(enc_x, dec_x, weights, doc_len, quest_lens, coords)
        results, pull_back = jax.vjp(forward, enc_in.astype(jnp.float32), dec_in.astype(jnp.float32), *params)
        gradients = pull_back((enc_cot.astype(jnp.float32), dec_cot.astype(jnp.float32)))
        totals = tuple((running + fresh for running, fresh in zip(totals, gradients[2:])))
        return (totals, (results[0].astype(jnp.bfloat16), results[1].astype(jnp.bfloat16), gradients[0], gradients[1]))
    totals, outputs = lax.scan(document_step, tuple((jnp.zeros_like(weight) for weight in params)), records)
    enc_out, dec_out, enc_grad, dec_grad = outputs
    layout = (MICRO, DOCS, ENC_LEN, D)
    block_output = jnp.stack([enc_out.reshape(layout), dec_out.reshape(layout)])
    input_grad = jnp.stack([enc_grad.reshape(layout), dec_grad.reshape(layout)])
    return (block_output, input_grad, totals[0][:4], totals[0][4], totals[1], totals[2], totals[3], totals[4], totals[5], totals[6], totals[7], totals[8])
```

```python
from functools import partial
import math

import jax
import jax.numpy as jnp
from jax import lax
from jax.experimental import pallas as pl
from jax.experimental.pallas import tpu as pltpu
from jax.sharding import PartitionSpec as P

HEAD = 64
LANES = 128
NEGATIVE = -1e30
EPSILON = 1e-06
TQ = 512
TI = 128
VMEM_LIMIT = 56 * 1024 * 1024
NT = (((1,), (1,)), ((), ()))
NN = (((1,), (0,)), ((), ()))


def edge_list(exact_span, bucket_count, far_reach):
    log_edges = [
        int(
            math.ceil(
                exact_span * (far_reach / exact_span) ** (power_index / (bucket_count - exact_span))
            )
        )
        for power_index in range(1, bucket_count - exact_span)
    ]
    return list(range(1, exact_span + 1)) + log_edges


def magnitude(distance, exact_span, bucket_count, far_reach):
    bucket = jnp.minimum(distance, exact_span)
    for threshold in edge_list(exact_span, bucket_count, far_reach)[exact_span:]:
        bucket = bucket + (distance >= threshold).astype(jnp.int32)
    return bucket


def two_sided(relative, far_reach):
    return magnitude(jnp.abs(relative), 8, 16, far_reach) + jnp.where(relative > 0, 16, 0)


def one_sided(relative):
    return magnitude(jnp.maximum(-relative, 0), 16, 32, 128)


def half_lanes(block, head):
    lane = lax.broadcasted_iota(jnp.int32, block.shape, 1)
    keep = lane < HEAD if head == 0 else lane >= HEAD
    return jnp.where(keep, block, jnp.zeros_like(block))


def dot(a, b, dims=NN):
    return lax.dot_general(a, b, dims, preferred_element_type=jnp.float32)


def pick_lanes(row, index):
    return jnp.take_along_axis(jnp.broadcast_to(row, index.shape), index, axis=1)


def pick_sublanes(table_ref, head, low, odd, upper):
    parts = [
        jnp.take_along_axis(table_ref[head, 8 * part : 8 * part + 8, :], low, axis=0)
        for part in range(4)
    ]
    return jnp.where(upper, jnp.where(odd, parts[3], parts[2]), jnp.where(odd, parts[1], parts[0]))


def fwd_kernel(kind, tq, span, heads, len_ref, tabn_ref, tabx_ref, taby_ref, crow_ref, ccol_ref, q_ref, k_ref, v_ref, o_ref, p_ref, s_ref, idx_ref, mask_ref, near_ref, bias_ref):
    step, pair = pl.program_id(0), pl.program_id(1)
    per = span // tq
    inner = lax.rem(step, per)
    chunk = 16

    if kind != "cross":
        @pl.when((step == 0) & (pair == 0))
        def _():
            def near_rows(r, carry):
                rows = pl.ds(pl.multiple_of(r * 8, 8), 8)
                query = r * 8 + lax.broadcasted_iota(jnp.int32, (8, LANES), 0)
                for d in range(-2, 3):
                    key = d * LANES + lax.broadcasted_iota(jnp.int32, (8, LANES), 1)
                    bucket = one_sided(key - query) if kind == "dec" else two_sided(key - query, 128)
                    for head in range(heads):
                        value = pick_lanes(tabn_ref[head : head + 1, :], bucket)
                        if kind == "dec":
                            value = jnp.where(key <= query, value, NEGATIVE)
                        near_ref[head, rows, (d + 2) * LANES : (d + 3) * LANES] = value
                return carry

            lax.fori_loop(0, LANES // 8, near_rows, 0)

    @pl.when(pair == 0)
    def _():
        key = lax.broadcasted_iota(jnp.int32, (8, span), 1)
        limit = len_ref[1 + lax.div(step, per)] if kind == "dec" else len_ref[0]
        mask_ref[...] = jnp.where(key < limit, 0.0, NEGATIVE)
        if kind == "enc":

            def bucket_rows(r, carry):
                rows = pl.ds(pl.multiple_of(r * chunk, chunk), chunk)
                for axis in range(2):
                    far = crow_ref[axis : axis + 1, :] - ccol_ref[rows, axis : axis + 1]
                    idx_ref[axis, rows, :] = two_sided(far, 500)
                return carry

            lax.fori_loop(0, tq // chunk, bucket_rows, 0)

            def bias_rows(r, carry):
                rows = pl.ds(pl.multiple_of(r * 8, 8), 8)
                for c in range(0, span, LANES):
                    lanes = slice(c, c + LANES)
                    across = idx_ref[0, rows, lanes]
                    upward = idx_ref[1, rows, lanes]
                    low, odd, upper = upward & 7, (upward & 8) != 0, upward >= 16
                    for head in range(heads):
                        bias_ref[head, rows, lanes] = pick_lanes(
                            tabx_ref[head : head + 1, :], across
                        ) + pick_sublanes(taby_ref, head, low, odd, upper)
                return carry

            lax.fori_loop(0, tq // 8, bias_rows, 0, unroll=2)

    for head in range(2):
        s_ref[head] = dot(half_lanes(q_ref[...], head), k_ref[...], NT)
        for r in range(0, tq, chunk):
            rows = slice(r, r + chunk)
            pieces = []
            for c in range(0, span, LANES):
                lanes = slice(c, c + LANES)
                piece = s_ref[head, rows, lanes] + mask_ref[0:1, lanes]
                if kind != "cross":
                    apart = jnp.clip(c // LANES - (inner * (tq // LANES) + r // LANES), -2, 2) + 2
                    apart = pl.multiple_of(apart * LANES, LANES)
                    piece = piece + near_ref[2 * pair + head, r % LANES : r % LANES + chunk, pl.ds(apart, LANES)]
                if kind == "enc":
                    piece = piece + bias_ref[2 * pair + head, rows, lanes]
                pieces.append(piece)
            score = jnp.concatenate(pieces, axis=1)
            score = jnp.exp(score - jnp.max(score, axis=1, keepdims=True))
            score = score * (1.0 / jnp.sum(score, axis=1, keepdims=True))
            p_ref[head, rows, :] = score.astype(jnp.bfloat16)
    first = dot(p_ref[0], v_ref[...])
    second = dot(p_ref[1], v_ref[...])
    lane = lax.broadcasted_iota(jnp.int32, first.shape, 1)
    o_ref[...] = jnp.where(lane < HEAD, first, second).astype(jnp.bfloat16)


def bwd_kernel(tq, span, p_ref, do_ref, o_ref, q_ref, k_ref, v_ref, dq_ref, dk_ref, dv_ref, low_ref, dp_ref, dkt_ref, dvt_ref):
    step, pair = pl.program_id(0), pl.program_id(1)
    per = span // tq
    inner = lax.rem(step, per)
    chunk = 16

    @pl.when(inner == 0)
    def _():
        dkt_ref[pair] = jnp.zeros((LANES, span), jnp.float32)
        dvt_ref[pair] = jnp.zeros((LANES, span), jnp.float32)

    q_t = jnp.transpose(q_ref[...].astype(jnp.float32)).astype(jnp.bfloat16)
    do_t = jnp.transpose(do_ref[...].astype(jnp.float32)).astype(jnp.bfloat16)
    grads = []
    for head in range(2):
        d_out = half_lanes(do_ref[...], head)
        delta = jnp.sum(d_out.astype(jnp.float32) * o_ref[...].astype(jnp.float32), axis=1, keepdims=True)
        dp_ref[head] = dot(d_out, v_ref[...], NT)
        for r in range(0, tq, chunk):
            rows = slice(r, r + chunk)
            prob = p_ref[head, rows, :].astype(jnp.float32)
            low_ref[head, rows, :] = (prob * (dp_ref[head, rows, :] - delta[rows, :])).astype(jnp.bfloat16)
        grads.append(dot(low_ref[head], k_ref[...]))
        half = pl.ds(head * HEAD, HEAD)
        rows = slice(head * HEAD, (head + 1) * HEAD)
        dkt_ref[pair, half, :] += dot(q_t[rows], low_ref[head])
        dvt_ref[pair, half, :] += dot(do_t[rows], p_ref[head])
    lane = lax.broadcasted_iota(jnp.int32, grads[0].shape, 1)
    dq_ref[...] = jnp.where(lane < HEAD, grads[0], grads[1]).astype(jnp.bfloat16)

    @pl.when(inner == per - 1)
    def _():
        dk_ref[...] = jnp.transpose(dkt_ref[pair]).astype(jnp.bfloat16)
        dv_ref[...] = jnp.transpose(dvt_ref[pair]).astype(jnp.bfloat16)


def table_kernel(kind, ti, span, heads, low_ref, crow_ref, ccol_ref, tab_ref, diag_ref, row_ref, wide_ref, idx_ref):
    step = pl.program_id(0)
    group = 16
    wide = diag_ref.shape[2]
    pad = wide - span

    @pl.when(step == 0)
    def _():
        tab_ref[...] = jnp.zeros_like(tab_ref)

    if kind == "enc":
        for r in range(0, ti, 16):
            for axis in range(2):
                far = crow_ref[axis : axis + 1, :] - ccol_ref[r : r + 16, axis : axis + 1]
                idx_ref[axis, r : r + 16, :] = two_sided(far, 500).astype(jnp.float32)
    out_row = lax.broadcasted_iota(jnp.int32, (256, 256), 0)
    in_row = lax.broadcasted_iota(jnp.int32, (256, 256), 1)
    swap = (lax.div(out_row, 16) == lax.rem(in_row, 16)) & (lax.rem(out_row, 16) == lax.div(in_row, 16))
    swap = jnp.where(swap, 1.0, 0.0).astype(jnp.bfloat16)
    blank = jnp.zeros(((16 - heads) * 16, span), jnp.bfloat16)
    which = lax.broadcasted_iota(jnp.int32, (32, span), 0).astype(jnp.bfloat16)

    def body(g, carry):
        tab, diag = carry
        first = pl.multiple_of(g * group, group)
        block = jnp.concatenate([low_ref[h, pl.ds(first, group), :] for h in range(heads)] + [blank], axis=0)
        wide_ref[...] = dot(swap, block)
        if kind == "enc":
            row_ref[...] = wide_ref[...].astype(jnp.bfloat16)
        for j in range(group):
            part = slice(16 * j, 16 * j + 16)
            if kind == "enc":
                hot = []
                for axis in range(2):
                    bucket = jnp.broadcast_to(idx_ref[axis, pl.ds(first + j, 1), :], (32, span)).astype(jnp.bfloat16)
                    hot.append(jnp.where(bucket == which, jnp.bfloat16(1), jnp.bfloat16(0)))
                tab = tab + dot(row_ref[part, :], jnp.concatenate(hot, axis=0), NT)
            line = wide_ref[part, :]
            if pad:
                line = jnp.concatenate([line, jnp.zeros((16, pad), jnp.float32)], axis=1)
            diag = diag + pltpu.roll(line, lax.rem(wide - (first + j), wide), 1)
        return tab, diag

    tab, diag = lax.fori_loop(
        0, ti // group, body,
        (jnp.zeros(tab_ref.shape, jnp.float32), jnp.zeros((16, wide), jnp.float32)),
    )
    tab_ref[...] += tab
    diag_ref[0] = diag


def near_width(kind, tq, span):
    return span + tq if kind == "enc" else span


def near_buckets(kind, tq, span, steps):
    wide = near_width(kind, tq, span)
    column = lax.broadcasted_iota(jnp.int32, (steps, wide), 1)
    inner = lax.rem(lax.broadcasted_iota(jnp.int32, (steps, wide), 0), span // tq)
    relative = jnp.where(column > wide - tq, column - wide, column) - inner * tq
    bucket = one_sided(relative) if kind == "dec" else two_sided(relative, 128)
    return (bucket[..., None] == lax.iota(jnp.int32, 32)).astype(jnp.float32)


def diag_sums(kind, diag, ti, span):
    hot = near_buckets(kind, ti, span, diag.shape[0])
    return jnp.einsum("swb,shw->bh", hot, diag, precision=lax.Precision.HIGHEST)


def column(source, which, pairs, pair):
    kinds = source.shape[1] // (pairs * LANES)
    half = pairs // 2
    return which * half + pair + jnp.where(pair >= half, (kinds - 1) * half, 0)


def attend_forward(kind, tq, lens, tables, coords, q_src, q_col, kv_src, k_col, v_col, pairs, quests, wide_scores):
    rows = q_src.shape[0]
    heads = 2 * pairs
    span = rows // quests if kind == "dec" else kv_src.shape[0]
    per = span // tq
    steps = rows // tq
    key_row = (lambda i: i // per) if kind == "dec" else (lambda i: 0)
    flops = 4 * rows * span * pairs * LANES
    tab_n = tab_x = jnp.zeros((16, LANES), jnp.float32)
    tab_y = jnp.zeros((1, 8, LANES), jnp.float32)
    if kind != "cross":
        tab_n = jnp.pad(tables[0].T, ((0, 16 - heads), (0, LANES - 32)))
    if kind == "enc":
        tab_x = jnp.pad(tables[1].T, ((0, 16 - heads), (0, LANES - 32)))
        tab_y = jnp.broadcast_to(tables[2].T[:, :, None], (heads, 32, LANES))
    return pl.pallas_call(
        partial(fwd_kernel, kind, tq, span, heads),
        grid=(steps, pairs),
        in_specs=[
            pl.BlockSpec(memory_space=pltpu.SMEM),
            pl.BlockSpec(tab_n.shape, lambda i, h: (0, 0)),
            pl.BlockSpec(tab_x.shape, lambda i, h: (0, 0)),
            pl.BlockSpec(tab_y.shape, lambda i, h: (0, 0, 0)),
            pl.BlockSpec(coords.shape, lambda i, h: (0, 0)),
            pl.BlockSpec((tq, 2), lambda i, h: (i, 0)),
            pl.BlockSpec((tq, LANES), lambda i, h: (i, column(q_src, q_col, pairs, h))),
            pl.BlockSpec((span, LANES), lambda i, h: (key_row(i), column(kv_src, k_col, pairs, h))),
            pl.BlockSpec((span, LANES), lambda i, h: (key_row(i), column(kv_src, v_col, pairs, h))),
        ],
        out_specs=[
            pl.BlockSpec((tq, LANES), lambda i, h: (i, h)),
            pl.BlockSpec((2, tq, span), lambda i, h: (h, i, 0)),
        ],
        out_shape=[
            jax.ShapeDtypeStruct((rows, pairs * LANES), jnp.bfloat16),
            jax.ShapeDtypeStruct((heads, rows, rows if wide_scores else span), jnp.bfloat16),
        ],
        scratch_shapes=[
            pltpu.VMEM((2, tq, span), jnp.float32),
            pltpu.VMEM((2, tq, span) if kind == "enc" else (1, 8, LANES), jnp.int32),
            pltpu.VMEM((8, span), jnp.float32),
            pltpu.VMEM((1, 8, LANES) if kind == "cross" else (heads, LANES, 5 * LANES), jnp.float32),
            pltpu.VMEM((heads, tq, span) if kind == "enc" else (1, 8, LANES), jnp.float32),
        ],
        compiler_params=pltpu.CompilerParams(vmem_limit_bytes=VMEM_LIMIT),
        cost_estimate=pl.CostEstimate(
            flops=flops, bytes_accessed=4 * rows * span * pairs, transcendentals=2 * rows * span * pairs
        ),
        name="attend_forward_" + kind,
    )(lens, tab_n, tab_x, tab_y, coords, coords.T, q_src, kv_src, kv_src)


def attend_backward(kind, tq, prob, grad_out, out, q_src, q_col, kv_src, k_col, v_col, pairs, quests, wide_scores):
    rows = q_src.shape[0]
    span = rows // quests if kind == "dec" else kv_src.shape[0]
    per = span // tq
    steps = rows // tq
    key_row = (lambda i: i // per) if kind == "dec" else (lambda i: 0)
    key_out = pl.BlockSpec((span, LANES), lambda i, h: (key_row(i), jnp.where(lax.rem(i, per) == per - 1, h, 0)))
    score_block = pl.BlockSpec((2, tq, span), lambda i, h: (h, i, 0))
    if kind == "cross":
        score_out = pl.BlockSpec((2, tq, span), lambda i, h: (0, 0, 0))
        score_shape = (2, tq, span)
    else:
        score_out = score_block
        score_shape = (2 * pairs, rows, rows if wide_scores else span)
    flops = 10 * rows * span * pairs * LANES
    key_rows = rows if kind == "dec" else span
    return pl.pallas_call(
        partial(bwd_kernel, tq, span),
        grid=(steps, pairs),
        in_specs=[
            score_block,
            pl.BlockSpec((tq, LANES), lambda i, h: (i, h)),
            pl.BlockSpec((tq, LANES), lambda i, h: (i, h)),
            pl.BlockSpec((tq, LANES), lambda i, h: (i, column(q_src, q_col, pairs, h))),
            pl.BlockSpec((span, LANES), lambda i, h: (key_row(i), column(kv_src, k_col, pairs, h))),
            pl.BlockSpec((span, LANES), lambda i, h: (key_row(i), column(kv_src, v_col, pairs, h))),
        ],
        out_specs=[pl.BlockSpec((tq, LANES), lambda i, h: (i, h)), key_out, key_out, score_out],
        out_shape=[
            jax.ShapeDtypeStruct((rows, pairs * LANES), jnp.bfloat16),
            jax.ShapeDtypeStruct((key_rows, pairs * LANES), jnp.bfloat16),
            jax.ShapeDtypeStruct((key_rows, pairs * LANES), jnp.bfloat16),
            jax.ShapeDtypeStruct(score_shape, jnp.bfloat16),
        ],
        scratch_shapes=[
            pltpu.VMEM((2, tq, span), jnp.float32),
            pltpu.VMEM((pairs, LANES, span), jnp.float32),
            pltpu.VMEM((pairs, LANES, span), jnp.float32),
        ],
        compiler_params=pltpu.CompilerParams(vmem_limit_bytes=VMEM_LIMIT),
        cost_estimate=pl.CostEstimate(
            flops=flops, bytes_accessed=4 * rows * span * pairs, transcendentals=0
        ),
        name="attend_backward_" + kind,
    )(prob, grad_out, out, q_src, kv_src, kv_src)


def table_sums(kind, ti, coords, low, quests):
    heads, rows, span = low.shape
    span = span // quests if kind == "dec" else span
    steps = rows // ti
    wide = near_width(kind, ti, span)
    tab, diag = pl.pallas_call(
        partial(table_kernel, kind, ti, span, heads),
        grid=(steps,),
        in_specs=[
            pl.BlockSpec((heads, ti, span), lambda i: (0, i, 0)),
            pl.BlockSpec(coords.shape, lambda i: (0, 0)),
            pl.BlockSpec((ti, 2), lambda i: (i, 0)),
        ],
        out_specs=[
            pl.BlockSpec((16, 64), lambda i: (0, 0)),
            pl.BlockSpec((1, 16, wide), lambda i: (i, 0, 0)),
        ],
        out_shape=[
            jax.ShapeDtypeStruct((16, 64), jnp.float32),
            jax.ShapeDtypeStruct((steps, 16, wide), jnp.float32),
        ],
        scratch_shapes=[
            pltpu.VMEM((256, span), jnp.bfloat16),
            pltpu.VMEM((256, span), jnp.float32),
            pltpu.VMEM((2, ti, span) if kind == "enc" else (1, 8, LANES), jnp.float32),
        ],
        compiler_params=pltpu.CompilerParams(vmem_limit_bytes=VMEM_LIMIT),
        cost_estimate=pl.CostEstimate(
            flops=rows * span * 4096, bytes_accessed=2 * heads * rows * span, transcendentals=0
        ),
        name="table_sums_" + kind,
    )(low, coords, coords.T)
    near = diag_sums(kind, diag, ti, span)[:, :heads]
    if kind == "dec":
        return near
    return near, tab[:heads, :32].T, tab[:heads, 32:].T


def pair_permute(x, axis, bit):
    pairs = [(i, i ^ (1 << bit)) for i in range(lax.axis_size(axis))]
    return lax.ppermute(x, axis, pairs)


def shifted(x, axis, by):
    peers = lax.axis_size(axis)
    pairs = [(i, i + by) for i in range(peers) if 0 <= i + by < peers]
    return lax.ppermute(x, axis, pairs)


def in_order(flag, first, second, axis):
    return jnp.where(
        flag == 0,
        jnp.concatenate([first, second], axis=axis),
        jnp.concatenate([second, first], axis=axis),
    )


def pick(x, index, axis):
    return lax.dynamic_index_in_dim(x, index, axis, False)


def gather_rows(block, where_mp):
    own = pick(block, where_mp, 0)
    arrived = pair_permute(pick(block, 1 - where_mp, 0), "mp", 0)
    return in_order(where_mp, own, arrived, 0)


def scatter_rows(rows, where_mp, sent_as):
    halves = rows.reshape(2, -1, rows.shape[1])
    own = pick(halves, where_mp, 0)
    arrived = pair_permute(pick(halves, 1 - where_mp, 0).astype(sent_as), "mp", 0).astype(rows.dtype)
    return in_order(where_mp, own[None], arrived[None], 0)


def other_shard(shard, core):
    half = shard.shape[0] // 2
    far = pair_permute(lax.dynamic_slice_in_dim(shard, core * half, half, 0), "mp", 0)
    near = pair_permute(far, "dp", 0)
    return in_order(core, far, near, 0)


def both_shards(shard, core, axis):
    return jnp.concatenate([shard, other_shard(shard, core)], axis=axis)


def reduce_rows(left_t, right, core, dp_index, section=None):
    parts = lax.axis_size("dp")
    bits = parts.bit_length() - 1
    groups = 1 if section is None else 2
    row_count, span = left_t.shape
    slices = left_t.reshape(groups * parts // 2, 2, row_count // (groups * parts), span)
    peer = pick(slices, 1 - core, 1).reshape(-1, span)
    mine = pick(slices, core, 1).reshape(-1, span)
    send = dot(peer, right).astype(jnp.bfloat16)
    total = dot(mine, right) + pair_permute(send, "dp", 0).astype(jnp.float32)
    if section is not None:
        halves = total.reshape(2, -1, total.shape[1])
        moved = shifted(halves[0].astype(jnp.bfloat16), "section", -1).astype(jnp.float32)
        total = jnp.where(section == 0, moved, halves[1])
    width = total.shape[1] // 2
    arrived = pair_permute(total[:, width:].astype(jnp.bfloat16), "mp", 0)
    total = total[:, :width] + arrived.astype(jnp.float32)
    for bit in range(1, bits):
        mark = (dp_index >> bit) & 1
        halves = total.reshape(parts >> (bit + 1), 2, -1, width)
        arrived = pair_permute(pick(halves, 1 - mark, 1).astype(jnp.bfloat16), "dp", bit)
        total = (pick(halves, mark, 1) + arrived.astype(jnp.float32)).reshape(-1, width)
    return total


def rms_norm(inputs, gain_row):
    return (
        inputs * lax.rsqrt(jnp.mean(inputs * inputs, axis=-1, keepdims=True) + EPSILON) * gain_row
    )


def norm_back(rows, gain_row, grad_normed):
    return jax.vjp(rms_norm, rows, gain_row)[1](grad_normed)


def low(x):
    return x.astype(jnp.bfloat16)


def local(
    block_input,
    out_cotangent,
    doc_lengths,
    question_lengths,
    coordinates,
    gains,
    bias_tables,
    self_qkv,
    self_out,
    ffn_in,
    ffn_out,
    cross_q,
    cross_kv,
    cross_out,
):
    section = lax.axis_index("section")
    on_encoder = section == 0
    dp_index = lax.axis_index("dp")
    core = dp_index & 1
    where_mp = lax.axis_index("mp")
    width = block_input.shape[4]
    quests = question_lengths.shape[2]
    own = self_qkv.shape[3]
    pairs = 2 * own // LANES
    heads = 2 * pairs

    rows_low = gather_rows(block_input[0, :, 0], where_mp)
    w_qkv = both_shards(self_qkv[0].reshape(width, -1), core, 1)
    w_out = both_shards(self_out[0], core, 0)
    w_in = both_shards(ffn_in[0], core, 1)
    w_down = both_shards(ffn_out[0], core, 0)
    w_query = both_shards(cross_q, core, 1)
    w_pair = both_shards(cross_kv.reshape(width, -1), core, 1)
    w_cross = both_shards(cross_out, core, 0)
    cot_low = gather_rows(out_cotangent[0, :, 0], where_mp)

    lens = jnp.concatenate(
        [pick(doc_lengths, where_mp, 0), pick(question_lengths, where_mp, 0)[0]]
    ).astype(jnp.int32)
    coords = pick(coordinates, where_mp, 0)[0]
    tables = jnp.where(where_mp == 0, bias_tables, jnp.roll(bias_tables, heads // 2, axis=2))

    rows = rows_low.astype(jnp.float32)
    gain_self = jnp.where(on_encoder, gains[0], gains[2])
    normed_self = low(rms_norm(rows, gain_self))
    projected = low(dot(normed_self, w_qkv))
    merged, prob = lax.cond(
        on_encoder,
        lambda: attend_forward("enc", TQ, lens, tables[:3], coords, projected, 0, projected, 1, 2, pairs, quests, True),
        lambda: attend_forward("dec", TQ, lens, tables[3:], coords, projected, 0, projected, 1, 2, pairs, quests, True),
    )
    middle = rows + dot(merged, w_out)

    memory = middle + dot(low(jax.nn.gelu(dot(low(rms_norm(middle, gains[1])), w_in))), w_down)
    memory_low = low(memory)
    arrived = shifted(memory_low, "section", 1)

    normed_cross = low(rms_norm(middle, gains[3]))
    queries = low(dot(normed_cross, w_query))
    pair_rows = low(dot(arrived, w_pair))
    cross_merged, cross_prob = attend_forward(
        "cross", TQ, lens, None, coords, queries, 0, pair_rows, 0, 1, pairs, quests, False
    )
    second = middle + dot(cross_merged, w_cross)
    hidden = dot(low(rms_norm(second, gains[4])), w_in)
    output = second + dot(low(jax.nn.gelu(hidden)), w_down)
    cot = cot_low.astype(jnp.float32)
    hidden_grad = low(jax.vjp(jax.nn.gelu, hidden)[1](dot(cot_low, w_down, NT))[0])
    grad_second = cot + norm_back(second, gains[4], dot(hidden_grad, w_in, NT))[0]
    second_low = low(grad_second)
    cross_grads = attend_backward(
        "cross", TQ, cross_prob, low(dot(second_low, w_cross, NT)), cross_merged, queries, 0, pair_rows, 0, 1, pairs, quests, False
    )
    half = own
    pair_grad = jnp.concatenate(
        [cross_grads[1][:, :half], cross_grads[2][:, :half], cross_grads[1][:, half:], cross_grads[2][:, half:]], axis=1
    )
    returned = shifted(low(dot(pair_grad, w_pair, NT)), "section", -1)
    input_part, gain_cross = norm_back(middle, gains[3], dot(cross_grads[0], w_query, NT))
    grad_first = grad_second + input_part
    cross_shards = (
        reduce_rows(normed_cross.T, cross_grads[0], core, dp_index, section),
        reduce_rows(arrived.T, pair_grad, core, dp_index, section),
        reduce_rows(second_low.T, cross_merged, core, dp_index, section),
    )

    ffn_rows = jnp.where(on_encoder, middle, second)
    gain_ffn = jnp.where(on_encoder, gains[1], gains[4])
    grad_ffn = cot + returned.astype(jnp.float32)
    grad_ffn_low = low(grad_ffn)
    normed_ffn = low(rms_norm(ffn_rows, gain_ffn))
    hidden = dot(normed_ffn, w_in)
    activated, pull = jax.vjp(jax.nn.gelu, hidden)
    hidden_grad = low(pull(dot(grad_ffn_low, w_down, NT))[0])
    input_part, gain_ffn_grad = norm_back(ffn_rows, gain_ffn, dot(hidden_grad, w_in, NT))
    grad_middle = jnp.where(on_encoder, grad_ffn + input_part, grad_first)
    in_shard = reduce_rows(normed_ffn.T, hidden_grad, core, dp_index)
    down_shard = reduce_rows(grad_ffn_low.T, low(activated), core, dp_index)

    middle_low = low(grad_middle)
    merged_grad = low(dot(middle_low, w_out, NT))
    query_grad, key_grad, value_grad, scores = lax.cond(
        on_encoder,
        lambda: attend_backward("enc", TQ, prob, merged_grad, merged, projected, 0, projected, 1, 2, pairs, quests, True),
        lambda: attend_backward("dec", TQ, prob, merged_grad, merged, projected, 0, projected, 1, 2, pairs, quests, True),
    )
    out_shard = reduce_rows(middle_low.T, merged, core, dp_index)
    stacked = jnp.concatenate(
        [grad[:, :half] for grad in (query_grad, key_grad, value_grad)]
        + [grad[:, half:] for grad in (query_grad, key_grad, value_grad)],
        axis=1,
    )
    qkv_shard = reduce_rows(normed_self.T, stacked, core, dp_index)
    input_part, gain_self_grad = norm_back(rows, gain_self, dot(stacked, w_qkv, NT))
    input_grad = grad_middle + input_part

    def encoder_tables():
        near, across, upward = table_sums("enc", TI, coords, scores, quests)
        return jnp.stack([near, across, upward, jnp.zeros_like(near)])

    def decoder_tables():
        near = table_sums("dec", TI, coords, scores, quests)
        blank = jnp.zeros_like(near)
        return jnp.stack([blank, blank, blank, near])

    table_grad = lax.cond(on_encoder, encoder_tables, decoder_tables)
    table_grad = jnp.where(where_mp == 0, table_grad, jnp.roll(table_grad, heads // 2, axis=2))
    blank = jnp.zeros_like(gain_cross)
    gain_grad = jnp.where(
        on_encoder,
        jnp.stack([gain_self_grad, gain_ffn_grad, blank, blank, blank]),
        jnp.stack([blank, blank, gain_self_grad, gain_cross, gain_ffn_grad]),
    )
    gain_sum, table_sum = lax.psum((gain_grad, table_grad), ("section", "dp", "mp"))

    output_low = jnp.where(on_encoder, memory_low, low(output))
    output_rows = scatter_rows(output_low, where_mp, jnp.bfloat16)
    grad_rows = scatter_rows(input_grad, where_mp, jnp.bfloat16)
    return (
        output_rows[None, :, None],
        grad_rows[None, :, None],
        gain_sum[:4],
        gain_sum[4],
        table_sum,
        qkv_shard.reshape(-1, 3, own)[None],
        out_shard.T[None],
        in_shard[None],
        down_shard.T[None],
        cross_shards[0],
        cross_shards[1].reshape(-1, 2, own),
        cross_shards[2].T,
    )


def solution(mesh):
    return jax.shard_map(
        local,
        mesh=mesh,
        in_specs=(
            P("section", None, "dp", "mp", None),
            P("section", None, "dp", "mp", None),
            P(None, "dp"),
            P(None, "dp", None),
            P(None, "dp", None, None),
            P(),
            P(),
            P("section", None, None, "mp"),
            P("section", "mp", None),
            P("section", None, "mp"),
            P("section", "mp", None),
            P(None, "mp"),
            P(None, None, "mp"),
            P("mp", None),
        ),
        out_specs=(
            P("section", None, "dp", "mp", None),
            P("section", None, "dp", "mp", None),
            P(),
            P(),
            P(),
            P("section", "dp", None, "mp"),
            P("section", "mp", "dp"),
            P("section", "dp", "mp"),
            P("section", "mp", "dp"),
            P(("section", "dp"), "mp"),
            P(("section", "dp"), None, "mp"),
            P("mp", ("section", "dp")),
        ),
        check_vma=False,
    )
```

```python
import functools
from functools import partial
import math

import jax
import jax.numpy as jnp
from jax import lax
from jax.experimental import pallas as pl
from jax.experimental.pallas import tpu as pltpu
from jax.sharding import PartitionSpec as P

HEAD = 64
LANES = 128
NEGATIVE = -1e30
EPSILON = 1e-06
GELU_SCALE = math.sqrt(2 / math.pi)
GELU_CUBE = 0.044715
TI = 64
TR = 256
VMEM_LIMIT = 56 * 1024 * 1024
NT = (((1,), (1,)), ((), ()))
NN = (((1,), (0,)), ((), ()))


def edge_list(exact_span, bucket_count, far_reach):
    log_edges = [
        int(
            math.ceil(
                exact_span * (far_reach / exact_span) ** (power_index / (bucket_count - exact_span))
            )
        )
        for power_index in range(1, bucket_count - exact_span)
    ]
    return list(range(1, exact_span + 1)) + log_edges


def magnitude(distance, exact_span, bucket_count, far_reach):
    bucket = jnp.minimum(distance, exact_span)
    for threshold in edge_list(exact_span, bucket_count, far_reach)[exact_span:]:
        bucket = bucket + (distance >= threshold).astype(jnp.int32)
    return bucket


def two_sided(relative, far_reach):
    return magnitude(jnp.abs(relative), 8, 16, far_reach) + jnp.where(relative > 0, 16, 0)


def one_sided(relative):
    return magnitude(jnp.maximum(-relative, 0), 16, 32, 128)


def half_lanes(block, head):
    lane = lax.broadcasted_iota(jnp.int32, block.shape, 1)
    keep = lane < HEAD if head == 0 else lane >= HEAD
    return jnp.where(keep, block, jnp.zeros_like(block))


def dot(a, b, dims=NN):
    return lax.dot_general(a, b, dims, preferred_element_type=jnp.float32)


def pick_lanes(row, index):
    return jnp.take_along_axis(jnp.broadcast_to(row, index.shape), index, axis=1)


def pick_sublanes(table_ref, head, low, odd, upper):
    parts = [
        jnp.take_along_axis(table_ref[head, 8 * part : 8 * part + 8, :], low, axis=0)
        for part in range(4)
    ]
    return jnp.where(upper, jnp.where(odd, parts[3], parts[2]), jnp.where(odd, parts[1], parts[0]))


def fwd_kernel(kind, part, tq, span, heads, len_ref, tabn_ref, tabx_ref, taby_ref, crow_ref, ccol_ref, q_ref, k_ref, v_ref, o_ref, p_ref, s_ref, idx_ref, mask_ref, near_ref, bias_ref):
    pair = pl.program_id(0)
    first_block = 0 if kind == "dec" else part * tq // LANES
    chunk = 16

    @pl.when(pair == 0)
    def _():
        key = lax.broadcasted_iota(jnp.int32, (8, span), 1)
        limit = len_ref[1 + part] if kind == "dec" else len_ref[0]
        mask_ref[...] = jnp.where(key < limit, 0.0, NEGATIVE)
        if kind != "cross":
            def near_rows(r, carry):
                rows = pl.ds(pl.multiple_of(r * 8, 8), 8)
                query = r * 8 + lax.broadcasted_iota(jnp.int32, (8, LANES), 0)
                for d in range(-2, 3):
                    key = d * LANES + lax.broadcasted_iota(jnp.int32, (8, LANES), 1)
                    bucket = one_sided(key - query) if kind == "dec" else two_sided(key - query, 128)
                    for head in range(heads):
                        value = pick_lanes(tabn_ref[head : head + 1, :], bucket)
                        if kind == "dec":
                            value = jnp.where(key <= query, value, NEGATIVE)
                        near_ref[head, rows, (d + 2) * LANES : (d + 3) * LANES] = value
                return carry

            lax.fori_loop(0, LANES // 8, near_rows, 0)
        if kind == "enc":

            def bucket_rows(r, carry):
                rows = pl.ds(pl.multiple_of(r * chunk, chunk), chunk)
                for axis in range(2):
                    far = crow_ref[axis : axis + 1, :] - ccol_ref[rows, axis : axis + 1]
                    idx_ref[axis, rows, :] = two_sided(far, 500)
                return carry

            lax.fori_loop(0, tq // chunk, bucket_rows, 0)

            def bias_rows(r, carry):
                rows = pl.ds(pl.multiple_of(r * 8, 8), 8)
                for c in range(0, span, LANES):
                    lanes = slice(c, c + LANES)
                    across = idx_ref[0, rows, lanes]
                    upward = idx_ref[1, rows, lanes]
                    low, odd, upper = upward & 7, (upward & 8) != 0, upward >= 16
                    for head in range(heads):
                        bias_ref[head, rows, lanes] = pick_lanes(
                            tabx_ref[head : head + 1, :], across
                        ) + pick_sublanes(taby_ref, head, low, odd, upper)
                return carry

            lax.fori_loop(0, tq // 8, bias_rows, 0, unroll=2)

    for head in range(2):
        s_ref[head] = dot(half_lanes(q_ref[...], head), k_ref[...], NT)
        for r in range(0, tq, chunk):
            rows = slice(r, r + chunk)
            pieces = []
            for c in range(0, span, LANES):
                lanes = slice(c, c + LANES)
                piece = s_ref[head, rows, lanes] + mask_ref[0:1, lanes]
                if kind != "cross":
                    apart = min(max(c // LANES - (first_block + r // LANES), -2), 2) + 2
                    near = slice(apart * LANES, (apart + 1) * LANES)
                    piece = piece + near_ref[2 * pair + head, r % LANES : r % LANES + chunk, near]
                if kind == "enc":
                    piece = piece + bias_ref[2 * pair + head, rows, lanes]
                pieces.append(piece)
            score = jnp.concatenate(pieces, axis=1)
            score = jnp.exp(score - jnp.max(score, axis=1, keepdims=True))
            score = score * (1.0 / jnp.sum(score, axis=1, keepdims=True))
            p_ref[head, rows, :] = score.astype(jnp.bfloat16)
    first = dot(p_ref[0], v_ref[...])
    second = dot(p_ref[1], v_ref[...])
    lane = lax.broadcasted_iota(jnp.int32, first.shape, 1)
    o_ref[...] = jnp.where(lane < HEAD, first, second).astype(jnp.bfloat16)


def bwd_kernel(kind, part, rows, span, p_ref, do_ref, o_ref, q_ref, k_ref, v_ref, *refs):
    carry = refs[: 2 if kind != "cross" else 1] if part else ()
    outs = refs[len(carry) :]
    dq_ref, dk_ref, dv_ref = outs[:3]
    low_ref, dp_ref = outs[3:]
    chunk = 16
    q_t = jnp.transpose(q_ref[...].astype(jnp.float32)).astype(jnp.bfloat16)
    do_t = jnp.transpose(do_ref[...].astype(jnp.float32)).astype(jnp.bfloat16)
    grads, key_grads, value_grads = [], [], []
    for head in range(2):
        d_out = half_lanes(do_ref[...], head)
        delta = jnp.sum(d_out.astype(jnp.float32) * o_ref[...].astype(jnp.float32), axis=1, keepdims=True)
        dp_ref[head] = dot(d_out, v_ref[...], NT)
        for r in range(0, rows, chunk):
            part_rows = slice(r, r + chunk)
            prob = p_ref[head, part_rows, :].astype(jnp.float32)
            low_ref[head, part_rows, :] = (
                prob * (dp_ref[head, part_rows, :] - delta[part_rows, :])
            ).astype(jnp.bfloat16)
        grads.append(dot(low_ref[head], k_ref[...]))
        half = slice(head * HEAD, (head + 1) * HEAD)
        key_grads.append(dot(q_t[half], low_ref[head]))
        value_grads.append(dot(do_t[half], p_ref[head]))
    lane = lax.broadcasted_iota(jnp.int32, grads[0].shape, 1)
    query_grad = jnp.where(lane < HEAD, grads[0], grads[1])
    if kind == "cross" and part:
        query_grad = query_grad + carry[0][...]
    dq_ref[...] = query_grad.astype(dq_ref.dtype)
    for index, (out_ref, pieces) in enumerate(((dk_ref, key_grads), (dv_ref, value_grads))):
        grad = jnp.transpose(jnp.concatenate(pieces, axis=0))
        if kind == "enc" and part:
            grad = grad + carry[index][...]
        if kind == "dec":
            if part:
                out_ref[0:span, :] = carry[index][0:span, :].astype(out_ref.dtype)
            out_ref[part * span : (part + 1) * span, :] = grad.astype(out_ref.dtype)
        else:
            out_ref[...] = grad.astype(out_ref.dtype)


def table_kernel(kind, ti, span, heads, low_ref, crow_ref, ccol_ref, tab_ref, diag_ref, row_ref, wide_ref, idx_ref):
    step = pl.program_id(0)
    group = 16
    wide = diag_ref.shape[2]
    pad = wide - span

    @pl.when(step == 0)
    def _():
        tab_ref[...] = jnp.zeros_like(tab_ref)

    if kind == "enc":
        for r in range(0, ti, 16):
            for axis in range(2):
                far = crow_ref[axis : axis + 1, :] - ccol_ref[r : r + 16, axis : axis + 1]
                idx_ref[axis, r : r + 16, :] = two_sided(far, 500).astype(jnp.float32)
    out_row = lax.broadcasted_iota(jnp.int32, (256, 256), 0)
    in_row = lax.broadcasted_iota(jnp.int32, (256, 256), 1)
    swap = (lax.div(out_row, 16) == lax.rem(in_row, 16)) & (lax.rem(out_row, 16) == lax.div(in_row, 16))
    swap = jnp.where(swap, 1.0, 0.0).astype(jnp.bfloat16)
    blank = jnp.zeros(((16 - heads) * 16, span), jnp.bfloat16)
    which = lax.broadcasted_iota(jnp.int32, (32, span), 0).astype(jnp.bfloat16)

    tab = jnp.zeros(tab_ref.shape, jnp.float32)
    diag = jnp.zeros((16, wide), jnp.float32)
    for g in range(ti // group):
        first = g * group
        block = jnp.concatenate([low_ref[h, first : first + group, :] for h in range(heads)] + [blank], axis=0)
        wide_ref[g] = dot(swap, block)
        if kind == "enc":
            row_ref[g] = wide_ref[g].astype(jnp.bfloat16)
        for j in range(group):
            lines = slice(16 * j, 16 * j + 16)
            if kind == "enc":
                hot = []
                for axis in range(2):
                    bucket = idx_ref[axis, first + j : first + j + 1, :]
                    bucket = jnp.broadcast_to(bucket, (32, span)).astype(jnp.bfloat16)
                    hot.append(jnp.where(bucket == which, jnp.bfloat16(1), jnp.bfloat16(0)))
                tab = tab + dot(row_ref[g, lines, :], jnp.concatenate(hot, axis=0), NT)
            line = wide_ref[g, lines, :]
            if pad:
                line = jnp.concatenate([line, jnp.zeros((16, pad), jnp.float32)], axis=1)
            diag = diag + pltpu.roll(line, (wide - (first + j)) % wide, 1)
    tab_ref[...] += tab
    diag_ref[0] = diag


def near_width(kind, ti, span):
    return span + ti if kind == "enc" else span


def diag_sums(kind, diag, first, ti, span):
    steps, _, wide = diag.shape
    column = lax.broadcasted_iota(jnp.int32, (steps, wide), 1)
    start = (first + lax.broadcasted_iota(jnp.int32, (steps, wide), 0)) * ti
    if kind == "dec":
        relative = jnp.where(column > start, column - wide, column) - start
        bucket = one_sided(relative)
    else:
        relative = jnp.where(column > wide - ti, column - wide, column) - start
        bucket = two_sided(relative, 128)
    hot = (bucket[..., None] == lax.iota(jnp.int32, 32)).astype(jnp.float32)
    return jnp.einsum("swb,shw->bh", hot, diag, precision=lax.Precision.HIGHEST)


def column(source, which, pairs, pair):
    kinds = source.shape[1] // (pairs * LANES)
    half = pairs // 2
    return which * half + pair + jnp.where(pair >= half, (kinds - 1) * half, 0)


def attend_forward(kind, part, tq, lens, tables, coords, q_src, q_col, kv_src, k_col, v_col, pairs, quests):
    heads = 2 * pairs
    key_rows = kv_src.shape[0]
    span = key_rows // quests if kind == "dec" else key_rows
    key_block = part if kind == "dec" else 0
    flops = tq * span * (60000 if kind == "enc" else 25000)
    tab_n = tab_x = jnp.zeros((16, LANES), jnp.float32)
    tab_y = jnp.zeros((1, 8, LANES), jnp.float32)
    if kind != "cross":
        tab_n = jnp.pad(tables[0].T, ((0, 16 - heads), (0, LANES - 32)))
    if kind == "enc":
        tab_x = jnp.pad(tables[1].T, ((0, 16 - heads), (0, LANES - 32)))
        tab_y = jnp.broadcast_to(tables[2].T[:, :, None], (heads, 32, LANES))
    return pl.pallas_call(
        partial(fwd_kernel, kind, part, tq, span, heads),
        grid=(pairs,),
        in_specs=[
            pl.BlockSpec(memory_space=pltpu.SMEM),
            pl.BlockSpec(tab_n.shape, lambda h: (0, 0)),
            pl.BlockSpec(tab_x.shape, lambda h: (0, 0)),
            pl.BlockSpec(tab_y.shape, lambda h: (0, 0, 0)),
            pl.BlockSpec(coords.shape, lambda h: (0, 0)),
            pl.BlockSpec((tq, 2), lambda h: (part, 0)),
            pl.BlockSpec((tq, LANES), lambda h: (part, column(q_src, q_col, pairs, h))),
            pl.BlockSpec((span, LANES), lambda h: (key_block, column(kv_src, k_col, pairs, h))),
            pl.BlockSpec((span, LANES), lambda h: (key_block, column(kv_src, v_col, pairs, h))),
        ],
        out_specs=[
            pl.BlockSpec((tq, LANES), lambda h: (0, h)),
            pl.BlockSpec((2, tq, span), lambda h: (h, 0, 0)),
        ],
        out_shape=[
            jax.ShapeDtypeStruct((tq, pairs * LANES), jnp.bfloat16),
            jax.ShapeDtypeStruct((heads, tq, key_rows), jnp.bfloat16),
        ],
        scratch_shapes=[
            pltpu.VMEM((2, tq, span), jnp.float32),
            pltpu.VMEM((2, tq, span) if kind == "enc" else (1, 8, LANES), jnp.int32),
            pltpu.VMEM((8, span), jnp.float32),
            pltpu.VMEM((1, 8, LANES) if kind == "cross" else (heads, LANES, 5 * LANES), jnp.float32),
            pltpu.VMEM((heads, tq, span) if kind == "enc" else (1, 8, LANES), jnp.float32),
        ],
        compiler_params=pltpu.CompilerParams(vmem_limit_bytes=VMEM_LIMIT),
        cost_estimate=pl.CostEstimate(
            flops=flops, bytes_accessed=4 * tq * span * pairs, transcendentals=2 * tq * span * pairs
        ),
        name="attend_forward_" + kind,
    )(lens, tab_n, tab_x, tab_y, coords, coords.T, q_src, kv_src, kv_src)


def attend_backward(kind, part, prob, grad_out, out, q_src, q_col, kv_src, k_col, v_col, pairs, quests, carry=()):
    rows = grad_out.shape[0]
    key_rows = kv_src.shape[0]
    width = pairs * LANES
    span = key_rows if kind == "enc" else key_rows // 2
    key_block = 0 if kind == "enc" else part
    query_block = 0 if kind == "cross" else part
    score_block = part if kind == "cross" else 0
    carried = pl.BlockSpec((rows if kind == "cross" else key_rows, LANES), lambda h: (0, h))
    key_out = span if kind == "cross" else key_rows
    query_type = jnp.float32 if kind == "cross" and not part else jnp.bfloat16
    key_type = jnp.bfloat16 if kind == "cross" or part else jnp.float32
    low_block = pl.BlockSpec((2, rows, span), (lambda h: (0, 0, 0)) if kind == "cross" else (lambda h: (h, 0, 0)))
    low_shape = (2, rows, span) if kind == "cross" else (2 * pairs, rows, key_rows)
    return pl.pallas_call(
        partial(bwd_kernel, kind, part, rows, span),
        grid=(pairs,),
        in_specs=[
            pl.BlockSpec((2, rows, span), lambda h: (h, 0, score_block)),
            pl.BlockSpec((rows, LANES), lambda h: (0, h)),
            pl.BlockSpec((rows, LANES), lambda h: (0, h)),
            pl.BlockSpec((rows, LANES), lambda h: (query_block, column(q_src, q_col, pairs, h))),
            pl.BlockSpec((span, LANES), lambda h: (key_block, column(kv_src, k_col, pairs, h))),
            pl.BlockSpec((span, LANES), lambda h: (key_block, column(kv_src, v_col, pairs, h))),
        ]
        + [carried] * len(carry),
        out_specs=[
            pl.BlockSpec((rows, LANES), lambda h: (0, h)),
            pl.BlockSpec((key_out, LANES), lambda h: (0, h)),
            pl.BlockSpec((key_out, LANES), lambda h: (0, h)),
            low_block,
        ],
        out_shape=[
            jax.ShapeDtypeStruct((rows, width), query_type),
            jax.ShapeDtypeStruct((key_out, width), key_type),
            jax.ShapeDtypeStruct((key_out, width), key_type),
            jax.ShapeDtypeStruct(low_shape, jnp.bfloat16),
        ],
        scratch_shapes=[pltpu.VMEM((2, rows, span), jnp.float32)],
        compiler_params=pltpu.CompilerParams(vmem_limit_bytes=VMEM_LIMIT),
        cost_estimate=pl.CostEstimate(
            flops=rows * span * 28000, bytes_accessed=4 * rows * span * pairs, transcendentals=0
        ),
        name="attend_backward_" + kind,
    )(prob, grad_out, out, q_src, kv_src, kv_src, *carry)


def table_sums(kind, part, quarter, coords, low, quests):
    heads, rows, key_rows = low.shape
    rows = rows // 2
    span = key_rows // quests if kind == "dec" else key_rows
    steps = rows // TI
    wide = near_width(kind, TI, span)
    first = (2 * part + quarter) * steps
    tab, diag = pl.pallas_call(
        partial(table_kernel, kind, TI, span, heads),
        grid=(steps,),
        in_specs=[
            pl.BlockSpec((heads, TI, span), lambda i: (0, quarter * steps + i, 0)),
            pl.BlockSpec(coords.shape, lambda i: (0, 0)),
            pl.BlockSpec((TI, 2), lambda i: (first + i, 0)),
        ],
        out_specs=[
            pl.BlockSpec((16, 64), lambda i: (0, 0)),
            pl.BlockSpec((1, 16, wide), lambda i: (i, 0, 0)),
        ],
        out_shape=[
            jax.ShapeDtypeStruct((16, 64), jnp.float32),
            jax.ShapeDtypeStruct((steps, 16, wide), jnp.float32),
        ],
        scratch_shapes=[
            pltpu.VMEM((TI // 16, 256, span), jnp.bfloat16),
            pltpu.VMEM((TI // 16, 256, span), jnp.float32),
            pltpu.VMEM((2, TI, span) if kind == "enc" else (1, 8, LANES), jnp.float32),
        ],
        compiler_params=pltpu.CompilerParams(vmem_limit_bytes=VMEM_LIMIT),
        cost_estimate=pl.CostEstimate(
            flops=rows * span * 40000, bytes_accessed=2 * heads * rows * span, transcendentals=0
        ),
        name="table_sums_" + kind,
    )(low, coords, coords.T)
    near = diag_sums(kind, diag, quarter * steps if kind == "dec" else first, TI, span)[:, :heads]
    if kind == "dec":
        blank = jnp.zeros_like(near)
        return jnp.stack([blank, blank, blank, near])
    return jnp.stack([near, tab[:heads, :32].T, tab[:heads, 32:].T, jnp.zeros_like(near)])


def ffn_kernel(mode, x_ref, gain_ref, wi_ref, wd_ref, *refs):
    rows, width = x_ref.shape
    hidden = wi_ref.shape[1]
    block, chunk = 512, 32
    if mode == "fwd":
        out_ref, z_ref, u_ref = refs
    elif mode == "both":
        g_ref, out_ref, dx_ref, z_ref, u_ref, du_ref, dz_ref = refs
        grad = g_ref[...].astype(jnp.float32)
        grad_low = g_ref[...]
    else:
        g_ref, more_ref = refs[:2]
        dx_ref, hn_ref, gl_ref, act_ref, dzo_ref, dgain_ref, z_ref, du_ref = refs[-8:]
        grad = g_ref[...].astype(jnp.float32) + more_ref[...].astype(jnp.float32)
        grad_low = grad.astype(jnp.bfloat16)
        gl_ref[...] = grad_low
    x = x_ref[...]
    gain = gain_ref[0:1, :]
    scale = lax.rsqrt(jnp.mean(x * x, axis=1, keepdims=True) + EPSILON)
    normed = (x * scale * gain).astype(jnp.bfloat16)
    if mode == "back":
        hn_ref[...] = normed
    total = jnp.zeros((rows, width), jnp.float32)
    back = jnp.zeros((rows, width), jnp.float32)
    for c in range(0, hidden, block):
        cols = slice(c, c + block)
        slot = (c // block) % 2
        z_ref[slot] = dot(normed, wi_ref[:, cols])
        if mode != "fwd":
            du_ref[slot] = dot(grad_low, wd_ref[cols, :], NT)
        for r in range(0, rows, chunk):
            part = slice(r, r + chunk)
            z = z_ref[slot, part, :]
            square = z * z
            tanh = jnp.tanh(GELU_SCALE * z * (1.0 + GELU_CUBE * square))
            half = 0.5 * (1.0 + tanh)
            act = (z * half).astype(jnp.bfloat16)
            if mode == "back":
                act_ref[part, cols] = act
            else:
                u_ref[slot, part, :] = act
            if mode != "fwd":
                slope = half + 0.5 * z * (1.0 - tanh * tanh) * (GELU_SCALE * (1.0 + 3.0 * GELU_CUBE * square))
                d_hidden = (du_ref[slot, part, :] * slope).astype(jnp.bfloat16)
                if mode == "back":
                    dzo_ref[part, cols] = d_hidden
                else:
                    dz_ref[slot, part, :] = d_hidden
        if mode != "back":
            total = total + dot(u_ref[slot], wd_ref[cols, :])
        if mode == "back":
            back = back + dot(dzo_ref[:, cols], wi_ref[:, cols], NT)
        elif mode == "both":
            back = back + dot(dz_ref[slot], wi_ref[:, cols], NT)
    if mode != "back":
        out_ref[...] = (x + total).astype(jnp.bfloat16)
    if mode != "fwd":
        scaled = back * gain
        mean = jnp.mean(scaled * x, axis=1, keepdims=True)
        dx_ref[...] = grad + scale * scaled - x * (scale * scale * scale * mean)
    if mode == "back":
        @pl.when(pl.program_id(0) == 0)
        def _():
            dgain_ref[...] = jnp.zeros_like(dgain_ref)

        dgain_ref[...] += jnp.sum((back * x * scale).reshape(rows // 8, 8, width), axis=0)


def feed_forward(mode, x, gain, w_in, w_down, grads=(), held=None, part=0):
    rows, width = x.shape
    hidden = w_in.shape[1]
    steps = rows // TR
    row_block = pl.BlockSpec((TR, width), lambda i: (i, 0))
    place_block = pl.BlockSpec((TR, width), lambda i: (part * steps + i, 0))
    hidden_block = pl.BlockSpec((TR, hidden), lambda i: (part * steps + i, 0))
    low = jax.ShapeDtypeStruct((rows, width), jnp.bfloat16)
    full = jax.ShapeDtypeStruct((rows, width), jnp.float32)
    both = jax.ShapeDtypeStruct((2 * rows, width), jnp.bfloat16)
    wide = jax.ShapeDtypeStruct((2 * rows, hidden), jnp.bfloat16)
    outs = {
        "fwd": ([row_block], [low]),
        "both": ([row_block] * 2, [low, full]),
        "back": (
            [row_block] + [place_block] * 2 + [hidden_block] * 2 + [pl.BlockSpec((8, width), lambda i: (0, 0))],
            [full, both, both, wide, wide, jax.ShapeDtypeStruct((8, width), jnp.float32)],
        ),
    }[mode]
    slab32, slab16 = pltpu.VMEM((2, TR, 512), jnp.float32), pltpu.VMEM((2, TR, 512), jnp.bfloat16)
    scratch = {"fwd": [slab32, slab16], "both": [slab32, slab16, slab32, slab16], "back": [slab32, slab32]}[mode]
    matmuls = {"fwd": 2, "both": 4, "back": 3}[mode]
    held = held or ()
    return pl.pallas_call(
        partial(ffn_kernel, mode),
        grid=(steps,),
        in_specs=[
            row_block,
            pl.BlockSpec((8, width), lambda i: (0, 0)),
            pl.BlockSpec(w_in.shape, lambda i: (0, 0)),
            pl.BlockSpec(w_down.shape, lambda i: (0, 0)),
        ]
        + [row_block] * len(grads)
        + [pl.BlockSpec(memory_space=pl.ANY)] * len(held),
        out_specs=outs[0],
        out_shape=outs[1],
        scratch_shapes=scratch,
        input_output_aliases={4 + len(grads) + index: 1 + index for index in range(len(held))},
        compiler_params=pltpu.CompilerParams(vmem_limit_bytes=VMEM_LIMIT),
        cost_estimate=pl.CostEstimate(
            flops=2 * matmuls * rows * width * hidden,
            bytes_accessed=4 * width * hidden + 8 * rows * width,
            transcendentals=rows * hidden,
        ),
        name="feed_forward_" + mode,
    )(x, jnp.broadcast_to(gain[None], (8, width)), w_in, w_down, *grads, *held)


def product_kernel(count, slices, which, core_ref, *refs):
    lefts, rights = refs[:count], refs[count : 2 * count]
    outs, turned_ref = refs[2 * count : -1], refs[-1]
    step = pl.program_id(0)

    @pl.when(step == 0)
    def _():
        for index in range(count):
            turned_ref[index] = jnp.transpose(lefts[index][...].astype(jnp.float32)).astype(jnp.bfloat16)

    size = turned_ref.shape[1] // slices
    for index in range(count):
        steps = [s for s, owner in enumerate(which) if owner == index]
        chosen = functools.reduce(lambda a, b: a | b, [step == s for s in steps])

        @pl.when(chosen)
        def _(index=index):
            result = dot(turned_ref[index], rights[index][...])
            if len(outs) == 1:
                outs[0][...] = result.astype(jnp.bfloat16)
                return
            send_ref, keep_ref = outs
            for part in range(slices // 2):
                first = result[2 * part * size : (2 * part + 1) * size]
                second = result[(2 * part + 1) * size : (2 * part + 2) * size]
                rows = slice(part * size, (part + 1) * size)
                is_second = core_ref[0] == 1
                send_ref[rows, :] = jnp.where(is_second, first, second).astype(jnp.bfloat16)
                keep_ref[rows, :] = jnp.where(is_second, second, first).astype(jnp.bfloat16)


def products(lefts, rights, block, slices, core):
    span, rows = lefts[0].shape
    counts = [right.shape[1] // (2 * block) for right in rights]
    which, place = [], []
    for half in range(2):
        for index, number in enumerate(counts):
            for b in range(number):
                which.append(index)
                place.append(half * number + b)
    maps = []
    for index in range(len(rights)):
        held, column_of = 0, []
        for s, owner in enumerate(which):
            if owner == index:
                held = place[s]
            column_of.append(held)
        maps.append(column_of)
    steps = len(which)
    total = steps * block

    def right_map(column_of):
        def index_map(s):
            value = 0
            for position in range(steps):
                if column_of[position]:
                    value = value + jnp.where(s == position, column_of[position], 0)
            return (0, value)

        return index_map

    size = rows // slices
    apart = size % 16 == 0
    out_rows = rows // 2 if apart else rows
    out = jax.ShapeDtypeStruct((out_rows, total), jnp.bfloat16)
    results = pl.pallas_call(
        partial(product_kernel, len(lefts), slices, which),
        grid=(steps,),
        in_specs=[pl.BlockSpec(memory_space=pltpu.SMEM)]
        + [pl.BlockSpec((span, rows), lambda s: (0, 0)) for _ in lefts]
        + [pl.BlockSpec((span, block), right_map(column_of)) for column_of in maps],
        out_specs=[pl.BlockSpec((out_rows, block), lambda s: (0, s))] * (2 if apart else 1),
        out_shape=[out] * (2 if apart else 1),
        scratch_shapes=[pltpu.VMEM((len(lefts), rows, span), jnp.bfloat16)],
        compiler_params=pltpu.CompilerParams(vmem_limit_bytes=VMEM_LIMIT),
        cost_estimate=pl.CostEstimate(
            flops=2 * span * rows * total, bytes_accessed=2 * (span + rows) * total, transcendentals=0
        ),
        name="weight_products",
    )(core.reshape(1), *lefts, *rights)
    if apart:
        return results
    cut = results[0].reshape(slices // 2, 2, size, total)
    return pick(cut, 1 - core, 1).reshape(-1, total), pick(cut, core, 1).reshape(-1, total)


def sum_kernel(partners, x_ref, out_ref, slots, send_sems, recv_sems):
    ids = []
    for axis, bit in partners:
        place = lax.axis_index(axis)
        ids.append({axis: place + (1 << bit) - 2 * (1 << bit) * lax.rem(lax.div(place, 1 << bit), 2)})
    barrier = pltpu.get_barrier_semaphore()
    for device in ids:
        pl.semaphore_signal(barrier, inc=1, device_id=device, device_id_type=pl.DeviceIdType.MESH)
    pl.semaphore_wait(barrier, len(ids))
    out_ref[...] = x_ref[...]
    for step, device in enumerate(ids):
        slots[0, step] = out_ref[...]
        copy = pltpu.make_async_remote_copy(
            src_ref=slots.at[0, step],
            dst_ref=slots.at[1, step],
            send_sem=send_sems.at[step],
            recv_sem=recv_sems.at[step],
            device_id=device,
            device_id_type=pl.DeviceIdType.MESH,
        )
        copy.start()
        copy.wait()
        out_ref[...] += slots[1, step]


def sum_everywhere(x):
    partners = [
        (axis, bit) for axis in ("dp", "mp", "section") for bit in range(lax.axis_size(axis).bit_length() - 1)
    ]
    count = len(partners)
    return pl.pallas_call(
        partial(sum_kernel, partners),
        out_shape=jax.ShapeDtypeStruct(x.shape, x.dtype),
        in_specs=[pl.BlockSpec(memory_space=pltpu.VMEM)],
        out_specs=pl.BlockSpec(memory_space=pltpu.VMEM),
        scratch_shapes=[
            pltpu.VMEM((2, count) + x.shape, x.dtype),
            pltpu.SemaphoreType.DMA((count,)),
            pltpu.SemaphoreType.DMA((count,)),
        ],
        compiler_params=pltpu.CompilerParams(collective_id=0, has_side_effects=True),
        name="sum_everywhere",
    )(x)


def pair_permute(x, axis, bit):
    pairs = [(i, i ^ (1 << bit)) for i in range(lax.axis_size(axis))]
    return lax.ppermute(x, axis, pairs)


def shifted(x, axis, by):
    peers = lax.axis_size(axis)
    pairs = [(i, i + by) for i in range(peers) if 0 <= i + by < peers]
    return lax.ppermute(x, axis, pairs)


def in_order(flag, first, second, axis):
    return jnp.where(
        flag == 0,
        jnp.concatenate([first, second], axis=axis),
        jnp.concatenate([second, first], axis=axis),
    )


def pick(x, index, axis):
    return lax.dynamic_index_in_dim(x, index, axis, False)


def after(values, *others):
    return lax.optimization_barrier((values, others))[0]


def gather_rows(block, where_mp):
    own = pick(block, where_mp, 0)
    arrived = pair_permute(pick(block, 1 - where_mp, 0), "mp", 0)
    return in_order(where_mp, own, arrived, 0)


def scatter_rows(rows, where_mp):
    halves = rows.reshape(2, -1, rows.shape[1])
    own = pick(halves, where_mp, 0)
    arrived = pair_permute(pick(halves, 1 - where_mp, 0).astype(jnp.bfloat16), "mp", 0)
    return in_order(where_mp, own[None], arrived.astype(rows.dtype)[None], 0)


def other_shard(shard, core):
    half = shard.shape[0] // 2
    far = pair_permute(lax.dynamic_slice_in_dim(shard, core * half, half, 0), "mp", 0)
    near = pair_permute(far, "dp", 0)
    return in_order(core, far, near, 0)


def reduce_rows(send, keep, dp_index, section=None):
    parts = lax.axis_size("dp")
    bits = parts.bit_length() - 1
    total = keep.astype(jnp.float32) + pair_permute(send, "dp", 0).astype(jnp.float32)
    if section is not None:
        halves = total.reshape(2, -1, total.shape[1])
        moved = shifted(halves[0].astype(jnp.bfloat16), "section", -1).astype(jnp.float32)
        total = jnp.where(section == 0, moved, halves[1])
    width = total.shape[1] // 2
    arrived = pair_permute(total[:, width:].astype(jnp.bfloat16), "mp", 0)
    total = total[:, :width] + arrived.astype(jnp.float32)
    for bit in range(1, bits):
        mark = (dp_index >> bit) & 1
        halves = total.reshape(parts >> (bit + 1), 2, -1, width)
        arrived = pair_permute(pick(halves, 1 - mark, 1).astype(jnp.bfloat16), "dp", bit)
        total = (pick(halves, mark, 1) + arrived.astype(jnp.float32)).reshape(-1, width)
    return total


def rms_norm(inputs, gain_row):
    return (
        inputs * lax.rsqrt(jnp.mean(inputs * inputs, axis=-1, keepdims=True) + EPSILON) * gain_row
    )


def norm_back(rows, gain_row, grad_normed):
    return jax.vjp(rms_norm, rows, gain_row)[1](grad_normed)


def low(x):
    return x.astype(jnp.bfloat16)


def own_first(arrays):
    half = arrays[0].shape[1] // 2
    return jnp.concatenate([x[:, :half] for x in arrays] + [x[:, half:] for x in arrays], axis=1)


def local(
    block_input,
    out_cotangent,
    doc_lengths,
    question_lengths,
    coordinates,
    gains,
    bias_tables,
    self_qkv,
    self_out,
    ffn_in,
    ffn_out,
    cross_q,
    cross_kv,
    cross_out,
):
    section = lax.axis_index("section")
    on_encoder = section == 0
    dp_index = lax.axis_index("dp")
    core = dp_index & 1
    where_mp = lax.axis_index("mp")
    width = block_input.shape[4]
    quests = question_lengths.shape[2]
    own = self_qkv.shape[3]
    pairs = 2 * own // LANES
    heads = 2 * pairs
    parts = lax.axis_size("dp")

    rows_low = gather_rows(block_input[0, :, 0], where_mp)
    qkv_own = self_qkv[0].reshape(width, -1)
    qkv_other = other_shard(qkv_own, core)
    w_qkv = jnp.concatenate([qkv_own, qkv_other], axis=1)
    in_own, down_own = after((ffn_in[0], jnp.concatenate([self_out[0], ffn_out[0]], axis=0)), rows_low, qkv_other)
    in_other, down_other = other_shard(in_own, core), other_shard(down_own, core)
    w_in = jnp.concatenate([in_own, in_other], axis=1)
    w_out = jnp.concatenate([self_out[0], down_other[:own]], axis=0)
    w_down = jnp.concatenate([ffn_out[0], down_other[own:]], axis=0)
    pair_own, cross_own, cot_own = after(
        (jnp.concatenate([cross_q, cross_kv.reshape(width, -1)], axis=1), cross_out, out_cotangent[0, :, 0]),
        in_other,
        down_other,
    )
    pair_other, cross_other = other_shard(pair_own, core), other_shard(cross_own, core)
    w_query = jnp.concatenate([cross_q, pair_other[:, :own]], axis=1)
    w_pair = jnp.concatenate([pair_own[:, own:], pair_other[:, own:]], axis=1)
    w_cross = jnp.concatenate([cross_own, cross_other], axis=0)
    cot_low = gather_rows(cot_own, where_mp)

    lens = jnp.concatenate(
        [pick(doc_lengths, where_mp, 0), pick(question_lengths, where_mp, 0)[0]]
    ).astype(jnp.int32)
    coords = pick(coordinates, where_mp, 0)[0]
    tables = jnp.where(where_mp == 0, bias_tables, jnp.roll(bias_tables, heads // 2, axis=2))

    rows = rows_low.astype(jnp.float32)
    span = rows.shape[0]
    half = span // 2
    halves = (slice(0, half), slice(half, span))
    gain_self = jnp.where(on_encoder, gains[0], gains[2])
    normed_self = low(rms_norm(rows, gain_self))
    projected = low(dot(normed_self, w_qkv))
    merged, probs, middles, memories, arrivals = [], [], [], [], []
    for part in range(2):
        source = after(projected, memories[0]) if part else projected

        def forward(kind, chosen):
            return attend_forward(kind, part, half, lens, chosen, coords, source, 0, source, 1, 2, pairs, quests)

        out, prob = lax.cond(on_encoder, lambda: forward("enc", tables[:3]), lambda: forward("dec", tables[3:]))
        middle = rows[halves[part]] + dot(out, w_out)
        memory = feed_forward("fwd", middle, gains[1], w_in, w_down)[0]
        arrivals.append(shifted(memory, "section", 1))
        merged.append(out)
        probs.append(prob)
        middles.append(middle)
        memories.append(memory)
    middle = jnp.concatenate(middles, axis=0)
    arrived = jnp.concatenate(arrivals, axis=0)

    normed_cross = low(rms_norm(middle, gains[3]))
    queries = low(dot(normed_cross, w_query))
    pair_rows = low(dot(arrived, w_pair))
    cross_merged, cross_prob = attend_forward(
        "cross", 0, span, lens, None, coords, queries, 0, pair_rows, 0, 1, pairs, quests
    )
    second = middle + dot(cross_merged, w_cross)
    output_low, grad_second = feed_forward("both", second, gains[4], w_in, w_down, (cot_low,))
    second_low = low(grad_second)
    cross_grad = low(dot(second_low, w_cross, NT))
    pair_grads, returns, carry = [], [], ()
    for part in range(2):
        source = after(cross_prob, returns[0]) if part else cross_prob
        query_grad, key_grad, value_grad, _ = attend_backward(
            "cross", part, source, cross_grad, cross_merged, queries, 0, pair_rows, 0, 1, pairs, quests, carry
        )
        carry = (query_grad,)
        pair_grads.append(own_first([key_grad, value_grad]))
        returns.append(low(dot(pair_grads[part], w_pair, NT)))
    returned = [shifted(x, "section", -1) for x in returns]
    left_cross, left_memory, left_second = after((normed_cross, arrived, second_low), returns[1])
    pair_grad = jnp.concatenate(pair_grads, axis=0)
    input_part, gain_cross = norm_back(middle, gains[3], dot(after(query_grad, returns[1]), w_query, NT))
    grad_first = grad_second + input_part
    cross_send, cross_keep = products(
        [left_cross, left_memory, left_second], [query_grad, pair_grad, cross_merged], own, 2 * parts, core
    )

    ffn_rows = jnp.where(on_encoder, middle, second)
    gain_ffn = jnp.where(on_encoder, gains[1], gains[4])
    held, scores, query_grads, lows, gain_ffn_grad, carry, grads_middle = None, [], [], [], 0.0, (), []
    for part in range(2):
        x = ffn_rows[halves[part]]
        if part:
            x = after(x, scores[0])
        grad_ffn, *held, gain_part = feed_forward(
            "back", x, gain_ffn, w_in, w_down, (cot_low[halves[part]], returned[part]), held, part
        )
        gain_ffn_grad = gain_ffn_grad + jnp.sum(gain_part, axis=0)
        grad_middle = jnp.where(on_encoder, grad_ffn, grad_first[halves[part]])
        middle_low = low(grad_middle)
        merged_grad = low(dot(middle_low, w_out, NT))
        if part:
            ffn_send, ffn_keep = products([held[0], held[1]], [held[3], held[2]], 2 * own, parts, core)
            merged_grad = after(merged_grad, ffn_send)

        def backward(kind):
            return attend_backward(
                kind, part, probs[part], merged_grad, merged[part], projected, 0, projected, 1, 2, pairs, quests, carry
            )

        query_grad, key_grad, value_grad, score = lax.cond(
            on_encoder, lambda: backward("enc"), lambda: backward("dec")
        )
        carry = (key_grad, value_grad)
        query_grads.append(query_grad)
        scores.append(score)
        lows.append(middle_low)
        grads_middle.append(grad_middle)
    stacked = own_first([jnp.concatenate(query_grads, axis=0), key_grad, value_grad])
    self_send, self_keep = products(
        [normed_self, jnp.concatenate(lows, axis=0)],
        [stacked, jnp.concatenate(merged, axis=0)],
        own,
        parts,
        core,
    )
    input_part, gain_self_grad = norm_back(rows, gain_self, dot(stacked, w_qkv, NT))
    input_grad = jnp.concatenate(grads_middle, axis=0) + input_part

    table_grad = 0.0
    score_pair = after(tuple(scores), self_send, input_grad)
    for part in range(2):
        for quarter in range(2):
            score = score_pair[part]
            table_grad = table_grad + lax.cond(
                on_encoder,
                lambda: table_sums("enc", part, quarter, coords, score, quests),
                lambda: table_sums("dec", part, quarter, coords, score, quests),
            )
    table_grad = jnp.where(where_mp == 0, table_grad, jnp.roll(table_grad, heads // 2, axis=2))
    blank = jnp.zeros_like(gain_cross)
    gain_grad = jnp.where(
        on_encoder,
        jnp.stack([gain_self_grad, gain_ffn_grad, blank, blank, blank]),
        jnp.stack([blank, blank, gain_self_grad, gain_cross, gain_ffn_grad]),
    )
    small = jnp.concatenate([gain_grad.reshape(-1, LANES), table_grad.reshape(-1, LANES)], axis=0)
    count = small.shape[0]
    small = sum_everywhere(jnp.pad(small, ((0, -count % 8), (0, 0))))
    gain_count = gain_grad.size // LANES
    gain_sum = small[:gain_count].reshape(gain_grad.shape)
    table_sum = small[gain_count:count].reshape(table_grad.shape)

    cross_shard = reduce_rows(cross_send, cross_keep, dp_index, section)
    ffn_shard = reduce_rows(ffn_send, ffn_keep, dp_index)
    self_shard = reduce_rows(self_send, self_keep, dp_index)
    output_rows = scatter_rows(
        jnp.where(on_encoder, jnp.concatenate(memories, axis=0), output_low), where_mp
    )
    grad_rows = scatter_rows(input_grad, where_mp)
    hidden = ffn_in.shape[2]
    return (
        output_rows[None, :, None],
        grad_rows[None, :, None],
        gain_sum[:4],
        gain_sum[4],
        table_sum,
        self_shard[:, : 3 * own].reshape(-1, 3, own)[None],
        self_shard[:, 3 * own :].T[None],
        ffn_shard[:, :hidden][None],
        ffn_shard[:, hidden:].T[None],
        cross_shard[:, :own],
        cross_shard[:, own : 3 * own].reshape(-1, 2, own),
        cross_shard[:, 3 * own :].T,
    )


def solution(mesh):
    return jax.shard_map(
        local,
        mesh=mesh,
        in_specs=(
            P("section", None, "dp", "mp", None),
            P("section", None, "dp", "mp", None),
            P(None, "dp"),
            P(None, "dp", None),
            P(None, "dp", None, None),
            P(),
            P(),
            P("section", None, None, "mp"),
            P("section", "mp", None),
            P("section", None, "mp"),
            P("section", "mp", None),
            P(None, "mp"),
            P(None, None, "mp"),
            P("mp", None),
        ),
        out_specs=(
            P("section", None, "dp", "mp", None),
            P("section", None, "dp", "mp", None),
            P(),
            P(),
            P(),
            P("section", "dp", None, "mp"),
            P("section", "mp", "dp"),
            P("section", "dp", "mp"),
            P("section", "mp", "dp"),
            P(("section", "dp"), "mp"),
            P(("section", "dp"), None, "mp"),
            P("mp", ("section", "dp")),
        ),
        check_vma=False,
    )
```

```python
import functools
from functools import partial
import math

import jax
import jax.numpy as jnp
from jax import lax
from jax.experimental import pallas as pl
from jax.experimental.pallas import tpu as pltpu
from jax.sharding import PartitionSpec as P

HEAD = 64
LANES = 128
NEGATIVE = -1e30
EPSILON = 1e-06
GELU_SCALE = math.sqrt(2 / math.pi)
GELU_CUBE = 0.044715
TI = 64
TR = 256
VMEM_LIMIT = 56 * 1024 * 1024
NT = (((1,), (1,)), ((), ()))
NN = (((1,), (0,)), ((), ()))


def edge_list(exact_span, bucket_count, far_reach):
    log_edges = [
        int(
            math.ceil(
                exact_span * (far_reach / exact_span) ** (power_index / (bucket_count - exact_span))
            )
        )
        for power_index in range(1, bucket_count - exact_span)
    ]
    return list(range(1, exact_span + 1)) + log_edges


def magnitude(distance, exact_span, bucket_count, far_reach):
    bucket = jnp.minimum(distance, exact_span)
    for threshold in edge_list(exact_span, bucket_count, far_reach)[exact_span:]:
        bucket = bucket + (distance >= threshold).astype(jnp.int32)
    return bucket


def two_sided(relative, far_reach):
    return magnitude(jnp.abs(relative), 8, 16, far_reach) + jnp.where(relative > 0, 16, 0)


def one_sided(relative):
    return magnitude(jnp.maximum(-relative, 0), 16, 32, 128)


def half_lanes(block, head):
    lane = lax.broadcasted_iota(jnp.int32, block.shape, 1)
    keep = lane < HEAD if head == 0 else lane >= HEAD
    return jnp.where(keep, block, jnp.zeros_like(block))


def dot(a, b, dims=NN):
    return lax.dot_general(a, b, dims, preferred_element_type=jnp.float32)


def pick_lanes(row, index):
    return jnp.take_along_axis(jnp.broadcast_to(row, index.shape), index, axis=1)


def pick_sublanes(table_ref, head, low, odd, upper):
    parts = [
        jnp.take_along_axis(table_ref[head, 8 * part : 8 * part + 8, :], low, axis=0)
        for part in range(4)
    ]
    return jnp.where(upper, jnp.where(odd, parts[3], parts[2]), jnp.where(odd, parts[1], parts[0]))


def fwd_kernel(kind, part, tq, span, heads, len_ref, tabn_ref, tabx_ref, taby_ref, crow_ref, ccol_ref, q_ref, k_ref, v_ref, o_ref, p_ref, s_ref, idx_ref, mask_ref, near_ref, bias_ref):
    pair = pl.program_id(0)
    first_block = 0 if kind == "dec" else part * tq // LANES
    chunk = 16

    @pl.when(pair == 0)
    def _():
        key = lax.broadcasted_iota(jnp.int32, (8, span), 1)
        limit = len_ref[1 + part] if kind == "dec" else len_ref[0]
        mask_ref[...] = jnp.where(key < limit, 0.0, NEGATIVE)
        if kind != "cross":
            def near_rows(r, carry):
                rows = pl.ds(pl.multiple_of(r * 8, 8), 8)
                query = r * 8 + lax.broadcasted_iota(jnp.int32, (8, LANES), 0)
                for d in range(-2, 3):
                    key = d * LANES + lax.broadcasted_iota(jnp.int32, (8, LANES), 1)
                    bucket = one_sided(key - query) if kind == "dec" else two_sided(key - query, 128)
                    for head in range(heads):
                        value = pick_lanes(tabn_ref[head : head + 1, :], bucket)
                        if kind == "dec":
                            value = jnp.where(key <= query, value, NEGATIVE)
                        near_ref[head, rows, (d + 2) * LANES : (d + 3) * LANES] = value
                return carry

            lax.fori_loop(0, LANES // 8, near_rows, 0)
        if kind == "enc":

            def bucket_rows(r, carry):
                rows = pl.ds(pl.multiple_of(r * chunk, chunk), chunk)
                for axis in range(2):
                    far = crow_ref[axis : axis + 1, :] - ccol_ref[rows, axis : axis + 1]
                    idx_ref[axis, rows, :] = two_sided(far, 500)
                return carry

            lax.fori_loop(0, tq // chunk, bucket_rows, 0)

            def bias_rows(r, carry):
                rows = pl.ds(pl.multiple_of(r * 8, 8), 8)
                for c in range(0, span, LANES):
                    lanes = slice(c, c + LANES)
                    across = idx_ref[0, rows, lanes]
                    upward = idx_ref[1, rows, lanes]
                    low, odd, upper = upward & 7, (upward & 8) != 0, upward >= 16
                    for head in range(heads):
                        bias_ref[head, rows, lanes] = pick_lanes(
                            tabx_ref[head : head + 1, :], across
                        ) + pick_sublanes(taby_ref, head, low, odd, upper)
                return carry

            lax.fori_loop(0, tq // 8, bias_rows, 0, unroll=2)

    for head in range(2):
        s_ref[head] = dot(half_lanes(q_ref[...], head), k_ref[...], NT)
        for r in range(0, tq, chunk):
            rows = slice(r, r + chunk)
            pieces = []
            for c in range(0, span, LANES):
                lanes = slice(c, c + LANES)
                piece = s_ref[head, rows, lanes] + mask_ref[0:1, lanes]
                if kind != "cross":
                    apart = min(max(c // LANES - (first_block + r // LANES), -2), 2) + 2
                    near = slice(apart * LANES, (apart + 1) * LANES)
                    piece = piece + near_ref[2 * pair + head, r % LANES : r % LANES + chunk, near]
                if kind == "enc":
                    piece = piece + bias_ref[2 * pair + head, rows, lanes]
                pieces.append(piece)
            score = jnp.concatenate(pieces, axis=1)
            score = jnp.exp(score - jnp.max(score, axis=1, keepdims=True))
            score = score * (1.0 / jnp.sum(score, axis=1, keepdims=True))
            p_ref[head, rows, :] = score.astype(jnp.bfloat16)
    first = dot(p_ref[0], v_ref[...])
    second = dot(p_ref[1], v_ref[...])
    lane = lax.broadcasted_iota(jnp.int32, first.shape, 1)
    o_ref[...] = jnp.where(lane < HEAD, first, second).astype(jnp.bfloat16)


def bwd_kernel(kind, part, rows, span, p_ref, do_ref, o_ref, q_ref, k_ref, v_ref, *refs):
    carry = refs[: 2 if kind != "cross" else 3] if part else ()
    outs = refs[len(carry) :]
    dq_ref, dk_ref, dv_ref = outs[:3]
    low_ref, dp_ref = outs[3:]
    chunk = 16
    q_t = jnp.transpose(q_ref[...].astype(jnp.float32)).astype(jnp.bfloat16)
    do_t = jnp.transpose(do_ref[...].astype(jnp.float32)).astype(jnp.bfloat16)
    grads, key_grads, value_grads = [], [], []
    for head in range(2):
        d_out = half_lanes(do_ref[...], head)
        delta = jnp.sum(d_out.astype(jnp.float32) * o_ref[...].astype(jnp.float32), axis=1, keepdims=True)
        dp_ref[head] = dot(d_out, v_ref[...], NT)
        for r in range(0, rows, chunk):
            part_rows = slice(r, r + chunk)
            prob = p_ref[head, part_rows, :].astype(jnp.float32)
            low_ref[head, part_rows, :] = (
                prob * (dp_ref[head, part_rows, :] - delta[part_rows, :])
            ).astype(jnp.bfloat16)
        grads.append(dot(low_ref[head], k_ref[...]))
        half = slice(head * HEAD, (head + 1) * HEAD)
        key_grads.append(dot(q_t[half], low_ref[head]))
        value_grads.append(dot(do_t[half], p_ref[head]))
    lane = lax.broadcasted_iota(jnp.int32, grads[0].shape, 1)
    query_grad = jnp.where(lane < HEAD, grads[0], grads[1])
    if kind == "cross" and part:
        query_grad = query_grad + carry[0][...]
    dq_ref[...] = query_grad.astype(dq_ref.dtype)
    for index, (out_ref, pieces) in enumerate(((dk_ref, key_grads), (dv_ref, value_grads))):
        grad = jnp.transpose(jnp.concatenate(pieces, axis=0))
        if kind == "enc" and part:
            grad = grad + carry[index][...]
        if kind == "dec":
            if part:
                out_ref[0:span, :] = carry[index][0:span, :].astype(out_ref.dtype)
            out_ref[part * span : (part + 1) * span, :] = grad.astype(out_ref.dtype)
        else:
            out_ref[...] = grad.astype(out_ref.dtype)


def table_kernel(kind, ti, span, heads, low_ref, crow_ref, ccol_ref, tab_ref, diag_ref, row_ref, wide_ref, idx_ref):
    step = pl.program_id(0)
    group = 16
    wide = diag_ref.shape[2]
    pad = wide - span

    @pl.when(step == 0)
    def _():
        tab_ref[...] = jnp.zeros_like(tab_ref)

    if kind == "enc":
        for r in range(0, ti, 16):
            for axis in range(2):
                far = crow_ref[axis : axis + 1, :] - ccol_ref[r : r + 16, axis : axis + 1]
                idx_ref[axis, r : r + 16, :] = two_sided(far, 500).astype(jnp.float32)
    out_row = lax.broadcasted_iota(jnp.int32, (256, 256), 0)
    in_row = lax.broadcasted_iota(jnp.int32, (256, 256), 1)
    swap = (lax.div(out_row, 16) == lax.rem(in_row, 16)) & (lax.rem(out_row, 16) == lax.div(in_row, 16))
    swap = jnp.where(swap, 1.0, 0.0).astype(jnp.bfloat16)
    blank = jnp.zeros(((16 - heads) * 16, span), jnp.bfloat16)
    which = lax.broadcasted_iota(jnp.int32, (32, span), 0).astype(jnp.bfloat16)

    tab = jnp.zeros(tab_ref.shape, jnp.float32)
    diag = jnp.zeros((16, wide), jnp.float32)
    for g in range(ti // group):
        first = g * group
        block = jnp.concatenate([low_ref[h, first : first + group, :] for h in range(heads)] + [blank], axis=0)
        wide_ref[g] = dot(swap, block)
        if kind == "enc":
            row_ref[g] = wide_ref[g].astype(jnp.bfloat16)
        for j in range(group):
            lines = slice(16 * j, 16 * j + 16)
            if kind == "enc":
                hot = []
                for axis in range(2):
                    bucket = idx_ref[axis, first + j : first + j + 1, :]
                    bucket = jnp.broadcast_to(bucket, (32, span)).astype(jnp.bfloat16)
                    hot.append(jnp.where(bucket == which, jnp.bfloat16(1), jnp.bfloat16(0)))
                tab = tab + dot(row_ref[g, lines, :], jnp.concatenate(hot, axis=0), NT)
            line = wide_ref[g, lines, :]
            if pad:
                line = jnp.concatenate([line, jnp.zeros((16, pad), jnp.float32)], axis=1)
            diag = diag + pltpu.roll(line, (wide - (first + j)) % wide, 1)
    tab_ref[...] += tab
    diag_ref[0] = diag


ANY = pl.BlockSpec(memory_space=pl.ANY)


def without(kernel, first, count):
    return lambda *refs: kernel(*refs[:first], *refs[first + count :])


def near_width(kind, ti, span):
    return span + ti if kind == "enc" else span


def diag_sums(kind, diag, starts):
    wide = diag.shape[2]
    column = lax.broadcasted_iota(jnp.int32, (len(starts), wide), 1)
    start = jnp.array(starts, jnp.int32)[:, None]
    if kind == "dec":
        bucket = one_sided(jnp.where(column > start, column - wide, column) - start)
    else:
        bucket = two_sided(jnp.where(column > wide - TI, column - wide, column) - start, 128)
    hot = (bucket[..., None] == lax.iota(jnp.int32, 32)).astype(jnp.float32)
    return jnp.einsum("swb,shw->bh", hot, diag, precision=lax.Precision.HIGHEST)


def attend_forward(kind, part, tq, lens, tables, coords, q_src, q_col, kv_src, k_col, v_col, pairs, quests, deps=()):
    heads = 2 * pairs
    key_rows = kv_src.shape[0]
    span = key_rows // quests if kind == "dec" else key_rows
    key_block = part if kind == "dec" else 0
    flops = tq * span * (60000 if kind == "enc" else 25000)
    tab_n = tab_x = jnp.zeros((16, LANES), jnp.float32)
    tab_y = jnp.zeros((1, 8, LANES), jnp.float32)
    if kind != "cross":
        tab_n = jnp.pad(tables[0].T, ((0, 16 - heads), (0, LANES - 32)))
    if kind == "enc":
        tab_x = jnp.pad(tables[1].T, ((0, 16 - heads), (0, LANES - 32)))
        tab_y = jnp.broadcast_to(tables[2].T[:, :, None], (heads, 32, LANES))
    return pl.pallas_call(
        without(partial(fwd_kernel, kind, part, tq, span, heads), 9, len(deps)),
        grid=(pairs,),
        in_specs=[
            pl.BlockSpec(memory_space=pltpu.SMEM),
            pl.BlockSpec(tab_n.shape, lambda h: (0, 0)),
            pl.BlockSpec(tab_x.shape, lambda h: (0, 0)),
            pl.BlockSpec(tab_y.shape, lambda h: (0, 0, 0)),
            pl.BlockSpec(coords.shape, lambda h: (0, 0)),
            pl.BlockSpec((tq, 2), lambda h: (part, 0)),
            pl.BlockSpec((tq, LANES), lambda h: (part, q_col * pairs + h)),
            pl.BlockSpec((span, LANES), lambda h: (key_block, k_col * pairs + h)),
            pl.BlockSpec((span, LANES), lambda h: (key_block, v_col * pairs + h)),
        ]
        + [ANY] * len(deps),
        out_specs=[
            pl.BlockSpec((tq, LANES), lambda h: (0, h)),
            pl.BlockSpec((2, tq, span), lambda h: (h, 0, 0)),
        ],
        out_shape=[
            jax.ShapeDtypeStruct((tq, pairs * LANES), jnp.bfloat16),
            jax.ShapeDtypeStruct((heads, tq, key_rows), jnp.bfloat16),
        ],
        scratch_shapes=[
            pltpu.VMEM((2, tq, span), jnp.float32),
            pltpu.VMEM((2, tq, span) if kind == "enc" else (1, 8, LANES), jnp.int32),
            pltpu.VMEM((8, span), jnp.float32),
            pltpu.VMEM((1, 8, LANES) if kind == "cross" else (heads, LANES, 5 * LANES), jnp.float32),
            pltpu.VMEM((heads, tq, span) if kind == "enc" else (1, 8, LANES), jnp.float32),
        ],
        compiler_params=pltpu.CompilerParams(vmem_limit_bytes=VMEM_LIMIT),
        cost_estimate=pl.CostEstimate(
            flops=flops, bytes_accessed=4 * tq * span * pairs, transcendentals=2 * tq * span * pairs
        ),
        name="attend_forward_" + kind,
    )(lens, tab_n, tab_x, tab_y, coords, coords.T, q_src, kv_src, kv_src, *deps)


def attend_backward(kind, part, prob, grad_out, out, q_src, q_col, kv_src, k_col, v_col, pairs, quests, carry=(), deps=()):
    rows = grad_out.shape[0]
    key_rows = kv_src.shape[0]
    width = pairs * LANES
    span = key_rows if kind == "enc" else key_rows // 2
    key_block = 0 if kind == "enc" else part
    query_block = 0 if kind == "cross" else part
    score_block = part if kind == "cross" else 0
    if kind == "cross":
        carried = [pl.BlockSpec((rows, LANES), lambda h: (0, h))] + [pl.BlockSpec(memory_space=pl.ANY)] * 2
        key_out = pl.BlockSpec((span, LANES), lambda h: (part, h))
        aliases = {7: 1, 8: 2} if part else {}
    else:
        carried = [pl.BlockSpec((key_rows, LANES), lambda h: (0, h))] * 2
        key_out = pl.BlockSpec((key_rows, LANES), lambda h: (0, h))
        aliases = {}
    query_type = jnp.float32 if kind == "cross" and not part else jnp.bfloat16
    key_type = jnp.bfloat16 if kind == "cross" or part else jnp.float32
    low_block = pl.BlockSpec((2, rows, span), (lambda h: (0, 0, 0)) if kind == "cross" else (lambda h: (h, 0, 0)))
    low_shape = (2, rows, span) if kind == "cross" else (2 * pairs, rows, key_rows)
    return pl.pallas_call(
        without(partial(bwd_kernel, kind, part, rows, span), 6 + len(carry), len(deps)),
        grid=(pairs,),
        in_specs=[
            pl.BlockSpec((2, rows, span), lambda h: (h, 0, score_block)),
            pl.BlockSpec((rows, LANES), lambda h: (0, h)),
            pl.BlockSpec((rows, LANES), lambda h: (0, h)),
            pl.BlockSpec((rows, LANES), lambda h: (query_block, q_col * pairs + h)),
            pl.BlockSpec((span, LANES), lambda h: (key_block, k_col * pairs + h)),
            pl.BlockSpec((span, LANES), lambda h: (key_block, v_col * pairs + h)),
        ]
        + carried[: len(carry)]
        + [ANY] * len(deps),
        out_specs=[
            pl.BlockSpec((rows, LANES), lambda h: (0, h)),
            key_out,
            key_out,
            low_block,
        ],
        out_shape=[
            jax.ShapeDtypeStruct((rows, width), query_type),
            jax.ShapeDtypeStruct((key_rows, width), key_type),
            jax.ShapeDtypeStruct((key_rows, width), key_type),
            jax.ShapeDtypeStruct(low_shape, jnp.bfloat16),
        ],
        scratch_shapes=[pltpu.VMEM((2, rows, span), jnp.float32)],
        input_output_aliases=aliases,
        compiler_params=pltpu.CompilerParams(vmem_limit_bytes=VMEM_LIMIT),
        cost_estimate=pl.CostEstimate(
            flops=rows * span * 28000, bytes_accessed=4 * rows * span * pairs, transcendentals=0
        ),
        name="attend_backward_" + kind,
    )(prob, grad_out, out, q_src, kv_src, kv_src, *carry, *deps)


def table_sums(kind, part, quarter, coords, low, quests, deps=()):
    heads, rows, key_rows = low.shape
    rows = rows // 2
    span = key_rows // quests if kind == "dec" else key_rows
    steps = rows // TI
    wide = near_width(kind, TI, span)
    first = (2 * part + quarter) * steps
    tab, diag = pl.pallas_call(
        without(partial(table_kernel, kind, TI, span, heads), 3, len(deps)),
        grid=(steps,),
        in_specs=[
            pl.BlockSpec((heads, TI, span), lambda i: (0, quarter * steps + i, 0)),
            pl.BlockSpec(coords.shape, lambda i: (0, 0)),
            pl.BlockSpec((TI, 2), lambda i: (first + i, 0)),
        ]
        + [ANY] * len(deps),
        out_specs=[
            pl.BlockSpec((16, 64), lambda i: (0, 0)),
            pl.BlockSpec((1, 16, wide), lambda i: (i, 0, 0)),
        ],
        out_shape=[
            jax.ShapeDtypeStruct((16, 64), jnp.float32),
            jax.ShapeDtypeStruct((steps, 16, near_width("enc", TI, key_rows)), jnp.float32),
        ],
        scratch_shapes=[
            pltpu.VMEM((TI // 16, 256, span), jnp.bfloat16),
            pltpu.VMEM((TI // 16, 256, span), jnp.float32),
            pltpu.VMEM((2, TI, span) if kind == "enc" else (1, 8, LANES), jnp.float32),
        ],
        compiler_params=pltpu.CompilerParams(vmem_limit_bytes=VMEM_LIMIT),
        cost_estimate=pl.CostEstimate(
            flops=rows * span * 40000, bytes_accessed=2 * heads * rows * span, transcendentals=0
        ),
        name="table_sums_" + kind,
    )(low, coords, coords.T, *deps)
    return tab, diag


def table_grads(kind, tabs, diags, rows, quests, heads):
    steps = diags[0].shape[0]
    starts = [step * TI for step in range(4 * steps)]
    diag = jnp.concatenate(diags, axis=0)
    if kind == "dec":
        span = rows // quests
        near = diag_sums(kind, diag[:, :, :span], [start % span for start in starts])[:, :heads]
        blank = jnp.zeros_like(near)
        return jnp.stack([blank, blank, blank, near])
    tab = sum(tabs)
    near = diag_sums(kind, diag, starts)[:, :heads]
    return jnp.stack([near, tab[:heads, :32].T, tab[:heads, 32:].T, jnp.zeros_like(near)])


def weight_copies(core, pieces, wi_ref, wd_ref, sems):
    in_own, in_far, in_near, down_own, down_far, down_near = pieces
    own = in_own.shape[1]
    block = own // 2
    rows_in, rows_down = in_far.shape[0], down_far.shape[0]
    far_in = pl.ds(pl.multiple_of(core * rows_in, rows_in), rows_in)
    near_in = pl.ds(pl.multiple_of((1 - core) * rows_in, rows_in), rows_in)
    far_down = pl.ds(pl.multiple_of(own + core * rows_down, rows_down), rows_down)
    near_down = pl.ds(pl.multiple_of(own + (1 - core) * rows_down, rows_down), rows_down)
    moves = []
    for b in range(2):
        part = slice(b * block, (b + 1) * block)
        moves.append((in_own.at[:, part], wi_ref.at[:, part]))
        moves.append((down_own.at[part, :], wd_ref.at[part, :]))
    other = slice(own, 2 * own)
    moves.append((in_far, wi_ref.at[far_in, other]))
    moves.append((in_near, wi_ref.at[near_in, other]))
    moves.append((down_far, wd_ref.at[far_down, :]))
    moves.append((down_near, wd_ref.at[near_down, :]))
    return [pltpu.make_async_copy(src, dst, sems.at[i]) for i, (src, dst) in enumerate(moves)], (2, 4, 8, 8)


def ffn_kernel(mode, first_block, half_blocks, flag_ref, x_ref, gain_ref, *refs):
    pieces, refs = refs[:6], refs[6:]
    refs, (wi_ref, wd_ref, sems) = refs[:-3], refs[-3:]
    rows, width = x_ref.shape
    hidden = wi_ref.shape[1]
    block, chunk = hidden // 4, 32
    first_step = pl.program_id(0) == 0
    copies, needed = weight_copies(flag_ref[0], pieces, wi_ref, wd_ref, sems)

    @pl.when(first_step)
    def _():
        for copy in copies:
            copy.start()

    if mode != "fwd":
        is_own = lax.div(first_block + pl.program_id(0), half_blocks) == flag_ref[1]
        grad_low = jnp.where(is_own, refs[0][...], refs[1][...])
        grad = grad_low.astype(jnp.float32)
    if mode == "fwd":
        out_ref, z_ref, u_ref = refs
    elif mode == "both":
        out_ref, dx_ref, z_ref, u_ref, du_ref, dz_ref = refs[2:]
    else:
        more_ref = refs[2]
        dx_ref, hn_ref, gl_ref, act_ref, dzo_ref, dgain_ref, z_ref, du_ref = refs[-8:]
        grad = grad + more_ref[...].astype(jnp.float32)
        grad_low = grad.astype(jnp.bfloat16)
        gl_ref[...] = grad_low
    x = x_ref[...]
    gain = gain_ref[0:1, :]
    scale = lax.rsqrt(jnp.mean(x * x, axis=1, keepdims=True) + EPSILON)
    normed = (x * scale * gain).astype(jnp.bfloat16)
    if mode == "back":
        hn_ref[...] = normed
    total = jnp.zeros((rows, width), jnp.float32)
    back = jnp.zeros((rows, width), jnp.float32)
    waited = 0
    for index in range(4):
        if needed[index] > waited:

            @pl.when(first_step)
            def _(start=waited, stop=needed[index]):
                for copy in copies[start:stop]:
                    copy.wait()

            waited = needed[index]
        cols = slice(index * block, (index + 1) * block)
        slot = index % 2
        z_ref[slot] = dot(normed, wi_ref[:, cols])
        if mode != "fwd":
            du_ref[slot] = dot(grad_low, wd_ref[cols, :], NT)
        for r in range(0, rows, chunk):
            part = slice(r, r + chunk)
            z = z_ref[slot, part, :]
            square = z * z
            tanh = jnp.tanh(GELU_SCALE * z * (1.0 + GELU_CUBE * square))
            half = 0.5 * (1.0 + tanh)
            act = (z * half).astype(jnp.bfloat16)
            if mode == "back":
                act_ref[part, cols] = act
            else:
                u_ref[slot, part, :] = act
            if mode != "fwd":
                slope = half + 0.5 * z * (1.0 - tanh * tanh) * (GELU_SCALE * (1.0 + 3.0 * GELU_CUBE * square))
                d_hidden = (du_ref[slot, part, :] * slope).astype(jnp.bfloat16)
                if mode == "back":
                    dzo_ref[part, cols] = d_hidden
                else:
                    dz_ref[slot, part, :] = d_hidden
        if mode != "back":
            total = total + dot(u_ref[slot], wd_ref[cols, :])
        if mode == "back":
            back = back + dot(dzo_ref[:, cols], wi_ref[:, cols], NT)
        elif mode == "both":
            back = back + dot(dz_ref[slot], wi_ref[:, cols], NT)
    if mode != "back":
        out_ref[...] = (x + total).astype(jnp.bfloat16)
    if mode != "fwd":
        scaled = back * gain
        mean = jnp.mean(scaled * x, axis=1, keepdims=True)
        dx_ref[...] = grad + scale * scaled - x * (scale * scale * scale * mean)
    if mode == "back":
        @pl.when(first_step)
        def _():
            dgain_ref[...] = jnp.zeros_like(dgain_ref)

        dgain_ref[...] += jnp.sum((back * x * scale).reshape(rows // 8, 8, width), axis=0)


def feed_forward(mode, x, gain, flags, pieces, cot=(), more=(), held=None, part=0, deps=()):
    rows, width = x.shape
    hidden = 2 * pieces[0].shape[1]
    steps = rows // TR
    row_block = pl.BlockSpec((TR, width), lambda i: (i, 0))
    place_block = pl.BlockSpec((TR, width), lambda i: (part * steps + i, 0))
    hidden_block = pl.BlockSpec((TR, hidden), lambda i: (part * steps + i, 0))
    low = jax.ShapeDtypeStruct((rows, width), jnp.bfloat16)
    full = jax.ShapeDtypeStruct((rows, width), jnp.float32)
    both = jax.ShapeDtypeStruct((2 * rows, width), jnp.bfloat16)
    wide = jax.ShapeDtypeStruct((2 * rows, hidden), jnp.bfloat16)
    outs = {
        "fwd": ([row_block], [low]),
        "both": ([row_block] * 2, [low, full]),
        "back": (
            [row_block] + [place_block] * 2 + [hidden_block] * 2 + [pl.BlockSpec((8, width), lambda i: (0, 0))],
            [full, both, both, wide, wide, jax.ShapeDtypeStruct((8, width), jnp.float32)],
        ),
    }[mode]
    slab = (2, TR, hidden // 4)
    slab32, slab16 = pltpu.VMEM(slab, jnp.float32), pltpu.VMEM(slab, jnp.bfloat16)
    scratch = {"fwd": [slab32, slab16], "both": [slab32, slab16, slab32, slab16], "back": [slab32, slab32]}[mode]
    matmuls = {"fwd": 2, "both": 4, "back": 3}[mode]
    held = held or ()
    block_input_steps = steps if mode == "back" else steps // 2
    return pl.pallas_call(
        without(partial(ffn_kernel, mode, part * steps, block_input_steps), 9 + len(cot) + len(more) + len(held), len(deps)),
        grid=(steps,),
        in_specs=[
            pl.BlockSpec(memory_space=pltpu.SMEM),
            row_block,
            pl.BlockSpec((8, width), lambda i: (0, 0)),
        ]
        + [pl.BlockSpec(memory_space=pl.ANY)] * 6
        + [pl.BlockSpec((TR, width), lambda i: (i % block_input_steps, 0))] * len(cot)
        + [row_block] * len(more)
        + [ANY] * (len(held) + len(deps)),
        out_specs=outs[0],
        out_shape=outs[1],
        scratch_shapes=scratch
        + [
            pltpu.VMEM((width, hidden), jnp.bfloat16),
            pltpu.VMEM((hidden, width), jnp.bfloat16),
            pltpu.SemaphoreType.DMA((8,)),
        ],
        input_output_aliases={9 + len(cot) + len(more) + index: 1 + index for index in range(len(held))},
        compiler_params=pltpu.CompilerParams(vmem_limit_bytes=VMEM_LIMIT),
        cost_estimate=pl.CostEstimate(
            flops=4 * matmuls * rows * width * hidden,
            bytes_accessed=4 * width * hidden + 8 * rows * width,
            transcendentals=rows * hidden,
        ),
        name="feed_forward_" + mode,
    )(flags, x, jnp.broadcast_to(gain[None], (8, width)), *pieces, *cot, *more, *held, *deps)


def product_kernel(left_of, slices, which, core_ref, *refs):
    count, left_count = len(left_of), max(left_of) + 1
    lefts, rights = refs[:left_count], refs[left_count : left_count + count]
    outs, turned_ref = refs[left_count + count : -1], refs[-1]
    step = pl.program_id(0)

    @pl.when(step == 0)
    def _():
        for index in range(left_count):
            turned_ref[index] = jnp.transpose(lefts[index][...].astype(jnp.float32)).astype(jnp.bfloat16)

    size = turned_ref.shape[1] // slices
    for index in range(count):
        steps = [s for s, owner in enumerate(which) if owner == index]
        chosen = functools.reduce(lambda a, b: a | b, [step == s for s in steps])

        @pl.when(chosen)
        def _(index=index):
            result = dot(turned_ref[left_of[index]], rights[index][...])
            if len(outs) == 1:
                outs[0][...] = result.astype(jnp.bfloat16)
                return
            send_ref, keep_ref = outs
            for part in range(slices // 2):
                first = result[2 * part * size : (2 * part + 1) * size]
                second = result[(2 * part + 1) * size : (2 * part + 2) * size]
                rows = slice(part * size, (part + 1) * size)
                is_second = core_ref[0] == 1
                send_ref[rows, :] = jnp.where(is_second, first, second).astype(jnp.bfloat16)
                keep_ref[rows, :] = jnp.where(is_second, second, first).astype(jnp.bfloat16)


def products(lefts, left_of, rights, block, slices, core, deps=()):
    span, rows = lefts[0].shape
    counts = [right.shape[1] // (2 * block) for right in rights]
    which, place = [], []
    for half in range(2):
        for index, number in enumerate(counts):
            for b in range(number):
                which.append(index)
                place.append(half * number + b)
    maps = []
    for index in range(len(rights)):
        held, column_of = 0, []
        for s, owner in enumerate(which):
            if owner == index:
                held = place[s]
            column_of.append(held)
        maps.append(column_of)
    steps = len(which)
    total = steps * block

    def right_map(column_of):
        def index_map(s):
            value = 0
            for position in range(steps):
                if column_of[position]:
                    value = value + jnp.where(s == position, column_of[position], 0)
            return (0, value)

        return index_map

    size = rows // slices
    apart = size % 16 == 0
    out_rows = rows // 2 if apart else rows
    out = jax.ShapeDtypeStruct((out_rows, total), jnp.bfloat16)
    results = pl.pallas_call(
        without(partial(product_kernel, left_of, slices, which), 1 + len(lefts) + len(rights), len(deps)),
        grid=(steps,),
        in_specs=[pl.BlockSpec(memory_space=pltpu.SMEM)]
        + [pl.BlockSpec((span, rows), lambda s: (0, 0)) for _ in lefts]
        + [pl.BlockSpec((span, block), right_map(column_of)) for column_of in maps]
        + [ANY] * len(deps),
        out_specs=[pl.BlockSpec((out_rows, block), lambda s: (0, s))] * (2 if apart else 1),
        out_shape=[out] * (2 if apart else 1),
        scratch_shapes=[pltpu.VMEM((len(lefts), rows, span), jnp.bfloat16)],
        compiler_params=pltpu.CompilerParams(vmem_limit_bytes=VMEM_LIMIT),
        cost_estimate=pl.CostEstimate(
            flops=2 * span * rows * total, bytes_accessed=2 * (span + rows) * total, transcendentals=0
        ),
        name="weight_products",
    )(core.reshape(1), *lefts, *rights, *deps)
    if apart:
        return results
    cut = results[0].reshape(slices // 2, 2, size, total)
    return pick(cut, 1 - core, 1).reshape(-1, total), pick(cut, core, 1).reshape(-1, total)


def sum_kernel(rounds, x_ref, out_ref, *refs):
    slots, send_sems, recv_sems = refs[: len(rounds)], refs[len(rounds)], refs[len(rounds) + 1]
    barrier = pltpu.get_barrier_semaphore()
    places, peers = [], []
    for axes in rounds:
        place, count = 0, 1
        for axis in axes:
            place = place * lax.axis_size(axis) + lax.axis_index(axis)
            count = count * lax.axis_size(axis)
        found = []
        for step in range(1, count):
            rest, device = lax.rem(place + step, count), {}
            for axis in reversed(axes):
                device[axis] = lax.rem(rest, lax.axis_size(axis))
                rest = lax.div(rest, lax.axis_size(axis))
            found.append(device)
        places.append(place)
        peers.append(found)
    for device in peers[0] + peers[1]:
        pl.semaphore_signal(barrier, inc=1, device_id=device, device_id_type=pl.DeviceIdType.MESH)
    pl.semaphore_wait(barrier, len(peers[0]) + len(peers[1]))
    value = x_ref[...]
    first = 0
    for slot, place, found in zip(slots, places, peers):
        slot[place] = value
        copies = []
        for step, device in enumerate(found):
            copies.append(
                pltpu.make_async_remote_copy(
                    src_ref=slot.at[place],
                    dst_ref=slot.at[place],
                    send_sem=send_sems.at[first + step],
                    recv_sem=recv_sems.at[first + step],
                    device_id=device,
                    device_id_type=pl.DeviceIdType.MESH,
                )
            )
        for copy in copies:
            copy.start()
        for copy in copies:
            copy.wait()
        first += len(found)
        value = slot[0]
        for index in range(1, len(found) + 1):
            value = value + slot[index]
    out_ref[...] = value


def sum_everywhere(x):
    rounds = (("dp",), ("section", "mp"))
    counts = [math.prod(lax.axis_size(axis) for axis in axes) for axes in rounds]
    copies = sum(counts) - len(counts)
    return pl.pallas_call(
        partial(sum_kernel, rounds),
        out_shape=jax.ShapeDtypeStruct(x.shape, x.dtype),
        in_specs=[pl.BlockSpec(memory_space=pltpu.VMEM)],
        out_specs=pl.BlockSpec(memory_space=pltpu.VMEM),
        scratch_shapes=[pltpu.VMEM((count,) + x.shape, x.dtype) for count in counts]
        + [pltpu.SemaphoreType.DMA((copies,)), pltpu.SemaphoreType.DMA((copies,))],
        compiler_params=pltpu.CompilerParams(collective_id=0, has_side_effects=True),
        name="sum_everywhere",
    )(x)


def pair_permute(x, axis, bit):
    pairs = [(i, i ^ (1 << bit)) for i in range(lax.axis_size(axis))]
    return lax.ppermute(x, axis, pairs)


def shifted(x, axis, by):
    peers = lax.axis_size(axis)
    pairs = [(i, i + by) for i in range(peers) if 0 <= i + by < peers]
    return lax.ppermute(x, axis, pairs)


def in_order(flag, first, second, axis):
    return jnp.where(
        flag == 0,
        jnp.concatenate([first, second], axis=axis),
        jnp.concatenate([second, first], axis=axis),
    )


def pick(x, index, axis):
    return lax.dynamic_index_in_dim(x, index, axis, False)


def after(values, *others):
    return lax.optimization_barrier((values, others))[0]


def exchange_rows(block, where_mp):
    return pick(block, where_mp, 0), pair_permute(pick(block, 1 - where_mp, 0), "mp", 0)


def scatter_rows(rows, where_mp):
    halves = rows.reshape(2, -1, rows.shape[1])
    own = pick(halves, where_mp, 0)
    arrived = pair_permute(pick(halves, 1 - where_mp, 0).astype(jnp.bfloat16), "mp", 0)
    return in_order(where_mp, own[None], arrived.astype(rows.dtype)[None], 0), arrived


def fetch_far(shard, core):
    half = shard.shape[0] // 2
    return pair_permute(lax.dynamic_slice_in_dim(shard, core * half, half, 0), "mp", 0)


def fetch_near(far):
    return pair_permute(far, "dp", 0)


class Reduction:
    def __init__(self, send, keep, dp_index, section=None):
        self.total, self.arrived = keep, pair_permute(send, "dp", 0)
        self.dp_index = dp_index
        bits = lax.axis_size("dp").bit_length() - 1
        self.left = ([("section", section)] if section is not None else []) + [("mp", None)]
        self.left += [("dp", bit) for bit in range(1, bits)]

    def settle(self):
        self.total = self.total.astype(jnp.float32) + self.arrived.astype(jnp.float32)

    def hop(self, *ties):
        brought = self.arrived
        self.arrived = after(self.arrived, *ties)
        axis, which = self.left.pop(0)
        if axis == "section":
            self.settle()
            halves = self.total.reshape(2, -1, self.total.shape[1])
            self.arrived = shifted(halves[0].astype(jnp.bfloat16), "section", -1)
            self.total = jnp.where(which == 0, 0.0, halves[1])
        elif axis == "mp":
            self.settle()
            width = self.total.shape[1] // 2
            self.arrived = pair_permute(self.total[:, width:].astype(jnp.bfloat16), "mp", 0)
            self.total = self.total[:, :width]
        else:
            self.settle()
            mark = (self.dp_index >> which) & 1
            width = self.total.shape[-1]
            halves = self.total.reshape(lax.axis_size("dp") >> (which + 1), 2, -1, width)
            self.arrived = pair_permute(pick(halves, 1 - mark, 1).astype(jnp.bfloat16), "dp", which)
            self.total = pick(halves, mark, 1)
        return brought

    def finish(self, *ties):
        while self.left:
            self.hop(*ties)
        self.settle()
        return self.total.reshape(-1, self.total.shape[-1])


def rms_norm(inputs, gain_row):
    return (
        inputs * lax.rsqrt(jnp.mean(inputs * inputs, axis=-1, keepdims=True) + EPSILON) * gain_row
    )


def norm_back(rows, gain_row, grad_normed):
    return jax.vjp(rms_norm, rows, gain_row)[1](grad_normed)


def low(x):
    return x.astype(jnp.bfloat16)


def local(
    block_input,
    out_cotangent,
    doc_lengths,
    question_lengths,
    coordinates,
    gains,
    bias_tables,
    self_qkv,
    self_out,
    ffn_in,
    ffn_out,
    cross_q,
    cross_kv,
    cross_out,
):
    section = lax.axis_index("section")
    on_encoder = section == 0
    dp_index = lax.axis_index("dp")
    core = dp_index & 1
    where_mp = lax.axis_index("mp")
    width = block_input.shape[4]
    quests = question_lengths.shape[2]
    own = self_qkv.shape[3]
    pairs = 2 * own // LANES
    heads = 2 * pairs
    parts = lax.axis_size("dp")
    flags = jnp.stack([core, where_mp]).astype(jnp.int32)

    rows_low = in_order(where_mp, *exchange_rows(block_input[0, :, 0], where_mp), 0)
    qkv_own = self_qkv[0].reshape(width, -1)
    qkv_far = fetch_far(qkv_own, core)
    qkv_other = in_order(core, qkv_far, fetch_near(qkv_far), 0)
    w_qkv = jnp.concatenate(
        [x[:, t * own : (t + 1) * own] for t in range(3) for x in (qkv_own, qkv_other)], axis=1
    )
    owned = after((ffn_in[0], ffn_out[0], self_out[0]), rows_low, qkv_far)
    fars = [fetch_far(x, core) for x in owned]

    lens = jnp.concatenate(
        [pick(doc_lengths, where_mp, 0), pick(question_lengths, where_mp, 0)[0]]
    ).astype(jnp.int32)
    coords = pick(coordinates, where_mp, 0)[0]
    tables = jnp.where(where_mp == 0, bias_tables, jnp.roll(bias_tables, heads // 2, axis=2))

    rows = rows_low.astype(jnp.float32)
    span = rows.shape[0]
    half = span // 2
    halves = (slice(0, half), slice(half, span))
    gain_self = jnp.where(on_encoder, gains[0], gains[2])
    normed_self = low(rms_norm(rows, gain_self))
    projected = low(dot(normed_self, w_qkv))
    merged, probs, middles, memories, arrivals = [], [], [], [], []
    for part in range(2):
        deps = memories[:1]

        def forward(kind, chosen):
            return attend_forward(
                kind, part, half, lens, chosen, coords, projected, 0, projected, 1, 2, pairs, quests, deps
            )

        out, prob = lax.cond(on_encoder, lambda: forward("enc", tables[:3]), lambda: forward("dec", tables[3:]))
        if not part:
            fars = after(fars, out)
            nears = [fetch_near(x) for x in fars]
            w_out = jnp.concatenate([self_out[0], in_order(core, fars[2], nears[2], 0)], axis=0)
            pieces = (ffn_in[0], fars[0], nears[0], ffn_out[0], fars[1], nears[1])
            cross_owned = after(
                (jnp.concatenate([cross_q, cross_kv.reshape(width, -1)], axis=1), cross_out, out_cotangent[0, :, 0]), fars
            )
            cross_fars = [fetch_far(x, core) for x in cross_owned[:2]]
            cot = exchange_rows(cross_owned[2], where_mp)
        else:
            cross_fars = after(cross_fars, out)
        middle = rows[halves[part]] + dot(out, w_out)
        memory = feed_forward("fwd", middle, gains[1], flags, pieces)[0]
        arrivals.append(shifted(memory, "section", 1))
        merged.append(out)
        probs.append(prob)
        middles.append(middle)
        memories.append(memory)
    query_other, cross_other = (in_order(core, far, fetch_near(far), 0) for far in cross_fars)
    w_query = jnp.concatenate([cross_q, query_other[:, :own]], axis=1)
    w_pair = jnp.concatenate(
        [x for t in range(2) for x in (cross_kv[:, t], query_other[:, (t + 1) * own : (t + 2) * own])], axis=1
    )
    w_cross = jnp.concatenate([cross_out, cross_other], axis=0)
    middle = jnp.concatenate(middles, axis=0)
    arrived = jnp.concatenate(arrivals, axis=0)

    normed_cross = low(rms_norm(middle, gains[3]))
    queries = low(dot(normed_cross, w_query))
    pair_rows = low(dot(arrived, w_pair))
    cross_merged, cross_prob = attend_forward(
        "cross", 0, span, lens, None, coords, queries, 0, pair_rows, 0, 1, pairs, quests
    )
    second = middle + dot(cross_merged, w_cross)
    output_low, grad_second = feed_forward("both", second, gains[4], flags, pieces, cot)
    output_rows, output_arrived = scatter_rows(
        jnp.where(on_encoder, jnp.concatenate(memories, axis=0), output_low), where_mp
    )
    second_low = low(grad_second)
    cross_grad = low(dot(second_low, w_cross, NT))
    returns, returned, carry = [], [], ()
    for part in range(2):
        query_grad, key_grad, value_grad, _ = attend_backward(
            "cross", part, cross_prob, cross_grad, cross_merged, queries, 0, pair_rows, 0, 1, pairs, quests, carry, returns[:1]
        )
        carry = (query_grad, key_grad, value_grad)
        returns.append(
            low(
                dot(key_grad[halves[part]], w_pair[:, : 2 * own], NT)
                + dot(value_grad[halves[part]], w_pair[:, 2 * own :], NT)
            )
        )
        returned.append(shifted(returns[part], "section", -1))
    query_cross = after(query_grad, returns[1])
    input_part, gain_cross = norm_back(middle, gains[3], dot(query_cross, w_query, NT))
    grad_first = grad_second + input_part

    def cross_products():
        return tuple(
            products(
                [normed_cross, arrived, second_low],
                [0, 1, 1, 2],
                [query_cross, key_grad, value_grad, cross_merged],
                own,
                2 * parts,
                core,
                returns[1:],
            )
        )

    def no_products():
        blank = jnp.zeros((width // 2, 8 * own), jnp.bfloat16)
        return blank, blank

    cross_steps = Reduction(*lax.cond(on_encoder, no_products, cross_products), dp_index, section)

    ffn_rows = jnp.where(on_encoder, middle, second)
    gain_ffn = jnp.where(on_encoder, gains[1], gains[4])
    held, gain_ffn_grad, grads_middle = None, 0.0, []
    for part in range(2):
        deps = [output_arrived]
        if part:
            returned[1] = after(returned[1], grad_ffn)
            deps.append(cross_steps.hop(grad_ffn))
        grad_ffn, *held, gain_part = feed_forward(
            "back",
            ffn_rows[halves[part]],
            gain_ffn,
            flags,
            pieces,
            cot,
            (returned[part],),
            held,
            part,
            deps,
        )
        gain_ffn_grad = gain_ffn_grad + jnp.sum(gain_part, axis=0)
        grads_middle.append(jnp.where(on_encoder, grad_ffn, grad_first[halves[part]]))
    ffn_send, ffn_keep = products([held[0], held[1]], [0, 1], [held[3], held[2]], own, parts, core)
    ffn_steps = Reduction(ffn_send, ffn_keep, dp_index)
    grad_middle = jnp.concatenate(grads_middle, axis=0)
    middle_low = low(grad_middle)
    merged_grad = low(dot(middle_low, w_out, NT))
    scores, query_grads, carry = [], [], ()
    for part in range(2):
        grad_part = merged_grad[halves[part]]
        if part:
            deps = (ffn_steps.hop(scores[0]), cross_steps.hop(scores[0]))
        else:
            deps = (ffn_send,)

        def backward(kind):
            return attend_backward(
                kind, part, probs[part], grad_part, merged[part], projected, 0, projected, 1, 2, pairs, quests, carry, deps
            )

        query_grad, key_grad, value_grad, score = lax.cond(
            on_encoder, lambda: backward("enc"), lambda: backward("dec")
        )
        carry = (key_grad, value_grad)
        query_grads.append(query_grad)
        scores.append(score)
    query_grad = jnp.concatenate(query_grads, axis=0)
    self_send, self_keep = products(
        [normed_self, middle_low],
        [0, 0, 0, 1],
        [query_grad, key_grad, value_grad, jnp.concatenate(merged, axis=0)],
        own,
        parts,
        core,
        [cross_steps.hop(scores[1])],
    )
    self_steps = Reduction(self_send, self_keep, dp_index)
    normed_grad = sum(
        dot(grad, w_qkv[:, 2 * own * t : 2 * own * (t + 1)], NT)
        for t, grad in enumerate((after(query_grad, self_send), key_grad, value_grad))
    )
    input_part, gain_self_grad = norm_back(rows, gain_self, normed_grad)
    input_grad = grad_middle + input_part
    grad_rows, grad_arrived = scatter_rows(input_grad, where_mp)

    tabs, diags = [], []
    deps = (self_send, input_grad, cross_steps.hop(self_send))
    for part in range(2):
        for quarter in range(2):
            tab, diag = lax.cond(
                on_encoder,
                lambda: table_sums("enc", part, quarter, coords, scores[part], quests, deps),
                lambda: table_sums("dec", part, quarter, coords, scores[part], quests, deps),
            )
            tabs.append(tab)
            diags.append(diag)
            if len(tabs) == 1:
                deps = (tab, self_steps.hop(tab), ffn_steps.hop(tab))
            elif len(tabs) == 2:
                deps = (tab,)
            elif len(tabs) == 3:
                deps = (tab, self_steps.hop(tab), ffn_steps.hop(tab), grad_arrived)
    table_grad = lax.cond(
        on_encoder,
        lambda: table_grads("enc", tabs, diags, span, quests, heads),
        lambda: table_grads("dec", tabs, diags, span, quests, heads),
    )
    table_grad = jnp.where(where_mp == 0, table_grad, jnp.roll(table_grad, heads // 2, axis=2))
    blank = jnp.zeros_like(gain_cross)
    gain_grad = jnp.where(
        on_encoder,
        jnp.stack([gain_self_grad, gain_ffn_grad, blank, blank, blank]),
        jnp.stack([blank, blank, gain_self_grad, gain_cross, gain_ffn_grad]),
    )
    small = jnp.concatenate([gain_grad.reshape(-1, LANES), table_grad.reshape(-1, LANES)], axis=0)
    count = small.shape[0]
    small = sum_everywhere(jnp.pad(small, ((0, -count % 8), (0, 0))))
    gain_count = gain_grad.size // LANES
    gain_sum = small[:gain_count].reshape(gain_grad.shape)
    table_sum = small[gain_count:count].reshape(table_grad.shape)
    cross_shard, ffn_shard, self_shard = cross_steps.finish(tab), ffn_steps.finish(tab), self_steps.finish(table_grad)
    hidden = ffn_in.shape[2]
    return (
        output_rows[None, :, None],
        grad_rows[None, :, None],
        gain_sum[:4],
        gain_sum[4],
        table_sum,
        self_shard[:, : 3 * own].reshape(-1, 3, own)[None],
        self_shard[:, 3 * own :].T[None],
        ffn_shard[:, :hidden][None],
        ffn_shard[:, hidden:].T[None],
        cross_shard[:, :own],
        cross_shard[:, own : 3 * own].reshape(-1, 2, own),
        cross_shard[:, 3 * own :].T,
    )


def solution(mesh):
    return jax.shard_map(
        local,
        mesh=mesh,
        in_specs=(
            P("section", None, "dp", "mp", None),
            P("section", None, "dp", "mp", None),
            P(None, "dp"),
            P(None, "dp", None),
            P(None, "dp", None, None),
            P(),
            P(),
            P("section", None, None, "mp"),
            P("section", "mp", None),
            P("section", None, "mp"),
            P("section", "mp", None),
            P(None, "mp"),
            P(None, None, "mp"),
            P("mp", None),
        ),
        out_specs=(
            P("section", None, "dp", "mp", None),
            P("section", None, "dp", "mp", None),
            P(),
            P(),
            P(),
            P("section", "dp", None, "mp"),
            P("section", "mp", "dp"),
            P("section", "dp", "mp"),
            P("section", "mp", "dp"),
            P(("section", "dp"), "mp"),
            P(("section", "dp"), None, "mp"),
            P("mp", ("section", "dp")),
        ),
        check_vma=False,
    )
```

```python
import functools
from functools import partial
import math

import jax
import jax.numpy as jnp
from jax import lax
from jax.experimental import pallas as pl
from jax.experimental.pallas import tpu as pltpu
from jax.sharding import PartitionSpec as P

HEAD = 64
LANES = 128
NEGATIVE = -1e30
EPSILON = 1e-06
GELU_SCALE = math.sqrt(2 / math.pi)
GELU_CUBE = 0.044715
TI = 64
FFN_BLOCKS = 4
VMEM_LIMIT = 56 * 1024 * 1024
NT = (((1,), (1,)), ((), ()))
NN = (((1,), (0,)), ((), ()))


def edge_list(exact_span, bucket_count, far_reach):
    log_edges = [
        int(
            math.ceil(
                exact_span * (far_reach / exact_span) ** (power_index / (bucket_count - exact_span))
            )
        )
        for power_index in range(1, bucket_count - exact_span)
    ]
    return list(range(1, exact_span + 1)) + log_edges


def magnitude(distance, exact_span, bucket_count, far_reach):
    bucket = jnp.minimum(distance, exact_span)
    for threshold in edge_list(exact_span, bucket_count, far_reach)[exact_span:]:
        bucket = bucket + (distance >= threshold).astype(jnp.int32)
    return bucket


def two_sided(relative, far_reach):
    return magnitude(jnp.abs(relative), 8, 16, far_reach) + jnp.where(relative > 0, 16, 0)


def one_sided(relative):
    return magnitude(jnp.maximum(-relative, 0), 16, 32, 128)


def half_lanes(block, head):
    lane = lax.broadcasted_iota(jnp.int32, block.shape, 1)
    keep = lane < HEAD if head == 0 else lane >= HEAD
    return jnp.where(keep, block, jnp.zeros_like(block))


def dot(a, b, dims=NN):
    return lax.dot_general(a, b, dims, preferred_element_type=jnp.float32)


def pick_lanes(row, index):
    return jnp.take_along_axis(jnp.broadcast_to(row, index.shape), index, axis=1)


def pick_sublanes(table_ref, head, low, odd, upper):
    parts = [
        jnp.take_along_axis(table_ref[head, 8 * part : 8 * part + 8, :], low, axis=0)
        for part in range(4)
    ]
    return jnp.where(upper, jnp.where(odd, parts[3], parts[2]), jnp.where(odd, parts[1], parts[0]))


def fwd_kernel(kind, part, tq, span, heads, len_ref, tabn_ref, tabx_ref, taby_ref, crow_ref, ccol_ref, q_ref, *refs):
    count = (len(refs) - 7) // 2
    k_refs, v_refs = refs[:count], refs[count : 2 * count]
    o_ref, p_ref, s_ref, idx_ref, mask_ref, near_ref, bias_ref = refs[-7:]
    length = span // count
    pair = pl.program_id(0)
    first_block = 0 if kind == "dec" else part * tq // LANES
    chunk = 16

    @pl.when(pair == 0)
    def _():
        key = lax.broadcasted_iota(jnp.int32, (8, span), 1)
        limit = len_ref[1 + part] if kind == "dec" else len_ref[0]
        mask_ref[...] = jnp.where(key < limit, 0.0, NEGATIVE)
        if kind != "cross":
            def near_rows(r, carry):
                rows = pl.ds(pl.multiple_of(r * 8, 8), 8)
                query = r * 8 + lax.broadcasted_iota(jnp.int32, (8, LANES), 0)
                for d in range(-2, 3):
                    key = d * LANES + lax.broadcasted_iota(jnp.int32, (8, LANES), 1)
                    bucket = one_sided(key - query) if kind == "dec" else two_sided(key - query, 128)
                    for head in range(heads):
                        value = pick_lanes(tabn_ref[head : head + 1, :], bucket)
                        if kind == "dec":
                            value = jnp.where(key <= query, value, NEGATIVE)
                        near_ref[head, rows, (d + 2) * LANES : (d + 3) * LANES] = value
                return carry

            lax.fori_loop(0, LANES // 8, near_rows, 0)
        if kind == "enc":

            def bucket_rows(r, carry):
                rows = pl.ds(pl.multiple_of(r * chunk, chunk), chunk)
                for axis in range(2):
                    far = crow_ref[axis : axis + 1, :] - ccol_ref[rows, axis : axis + 1]
                    idx_ref[axis, rows, :] = two_sided(far, 500)
                return carry

            lax.fori_loop(0, tq // chunk, bucket_rows, 0)

            def bias_rows(r, carry):
                rows = pl.ds(pl.multiple_of(r * 8, 8), 8)
                for c in range(0, span, LANES):
                    lanes = slice(c, c + LANES)
                    across = idx_ref[0, rows, lanes]
                    upward = idx_ref[1, rows, lanes]
                    low, odd, upper = upward & 7, (upward & 8) != 0, upward >= 16
                    for head in range(heads):
                        bias_ref[head, rows, lanes] = pick_lanes(
                            tabx_ref[head : head + 1, :], across
                        ) + pick_sublanes(taby_ref, head, low, odd, upper)
                return carry

            lax.fori_loop(0, tq // 8, bias_rows, 0, unroll=2)

    for head in range(2):
        query = half_lanes(q_ref[...], head)
        for index, k_ref in enumerate(k_refs):
            s_ref[head, :, index * length : (index + 1) * length] = dot(query, k_ref[...], NT)
        for r in range(0, tq, chunk):
            rows = slice(r, r + chunk)
            pieces = []
            for c in range(0, span, LANES):
                lanes = slice(c, c + LANES)
                piece = s_ref[head, rows, lanes] + mask_ref[0:1, lanes]
                if kind != "cross":
                    apart = min(max(c // LANES - (first_block + r // LANES), -2), 2) + 2
                    near = slice(apart * LANES, (apart + 1) * LANES)
                    piece = piece + near_ref[2 * pair + head, r % LANES : r % LANES + chunk, near]
                if kind == "enc":
                    piece = piece + bias_ref[2 * pair + head, rows, lanes]
                pieces.append(piece)
            score = jnp.concatenate(pieces, axis=1)
            score = jnp.exp(score - jnp.max(score, axis=1, keepdims=True))
            score = score * (1.0 / jnp.sum(score, axis=1, keepdims=True))
            p_ref[head, rows, :] = score.astype(jnp.bfloat16)
    first, second = (
        sum(
            dot(p_ref[head, :, index * length : (index + 1) * length], v_ref[...])
            for index, v_ref in enumerate(v_refs)
        )
        for head in range(2)
    )
    lane = lax.broadcasted_iota(jnp.int32, first.shape, 1)
    o_ref[...] = jnp.where(lane < HEAD, first, second).astype(jnp.bfloat16)


def bwd_kernel(kind, part, rows, span, p_ref, do_ref, o_ref, q_ref, k_ref, v_ref, *refs):
    carry = refs[: 2 if kind != "cross" else 3] if part else ()
    outs = refs[len(carry) :]
    dq_ref, dk_ref, dv_ref = outs[:3]
    low_ref, dp_ref = outs[3:]
    chunk = 16
    q_t = jnp.transpose(q_ref[...].astype(jnp.float32)).astype(jnp.bfloat16)
    do_t = jnp.transpose(do_ref[...].astype(jnp.float32)).astype(jnp.bfloat16)
    grads, key_grads, value_grads = [], [], []
    for head in range(2):
        d_out = half_lanes(do_ref[...], head)
        delta = jnp.sum(d_out.astype(jnp.float32) * o_ref[...].astype(jnp.float32), axis=1, keepdims=True)
        dp_ref[head] = dot(d_out, v_ref[...], NT)
        for r in range(0, rows, chunk):
            part_rows = slice(r, r + chunk)
            prob = p_ref[head, part_rows, :].astype(jnp.float32)
            low_ref[head, part_rows, :] = (
                prob * (dp_ref[head, part_rows, :] - delta[part_rows, :])
            ).astype(jnp.bfloat16)
        grads.append(dot(low_ref[head], k_ref[...]))
        half = slice(head * HEAD, (head + 1) * HEAD)
        key_grads.append(dot(q_t[half], low_ref[head]))
        value_grads.append(dot(do_t[half], p_ref[head]))
    lane = lax.broadcasted_iota(jnp.int32, grads[0].shape, 1)
    query_grad = jnp.where(lane < HEAD, grads[0], grads[1])
    if kind == "cross" and part:
        query_grad = query_grad + carry[0][...]
    dq_ref[...] = query_grad.astype(dq_ref.dtype)
    for index, (out_ref, pieces) in enumerate(((dk_ref, key_grads), (dv_ref, value_grads))):
        grad = jnp.transpose(jnp.concatenate(pieces, axis=0))
        if kind == "enc" and part:
            grad = grad + carry[index][...]
        if kind == "dec":
            if part:
                out_ref[0:span, :] = carry[index][0:span, :].astype(out_ref.dtype)
            out_ref[part * span : (part + 1) * span, :] = grad.astype(out_ref.dtype)
        else:
            out_ref[...] = grad.astype(out_ref.dtype)


def table_kernel(kind, ti, span, heads, low_ref, crow_ref, ccol_ref, tab_ref, diag_ref, row_ref, wide_ref, idx_ref):
    step = pl.program_id(0)
    group = 16
    wide = diag_ref.shape[2]
    pad = wide - span

    @pl.when(step == 0)
    def _():
        tab_ref[...] = jnp.zeros_like(tab_ref)

    if kind == "enc":
        for r in range(0, ti, 16):
            for axis in range(2):
                far = crow_ref[axis : axis + 1, :] - ccol_ref[r : r + 16, axis : axis + 1]
                idx_ref[axis, r : r + 16, :] = two_sided(far, 500).astype(jnp.float32)
    out_row = lax.broadcasted_iota(jnp.int32, (256, 256), 0)
    in_row = lax.broadcasted_iota(jnp.int32, (256, 256), 1)
    swap = (lax.div(out_row, 16) == lax.rem(in_row, 16)) & (lax.rem(out_row, 16) == lax.div(in_row, 16))
    swap = jnp.where(swap, 1.0, 0.0).astype(jnp.bfloat16)
    blank = jnp.zeros(((16 - heads) * 16, span), jnp.bfloat16)
    which = lax.broadcasted_iota(jnp.int32, (32, span), 0).astype(jnp.bfloat16)

    tab = jnp.zeros(tab_ref.shape, jnp.float32)
    diag = jnp.zeros((16, wide), jnp.float32)
    for g in range(ti // group):
        first = g * group
        block = jnp.concatenate([low_ref[h, first : first + group, :] for h in range(heads)] + [blank], axis=0)
        wide_ref[g] = dot(swap, block)
        if kind == "enc":
            row_ref[g] = wide_ref[g].astype(jnp.bfloat16)
        for j in range(group):
            lines = slice(16 * j, 16 * j + 16)
            if kind == "enc":
                hot = []
                for axis in range(2):
                    bucket = idx_ref[axis, first + j : first + j + 1, :]
                    bucket = jnp.broadcast_to(bucket, (32, span)).astype(jnp.bfloat16)
                    hot.append(jnp.where(bucket == which, jnp.bfloat16(1), jnp.bfloat16(0)))
                tab = tab + dot(row_ref[g, lines, :], jnp.concatenate(hot, axis=0), NT)
            line = wide_ref[g, lines, :]
            if pad:
                line = jnp.concatenate([line, jnp.zeros((16, pad), jnp.float32)], axis=1)
            diag = diag + pltpu.roll(line, (wide - (first + j)) % wide, 1)
    tab_ref[...] += tab
    diag_ref[0] = diag


ANY = pl.BlockSpec(memory_space=pl.ANY)


def without(kernel, first, count):
    return lambda *refs: kernel(*refs[:first], *refs[first + count :])


def near_width(kind, ti, span):
    return span + ti if kind == "enc" else span


def diag_sums(kind, diag, starts):
    wide = diag.shape[2]
    column = lax.broadcasted_iota(jnp.int32, (len(starts), wide), 1)
    start = jnp.array(starts, jnp.int32)[:, None]
    if kind == "dec":
        bucket = one_sided(jnp.where(column > start, column - wide, column) - start)
    else:
        bucket = two_sided(jnp.where(column > wide - TI, column - wide, column) - start, 128)
    hot = (bucket[..., None] == lax.iota(jnp.int32, 32)).astype(jnp.float32)
    return jnp.einsum("swb,shw->bh", hot, diag, precision=lax.Precision.HIGHEST)


def attend_forward(kind, part, tq, lens, tables, coords, q_src, q_col, kv_srcs, k_col, v_col, pairs, quests, deps=()):
    heads = 2 * pairs
    key_rows = sum(kv_src.shape[0] for kv_src in kv_srcs)
    span = key_rows // quests if kind == "dec" else key_rows
    key_block = part if kind == "dec" else 0
    count = len(kv_srcs)
    flops = tq * span * (60000 if kind == "enc" else 25000)
    tab_n = tab_x = jnp.zeros((16, LANES), jnp.float32)
    tab_y = jnp.zeros((1, 8, LANES), jnp.float32)
    if kind != "cross":
        tab_n = jnp.pad(tables[0].T, ((0, 16 - heads), (0, LANES - 32)))
    if kind == "enc":
        tab_x = jnp.pad(tables[1].T, ((0, 16 - heads), (0, LANES - 32)))
        tab_y = jnp.broadcast_to(tables[2].T[:, :, None], (heads, 32, LANES))
    return pl.pallas_call(
        without(partial(fwd_kernel, kind, part, tq, span, heads), 7 + 2 * count, len(deps)),
        grid=(pairs,),
        in_specs=[
            pl.BlockSpec(memory_space=pltpu.SMEM),
            pl.BlockSpec(tab_n.shape, lambda h: (0, 0)),
            pl.BlockSpec(tab_x.shape, lambda h: (0, 0)),
            pl.BlockSpec(tab_y.shape, lambda h: (0, 0, 0)),
            pl.BlockSpec(coords.shape, lambda h: (0, 0)),
            pl.BlockSpec((tq, 2), lambda h: (part, 0)),
            pl.BlockSpec((tq, LANES), lambda h: (part, q_col * pairs + h)),
        ]
        + [pl.BlockSpec((span // count, LANES), lambda h: (key_block, k_col * pairs + h))] * count
        + [pl.BlockSpec((span // count, LANES), lambda h: (key_block, v_col * pairs + h))] * count
        + [ANY] * len(deps),
        out_specs=[
            pl.BlockSpec((tq, LANES), lambda h: (0, h)),
            pl.BlockSpec((2, tq, span), lambda h: (h, 0, 0)),
        ],
        out_shape=[
            jax.ShapeDtypeStruct((tq, pairs * LANES), jnp.bfloat16),
            jax.ShapeDtypeStruct((heads, tq, key_rows), jnp.bfloat16),
        ],
        scratch_shapes=[
            pltpu.VMEM((2, tq, span), jnp.float32),
            pltpu.VMEM((2, tq, span) if kind == "enc" else (1, 8, LANES), jnp.int32),
            pltpu.VMEM((8, span), jnp.float32),
            pltpu.VMEM((1, 8, LANES) if kind == "cross" else (heads, LANES, 5 * LANES), jnp.float32),
            pltpu.VMEM((heads, tq, span) if kind == "enc" else (1, 8, LANES), jnp.float32),
        ],
        compiler_params=pltpu.CompilerParams(vmem_limit_bytes=VMEM_LIMIT),
        cost_estimate=pl.CostEstimate(
            flops=flops, bytes_accessed=4 * tq * span * pairs, transcendentals=2 * tq * span * pairs
        ),
        name="attend_forward_" + kind,
    )(lens, tab_n, tab_x, tab_y, coords, coords.T, q_src, *kv_srcs, *kv_srcs, *deps)


def attend_backward(kind, part, prob, grad_out, out, q_src, q_col, kv_src, k_col, v_col, pairs, quests, carry=(), deps=()):
    rows = grad_out.shape[0]
    key_rows = 2 * kv_src.shape[0] if kind == "cross" else kv_src.shape[0]
    width = pairs * LANES
    span = key_rows if kind == "enc" else key_rows // 2
    key_block = part if kind == "dec" else 0
    query_block = 0 if kind == "cross" else part
    score_block = part if kind == "cross" else 0
    if kind == "cross":
        carried = [pl.BlockSpec((rows, LANES), lambda h: (0, h))] + [pl.BlockSpec(memory_space=pl.ANY)] * 2
        key_out = pl.BlockSpec((span, LANES), lambda h: (part, h))
        aliases = {7: 1, 8: 2} if part else {}
    else:
        carried = [pl.BlockSpec((key_rows, LANES), lambda h: (0, h))] * 2
        key_out = pl.BlockSpec((key_rows, LANES), lambda h: (0, h))
        aliases = {}
    query_type = jnp.float32 if kind == "cross" and not part else jnp.bfloat16
    key_type = jnp.bfloat16 if kind == "cross" or part else jnp.float32
    low_block = pl.BlockSpec((2, rows, span), (lambda h: (0, 0, 0)) if kind == "cross" else (lambda h: (h, 0, 0)))
    low_shape = (2, rows, span) if kind == "cross" else (2 * pairs, rows, key_rows)
    return pl.pallas_call(
        without(partial(bwd_kernel, kind, part, rows, span), 6 + len(carry), len(deps)),
        grid=(pairs,),
        in_specs=[
            pl.BlockSpec((2, rows, span), lambda h: (h, 0, score_block)),
            pl.BlockSpec((rows, LANES), lambda h: (0, h)),
            pl.BlockSpec((rows, LANES), lambda h: (0, h)),
            pl.BlockSpec((rows, LANES), lambda h: (query_block, q_col * pairs + h)),
            pl.BlockSpec((span, LANES), lambda h: (key_block, k_col * pairs + h)),
            pl.BlockSpec((span, LANES), lambda h: (key_block, v_col * pairs + h)),
        ]
        + carried[: len(carry)]
        + [ANY] * len(deps),
        out_specs=[
            pl.BlockSpec((rows, LANES), lambda h: (0, h)),
            key_out,
            key_out,
            low_block,
        ],
        out_shape=[
            jax.ShapeDtypeStruct((rows, width), query_type),
            jax.ShapeDtypeStruct((key_rows, width), key_type),
            jax.ShapeDtypeStruct((key_rows, width), key_type),
            jax.ShapeDtypeStruct(low_shape, jnp.bfloat16),
        ],
        scratch_shapes=[pltpu.VMEM((2, rows, span), jnp.float32)],
        input_output_aliases=aliases,
        compiler_params=pltpu.CompilerParams(vmem_limit_bytes=VMEM_LIMIT),
        cost_estimate=pl.CostEstimate(
            flops=rows * span * 28000, bytes_accessed=4 * rows * span * pairs, transcendentals=0
        ),
        name="attend_backward_" + kind,
    )(prob, grad_out, out, q_src, kv_src, kv_src, *carry, *deps)


def table_sums(kind, part, quarter, coords, low, quests, deps=()):
    heads, rows, key_rows = low.shape
    rows = rows // 2
    span = key_rows // quests if kind == "dec" else key_rows
    steps = rows // TI
    wide = near_width(kind, TI, span)
    first = (2 * part + quarter) * steps
    tab, diag = pl.pallas_call(
        without(partial(table_kernel, kind, TI, span, heads), 3, len(deps)),
        grid=(steps,),
        in_specs=[
            pl.BlockSpec((heads, TI, span), lambda i: (0, quarter * steps + i, 0)),
            pl.BlockSpec(coords.shape, lambda i: (0, 0)),
            pl.BlockSpec((TI, 2), lambda i: (first + i, 0)),
        ]
        + [ANY] * len(deps),
        out_specs=[
            pl.BlockSpec((16, 64), lambda i: (0, 0)),
            pl.BlockSpec((1, 16, wide), lambda i: (i, 0, 0)),
        ],
        out_shape=[
            jax.ShapeDtypeStruct((16, 64), jnp.float32),
            jax.ShapeDtypeStruct((steps, 16, near_width("enc", TI, key_rows)), jnp.float32),
        ],
        scratch_shapes=[
            pltpu.VMEM((TI // 16, 256, span), jnp.bfloat16),
            pltpu.VMEM((TI // 16, 256, span), jnp.float32),
            pltpu.VMEM((2, TI, span) if kind == "enc" else (1, 8, LANES), jnp.float32),
        ],
        compiler_params=pltpu.CompilerParams(vmem_limit_bytes=VMEM_LIMIT),
        cost_estimate=pl.CostEstimate(
            flops=rows * span * 40000, bytes_accessed=2 * heads * rows * span, transcendentals=0
        ),
        name="table_sums_" + kind,
    )(low, coords, coords.T, *deps)
    return tab, diag


def table_grads(kind, tabs, diags, rows, quests, heads):
    steps = diags[0].shape[0]
    starts = [step * TI for step in range(4 * steps)]
    diag = jnp.concatenate(diags, axis=0)
    if kind == "dec":
        span = rows // quests
        near = diag_sums(kind, diag[:, :, :span], [start % span for start in starts])[:, :heads]
        blank = jnp.zeros_like(near)
        return jnp.stack([blank, blank, blank, near])
    tab = sum(tabs)
    near = diag_sums(kind, diag, starts)[:, :heads]
    return jnp.stack([near, tab[:heads, :32].T, tab[:heads, 32:].T, jnp.zeros_like(near)])


def weight_copies(core, pieces, wi_ref, wd_ref, sems):
    in_own, in_far, in_near, down_own, down_far, down_near = pieces
    own = in_own.shape[1]
    block = own // 2
    rows_in, rows_down = in_far.shape[0], down_far.shape[0]
    far_in = pl.ds(pl.multiple_of(core * rows_in, rows_in), rows_in)
    near_in = pl.ds(pl.multiple_of((1 - core) * rows_in, rows_in), rows_in)
    far_down = pl.ds(pl.multiple_of(own + core * rows_down, rows_down), rows_down)
    near_down = pl.ds(pl.multiple_of(own + (1 - core) * rows_down, rows_down), rows_down)
    moves = []
    for b in range(2):
        part = slice(b * block, (b + 1) * block)
        moves.append((in_own.at[:, part], wi_ref.at[:, part]))
        moves.append((down_own.at[part, :], wd_ref.at[part, :]))
    other = slice(own, 2 * own)
    moves.append((in_far, wi_ref.at[far_in, other]))
    moves.append((in_near, wi_ref.at[near_in, other]))
    moves.append((down_far, wd_ref.at[far_down, :]))
    moves.append((down_near, wd_ref.at[near_down, :]))
    return [pltpu.make_async_copy(src, dst, sems.at[i]) for i, (src, dst) in enumerate(moves)], (2, 4, 8, 8)


def ffn_kernel(mode, part, flag_ref, *refs):
    pieces, refs = refs[:6], refs[6:]
    refs, (wi_ref, wd_ref, sems) = refs[:-3], refs[-3:]
    copies, needed = weight_copies(flag_ref[0], pieces, wi_ref, wd_ref, sems)
    for copy in copies[: needed[0]]:
        copy.start()
    gain_ref, wa_ref = refs[:2]
    gain = gain_ref[0:1, :]
    if mode == "back":
        middle_ref, second_ref, own_ref, arrived_ref, more_ref, first_ref = refs[2:8]
        dx_ref, hn_ref, gl_ref, ml_ref, act_ref, dzo_ref, do_ref, dgain_ref, z_ref, du_ref = refs[-10:]
        on_encoder = flag_ref[2] == 0
        x = jnp.where(on_encoder, middle_ref[...], second_ref[...])
    else:
        base_ref, att_ref = refs[2:4]
        x = base_ref[...].astype(jnp.float32) + dot(att_ref[...], wa_ref[...])
        if mode == "fwd":
            out_ref, mid_ref, z_ref, u_ref = refs[4:]
        else:
            own_ref, arrived_ref, out_ref, mid_ref, dx_ref, low_ref, do_ref, z_ref, u_ref, du_ref, dz_ref = refs[4:]
        mid_ref[...] = x
    rows, width = x.shape
    hidden = wi_ref.shape[1]
    block, chunk = hidden // FFN_BLOCKS, 32
    if mode != "fwd":
        grad_low = jnp.where(part == flag_ref[1], own_ref[...], arrived_ref[...])
        grad = grad_low.astype(jnp.float32)
    scale = lax.rsqrt(jnp.mean(x * x, axis=1, keepdims=True) + EPSILON)
    normed_full = x * scale * gain
    normed = normed_full.astype(jnp.bfloat16)
    if mode == "back":
        grad = grad + more_ref[...].astype(jnp.float32)
        grad_low = grad.astype(jnp.bfloat16)
        hn_ref[...] = jnp.transpose(normed_full).astype(jnp.bfloat16)
        gl_ref[...] = jnp.transpose(grad).astype(jnp.bfloat16)
    total = jnp.zeros((rows, width), jnp.float32)
    back = jnp.zeros((rows, width), jnp.float32)
    waited = 0
    for index in range(FFN_BLOCKS + 1):
        if index < FFN_BLOCKS:
            stop = needed[index * 4 // FFN_BLOCKS]
            for copy in copies[waited:stop]:
                copy.wait()
            if index == 0:
                for copy in copies[stop:]:
                    copy.start()
            waited = max(waited, stop)
            cols = slice(index * block, (index + 1) * block)
            z_ref[index % 2] = dot(normed, wi_ref[:, cols])
            if mode != "fwd":
                du_ref[index % 2] = dot(grad_low, wd_ref[cols, :], NT)
        if index == 0:
            continue
        slot = (index - 1) % 2
        cols = slice((index - 1) * block, index * block)
        for r in range(0, rows, chunk):
            lines = slice(r, r + chunk)
            z = z_ref[slot, lines, :]
            square = z * z
            tanh = jnp.tanh(z * (GELU_SCALE + GELU_SCALE * GELU_CUBE * square))
            half = 0.5 + 0.5 * tanh
            act = (z * half).astype(jnp.bfloat16)
            if mode == "back":
                act_ref[lines, cols] = act
            else:
                u_ref[slot, lines, :] = act
            if mode != "fwd":
                slope = half + z * (0.5 - 0.5 * tanh * tanh) * (GELU_SCALE + 3.0 * GELU_SCALE * GELU_CUBE * square)
                d_hidden = (du_ref[slot, lines, :] * slope).astype(jnp.bfloat16)
                if mode == "back":
                    dzo_ref[lines, cols] = d_hidden
                else:
                    dz_ref[slot, lines, :] = d_hidden
        if mode != "back":
            total = total + dot(u_ref[slot], wd_ref[cols, :])
        if mode == "back":
            back = back + dot(dzo_ref[:, cols], wi_ref[:, cols], NT)
        elif mode == "both":
            back = back + dot(dz_ref[slot], wi_ref[:, cols], NT)
    if mode != "back":
        out_ref[...] = (x + total).astype(jnp.bfloat16)
    if mode != "fwd":
        scaled = back * gain
        mean = jnp.mean(scaled * x, axis=1, keepdims=True)
        grad = grad + scale * scaled - x * (scale * scale * scale * mean)
        if mode == "back":
            grad = jnp.where(on_encoder, grad, first_ref[...])
            ml_ref[...] = jnp.transpose(grad).astype(jnp.bfloat16)
            dgain_ref[...] = jnp.sum((back * x * scale).reshape(rows // 8, 8, width), axis=0)
        else:
            low_ref[...] = grad.astype(jnp.bfloat16)
        dx_ref[...] = grad
        do_ref[...] = dot(grad.astype(jnp.bfloat16), wa_ref[...], NT).astype(jnp.bfloat16)


def feed_forward(mode, part, flags, pieces, gain, w_att, rows_in, held=(), deps=()):
    width = w_att.shape[0]
    rows = min(x.shape[0] for x, _ in rows_in)
    hidden = 2 * pieces[0].shape[1]
    row_block = pl.BlockSpec((rows, width), lambda i: (0, 0))
    turned_block = pl.BlockSpec((width, rows), lambda i: (0, part))
    hidden_block = pl.BlockSpec((rows, hidden), lambda i: (part, 0))
    low = jax.ShapeDtypeStruct((rows, width), jnp.bfloat16)
    full = jax.ShapeDtypeStruct((rows, width), jnp.float32)
    turned = jax.ShapeDtypeStruct((width, 2 * rows), jnp.bfloat16)
    wide = jax.ShapeDtypeStruct((2 * rows, hidden), jnp.bfloat16)
    small = jax.ShapeDtypeStruct((8, width), jnp.float32)
    outs = {
        "fwd": ([row_block] * 2, [low, full]),
        "both": ([row_block] * 5, [low, full, full, low, low]),
        "back": (
            [row_block]
            + [turned_block] * 3
            + [hidden_block] * 2
            + [row_block, pl.BlockSpec((8, width), lambda i: (0, 0))],
            [full, turned, turned, turned, wide, wide, low, small],
        ),
    }[mode]
    slab = (2, rows, hidden // FFN_BLOCKS)
    slab32, slab16 = pltpu.VMEM(slab, jnp.float32), pltpu.VMEM(slab, jnp.bfloat16)
    scratch = {"fwd": [slab32, slab16], "both": [slab32, slab16, slab32, slab16], "back": [slab32, slab32]}[mode]
    matmuls = {"fwd": 2, "both": 4, "back": 3}[mode]
    inputs = 9 + len(rows_in)
    return pl.pallas_call(
        without(partial(ffn_kernel, mode, part), inputs, len(held) + len(deps)),
        grid=(1,),
        in_specs=[pl.BlockSpec(memory_space=pltpu.SMEM)]
        + [ANY] * 6
        + [pl.BlockSpec((8, width), lambda i: (0, 0)), pl.BlockSpec(w_att.shape, lambda i: (0, 0))]
        + [pl.BlockSpec((rows, width), lambda i, block=block: (block, 0)) for _, block in rows_in]
        + [ANY] * (len(held) + len(deps)),
        out_specs=outs[0],
        out_shape=outs[1],
        scratch_shapes=scratch
        + [
            pltpu.VMEM((width, hidden), jnp.bfloat16),
            pltpu.VMEM((hidden, width), jnp.bfloat16),
            pltpu.SemaphoreType.DMA((8,)),
        ],
        input_output_aliases={inputs + index: 1 + index for index in range(len(held))},
        compiler_params=pltpu.CompilerParams(vmem_limit_bytes=VMEM_LIMIT),
        cost_estimate=pl.CostEstimate(
            flops=4 * matmuls * rows * width * hidden,
            bytes_accessed=4 * width * hidden + 8 * rows * width,
            transcendentals=rows * hidden,
        ),
        name="feed_forward_" + mode,
    )(flags, *pieces, jnp.broadcast_to(gain[None], (8, width)), w_att, *(x for x, _ in rows_in), *held, *deps)


def product_kernel(left_of, parts_of, slices, which, core_ref, *refs):
    left_count, count = max(left_of) + 1, sum(parts_of)
    lefts, rights = refs[:left_count], refs[left_count : left_count + count]
    outs, held_ref = refs[left_count + count : -1], refs[-1]
    step = pl.program_id(0)
    rows, span = lefts[0].shape
    size = rows // slices
    half = rows // 2

    @pl.when(step == 0)
    def _():
        for index, left in enumerate(lefts):
            if len(outs) == 1:
                held_ref[index] = left[...]
                continue
            for first, core in ((0, 1 - core_ref[0]), (half, core_ref[0])):
                for part in range(slices // 2):
                    source = pl.ds(pl.multiple_of((2 * part + core) * size, 16), size)
                    held_ref[index, first + part * size : first + (part + 1) * size, :] = left[source, :]

    def product(index, lines):
        parts = rights[sum(parts_of[:index]) : sum(parts_of[: index + 1])]
        length = span // len(parts)
        return sum(
            dot(held_ref[left_of[index], lines, part * length : (part + 1) * length], right[...])
            for part, right in enumerate(parts)
        ).astype(jnp.bfloat16)

    for index in range(len(parts_of)):
        steps = [s for s, owner in enumerate(which) if owner == index]
        chosen = functools.reduce(lambda a, b: a | b, [step == s for s in steps])

        @pl.when(chosen)
        def _(index=index):
            if len(outs) == 1:
                outs[0][...] = product(index, slice(0, rows))
            else:
                outs[0][...] = product(index, slice(0, half))
                outs[1][...] = product(index, slice(half, rows))


def products(lefts, left_of, rights, block, slices, core, deps=()):
    rows, span = lefts[0].shape
    parts_of = [len(right) for right in rights]
    counts = [right[0].shape[1] // (2 * block) for right in rights]
    which, place = [], []
    for half in range(2):
        for index, number in enumerate(counts):
            for b in range(number):
                which.append(index)
                place.append(half * number + b)
    maps = []
    for index, right in enumerate(rights):
        held, column_of = 0, []
        for s, owner in enumerate(which):
            if owner == index:
                held = place[s]
            column_of.append(held)
        maps += [column_of] * len(right)
    steps = len(which)
    total = steps * block

    def right_map(column_of):
        def index_map(s):
            value = 0
            for position in range(steps):
                if column_of[position]:
                    value = value + jnp.where(s == position, column_of[position], 0)
            return (0, value)

        return index_map

    size = rows // slices
    apart = size % 16 == 0
    out_rows = rows // 2 if apart else rows
    out = jax.ShapeDtypeStruct((out_rows, total), jnp.bfloat16)
    flat = [part for right in rights for part in right]
    results = pl.pallas_call(
        without(
            partial(product_kernel, left_of, parts_of, slices, which), 1 + len(lefts) + len(flat), len(deps)
        ),
        grid=(steps,),
        in_specs=[pl.BlockSpec(memory_space=pltpu.SMEM)]
        + [pl.BlockSpec((rows, span), lambda s: (0, 0)) for _ in lefts]
        + [pl.BlockSpec((part.shape[0], block), right_map(column_of)) for part, column_of in zip(flat, maps)]
        + [ANY] * len(deps),
        out_specs=[pl.BlockSpec((out_rows, block), lambda s: (0, s))] * (2 if apart else 1),
        out_shape=[out] * (2 if apart else 1),
        scratch_shapes=[pltpu.VMEM((len(lefts), rows, span), jnp.bfloat16)],
        compiler_params=pltpu.CompilerParams(vmem_limit_bytes=VMEM_LIMIT),
        cost_estimate=pl.CostEstimate(
            flops=2 * span * rows * total, bytes_accessed=2 * (span + rows) * total, transcendentals=0
        ),
        name="weight_products",
    )(core.reshape(1), *lefts, *flat, *deps)
    if apart:
        return results
    cut = results[0].reshape(slices // 2, 2, size, total)
    return pick(cut, 1 - core, 1).reshape(-1, total), pick(cut, core, 1).reshape(-1, total)


def nothing(shapes):
    return pl.pallas_call(
        lambda *refs: None, out_shape=shapes, out_specs=[ANY] * len(shapes), name="nothing"
    )()


def sum_kernel(rounds, x_ref, out_ref, *refs):
    slots, send_sems, recv_sems = refs[: len(rounds)], refs[len(rounds)], refs[len(rounds) + 1]
    barrier = pltpu.get_barrier_semaphore()
    places, peers = [], []
    for axes in rounds:
        place, count = 0, 1
        for axis in axes:
            place = place * lax.axis_size(axis) + lax.axis_index(axis)
            count = count * lax.axis_size(axis)
        found = []
        for step in range(1, count):
            rest, device = lax.rem(place + step, count), {}
            for axis in reversed(axes):
                device[axis] = lax.rem(rest, lax.axis_size(axis))
                rest = lax.div(rest, lax.axis_size(axis))
            found.append(device)
        places.append(place)
        peers.append(found)
    for device in peers[0] + peers[1]:
        pl.semaphore_signal(barrier, inc=1, device_id=device, device_id_type=pl.DeviceIdType.MESH)
    pl.semaphore_wait(barrier, len(peers[0]) + len(peers[1]))
    value = x_ref[...]
    first = 0
    for slot, place, found in zip(slots, places, peers):
        slot[place] = value
        copies = []
        for step, device in enumerate(found):
            copies.append(
                pltpu.make_async_remote_copy(
                    src_ref=slot.at[place],
                    dst_ref=slot.at[place],
                    send_sem=send_sems.at[first + step],
                    recv_sem=recv_sems.at[first + step],
                    device_id=device,
                    device_id_type=pl.DeviceIdType.MESH,
                )
            )
        for copy in copies:
            copy.start()
        for copy in copies:
            copy.wait()
        first += len(found)
        value = slot[0]
        for index in range(1, len(found) + 1):
            value = value + slot[index]
    out_ref[...] = value


def sum_everywhere(x):
    rounds = (("dp",), ("section", "mp"))
    counts = [math.prod(lax.axis_size(axis) for axis in axes) for axes in rounds]
    copies = sum(counts) - len(counts)
    return pl.pallas_call(
        partial(sum_kernel, rounds),
        out_shape=jax.ShapeDtypeStruct(x.shape, x.dtype),
        in_specs=[pl.BlockSpec(memory_space=pltpu.VMEM)],
        out_specs=pl.BlockSpec(memory_space=pltpu.VMEM),
        scratch_shapes=[pltpu.VMEM((count,) + x.shape, x.dtype) for count in counts]
        + [pltpu.SemaphoreType.DMA((copies,)), pltpu.SemaphoreType.DMA((copies,))],
        compiler_params=pltpu.CompilerParams(collective_id=0, has_side_effects=True),
        name="sum_everywhere",
    )(x)


def pair_permute(x, axis, bit):
    pairs = [(i, i ^ (1 << bit)) for i in range(lax.axis_size(axis))]
    return lax.ppermute(x, axis, pairs)


def shifted(x, axis, by):
    peers = lax.axis_size(axis)
    pairs = [(i, i + by) for i in range(peers) if 0 <= i + by < peers]
    return lax.ppermute(x, axis, pairs)


def in_order(flag, first, second, axis):
    return jnp.where(
        flag == 0,
        jnp.concatenate([first, second], axis=axis),
        jnp.concatenate([second, first], axis=axis),
    )


def pick(x, index, axis):
    return lax.dynamic_index_in_dim(x, index, axis, False)


def after(values, *others):
    return lax.optimization_barrier((values, others))[0]


def exchange_rows(block, where_mp):
    return pick(block, where_mp, 0), pair_permute(pick(block, 1 - where_mp, 0), "mp", 0)


def scatter_rows(rows, where_mp):
    halves = rows.reshape(2, -1, rows.shape[1])
    return pick(halves, where_mp, 0), pair_permute(pick(halves, 1 - where_mp, 0).astype(jnp.bfloat16), "mp", 0)


def fetch_far(shard, core):
    half = shard.shape[0] // 2
    return pair_permute(lax.dynamic_slice_in_dim(shard, core * half, half, 0), "mp", 0)


def fetch_near(far):
    return pair_permute(far, "dp", 0)


class Reduction:
    def __init__(self, send, keep, dp_index, section=None):
        self.total, self.arrived = keep, pair_permute(send, "dp", 0)
        self.dp_index = dp_index
        bits = lax.axis_size("dp").bit_length() - 1
        self.left = ([("section", section)] if section is not None else []) + [("mp", None)]
        self.left += [("dp", bit) for bit in range(1, bits)]

    def settle(self):
        self.total = self.total.astype(jnp.float32) + self.arrived.astype(jnp.float32)

    def hop(self, *ties):
        brought = self.arrived
        self.arrived = after(self.arrived, *ties)
        axis, which = self.left.pop(0)
        if axis == "section":
            self.settle()
            halves = self.total.reshape(2, -1, self.total.shape[1])
            self.arrived = shifted(halves[0].astype(jnp.bfloat16), "section", -1)
            self.total = jnp.where(which == 0, 0.0, halves[1])
        elif axis == "mp":
            self.settle()
            width = self.total.shape[1] // 2
            self.arrived = pair_permute(self.total[:, width:].astype(jnp.bfloat16), "mp", 0)
            self.total = self.total[:, :width]
        else:
            self.settle()
            mark = (self.dp_index >> which) & 1
            width = self.total.shape[-1]
            halves = self.total.reshape(lax.axis_size("dp") >> (which + 1), 2, -1, width)
            self.arrived = pair_permute(pick(halves, 1 - mark, 1).astype(jnp.bfloat16), "dp", which)
            self.total = pick(halves, mark, 1)
        return brought

    def finish(self, *ties):
        while self.left:
            self.hop()
        self.arrived = after(self.arrived, *ties)
        self.settle()
        return self.total.reshape(-1, self.total.shape[-1])


def rms_norm(inputs, gain_row):
    return (
        inputs * lax.rsqrt(jnp.mean(inputs * inputs, axis=-1, keepdims=True) + EPSILON) * gain_row
    )


def norm_back(rows, gain_row, grad_normed):
    return jax.vjp(rms_norm, rows, gain_row)[1](grad_normed)


def low(x):
    return x.astype(jnp.bfloat16)


def local(
    block_input,
    out_cotangent,
    doc_lengths,
    question_lengths,
    coordinates,
    gains,
    bias_tables,
    self_qkv,
    self_out,
    ffn_in,
    ffn_out,
    cross_q,
    cross_kv,
    cross_out,
):
    section = lax.axis_index("section")
    on_encoder = section == 0
    dp_index = lax.axis_index("dp")
    core = dp_index & 1
    where_mp = lax.axis_index("mp")
    width = block_input.shape[4]
    quests = question_lengths.shape[2]
    own = self_qkv.shape[3]
    pairs = 2 * own // LANES
    heads = 2 * pairs
    parts = lax.axis_size("dp")
    flags = jnp.stack([core, where_mp, section]).astype(jnp.int32)

    rows_low = in_order(where_mp, *exchange_rows(block_input[0, :, 0], where_mp), 0)
    qkv_own = self_qkv[0].reshape(width, -1)
    qkv_far = fetch_far(qkv_own, core)
    qkv_other = in_order(core, qkv_far, fetch_near(qkv_far), 0)
    w_qkv = jnp.concatenate(
        [x[:, t * own : (t + 1) * own] for t in range(3) for x in (qkv_own, qkv_other)], axis=1
    )
    owned = after((ffn_in[0], ffn_out[0], self_out[0]), rows_low, qkv_far)
    fars = [fetch_far(x, core) for x in owned]

    lens = jnp.concatenate(
        [pick(doc_lengths, where_mp, 0), pick(question_lengths, where_mp, 0)[0]]
    ).astype(jnp.int32)
    coords = pick(coordinates, where_mp, 0)[0]
    tables = jnp.where(where_mp == 0, bias_tables, jnp.roll(bias_tables, heads // 2, axis=2))

    rows = rows_low.astype(jnp.float32)
    span = rows.shape[0]
    half = span // 2
    halves = (slice(0, half), slice(half, span))
    gain_self = jnp.where(on_encoder, gains[0], gains[2])
    normed_self = low(rms_norm(rows, gain_self))
    projected = low(dot(normed_self, w_qkv))
    merged, probs, middles, memories, arrivals = [], [], [], [], []
    for part in range(2):
        deps = memories[:1]

        def forward(kind, chosen):
            return attend_forward(
                kind, part, half, lens, chosen, coords, projected, 0, [projected], 1, 2, pairs, quests, deps
            )

        out, prob = lax.cond(on_encoder, lambda: forward("enc", tables[:3]), lambda: forward("dec", tables[3:]))
        if not part:
            fars = after(fars, out)
            nears = [fetch_near(x) for x in fars]
            w_out = jnp.concatenate([self_out[0], in_order(core, fars[2], nears[2], 0)], axis=0)
            pieces = (ffn_in[0], fars[0], nears[0], ffn_out[0], fars[1], nears[1])
            cross_owned = after(
                (jnp.concatenate([cross_q, cross_kv.reshape(width, -1)], axis=1), cross_out, out_cotangent[0, :, 0]), fars
            )
            cross_fars = [fetch_far(x, core) for x in cross_owned[:2]]
            cot = exchange_rows(cross_owned[2], where_mp)
        else:
            cross_fars = after(cross_fars, out)
        memory, middle = feed_forward("fwd", part, flags, pieces, gains[1], w_out, [(rows_low, part), (out, 0)])
        arrivals.append(shifted(memory, "section", 1))
        merged.append(out)
        probs.append(prob)
        middles.append(middle)
        memories.append(memory)
    query_other, cross_other = (in_order(core, far, fetch_near(far), 0) for far in cross_fars)
    w_query = jnp.concatenate([cross_q, query_other[:, :own]], axis=1)
    w_pair = jnp.concatenate(
        [x for t in range(2) for x in (cross_kv[:, t], query_other[:, (t + 1) * own : (t + 2) * own])], axis=1
    )
    w_cross = jnp.concatenate([cross_out, cross_other], axis=0)
    middle = jnp.concatenate(middles, axis=0)

    normed_cross = low(rms_norm(middle, gains[3]))
    queries = low(dot(normed_cross, w_query))
    first_pair = low(dot(arrivals[0], w_pair))
    arrivals[1] = after(arrivals[1], queries, first_pair)
    pair_rows = [first_pair, low(dot(arrivals[1], w_pair))]
    cross_merged, cross_prob = attend_forward(
        "cross", 0, span, lens, None, coords, queries, 0, pair_rows, 0, 1, pairs, quests
    )
    outputs, seconds, grads_second, lows_second, cross_grads = zip(
        *(
            feed_forward(
                "both",
                part,
                flags,
                pieces,
                gains[4],
                w_cross,
                [(middles[part], 0), (cross_merged, part), (cot[0], 0), (cot[1], 0)],
            )
            for part in range(2)
        )
    )
    output_own, output_arrived = scatter_rows(
        jnp.where(on_encoder, jnp.concatenate(memories, axis=0), jnp.concatenate(outputs, axis=0)), where_mp
    )
    cross_grad = jnp.concatenate(cross_grads, axis=0)
    returns, returned, carry = [], [], ()
    for part in range(2):
        query_grad, key_grad, value_grad, _ = attend_backward(
            "cross",
            part,
            cross_prob,
            cross_grad,
            cross_merged,
            queries,
            0,
            pair_rows[part],
            0,
            1,
            pairs,
            quests,
            carry,
            [returns[0], output_arrived] if part else [],
        )
        carry = (query_grad, key_grad, value_grad)
        returns.append(
            low(
                dot(key_grad[halves[part]], w_pair[:, : 2 * own], NT)
                + dot(value_grad[halves[part]], w_pair[:, 2 * own :], NT)
            )
        )
        returned.append(shifted(returns[part], "section", -1))
    query_cross = after(query_grad, returns[1])

    def cross_norm():
        input_part, gain_part = norm_back(middle, gains[3], dot(query_cross, w_query, NT))
        return jnp.concatenate(grads_second, axis=0) + input_part, gain_part

    def no_norm():
        return tuple(
            nothing([jax.ShapeDtypeStruct((span, width), jnp.float32), jax.ShapeDtypeStruct((width,), jnp.float32)])
        )

    grad_first, gain_cross = lax.cond(on_encoder, no_norm, cross_norm)

    gain_ffn = jnp.where(on_encoder, gains[1], gains[4])
    held, gain_ffn_grad, grads_middle, merged_grads = [], 0.0, [], []
    for part in range(2):
        if part:
            returned[1] = after(returned[1], grads_middle[0])
        grad_middle, *held, merged_grad, gain_part = feed_forward(
            "back",
            part,
            flags,
            pieces,
            gain_ffn,
            w_out,
            [
                (middles[part], 0),
                (seconds[part], 0),
                (cot[0], 0),
                (cot[1], 0),
                (returned[part], 0),
                (grad_first, part),
            ],
            held,
        )
        gain_ffn_grad = gain_ffn_grad + jnp.sum(gain_part, axis=0)
        grads_middle.append(grad_middle)
        merged_grads.append(merged_grad)
    hn_turned, gl_turned, ml_turned, activated, hidden_grad = held
    in_send, in_keep = products([hn_turned], [0], [[hidden_grad]], 2 * own, parts, core)
    down_send, down_keep = products([gl_turned], [0], [[activated]], 2 * own, parts, core, [in_send])
    in_steps = Reduction(in_send, in_keep, dp_index)
    down_steps = Reduction(down_send, down_keep, dp_index)

    def cross_products():
        return tuple(
            products(
                [normed_cross.T, jnp.concatenate(arrivals, axis=0).T, jnp.concatenate(lows_second, axis=0).T],
                [0, 1, 1, 2],
                [[query_cross], [key_grad], [value_grad], [cross_merged]],
                own,
                2 * parts,
                core,
                [down_send],
            )
        )

    def no_products():
        blank = jax.ShapeDtypeStruct((width // 2, 8 * own), jnp.bfloat16)
        return tuple(nothing([blank, blank]))

    cross_send, cross_keep = lax.cond(on_encoder, no_products, cross_products)
    cross_steps = Reduction(cross_send, cross_keep, dp_index, section)
    scores, query_grads, carry = [], [], ()
    for part in range(2):
        deps = (down_steps.hop(scores[0]), cross_steps.hop(scores[0])) if part else (down_send, cross_send, in_steps.hop())

        def backward(kind):
            return attend_backward(
                kind, part, probs[part], merged_grads[part], merged[part], projected, 0, projected, 1, 2, pairs, quests,
                carry, deps
            )

        query_grad, key_grad, value_grad, score = lax.cond(
            on_encoder, lambda: backward("enc"), lambda: backward("dec")
        )
        carry = (key_grad, value_grad)
        query_grads.append(query_grad)
        scores.append(score)
    self_send, self_keep = products(
        [normed_self.T, ml_turned],
        [0, 0, 0, 1],
        [query_grads, [key_grad], [value_grad], merged],
        own,
        parts,
        core,
    )
    self_steps = Reduction(self_send, self_keep, dp_index)
    normed_grad = (
        jnp.concatenate([dot(x, w_qkv[:, : 2 * own], NT) for x in query_grads], axis=0)
        + dot(key_grad, w_qkv[:, 2 * own : 4 * own], NT)
        + dot(value_grad, w_qkv[:, 4 * own :], NT)
    )
    input_part, gain_self_grad = norm_back(rows, gain_self, normed_grad)
    input_grad = jnp.concatenate(grads_middle, axis=0) + input_part
    grad_own, grad_arrived = scatter_rows(input_grad, where_mp)

    tabs, diags = [], []
    deps = (self_send, input_grad, in_steps.hop(scores[0]), cross_steps.hop(self_send))
    for part in range(2):
        for quarter in range(2):
            tab, diag = lax.cond(
                on_encoder,
                lambda: table_sums("enc", part, quarter, coords, scores[part], quests, deps),
                lambda: table_sums("dec", part, quarter, coords, scores[part], quests, deps),
            )
            tabs.append(tab)
            diags.append(diag)
            if len(tabs) == 1:
                deps = (tab, self_steps.hop(tab), down_steps.hop(self_send))
            elif len(tabs) == 2:
                deps = (tab, in_steps.hop(tab), cross_steps.hop(tab), grad_arrived)
            elif len(tabs) == 3:
                deps = (tab, down_steps.hop(tab), self_steps.hop(tab), in_steps.arrived)
    table_grad = lax.cond(
        on_encoder,
        lambda: table_grads("enc", tabs, diags, span, quests, heads),
        lambda: table_grads("dec", tabs, diags, span, quests, heads),
    )
    table_grad = jnp.where(where_mp == 0, table_grad, jnp.roll(table_grad, heads // 2, axis=2))
    blank = jnp.zeros((width,), jnp.float32)
    gain_grad = jnp.where(
        on_encoder,
        jnp.stack([gain_self_grad, gain_ffn_grad, blank, blank, blank]),
        jnp.stack([blank, blank, gain_self_grad, gain_cross, gain_ffn_grad]),
    )
    small = jnp.concatenate([gain_grad.reshape(-1, LANES), table_grad.reshape(-1, LANES)], axis=0)
    count = small.shape[0]
    small = jnp.pad(small, ((0, -count % 8), (0, 0)))
    cross_shard, in_shard, down_shard = (x.finish(tabs[3]) for x in (cross_steps, in_steps, down_steps))
    small = sum_everywhere(after(small, self_steps.hop(tab), down_steps.arrived, cross_steps.arrived))
    gain_count = gain_grad.size // LANES
    gain_sum = small[:gain_count].reshape(gain_grad.shape)
    table_sum = small[gain_count:count].reshape(table_grad.shape)
    self_shard = self_steps.finish(table_grad)
    output_rows, grad_rows = (
        in_order(where_mp, own_rows[None], after(arrived, tabs[2]).astype(own_rows.dtype)[None], 0)
        for own_rows, arrived in ((output_own, output_arrived), (grad_own, grad_arrived))
    )
    return (
        output_rows[None, :, None],
        grad_rows[None, :, None],
        gain_sum[:4],
        gain_sum[4],
        table_sum,
        self_shard[:, : 3 * own].reshape(-1, 3, own)[None],
        self_shard[:, 3 * own :].T[None],
        in_shard[None],
        down_shard.T[None],
        cross_shard[:, :own],
        cross_shard[:, own : 3 * own].reshape(-1, 2, own),
        cross_shard[:, 3 * own :].T,
    )


def solution(mesh):
    return jax.shard_map(
        local,
        mesh=mesh,
        in_specs=(
            P("section", None, "dp", "mp", None),
            P("section", None, "dp", "mp", None),
            P(None, "dp"),
            P(None, "dp", None),
            P(None, "dp", None, None),
            P(),
            P(),
            P("section", None, None, "mp"),
            P("section", "mp", None),
            P("section", None, "mp"),
            P("section", "mp", None),
            P(None, "mp"),
            P(None, None, "mp"),
            P("mp", None),
        ),
        out_specs=(
            P("section", None, "dp", "mp", None),
            P("section", None, "dp", "mp", None),
            P(),
            P(),
            P(),
            P("section", "dp", None, "mp"),
            P("section", "mp", "dp"),
            P("section", "dp", "mp"),
            P("section", "mp", "dp"),
            P(("section", "dp"), "mp"),
            P(("section", "dp"), None, "mp"),
            P("mp", ("section", "dp")),
        ),
        check_vma=False,
    )
```

```python
import functools
from functools import partial
import math

import jax
import jax.numpy as jnp
from jax import lax
from jax.experimental import pallas as pl
from jax.experimental.pallas import tpu as pltpu
from jax.sharding import PartitionSpec as P

HEAD = 64
LANES = 128
NEGATIVE = -1e30
EPSILON = 1e-06
GELU_SCALE = math.sqrt(2 / math.pi)
GELU_CUBE = 0.044715
TI = 64
FFN_BLOCKS = 4
TR = 256
VMEM_LIMIT = 56 * 1024 * 1024
NT = (((1,), (1,)), ((), ()))
NN = (((1,), (0,)), ((), ()))


def edge_list(exact_span, bucket_count, far_reach):
    log_edges = [
        int(
            math.ceil(
                exact_span * (far_reach / exact_span) ** (power_index / (bucket_count - exact_span))
            )
        )
        for power_index in range(1, bucket_count - exact_span)
    ]
    return list(range(1, exact_span + 1)) + log_edges


def magnitude(distance, exact_span, bucket_count, far_reach):
    bucket = jnp.minimum(distance, exact_span)
    for threshold in edge_list(exact_span, bucket_count, far_reach)[exact_span:]:
        bucket = bucket + (distance >= threshold).astype(jnp.int32)
    return bucket


def two_sided(relative, far_reach):
    return magnitude(jnp.abs(relative), 8, 16, far_reach) + jnp.where(relative > 0, 16, 0)


def one_sided(relative):
    return magnitude(jnp.maximum(-relative, 0), 16, 32, 128)


def half_lanes(block, head):
    lane = lax.broadcasted_iota(jnp.int32, block.shape, 1)
    keep = lane < HEAD if head == 0 else lane >= HEAD
    return jnp.where(keep, block, jnp.zeros_like(block))


def dot(a, b, dims=NN):
    return lax.dot_general(a, b, dims, preferred_element_type=jnp.float32)


def pick_lanes(row, index):
    return jnp.take_along_axis(jnp.broadcast_to(row, index.shape), index, axis=1)


def pick_sublanes(table_ref, head, low, odd, upper):
    parts = [
        jnp.take_along_axis(table_ref[head, 8 * part : 8 * part + 8, :], low, axis=0)
        for part in range(4)
    ]
    return jnp.where(upper, jnp.where(odd, parts[3], parts[2]), jnp.where(odd, parts[1], parts[0]))


def fwd_kernel(kind, part, tq, span, heads, len_ref, tabn_ref, tabx_ref, taby_ref, crow_ref, ccol_ref, q_ref, *refs):
    count = (len(refs) - 7) // 2
    k_refs, v_refs = refs[:count], refs[count : 2 * count]
    o_ref, p_ref, s_ref, idx_ref, mask_ref, near_ref, bias_ref = refs[-7:]
    length = span // count
    pair = pl.program_id(0)
    first_block = 0 if kind == "dec" else part * tq // LANES
    chunk = 16

    @pl.when(pair == 0)
    def _():
        key = lax.broadcasted_iota(jnp.int32, (8, span), 1)
        limit = len_ref[1 + part] if kind == "dec" else len_ref[0]
        mask_ref[...] = jnp.where(key < limit, 0.0, NEGATIVE)
        if kind != "cross":
            def near_rows(r, carry):
                rows = pl.ds(pl.multiple_of(r * 8, 8), 8)
                query = r * 8 + lax.broadcasted_iota(jnp.int32, (8, LANES), 0)
                for d in range(-2, 3):
                    key = d * LANES + lax.broadcasted_iota(jnp.int32, (8, LANES), 1)
                    bucket = one_sided(key - query) if kind == "dec" else two_sided(key - query, 128)
                    for head in range(heads):
                        value = pick_lanes(tabn_ref[head : head + 1, :], bucket)
                        if kind == "dec":
                            value = jnp.where(key <= query, value, NEGATIVE)
                        near_ref[head, rows, (d + 2) * LANES : (d + 3) * LANES] = value
                return carry

            lax.fori_loop(0, LANES // 8, near_rows, 0)
        if kind == "enc":

            def bucket_rows(r, carry):
                rows = pl.ds(pl.multiple_of(r * chunk, chunk), chunk)
                for axis in range(2):
                    far = crow_ref[axis : axis + 1, :] - ccol_ref[rows, axis : axis + 1]
                    idx_ref[axis, rows, :] = two_sided(far, 500)
                return carry

            lax.fori_loop(0, tq // chunk, bucket_rows, 0)

            def bias_rows(r, carry):
                rows = pl.ds(pl.multiple_of(r * 8, 8), 8)
                for c in range(0, span, LANES):
                    lanes = slice(c, c + LANES)
                    across = idx_ref[0, rows, lanes]
                    upward = idx_ref[1, rows, lanes]
                    low, odd, upper = upward & 7, (upward & 8) != 0, upward >= 16
                    for head in range(heads):
                        bias_ref[head, rows, lanes] = pick_lanes(
                            tabx_ref[head : head + 1, :], across
                        ) + pick_sublanes(taby_ref, head, low, odd, upper)
                return carry

            lax.fori_loop(0, tq // 8, bias_rows, 0, unroll=2)

    for head in range(2):
        query = half_lanes(q_ref[...], head)
        for index, k_ref in enumerate(k_refs):
            s_ref[head, :, index * length : (index + 1) * length] = dot(query, k_ref[...], NT)
        for r in range(0, tq, chunk):
            rows = slice(r, r + chunk)
            pieces = []
            for c in range(0, span, LANES):
                lanes = slice(c, c + LANES)
                piece = s_ref[head, rows, lanes] + mask_ref[0:1, lanes]
                if kind != "cross":
                    apart = min(max(c // LANES - (first_block + r // LANES), -2), 2) + 2
                    near = slice(apart * LANES, (apart + 1) * LANES)
                    piece = piece + near_ref[2 * pair + head, r % LANES : r % LANES + chunk, near]
                if kind == "enc":
                    piece = piece + bias_ref[2 * pair + head, rows, lanes]
                pieces.append(piece)
            score = jnp.concatenate(pieces, axis=1)
            score = jnp.exp(score - jnp.max(score, axis=1, keepdims=True))
            score = score * (1.0 / jnp.sum(score, axis=1, keepdims=True))
            p_ref[head, rows, :] = score.astype(jnp.bfloat16)
    first, second = (
        sum(
            dot(p_ref[head, :, index * length : (index + 1) * length], v_ref[...])
            for index, v_ref in enumerate(v_refs)
        )
        for head in range(2)
    )
    lane = lax.broadcasted_iota(jnp.int32, first.shape, 1)
    o_ref[...] = jnp.where(lane < HEAD, first, second).astype(jnp.bfloat16)


def bwd_kernel(kind, part, rows, span, p_ref, do_ref, o_ref, q_ref, k_ref, v_ref, *refs):
    carry = refs[: 2 if kind != "cross" else 3] if part else ()
    outs = refs[len(carry) :]
    dq_ref, dk_ref, dv_ref = outs[:3]
    low_ref, dp_ref = outs[3:]
    chunk = 16
    q_t = jnp.transpose(q_ref[...].astype(jnp.float32)).astype(jnp.bfloat16)
    do_t = jnp.transpose(do_ref[...].astype(jnp.float32)).astype(jnp.bfloat16)
    grads, key_grads, value_grads = [], [], []
    for head in range(2):
        d_out = half_lanes(do_ref[...], head)
        delta = jnp.sum(d_out.astype(jnp.float32) * o_ref[...].astype(jnp.float32), axis=1, keepdims=True)
        dp_ref[head] = dot(d_out, v_ref[...], NT)
        for r in range(0, rows, chunk):
            part_rows = slice(r, r + chunk)
            prob = p_ref[head, part_rows, :].astype(jnp.float32)
            low_ref[head, part_rows, :] = (
                prob * (dp_ref[head, part_rows, :] - delta[part_rows, :])
            ).astype(jnp.bfloat16)
        grads.append(dot(low_ref[head], k_ref[...]))
        half = slice(head * HEAD, (head + 1) * HEAD)
        key_grads.append(dot(q_t[half], low_ref[head]))
        value_grads.append(dot(do_t[half], p_ref[head]))
    lane = lax.broadcasted_iota(jnp.int32, grads[0].shape, 1)
    query_grad = jnp.where(lane < HEAD, grads[0], grads[1])
    if kind == "cross" and part:
        query_grad = query_grad + carry[0][...]
    dq_ref[...] = query_grad.astype(dq_ref.dtype)
    for index, (out_ref, pieces) in enumerate(((dk_ref, key_grads), (dv_ref, value_grads))):
        grad = jnp.transpose(jnp.concatenate(pieces, axis=0))
        if kind == "enc" and part:
            grad = grad + carry[index][...]
        if kind == "dec":
            if part:
                out_ref[0:span, :] = carry[index][0:span, :].astype(out_ref.dtype)
            out_ref[part * span : (part + 1) * span, :] = grad.astype(out_ref.dtype)
        else:
            out_ref[...] = grad.astype(out_ref.dtype)


def table_kernel(kind, ti, span, heads, low_ref, crow_ref, ccol_ref, tab_ref, diag_ref, row_ref, wide_ref, idx_ref):
    step = pl.program_id(0)
    group = 16
    wide = diag_ref.shape[2]
    pad = wide - span

    @pl.when(step == 0)
    def _():
        tab_ref[...] = jnp.zeros_like(tab_ref)

    if kind == "enc":
        for r in range(0, ti, 16):
            for axis in range(2):
                far = crow_ref[axis : axis + 1, :] - ccol_ref[r : r + 16, axis : axis + 1]
                idx_ref[axis, r : r + 16, :] = two_sided(far, 500).astype(jnp.float32)
    out_row = lax.broadcasted_iota(jnp.int32, (256, 256), 0)
    in_row = lax.broadcasted_iota(jnp.int32, (256, 256), 1)
    swap = (lax.div(out_row, 16) == lax.rem(in_row, 16)) & (lax.rem(out_row, 16) == lax.div(in_row, 16))
    swap = jnp.where(swap, 1.0, 0.0).astype(jnp.bfloat16)
    blank = jnp.zeros(((16 - heads) * 16, span), jnp.bfloat16)
    which = lax.broadcasted_iota(jnp.int32, (32, span), 0).astype(jnp.bfloat16)

    tab = jnp.zeros(tab_ref.shape, jnp.float32)
    diag = jnp.zeros((16, wide), jnp.float32)
    for g in range(ti // group):
        first = g * group
        block = jnp.concatenate([low_ref[h, first : first + group, :] for h in range(heads)] + [blank], axis=0)
        wide_ref[g] = dot(swap, block)
        if kind == "enc":
            row_ref[g] = wide_ref[g].astype(jnp.bfloat16)
        for j in range(group):
            lines = slice(16 * j, 16 * j + 16)
            if kind == "enc":
                hot = []
                for axis in range(2):
                    bucket = idx_ref[axis, first + j : first + j + 1, :]
                    bucket = jnp.broadcast_to(bucket, (32, span)).astype(jnp.bfloat16)
                    hot.append(jnp.where(bucket == which, jnp.bfloat16(1), jnp.bfloat16(0)))
                tab = tab + dot(row_ref[g, lines, :], jnp.concatenate(hot, axis=0), NT)
            line = wide_ref[g, lines, :]
            if pad:
                line = jnp.concatenate([line, jnp.zeros((16, pad), jnp.float32)], axis=1)
            diag = diag + pltpu.roll(line, (wide - (first + j)) % wide, 1)
    tab_ref[...] += tab
    diag_ref[0] = diag


ANY = pl.BlockSpec(memory_space=pl.ANY)


def without(kernel, first, count):
    return lambda *refs: kernel(*refs[:first], *refs[first + count :])


def near_width(kind, ti, span):
    return span + ti if kind == "enc" else span


def diag_sums(kind, diag, starts):
    wide = diag.shape[2]
    column = lax.broadcasted_iota(jnp.int32, (len(starts), wide), 1)
    start = jnp.array(starts, jnp.int32)[:, None]
    if kind == "dec":
        bucket = one_sided(jnp.where(column > start, column - wide, column) - start)
    else:
        bucket = two_sided(jnp.where(column > wide - TI, column - wide, column) - start, 128)
    hot = (bucket[..., None] == lax.iota(jnp.int32, 32)).astype(jnp.float32)
    return jnp.einsum("swb,shw->bh", hot, diag, precision=lax.Precision.HIGHEST)


def attend_forward(kind, part, tq, lens, tables, coords, q_src, q_col, kv_srcs, k_col, v_col, pairs, quests, deps=()):
    heads = 2 * pairs
    key_rows = sum(kv_src.shape[0] for kv_src in kv_srcs)
    span = key_rows // quests if kind == "dec" else key_rows
    key_block = part if kind == "dec" else 0
    count = len(kv_srcs)
    flops = tq * span * (60000 if kind == "enc" else 25000)
    tab_n = tab_x = jnp.zeros((16, LANES), jnp.float32)
    tab_y = jnp.zeros((1, 8, LANES), jnp.float32)
    if kind != "cross":
        tab_n = jnp.pad(tables[0].T, ((0, 16 - heads), (0, LANES - 32)))
    if kind == "enc":
        tab_x = jnp.pad(tables[1].T, ((0, 16 - heads), (0, LANES - 32)))
        tab_y = jnp.broadcast_to(tables[2].T[:, :, None], (heads, 32, LANES))
    return pl.pallas_call(
        without(partial(fwd_kernel, kind, part, tq, span, heads), 7 + 2 * count, len(deps)),
        grid=(pairs,),
        in_specs=[
            pl.BlockSpec(memory_space=pltpu.SMEM),
            pl.BlockSpec(tab_n.shape, lambda h: (0, 0)),
            pl.BlockSpec(tab_x.shape, lambda h: (0, 0)),
            pl.BlockSpec(tab_y.shape, lambda h: (0, 0, 0)),
            pl.BlockSpec(coords.shape, lambda h: (0, 0)),
            pl.BlockSpec((tq, 2), lambda h: (part, 0)),
            pl.BlockSpec((tq, LANES), lambda h: (part, q_col * pairs + h)),
        ]
        + [pl.BlockSpec((span // count, LANES), lambda h: (key_block, k_col * pairs + h))] * count
        + [pl.BlockSpec((span // count, LANES), lambda h: (key_block, v_col * pairs + h))] * count
        + [ANY] * len(deps),
        out_specs=[
            pl.BlockSpec((tq, LANES), lambda h: (0, h)),
            pl.BlockSpec((2, tq, span), lambda h: (h, 0, 0)),
        ],
        out_shape=[
            jax.ShapeDtypeStruct((tq, pairs * LANES), jnp.bfloat16),
            jax.ShapeDtypeStruct((heads, tq, key_rows), jnp.bfloat16),
        ],
        scratch_shapes=[
            pltpu.VMEM((2, tq, span), jnp.float32),
            pltpu.VMEM((2, tq, span) if kind == "enc" else (1, 8, LANES), jnp.int32),
            pltpu.VMEM((8, span), jnp.float32),
            pltpu.VMEM((1, 8, LANES) if kind == "cross" else (heads, LANES, 5 * LANES), jnp.float32),
            pltpu.VMEM((heads, tq, span) if kind == "enc" else (1, 8, LANES), jnp.float32),
        ],
        compiler_params=pltpu.CompilerParams(vmem_limit_bytes=VMEM_LIMIT),
        cost_estimate=pl.CostEstimate(
            flops=flops, bytes_accessed=4 * tq * span * pairs, transcendentals=2 * tq * span * pairs
        ),
        name="attend_forward_" + kind,
    )(lens, tab_n, tab_x, tab_y, coords, coords.T, q_src, *kv_srcs, *kv_srcs, *deps)


def attend_backward(kind, part, prob, grad_out, out, q_src, q_col, kv_src, k_col, v_col, pairs, quests, carry=(), deps=()):
    rows = grad_out.shape[0]
    key_rows = 2 * kv_src.shape[0] if kind == "cross" else kv_src.shape[0]
    width = pairs * LANES
    span = key_rows if kind == "enc" else key_rows // 2
    key_block = part if kind == "dec" else 0
    query_block = 0 if kind == "cross" else part
    score_block = part if kind == "cross" else 0
    if kind == "cross":
        carried = [pl.BlockSpec((rows, LANES), lambda h: (0, h))] + [pl.BlockSpec(memory_space=pl.ANY)] * 2
        key_out = pl.BlockSpec((span, LANES), lambda h: (part, h))
        aliases = {7: 1, 8: 2} if part else {}
    else:
        carried = [pl.BlockSpec((key_rows, LANES), lambda h: (0, h))] * 2
        key_out = pl.BlockSpec((key_rows, LANES), lambda h: (0, h))
        aliases = {}
    query_type = jnp.float32 if kind == "cross" and not part else jnp.bfloat16
    key_type = jnp.bfloat16 if kind == "cross" or part else jnp.float32
    low_block = pl.BlockSpec((2, rows, span), (lambda h: (0, 0, 0)) if kind == "cross" else (lambda h: (h, 0, 0)))
    low_shape = (2, rows, span) if kind == "cross" else (2 * pairs, rows, key_rows)
    return pl.pallas_call(
        without(partial(bwd_kernel, kind, part, rows, span), 6 + len(carry), len(deps)),
        grid=(pairs,),
        in_specs=[
            pl.BlockSpec((2, rows, span), lambda h: (h, 0, score_block)),
            pl.BlockSpec((rows, LANES), lambda h: (0, h)),
            pl.BlockSpec((rows, LANES), lambda h: (0, h)),
            pl.BlockSpec((rows, LANES), lambda h: (query_block, q_col * pairs + h)),
            pl.BlockSpec((span, LANES), lambda h: (key_block, k_col * pairs + h)),
            pl.BlockSpec((span, LANES), lambda h: (key_block, v_col * pairs + h)),
        ]
        + carried[: len(carry)]
        + [ANY] * len(deps),
        out_specs=[
            pl.BlockSpec((rows, LANES), lambda h: (0, h)),
            key_out,
            key_out,
            low_block,
        ],
        out_shape=[
            jax.ShapeDtypeStruct((rows, width), query_type),
            jax.ShapeDtypeStruct((key_rows, width), key_type),
            jax.ShapeDtypeStruct((key_rows, width), key_type),
            jax.ShapeDtypeStruct(low_shape, jnp.bfloat16),
        ],
        scratch_shapes=[pltpu.VMEM((2, rows, span), jnp.float32)],
        input_output_aliases=aliases,
        compiler_params=pltpu.CompilerParams(vmem_limit_bytes=VMEM_LIMIT),
        cost_estimate=pl.CostEstimate(
            flops=rows * span * 28000, bytes_accessed=4 * rows * span * pairs, transcendentals=0
        ),
        name="attend_backward_" + kind,
    )(prob, grad_out, out, q_src, kv_src, kv_src, *carry, *deps)


def table_sums(kind, part, quarter, coords, low, quests, deps=()):
    heads, rows, key_rows = low.shape
    rows = rows // 2
    span = key_rows // quests if kind == "dec" else key_rows
    steps = rows // TI
    wide = near_width(kind, TI, span)
    first = (2 * part + quarter) * steps
    tab, diag = pl.pallas_call(
        without(partial(table_kernel, kind, TI, span, heads), 3, len(deps)),
        grid=(steps,),
        in_specs=[
            pl.BlockSpec((heads, TI, span), lambda i: (0, quarter * steps + i, 0)),
            pl.BlockSpec(coords.shape, lambda i: (0, 0)),
            pl.BlockSpec((TI, 2), lambda i: (first + i, 0)),
        ]
        + [ANY] * len(deps),
        out_specs=[
            pl.BlockSpec((16, 64), lambda i: (0, 0)),
            pl.BlockSpec((1, 16, wide), lambda i: (i, 0, 0)),
        ],
        out_shape=[
            jax.ShapeDtypeStruct((16, 64), jnp.float32),
            jax.ShapeDtypeStruct((steps, 16, near_width("enc", TI, key_rows)), jnp.float32),
        ],
        scratch_shapes=[
            pltpu.VMEM((TI // 16, 256, span), jnp.bfloat16),
            pltpu.VMEM((TI // 16, 256, span), jnp.float32),
            pltpu.VMEM((2, TI, span) if kind == "enc" else (1, 8, LANES), jnp.float32),
        ],
        compiler_params=pltpu.CompilerParams(vmem_limit_bytes=VMEM_LIMIT),
        cost_estimate=pl.CostEstimate(
            flops=rows * span * 40000, bytes_accessed=2 * heads * rows * span, transcendentals=0
        ),
        name="table_sums_" + kind,
    )(low, coords, coords.T, *deps)
    return tab, diag


def table_grads(kind, tabs, diags, rows, quests, heads):
    steps = diags[0].shape[0]
    starts = [step * TI for step in range(4 * steps)]
    diag = jnp.concatenate(diags, axis=0)
    if kind == "dec":
        span = rows // quests
        near = diag_sums(kind, diag[:, :, :span], [start % span for start in starts])[:, :heads]
        blank = jnp.zeros_like(near)
        return jnp.stack([blank, blank, blank, near])
    tab = sum(tabs)
    near = diag_sums(kind, diag, starts)[:, :heads]
    return jnp.stack([near, tab[:heads, :32].T, tab[:heads, 32:].T, jnp.zeros_like(near)])


def weight_copies(core, pieces, wi_ref, wd_ref, sems):
    in_own, in_far, in_near, down_own, down_far, down_near = pieces
    own = in_own.shape[1]
    block = own // 2
    rows_in, rows_down = in_far.shape[0], down_far.shape[0]
    far_in = pl.ds(pl.multiple_of(core * rows_in, rows_in), rows_in)
    near_in = pl.ds(pl.multiple_of((1 - core) * rows_in, rows_in), rows_in)
    far_down = pl.ds(pl.multiple_of(own + core * rows_down, rows_down), rows_down)
    near_down = pl.ds(pl.multiple_of(own + (1 - core) * rows_down, rows_down), rows_down)
    moves = []
    for b in range(2):
        part = slice(b * block, (b + 1) * block)
        moves.append((in_own.at[:, part], wi_ref.at[:, part]))
        moves.append((down_own.at[part, :], wd_ref.at[part, :]))
    other = slice(own, 2 * own)
    moves.append((in_far, wi_ref.at[far_in, other]))
    moves.append((in_near, wi_ref.at[near_in, other]))
    moves.append((down_far, wd_ref.at[far_down, :]))
    moves.append((down_near, wd_ref.at[near_down, :]))
    return [pltpu.make_async_copy(src, dst, sems.at[i]) for i, (src, dst) in enumerate(moves)], (2, 4, 8, 8)


def ffn_kernel(mode, part, flag_ref, *refs):
    pieces, refs = refs[:6], refs[6:]
    refs, (wi_ref, wd_ref, sems) = refs[:-3], refs[-3:]
    copies, needed = weight_copies(flag_ref[0], pieces, wi_ref, wd_ref, sems)
    first_step = pl.program_id(0) == 0

    @pl.when(first_step)
    def _():
        for copy in copies[: needed[0]]:
            copy.start()

    gain_ref, wa_ref = refs[:2]
    gain = gain_ref[0:1, :]
    if mode == "back":
        middle_ref, second_ref, own_ref, arrived_ref, more_ref, first_ref = refs[2:8]
        dx_ref, hn_ref, gl_ref, ml_ref, act_ref, dzo_ref, do_ref, dgain_ref, z_ref, du_ref = refs[-10:]
        on_encoder = flag_ref[2] == 0
        x = jnp.where(on_encoder, middle_ref[...], second_ref[...])
    else:
        base_ref, att_ref = refs[2:4]
        x = base_ref[...].astype(jnp.float32) + dot(att_ref[...], wa_ref[...])
        if mode == "fwd":
            out_ref, mid_ref, z_ref, u_ref = refs[4:]
        else:
            own_ref, arrived_ref, out_ref, mid_ref, dx_ref, low_ref, do_ref, z_ref, u_ref, du_ref, dz_ref = refs[4:]
        mid_ref[...] = x
    rows, width = x.shape
    hidden = wi_ref.shape[1]
    block, chunk = hidden // FFN_BLOCKS, 32
    if mode != "fwd":
        half = part if mode == "back" else lax.div(2 * pl.program_id(0), pl.num_programs(0))
        grad_low = jnp.where(half == flag_ref[1], own_ref[...], arrived_ref[...])
        grad = grad_low.astype(jnp.float32)
    scale = lax.rsqrt(jnp.mean(x * x, axis=1, keepdims=True) + EPSILON)
    normed_full = x * scale * gain
    normed = normed_full.astype(jnp.bfloat16)
    if mode == "back":
        grad = grad + more_ref[...].astype(jnp.float32)
        grad_low = grad.astype(jnp.bfloat16)
        hn_ref[...] = jnp.transpose(normed_full).astype(jnp.bfloat16)
        gl_ref[...] = jnp.transpose(grad).astype(jnp.bfloat16)
    total = jnp.zeros((rows, width), jnp.float32)
    back = jnp.zeros((rows, width), jnp.float32)
    waited = 0
    for index in range(FFN_BLOCKS + 1):
        if index < FFN_BLOCKS:
            stop = needed[index * 4 // FFN_BLOCKS]
            if stop > waited:

                @pl.when(first_step)
                def _(waited=waited, stop=stop):
                    for copy in copies[waited:stop]:
                        copy.wait()
                    if waited == 0:
                        for copy in copies[stop:]:
                            copy.start()

                waited = stop
            cols = slice(index * block, (index + 1) * block)
            z_ref[index % 2] = dot(normed, wi_ref[:, cols])
            if mode != "fwd":
                du_ref[index % 2] = dot(grad_low, wd_ref[cols, :], NT)
        if index == 0:
            continue
        slot = (index - 1) % 2
        cols = slice((index - 1) * block, index * block)
        for r in range(0, rows, chunk):
            lines = slice(r, r + chunk)
            z = z_ref[slot, lines, :]
            square = z * z
            tanh = jnp.tanh(z * (GELU_SCALE + GELU_SCALE * GELU_CUBE * square))
            half = 0.5 + 0.5 * tanh
            act = (z * half).astype(jnp.bfloat16)
            if mode == "back":
                act_ref[lines, cols] = act
            else:
                u_ref[slot, lines, :] = act
            if mode != "fwd":
                slope = half + z * (0.5 - 0.5 * tanh * tanh) * (GELU_SCALE + 3.0 * GELU_SCALE * GELU_CUBE * square)
                d_hidden = (du_ref[slot, lines, :] * slope).astype(jnp.bfloat16)
                if mode == "back":
                    dzo_ref[lines, cols] = d_hidden
                else:
                    dz_ref[slot, lines, :] = d_hidden
        if mode != "back":
            total = total + dot(u_ref[slot], wd_ref[cols, :])
        if mode == "back":
            back = back + dot(dzo_ref[:, cols], wi_ref[:, cols], NT)
        elif mode == "both":
            back = back + dot(dz_ref[slot], wi_ref[:, cols], NT)
    if mode != "back":
        out_ref[...] = (x + total).astype(jnp.bfloat16)
    if mode != "fwd":
        scaled = back * gain
        mean = jnp.mean(scaled * x, axis=1, keepdims=True)
        grad = grad + scale * scaled - x * (scale * scale * scale * mean)
        if mode == "back":
            grad = jnp.where(on_encoder, grad, first_ref[...])
            ml_ref[...] = jnp.transpose(grad).astype(jnp.bfloat16)
            gain_part = jnp.sum((back * x * scale).reshape(rows // 8, 8, width), axis=0)
            dgain_ref[...] = jnp.where(first_step, gain_part, dgain_ref[...] + gain_part)
        else:
            low_ref[...] = grad.astype(jnp.bfloat16)
        dx_ref[...] = grad
        do_ref[...] = dot(grad.astype(jnp.bfloat16), wa_ref[...], NT).astype(jnp.bfloat16)


def feed_forward(mode, part, rows, flags, pieces, gain, w_att, rows_in, held=(), deps=()):
    width = w_att.shape[0]
    hidden = 2 * pieces[0].shape[1]
    steps = rows // TR
    row_block = pl.BlockSpec((TR, width), lambda i: (i, 0))
    turned_block = pl.BlockSpec((width, TR), lambda i: (0, part * steps + i))
    hidden_block = pl.BlockSpec((TR, hidden), lambda i: (part * steps + i, 0))
    low = jax.ShapeDtypeStruct((rows, width), jnp.bfloat16)
    full = jax.ShapeDtypeStruct((rows, width), jnp.float32)
    turned = jax.ShapeDtypeStruct((width, 2 * rows), jnp.bfloat16)
    wide = jax.ShapeDtypeStruct((2 * rows, hidden), jnp.bfloat16)
    small = jax.ShapeDtypeStruct((8, width), jnp.float32)
    outs = {
        "fwd": ([row_block] * 2, [low, full]),
        "both": ([row_block] * 5, [low, full, full, low, low]),
        "back": (
            [row_block]
            + [turned_block] * 3
            + [hidden_block] * 2
            + [row_block, pl.BlockSpec((8, width), lambda i: (0, 0))],
            [full, turned, turned, turned, wide, wide, low, small],
        ),
    }[mode]
    slab = (2, TR, hidden // FFN_BLOCKS)
    slab32, slab16 = pltpu.VMEM(slab, jnp.float32), pltpu.VMEM(slab, jnp.bfloat16)
    scratch = {"fwd": [slab32, slab16], "both": [slab32, slab16, slab32, slab16], "back": [slab32, slab32]}[mode]
    matmuls = {"fwd": 2, "both": 4, "back": 3}[mode]
    inputs = 9 + len(rows_in)
    return pl.pallas_call(
        without(partial(ffn_kernel, mode, part), inputs, len(held) + len(deps)),
        grid=(steps,),
        in_specs=[pl.BlockSpec(memory_space=pltpu.SMEM)]
        + [ANY] * 6
        + [pl.BlockSpec((8, width), lambda i: (0, 0)), pl.BlockSpec(w_att.shape, lambda i: (0, 0))]
        + [pl.BlockSpec((TR, width), lambda i, at=at, turn=turn: (at + i % turn, 0)) for _, at, turn in rows_in]
        + [ANY] * (len(held) + len(deps)),
        out_specs=outs[0],
        out_shape=outs[1],
        scratch_shapes=scratch
        + [
            pltpu.VMEM((width, hidden), jnp.bfloat16),
            pltpu.VMEM((hidden, width), jnp.bfloat16),
            pltpu.SemaphoreType.DMA((8,)),
        ],
        input_output_aliases={inputs + index: 1 + index for index in range(len(held))},
        compiler_params=pltpu.CompilerParams(vmem_limit_bytes=VMEM_LIMIT),
        cost_estimate=pl.CostEstimate(
            flops=4 * matmuls * rows * width * hidden,
            bytes_accessed=4 * width * hidden + 8 * rows * width,
            transcendentals=rows * hidden,
        ),
        name="feed_forward_" + mode,
    )(flags, *pieces, jnp.broadcast_to(gain[None], (8, width)), w_att, *(x for x, _, _ in rows_in), *held, *deps)


def product_kernel(left_of, parts_of, slices, which, core_ref, *refs):
    left_count, count = max(left_of) + 1, sum(parts_of)
    lefts, rights = refs[:left_count], refs[left_count : left_count + count]
    outs, held_ref = refs[left_count + count : -1], refs[-1]
    step = pl.program_id(0)
    rows, span = lefts[0].shape
    size = rows // slices
    half = rows // 2

    @pl.when(step == 0)
    def _():
        for index, left in enumerate(lefts):
            if len(outs) == 1:
                held_ref[index] = left[...]
                continue
            for first, core in ((0, 1 - core_ref[0]), (half, core_ref[0])):
                for part in range(slices // 2):
                    source = pl.ds(pl.multiple_of((2 * part + core) * size, 16), size)
                    held_ref[index, first + part * size : first + (part + 1) * size, :] = left[source, :]

    def product(index, lines):
        parts = rights[sum(parts_of[:index]) : sum(parts_of[: index + 1])]
        length = span // len(parts)
        return sum(
            dot(held_ref[left_of[index], lines, part * length : (part + 1) * length], right[...])
            for part, right in enumerate(parts)
        ).astype(jnp.bfloat16)

    for index in range(len(parts_of)):
        steps = [s for s, owner in enumerate(which) if owner == index]
        chosen = functools.reduce(lambda a, b: a | b, [step == s for s in steps])

        @pl.when(chosen)
        def _(index=index):
            if len(outs) == 1:
                outs[0][...] = product(index, slice(0, rows))
            else:
                outs[0][...] = product(index, slice(0, half))
                outs[1][...] = product(index, slice(half, rows))


def products(lefts, left_of, rights, block, slices, core, deps=()):
    rows, span = lefts[0].shape
    parts_of = [len(right) for right in rights]
    counts = [right[0].shape[1] // (2 * block) for right in rights]
    which, place = [], []
    for half in range(2):
        for index, number in enumerate(counts):
            for b in range(number):
                which.append(index)
                place.append(half * number + b)
    maps = []
    for index, right in enumerate(rights):
        held, column_of = 0, []
        for s, owner in enumerate(which):
            if owner == index:
                held = place[s]
            column_of.append(held)
        maps += [column_of] * len(right)
    steps = len(which)
    total = steps * block

    def right_map(column_of):
        def index_map(s):
            value = 0
            for position in range(steps):
                if column_of[position]:
                    value = value + jnp.where(s == position, column_of[position], 0)
            return (0, value)

        return index_map

    size = rows // slices
    apart = size % 16 == 0
    out_rows = rows // 2 if apart else rows
    out = jax.ShapeDtypeStruct((out_rows, total), jnp.bfloat16)
    flat = [part for right in rights for part in right]
    results = pl.pallas_call(
        without(
            partial(product_kernel, left_of, parts_of, slices, which), 1 + len(lefts) + len(flat), len(deps)
        ),
        grid=(steps,),
        in_specs=[pl.BlockSpec(memory_space=pltpu.SMEM)]
        + [pl.BlockSpec((rows, span), lambda s: (0, 0)) for _ in lefts]
        + [pl.BlockSpec((part.shape[0], block), right_map(column_of)) for part, column_of in zip(flat, maps)]
        + [ANY] * len(deps),
        out_specs=[pl.BlockSpec((out_rows, block), lambda s: (0, s))] * (2 if apart else 1),
        out_shape=[out] * (2 if apart else 1),
        scratch_shapes=[pltpu.VMEM((len(lefts), rows, span), jnp.bfloat16)],
        compiler_params=pltpu.CompilerParams(vmem_limit_bytes=VMEM_LIMIT),
        cost_estimate=pl.CostEstimate(
            flops=2 * span * rows * total, bytes_accessed=2 * (span + rows) * total, transcendentals=0
        ),
        name="weight_products",
    )(core.reshape(1), *lefts, *flat, *deps)
    if apart:
        return results
    cut = results[0].reshape(slices // 2, 2, size, total)
    return pick(cut, 1 - core, 1).reshape(-1, total), pick(cut, core, 1).reshape(-1, total)


def nothing(shapes):
    return pl.pallas_call(
        lambda *refs: None, out_shape=shapes, out_specs=[ANY] * len(shapes), name="nothing"
    )()


def input_kernel(gain_ref, w_ref, x_ref, first_ref, second_ref, dk_ref, dv_ref, grad_ref, out_ref, dgain_ref):
    step = pl.program_id(0)
    gain = gain_ref[0:1, :]
    rows, width = x_ref.shape
    d_query = jnp.where(2 * step < pl.num_programs(0), first_ref[...], second_ref[...])
    back = dot(d_query, w_ref[:, :width], NT)
    back = back + dot(dk_ref[...], w_ref[:, width : 2 * width], NT)
    back = back + dot(dv_ref[...], w_ref[:, 2 * width :], NT)
    x = x_ref[...].astype(jnp.float32)
    scale = lax.rsqrt(jnp.mean(x * x, axis=1, keepdims=True) + EPSILON)
    scaled = back * gain
    mean = jnp.mean(scaled * x, axis=1, keepdims=True)
    out_ref[...] = grad_ref[...] + scale * scaled - x * (scale * scale * scale * mean)
    gain_part = jnp.sum((back * x * scale).reshape(rows // 8, 8, width), axis=0)
    dgain_ref[...] = jnp.where(step == 0, gain_part, dgain_ref[...] + gain_part)


def input_gradient(x, gain, w_qkv, query_grads, key_grad, value_grad, grad, deps):
    rows, width = x.shape
    steps = rows // TR
    row_block = pl.BlockSpec((TR, width), lambda i: (i, 0))
    half_block = pl.BlockSpec((TR, width), lambda i: (i % (steps // 2), 0))
    fixed = pl.BlockSpec((8, width), lambda i: (0, 0))
    out, dgain = pl.pallas_call(
        without(input_kernel, 8, len(deps)),
        grid=(steps,),
        in_specs=[fixed, pl.BlockSpec(w_qkv.shape, lambda i: (0, 0)), row_block, half_block, half_block]
        + [row_block] * 3
        + [ANY] * len(deps),
        out_specs=[row_block, fixed],
        out_shape=[jax.ShapeDtypeStruct((rows, width), jnp.float32), jax.ShapeDtypeStruct((8, width), jnp.float32)],
        compiler_params=pltpu.CompilerParams(vmem_limit_bytes=VMEM_LIMIT),
        cost_estimate=pl.CostEstimate(
            flops=6 * rows * width * width, bytes_accessed=16 * rows * width, transcendentals=0
        ),
        name="input_gradient",
    )(jnp.broadcast_to(gain[None], (8, width)), w_qkv, x, *query_grads, key_grad, value_grad, grad, *deps)
    return out, jnp.sum(dgain, axis=0)


def sum_kernel(rounds, x_ref, out_ref, *refs):
    slots, send_sems, recv_sems = refs[: len(rounds)], refs[len(rounds)], refs[len(rounds) + 1]
    barrier = pltpu.get_barrier_semaphore()
    places, peers = [], []
    for axes in rounds:
        place, count = 0, 1
        for axis in axes:
            place = place * lax.axis_size(axis) + lax.axis_index(axis)
            count = count * lax.axis_size(axis)
        found = []
        for step in range(1, count):
            rest, device = lax.rem(place + step, count), {}
            for axis in reversed(axes):
                device[axis] = lax.rem(rest, lax.axis_size(axis))
                rest = lax.div(rest, lax.axis_size(axis))
            found.append(device)
        places.append(place)
        peers.append(found)
    for device in peers[0] + peers[1]:
        pl.semaphore_signal(barrier, inc=1, device_id=device, device_id_type=pl.DeviceIdType.MESH)
    pl.semaphore_wait(barrier, len(peers[0]) + len(peers[1]))
    value = x_ref[...]
    first = 0
    for slot, place, found in zip(slots, places, peers):
        slot[place] = value
        copies = []
        for step, device in enumerate(found):
            copies.append(
                pltpu.make_async_remote_copy(
                    src_ref=slot.at[place],
                    dst_ref=slot.at[place],
                    send_sem=send_sems.at[first + step],
                    recv_sem=recv_sems.at[first + step],
                    device_id=device,
                    device_id_type=pl.DeviceIdType.MESH,
                )
            )
        for copy in copies:
            copy.start()
        for copy in copies:
            copy.wait()
        first += len(found)
        value = slot[0]
        for index in range(1, len(found) + 1):
            value = value + slot[index]
    out_ref[...] = value


def sum_everywhere(x):
    rounds = (("dp",), ("section", "mp"))
    counts = [math.prod(lax.axis_size(axis) for axis in axes) for axes in rounds]
    copies = sum(counts) - len(counts)
    return pl.pallas_call(
        partial(sum_kernel, rounds),
        out_shape=jax.ShapeDtypeStruct(x.shape, x.dtype),
        in_specs=[pl.BlockSpec(memory_space=pltpu.VMEM)],
        out_specs=pl.BlockSpec(memory_space=pltpu.VMEM),
        scratch_shapes=[pltpu.VMEM((count,) + x.shape, x.dtype) for count in counts]
        + [pltpu.SemaphoreType.DMA((copies,)), pltpu.SemaphoreType.DMA((copies,))],
        compiler_params=pltpu.CompilerParams(collective_id=0, has_side_effects=True),
        name="sum_everywhere",
    )(x)


def pair_permute(x, axis, bit):
    pairs = [(i, i ^ (1 << bit)) for i in range(lax.axis_size(axis))]
    return lax.ppermute(x, axis, pairs)


def shifted(x, axis, by):
    peers = lax.axis_size(axis)
    pairs = [(i, i + by) for i in range(peers) if 0 <= i + by < peers]
    return lax.ppermute(x, axis, pairs)


def in_order(flag, first, second, axis):
    return jnp.where(
        flag == 0,
        jnp.concatenate([first, second], axis=axis),
        jnp.concatenate([second, first], axis=axis),
    )


def pick(x, index, axis):
    return lax.dynamic_index_in_dim(x, index, axis, False)


def after(values, *others):
    return lax.optimization_barrier((values, others))[0]


def exchange_rows(block, where_mp):
    return pick(block, where_mp, 0), pair_permute(pick(block, 1 - where_mp, 0), "mp", 0)


def scatter_rows(rows, where_mp):
    half = rows.shape[0] // 2
    send = lax.dynamic_slice_in_dim(rows, (1 - where_mp) * half, half, 0).astype(jnp.bfloat16)
    return lax.dynamic_slice_in_dim(rows, where_mp * half, half, 0), pair_permute(send, "mp", 0)


def fetch_far(shard, core):
    half = shard.shape[0] // 2
    return pair_permute(lax.dynamic_slice_in_dim(shard, core * half, half, 0), "mp", 0)


def fetch_near(far):
    return pair_permute(far, "dp", 0)


class Reduction:
    def __init__(self, send, keep, dp_index, section=None):
        self.total, self.arrived = keep, pair_permute(send, "dp", 0)
        self.dp_index = dp_index
        bits = lax.axis_size("dp").bit_length() - 1
        self.left = ([("section", section)] if section is not None else []) + [("mp", None)]
        self.left += [("dp", bit) for bit in range(1, bits)]

    def joined(self, cut):
        return cut(self.total).astype(jnp.float32) + cut(self.arrived).astype(jnp.float32)

    def hop(self, *ties):
        brought = self.arrived
        self.arrived = after(self.arrived, *ties)
        axis, which = self.left.pop(0)
        rows, width = self.total.shape
        if axis == "section":
            send = self.joined(lambda x: x[: rows // 2]).astype(jnp.bfloat16)
            keep = jnp.where(which == 0, 0.0, self.joined(lambda x: x[rows // 2 :]))
            self.total, self.arrived = keep, shifted(send, "section", -1)
        elif axis == "mp":
            send = self.joined(lambda x: x[:, width // 2 :]).astype(jnp.bfloat16)
            self.total, self.arrived = self.joined(lambda x: x[:, : width // 2]), pair_permute(send, "mp", 0)
        else:
            mark = (self.dp_index >> which) & 1
            halves = (lax.axis_size("dp") >> (which + 1), 2, -1, width)
            send = self.joined(lambda x: pick(x.reshape(halves), 1 - mark, 1)).astype(jnp.bfloat16)
            keep = self.joined(lambda x: pick(x.reshape(halves), mark, 1))
            self.total = keep.reshape(-1, width)
            self.arrived = pair_permute(send.reshape(-1, width), "dp", which)
        return brought

    def finish(self, *ties):
        while self.left:
            self.hop()
        self.arrived = after(self.arrived, *ties)
        return self.joined(lambda x: x)


def rms_norm(inputs, gain_row):
    return (
        inputs * lax.rsqrt(jnp.mean(inputs * inputs, axis=-1, keepdims=True) + EPSILON) * gain_row
    )


def norm_back(rows, gain_row, grad_normed):
    return jax.vjp(rms_norm, rows, gain_row)[1](grad_normed)


def low(x):
    return x.astype(jnp.bfloat16)


def local(
    block_input,
    out_cotangent,
    doc_lengths,
    question_lengths,
    coordinates,
    gains,
    bias_tables,
    self_qkv,
    self_out,
    ffn_in,
    ffn_out,
    cross_q,
    cross_kv,
    cross_out,
):
    section = lax.axis_index("section")
    on_encoder = section == 0
    dp_index = lax.axis_index("dp")
    core = dp_index & 1
    where_mp = lax.axis_index("mp")
    width = block_input.shape[4]
    quests = question_lengths.shape[2]
    own = self_qkv.shape[3]
    pairs = 2 * own // LANES
    heads = 2 * pairs
    parts = lax.axis_size("dp")
    flags = jnp.stack([core, where_mp, section]).astype(jnp.int32)

    rows_low = in_order(where_mp, *exchange_rows(block_input[0, :, 0], where_mp), 0)
    qkv_own = self_qkv[0].reshape(width, -1)
    qkv_far = fetch_far(qkv_own, core)
    qkv_other = in_order(core, qkv_far, fetch_near(qkv_far), 0)
    w_qkv = jnp.concatenate(
        [x[:, t * own : (t + 1) * own] for t in range(3) for x in (qkv_own, qkv_other)], axis=1
    )
    owned = after((ffn_in[0], ffn_out[0], self_out[0]), rows_low, qkv_far)
    fars = [fetch_far(x, core) for x in owned]

    lens = jnp.concatenate(
        [pick(doc_lengths, where_mp, 0), pick(question_lengths, where_mp, 0)[0]]
    ).astype(jnp.int32)
    coords = pick(coordinates, where_mp, 0)[0]
    tables = jnp.where(where_mp == 0, bias_tables, jnp.roll(bias_tables, heads // 2, axis=2))

    rows = rows_low.astype(jnp.float32)
    span = rows.shape[0]
    half = span // 2
    turn = half // TR
    halves = (slice(0, half), slice(half, span))
    gain_self = jnp.where(on_encoder, gains[0], gains[2])
    normed_self = low(rms_norm(rows, gain_self))
    projected = low(dot(normed_self, w_qkv))
    merged, probs, middles, memories, arrivals = [], [], [], [], []
    for part in range(2):
        deps = memories[:1]

        def forward(kind, chosen):
            return attend_forward(
                kind, part, half, lens, chosen, coords, projected, 0, [projected], 1, 2, pairs, quests, deps
            )

        out, prob = lax.cond(on_encoder, lambda: forward("enc", tables[:3]), lambda: forward("dec", tables[3:]))
        if not part:
            fars = after(fars, out)
            nears = [fetch_near(x) for x in fars]
            w_out = jnp.concatenate([self_out[0], in_order(core, fars[2], nears[2], 0)], axis=0)
            pieces = (ffn_in[0], fars[0], nears[0], ffn_out[0], fars[1], nears[1])
            cross_owned = after(
                (jnp.concatenate([cross_q, cross_kv.reshape(width, -1)], axis=1), cross_out, out_cotangent[0, :, 0]), fars
            )
            cross_fars = [fetch_far(x, core) for x in cross_owned[:2]]
            cot = exchange_rows(cross_owned[2], where_mp)
        else:
            cross_fars = after(cross_fars, out)
        memory, middle = feed_forward(
            "fwd", part, half, flags, pieces, gains[1], w_out, [(rows_low, part * turn, turn), (out, 0, turn)]
        )
        arrivals.append(shifted(memory, "section", 1))
        merged.append(out)
        probs.append(prob)
        middles.append(middle)
        memories.append(memory)
    query_other, cross_other = (in_order(core, far, fetch_near(far), 0) for far in cross_fars)
    w_query = jnp.concatenate([cross_q, query_other[:, :own]], axis=1)
    w_pair = jnp.concatenate(
        [x for t in range(2) for x in (cross_kv[:, t], query_other[:, (t + 1) * own : (t + 2) * own])], axis=1
    )
    w_cross = jnp.concatenate([cross_out, cross_other], axis=0)
    middle = jnp.concatenate(middles, axis=0)

    normed_cross = low(rms_norm(middle, gains[3]))
    queries = low(dot(normed_cross, w_query))
    first_pair = low(dot(arrivals[0], w_pair))
    arrivals[1] = after(arrivals[1], queries, first_pair)
    pair_rows = [first_pair, low(dot(arrivals[1], w_pair))]
    cross_merged, cross_prob = attend_forward(
        "cross", 0, span, lens, None, coords, queries, 0, pair_rows, 0, 1, pairs, quests
    )
    output_low, second, grad_second, second_low, cross_grad = feed_forward(
        "both",
        0,
        span,
        flags,
        pieces,
        gains[4],
        w_cross,
        [(middle, 0, 2 * turn), (cross_merged, 0, 2 * turn), (cot[0], 0, turn), (cot[1], 0, turn)],
    )
    output_own, output_arrived = scatter_rows(
        jnp.where(on_encoder, jnp.concatenate(memories, axis=0), output_low), where_mp
    )
    returns, returned, carry = [], [], ()
    for part in range(2):
        query_grad, key_grad, value_grad, _ = attend_backward(
            "cross",
            part,
            cross_prob,
            cross_grad,
            cross_merged,
            queries,
            0,
            pair_rows[part],
            0,
            1,
            pairs,
            quests,
            carry,
            [returns[0], output_arrived] if part else [],
        )
        carry = (query_grad, key_grad, value_grad)
        returns.append(
            low(
                dot(key_grad[halves[part]], w_pair[:, : 2 * own], NT)
                + dot(value_grad[halves[part]], w_pair[:, 2 * own :], NT)
            )
        )
        returned.append(shifted(returns[part], "section", -1))
    query_cross = after(query_grad, returns[1])

    def cross_norm():
        input_part, gain_part = norm_back(middle, gains[3], dot(query_cross, w_query, NT))
        return grad_second + input_part, gain_part

    def no_norm():
        return tuple(
            nothing([jax.ShapeDtypeStruct((span, width), jnp.float32), jax.ShapeDtypeStruct((width,), jnp.float32)])
        )

    grad_first, gain_cross = lax.cond(on_encoder, no_norm, cross_norm)

    gain_ffn = jnp.where(on_encoder, gains[1], gains[4])
    held, gain_ffn_grad, grads_middle, merged_grads = [], 0.0, [], []
    for part in range(2):
        if part:
            returned[1] = after(returned[1], grads_middle[0])
        grad_middle, *held, merged_grad, gain_part = feed_forward(
            "back",
            part,
            half,
            flags,
            pieces,
            gain_ffn,
            w_out,
            [
                (middles[part], 0, turn),
                (second, part * turn, turn),
                (cot[0], 0, turn),
                (cot[1], 0, turn),
                (returned[part], 0, turn),
                (grad_first, part * turn, turn),
            ],
            held,
        )
        gain_ffn_grad = gain_ffn_grad + jnp.sum(gain_part, axis=0)
        grads_middle.append(grad_middle)
        merged_grads.append(merged_grad)
    hn_turned, gl_turned, ml_turned, activated, hidden_grad = held
    in_send, in_keep = products([hn_turned], [0], [[hidden_grad]], 2 * own, parts, core)
    down_send, down_keep = products([gl_turned], [0], [[activated]], 2 * own, parts, core, [in_send])
    in_steps = Reduction(in_send, in_keep, dp_index)
    down_steps = Reduction(down_send, down_keep, dp_index)

    def cross_products():
        return tuple(
            products(
                [normed_cross.T, jnp.concatenate(arrivals, axis=0).T, second_low.T],
                [0, 1, 1, 2],
                [[query_cross], [key_grad], [value_grad], [cross_merged]],
                own,
                2 * parts,
                core,
                [down_send],
            )
        )

    def no_products():
        blank = jax.ShapeDtypeStruct((width // 2, 8 * own), jnp.bfloat16)
        return tuple(nothing([blank, blank]))

    cross_send, cross_keep = lax.cond(on_encoder, no_products, cross_products)
    cross_steps = Reduction(cross_send, cross_keep, dp_index, section)
    scores, query_grads, carry = [], [], ()
    for part in range(2):
        deps = (down_steps.hop(scores[0]), cross_steps.hop(scores[0])) if part else (down_send, cross_send, in_steps.hop())

        def backward(kind):
            return attend_backward(
                kind, part, probs[part], merged_grads[part], merged[part], projected, 0, projected, 1, 2, pairs, quests,
                carry, deps
            )

        query_grad, key_grad, value_grad, score = lax.cond(
            on_encoder, lambda: backward("enc"), lambda: backward("dec")
        )
        carry = (key_grad, value_grad)
        query_grads.append(query_grad)
        scores.append(score)
    self_send, self_keep = products(
        [normed_self.T, ml_turned],
        [0, 0, 0, 1],
        [query_grads, [key_grad], [value_grad], merged],
        own,
        parts,
        core,
    )
    self_steps = Reduction(self_send, self_keep, dp_index)
    input_grad, gain_self_grad = input_gradient(
        rows_low,
        gain_self,
        w_qkv,
        query_grads,
        key_grad,
        value_grad,
        jnp.concatenate(grads_middle, axis=0),
        [self_send],
    )
    grad_own, grad_arrived = scatter_rows(input_grad, where_mp)

    tabs, diags = [], []
    deps = (self_send, input_grad, in_steps.hop(scores[0]), cross_steps.hop(self_send))
    for part in range(2):
        for quarter in range(2):
            tab, diag = lax.cond(
                on_encoder,
                lambda: table_sums("enc", part, quarter, coords, scores[part], quests, deps),
                lambda: table_sums("dec", part, quarter, coords, scores[part], quests, deps),
            )
            tabs.append(tab)
            diags.append(diag)
            if len(tabs) == 1:
                deps = (tab, self_steps.hop(tab), down_steps.hop(self_send))
            elif len(tabs) == 2:
                deps = (tab, in_steps.hop(tab), cross_steps.hop(tab), grad_arrived)
            elif len(tabs) == 3:
                deps = (tab, down_steps.hop(tab), self_steps.hop(tab), in_steps.arrived)
    table_grad = lax.cond(
        on_encoder,
        lambda: table_grads("enc", tabs, diags, span, quests, heads),
        lambda: table_grads("dec", tabs, diags, span, quests, heads),
    )
    table_grad = jnp.where(where_mp == 0, table_grad, jnp.roll(table_grad, heads // 2, axis=2))
    blank = jnp.zeros((width,), jnp.float32)
    gain_grad = jnp.where(
        on_encoder,
        jnp.stack([gain_self_grad, gain_ffn_grad, blank, blank, blank]),
        jnp.stack([blank, blank, gain_self_grad, gain_cross, gain_ffn_grad]),
    )
    small = jnp.concatenate([gain_grad.reshape(-1, LANES), table_grad.reshape(-1, LANES)], axis=0)
    count = small.shape[0]
    small = jnp.pad(small, ((0, -count % 8), (0, 0)))
    cross_shard, in_shard, down_shard = (x.finish(tabs[3]) for x in (cross_steps, in_steps, down_steps))
    small = sum_everywhere(after(small, self_steps.hop(tab), down_steps.arrived, cross_steps.arrived))
    gain_count = gain_grad.size // LANES
    gain_sum = small[:gain_count].reshape(gain_grad.shape)
    table_sum = small[gain_count:count].reshape(table_grad.shape)
    self_shard = self_steps.finish(table_grad)
    output_rows, grad_rows = (
        in_order(where_mp, own_rows[None], after(arrived, tabs[2]).astype(own_rows.dtype)[None], 0)
        for own_rows, arrived in ((output_own, output_arrived), (grad_own, grad_arrived))
    )
    return (
        output_rows[None, :, None],
        grad_rows[None, :, None],
        gain_sum[:4],
        gain_sum[4],
        table_sum,
        self_shard[:, : 3 * own].reshape(-1, 3, own)[None],
        self_shard[:, 3 * own :].T[None],
        in_shard[None],
        down_shard.T[None],
        cross_shard[:, :own],
        cross_shard[:, own : 3 * own].reshape(-1, 2, own),
        cross_shard[:, 3 * own :].T,
    )


def solution(mesh):
    return jax.shard_map(
        local,
        mesh=mesh,
        in_specs=(
            P("section", None, "dp", "mp", None),
            P("section", None, "dp", "mp", None),
            P(None, "dp"),
            P(None, "dp", None),
            P(None, "dp", None, None),
            P(),
            P(),
            P("section", None, None, "mp"),
            P("section", "mp", None),
            P("section", None, "mp"),
            P("section", "mp", None),
            P(None, "mp"),
            P(None, None, "mp"),
            P("mp", None),
        ),
        out_specs=(
            P("section", None, "dp", "mp", None),
            P("section", None, "dp", "mp", None),
            P(),
            P(),
            P(),
            P("section", "dp", None, "mp"),
            P("section", "mp", "dp"),
            P("section", "dp", "mp"),
            P("section", "mp", "dp"),
            P(("section", "dp"), "mp"),
            P(("section", "dp"), None, "mp"),
            P("mp", ("section", "dp")),
        ),
        check_vma=False,
    )
```

```python
import functools
from functools import partial
import math

import jax
import jax.numpy as jnp
from jax import lax
from jax.experimental import pallas as pl
from jax.experimental.pallas import tpu as pltpu
from jax.sharding import PartitionSpec as P

HEAD = 64
LANES = 128
NEGATIVE = -1e30
EPSILON = 1e-06
GELU_SCALE = math.sqrt(2 / math.pi)
GELU_CUBE = 0.044715
TI = 64
FFN_BLOCKS = 4
TR = 256
VMEM_LIMIT = 56 * 1024 * 1024
NT = (((1,), (1,)), ((), ()))
NN = (((1,), (0,)), ((), ()))


def edge_list(exact_span, bucket_count, far_reach):
    log_edges = [
        int(
            math.ceil(
                exact_span * (far_reach / exact_span) ** (power_index / (bucket_count - exact_span))
            )
        )
        for power_index in range(1, bucket_count - exact_span)
    ]
    return list(range(1, exact_span + 1)) + log_edges


def magnitude(distance, exact_span, bucket_count, far_reach):
    bucket = jnp.minimum(distance, exact_span)
    for threshold in edge_list(exact_span, bucket_count, far_reach)[exact_span:]:
        bucket = bucket + (distance >= threshold).astype(jnp.int32)
    return bucket


def two_sided(relative, far_reach):
    return magnitude(jnp.abs(relative), 8, 16, far_reach) + jnp.where(relative > 0, 16, 0)


def one_sided(relative):
    return magnitude(jnp.maximum(-relative, 0), 16, 32, 128)


def half_lanes(block, head):
    lane = lax.broadcasted_iota(jnp.int32, block.shape, 1)
    keep = lane < HEAD if head == 0 else lane >= HEAD
    return jnp.where(keep, block, jnp.zeros_like(block))


def dot(a, b, dims=NN):
    return lax.dot_general(a, b, dims, preferred_element_type=jnp.float32)


def pick_lanes(row, index):
    return jnp.take_along_axis(jnp.broadcast_to(row, index.shape), index, axis=1)


def pick_sublanes(table_ref, head, low, odd, upper):
    parts = [
        jnp.take_along_axis(table_ref[head, 8 * part : 8 * part + 8, :], low, axis=0)
        for part in range(4)
    ]
    return jnp.where(upper, jnp.where(odd, parts[3], parts[2]), jnp.where(odd, parts[1], parts[0]))


def fwd_kernel(kind, part, tq, span, heads, len_ref, tabn_ref, tabx_ref, taby_ref, crow_ref, ccol_ref, q_ref, *refs):
    count = (len(refs) - 7) // 2
    k_refs, v_refs = refs[:count], refs[count : 2 * count]
    o_ref, p_ref, s_ref, idx_ref, mask_ref, near_ref, bias_ref = refs[-7:]
    length = span // count
    pair = pl.program_id(0)
    first_block = 0 if kind == "dec" else part * tq // LANES
    chunk = 16

    @pl.when(pair == 0)
    def _():
        key = lax.broadcasted_iota(jnp.int32, (8, span), 1)
        limit = len_ref[1 + part] if kind == "dec" else len_ref[0]
        mask_ref[...] = jnp.where(key < limit, 0.0, NEGATIVE)
        if kind != "cross":
            def near_rows(r, carry):
                rows = pl.ds(pl.multiple_of(r * 8, 8), 8)
                query = r * 8 + lax.broadcasted_iota(jnp.int32, (8, LANES), 0)
                for d in range(-2, 3):
                    key = d * LANES + lax.broadcasted_iota(jnp.int32, (8, LANES), 1)
                    bucket = one_sided(key - query) if kind == "dec" else two_sided(key - query, 128)
                    for head in range(heads):
                        value = pick_lanes(tabn_ref[head : head + 1, :], bucket)
                        if kind == "dec":
                            value = jnp.where(key <= query, value, NEGATIVE)
                        near_ref[head, rows, (d + 2) * LANES : (d + 3) * LANES] = value
                return carry

            lax.fori_loop(0, LANES // 8, near_rows, 0)
        if kind == "enc":

            def bucket_rows(r, carry):
                rows = pl.ds(pl.multiple_of(r * chunk, chunk), chunk)
                for axis in range(2):
                    far = crow_ref[axis : axis + 1, :] - ccol_ref[rows, axis : axis + 1]
                    idx_ref[axis, rows, :] = two_sided(far, 500)
                return carry

            lax.fori_loop(0, tq // chunk, bucket_rows, 0)

            def bias_rows(r, carry):
                rows = pl.ds(pl.multiple_of(r * 8, 8), 8)
                for c in range(0, span, LANES):
                    lanes = slice(c, c + LANES)
                    across = idx_ref[0, rows, lanes]
                    upward = idx_ref[1, rows, lanes]
                    low, odd, upper = upward & 7, (upward & 8) != 0, upward >= 16
                    for head in range(heads):
                        bias_ref[head, rows, lanes] = pick_lanes(
                            tabx_ref[head : head + 1, :], across
                        ) + pick_sublanes(taby_ref, head, low, odd, upper)
                return carry

            lax.fori_loop(0, tq // 8, bias_rows, 0, unroll=2)

    for head in range(2):
        query = half_lanes(q_ref[...], head)
        for index, k_ref in enumerate(k_refs):
            s_ref[head, :, index * length : (index + 1) * length] = dot(query, k_ref[...], NT)
        for r in range(0, tq, chunk):
            rows = slice(r, r + chunk)
            pieces = []
            for c in range(0, span, LANES):
                lanes = slice(c, c + LANES)
                piece = s_ref[head, rows, lanes] + mask_ref[0:1, lanes]
                if kind != "cross":
                    apart = min(max(c // LANES - (first_block + r // LANES), -2), 2) + 2
                    near = slice(apart * LANES, (apart + 1) * LANES)
                    piece = piece + near_ref[2 * pair + head, r % LANES : r % LANES + chunk, near]
                if kind == "enc":
                    piece = piece + bias_ref[2 * pair + head, rows, lanes]
                pieces.append(piece)
            score = jnp.concatenate(pieces, axis=1)
            score = jnp.exp(score - jnp.max(score, axis=1, keepdims=True))
            score = score * (1.0 / jnp.sum(score, axis=1, keepdims=True))
            p_ref[head, rows, :] = score.astype(jnp.bfloat16)
    first, second = (
        sum(
            dot(p_ref[head, :, index * length : (index + 1) * length], v_ref[...])
            for index, v_ref in enumerate(v_refs)
        )
        for head in range(2)
    )
    lane = lax.broadcasted_iota(jnp.int32, first.shape, 1)
    o_ref[...] = jnp.where(lane < HEAD, first, second).astype(jnp.bfloat16)


def bwd_kernel(kind, part, rows, span, p_ref, do_ref, o_ref, q_ref, k_ref, v_ref, *refs):
    carry = refs[: 2 if kind != "cross" else 3] if part else ()
    outs = refs[len(carry) :]
    dq_ref, dk_ref, dv_ref = outs[:3]
    low_ref, dp_ref = outs[3:]
    chunk = 16
    q_t = jnp.transpose(q_ref[...].astype(jnp.float32)).astype(jnp.bfloat16)
    do_t = jnp.transpose(do_ref[...].astype(jnp.float32)).astype(jnp.bfloat16)
    grads, key_grads, value_grads = [], [], []
    for head in range(2):
        d_out = half_lanes(do_ref[...], head)
        delta = jnp.sum(d_out.astype(jnp.float32) * o_ref[...].astype(jnp.float32), axis=1, keepdims=True)
        dp_ref[head] = dot(d_out, v_ref[...], NT)
        for r in range(0, rows, chunk):
            part_rows = slice(r, r + chunk)
            prob = p_ref[head, part_rows, :].astype(jnp.float32)
            low_ref[head, part_rows, :] = (
                prob * (dp_ref[head, part_rows, :] - delta[part_rows, :])
            ).astype(jnp.bfloat16)
        grads.append(dot(low_ref[head], k_ref[...]))
        half = slice(head * HEAD, (head + 1) * HEAD)
        key_grads.append(dot(q_t[half], low_ref[head]))
        value_grads.append(dot(do_t[half], p_ref[head]))
    lane = lax.broadcasted_iota(jnp.int32, grads[0].shape, 1)
    query_grad = jnp.where(lane < HEAD, grads[0], grads[1])
    if kind == "cross" and part:
        query_grad = query_grad + carry[0][...]
    dq_ref[...] = query_grad.astype(dq_ref.dtype)
    for index, (out_ref, pieces) in enumerate(((dk_ref, key_grads), (dv_ref, value_grads))):
        grad = jnp.transpose(jnp.concatenate(pieces, axis=0))
        if kind == "enc" and part:
            grad = grad + carry[index][...]
        if kind == "dec":
            if part:
                out_ref[0:span, :] = carry[index][0:span, :].astype(out_ref.dtype)
            out_ref[part * span : (part + 1) * span, :] = grad.astype(out_ref.dtype)
        else:
            out_ref[...] = grad.astype(out_ref.dtype)


def table_kernel(kind, ti, span, heads, low_ref, crow_ref, ccol_ref, tab_ref, diag_ref, row_ref, wide_ref, idx_ref):
    step = pl.program_id(0)
    group = 16
    wide = diag_ref.shape[2]
    pad = wide - span

    @pl.when(step == 0)
    def _():
        tab_ref[...] = jnp.zeros_like(tab_ref)

    if kind == "enc":
        for r in range(0, ti, 16):
            for axis in range(2):
                far = crow_ref[axis : axis + 1, :] - ccol_ref[r : r + 16, axis : axis + 1]
                idx_ref[axis, r : r + 16, :] = two_sided(far, 500).astype(jnp.float32)
    out_row = lax.broadcasted_iota(jnp.int32, (256, 256), 0)
    in_row = lax.broadcasted_iota(jnp.int32, (256, 256), 1)
    swap = (lax.div(out_row, 16) == lax.rem(in_row, 16)) & (lax.rem(out_row, 16) == lax.div(in_row, 16))
    swap = jnp.where(swap, 1.0, 0.0).astype(jnp.bfloat16)
    blank = jnp.zeros(((16 - heads) * 16, span), jnp.bfloat16)
    which = lax.broadcasted_iota(jnp.int32, (32, span), 0).astype(jnp.bfloat16)

    tab = jnp.zeros(tab_ref.shape, jnp.float32)
    diag = jnp.zeros((16, wide), jnp.float32)
    for g in range(ti // group):
        first = g * group
        block = jnp.concatenate([low_ref[h, first : first + group, :] for h in range(heads)] + [blank], axis=0)
        wide_ref[g] = dot(swap, block)
        if kind == "enc":
            row_ref[g] = wide_ref[g].astype(jnp.bfloat16)
        for j in range(group):
            lines = slice(16 * j, 16 * j + 16)
            if kind == "enc":
                hot = []
                for axis in range(2):
                    bucket = idx_ref[axis, first + j : first + j + 1, :]
                    bucket = jnp.broadcast_to(bucket, (32, span)).astype(jnp.bfloat16)
                    hot.append(jnp.where(bucket == which, jnp.bfloat16(1), jnp.bfloat16(0)))
                tab = tab + dot(row_ref[g, lines, :], jnp.concatenate(hot, axis=0), NT)
            line = wide_ref[g, lines, :]
            if pad:
                line = jnp.concatenate([line, jnp.zeros((16, pad), jnp.float32)], axis=1)
            diag = diag + pltpu.roll(line, (wide - (first + j)) % wide, 1)
    tab_ref[...] += tab
    diag_ref[0] = diag


ANY = pl.BlockSpec(memory_space=pl.ANY)


def cost(flops, bytes_accessed, transcendentals):
    return pl.CostEstimate(flops=flops // 10, bytes_accessed=bytes_accessed // 10, transcendentals=transcendentals // 10)


def without(kernel, first, count):
    return lambda *refs: kernel(*refs[:first], *refs[first + count :])


def near_width(kind, ti, span):
    return span + ti if kind == "enc" else span


def diag_sums(kind, diag, starts):
    wide = diag.shape[2]
    column = lax.broadcasted_iota(jnp.int32, (len(starts), wide), 1)
    start = jnp.array(starts, jnp.int32)[:, None]
    if kind == "dec":
        bucket = one_sided(jnp.where(column > start, column - wide, column) - start)
    else:
        bucket = two_sided(jnp.where(column > wide - TI, column - wide, column) - start, 128)
    hot = (bucket[..., None] == lax.iota(jnp.int32, 32)).astype(jnp.float32)
    return jnp.einsum("swb,shw->bh", hot, diag, precision=lax.Precision.HIGHEST)


def attend_forward(kind, part, tq, lens, tables, coords, q_src, q_col, kv_srcs, k_col, v_col, pairs, quests, deps=()):
    heads = 2 * pairs
    key_rows = sum(kv_src.shape[0] for kv_src in kv_srcs)
    span = key_rows // quests if kind == "dec" else key_rows
    key_block = part if kind == "dec" else 0
    count = len(kv_srcs)
    flops = tq * span * (60000 if kind == "enc" else 25000)
    tab_n = tab_x = jnp.zeros((16, LANES), jnp.float32)
    tab_y = jnp.zeros((1, 8, LANES), jnp.float32)
    if kind != "cross":
        tab_n = jnp.pad(tables[0].T, ((0, 16 - heads), (0, LANES - 32)))
    if kind == "enc":
        tab_x = jnp.pad(tables[1].T, ((0, 16 - heads), (0, LANES - 32)))
        tab_y = jnp.broadcast_to(tables[2].T[:, :, None], (heads, 32, LANES))
    return pl.pallas_call(
        without(partial(fwd_kernel, kind, part, tq, span, heads), 7 + 2 * count, len(deps)),
        grid=(pairs,),
        in_specs=[
            pl.BlockSpec(memory_space=pltpu.SMEM),
            pl.BlockSpec(tab_n.shape, lambda h: (0, 0)),
            pl.BlockSpec(tab_x.shape, lambda h: (0, 0)),
            pl.BlockSpec(tab_y.shape, lambda h: (0, 0, 0)),
            pl.BlockSpec(coords.shape, lambda h: (0, 0)),
            pl.BlockSpec((tq, 2), lambda h: (part, 0)),
            pl.BlockSpec((tq, LANES), lambda h: (part, q_col * pairs + h)),
        ]
        + [pl.BlockSpec((span // count, LANES), lambda h: (key_block, k_col * pairs + h))] * count
        + [pl.BlockSpec((span // count, LANES), lambda h: (key_block, v_col * pairs + h))] * count
        + [ANY] * len(deps),
        out_specs=[
            pl.BlockSpec((tq, LANES), lambda h: (0, h)),
            pl.BlockSpec((2, tq, span), lambda h: (h, 0, 0)),
        ],
        out_shape=[
            jax.ShapeDtypeStruct((tq, pairs * LANES), jnp.bfloat16),
            jax.ShapeDtypeStruct((heads, tq, key_rows), jnp.bfloat16),
        ],
        scratch_shapes=[
            pltpu.VMEM((2, tq, span), jnp.float32),
            pltpu.VMEM((2, tq, span) if kind == "enc" else (1, 8, LANES), jnp.int32),
            pltpu.VMEM((8, span), jnp.float32),
            pltpu.VMEM((1, 8, LANES) if kind == "cross" else (heads, LANES, 5 * LANES), jnp.float32),
            pltpu.VMEM((heads, tq, span) if kind == "enc" else (1, 8, LANES), jnp.float32),
        ],
        compiler_params=pltpu.CompilerParams(vmem_limit_bytes=VMEM_LIMIT),
        cost_estimate=cost(
            flops=flops, bytes_accessed=4 * tq * span * pairs, transcendentals=2 * tq * span * pairs
        ),
        name="attend_forward_" + kind,
    )(lens, tab_n, tab_x, tab_y, coords, coords.T, q_src, *kv_srcs, *kv_srcs, *deps)


def attend_backward(kind, part, prob, grad_out, out, q_src, q_col, kv_src, k_col, v_col, pairs, quests, carry=(), deps=()):
    rows = grad_out.shape[0]
    key_rows = 2 * kv_src.shape[0] if kind == "cross" else kv_src.shape[0]
    width = pairs * LANES
    span = key_rows if kind == "enc" else key_rows // 2
    key_block = part if kind == "dec" else 0
    query_block = 0 if kind == "cross" else part
    score_block = part if kind == "cross" else 0
    if kind == "cross":
        carried = [pl.BlockSpec((rows, LANES), lambda h: (0, h))] + [pl.BlockSpec(memory_space=pl.ANY)] * 2
        key_out = pl.BlockSpec((span, LANES), lambda h: (part, h))
        aliases = {7: 1, 8: 2} if part else {}
    else:
        carried = [pl.BlockSpec((key_rows, LANES), lambda h: (0, h))] * 2
        key_out = pl.BlockSpec((key_rows, LANES), lambda h: (0, h))
        aliases = {}
    query_type = jnp.float32 if kind == "cross" and not part else jnp.bfloat16
    key_type = jnp.bfloat16 if kind == "cross" or part else jnp.float32
    low_block = pl.BlockSpec((2, rows, span), (lambda h: (0, 0, 0)) if kind == "cross" else (lambda h: (h, 0, 0)))
    low_shape = (2, rows, span) if kind == "cross" else (2 * pairs, rows, key_rows)
    return pl.pallas_call(
        without(partial(bwd_kernel, kind, part, rows, span), 6 + len(carry), len(deps)),
        grid=(pairs,),
        in_specs=[
            pl.BlockSpec((2, rows, span), lambda h: (h, 0, score_block)),
            pl.BlockSpec((rows, LANES), lambda h: (0, h)),
            pl.BlockSpec((rows, LANES), lambda h: (0, h)),
            pl.BlockSpec((rows, LANES), lambda h: (query_block, q_col * pairs + h)),
            pl.BlockSpec((span, LANES), lambda h: (key_block, k_col * pairs + h)),
            pl.BlockSpec((span, LANES), lambda h: (key_block, v_col * pairs + h)),
        ]
        + carried[: len(carry)]
        + [ANY] * len(deps),
        out_specs=[
            pl.BlockSpec((rows, LANES), lambda h: (0, h)),
            key_out,
            key_out,
            low_block,
        ],
        out_shape=[
            jax.ShapeDtypeStruct((rows, width), query_type),
            jax.ShapeDtypeStruct((key_rows, width), key_type),
            jax.ShapeDtypeStruct((key_rows, width), key_type),
            jax.ShapeDtypeStruct(low_shape, jnp.bfloat16),
        ],
        scratch_shapes=[pltpu.VMEM((2, rows, span), jnp.float32)],
        input_output_aliases=aliases,
        compiler_params=pltpu.CompilerParams(vmem_limit_bytes=VMEM_LIMIT),
        cost_estimate=cost(
            flops=rows * span * 28000, bytes_accessed=4 * rows * span * pairs, transcendentals=0
        ),
        name="attend_backward_" + kind,
    )(prob, grad_out, out, q_src, kv_src, kv_src, *carry, *deps)


def table_sums(kind, part, quarter, coords, low, quests, deps=()):
    heads, rows, key_rows = low.shape
    rows = rows // 2
    span = key_rows // quests if kind == "dec" else key_rows
    steps = rows // TI
    wide = near_width(kind, TI, span)
    first = (2 * part + quarter) * steps
    tab, diag = pl.pallas_call(
        without(partial(table_kernel, kind, TI, span, heads), 3, len(deps)),
        grid=(steps,),
        in_specs=[
            pl.BlockSpec((heads, TI, span), lambda i: (0, quarter * steps + i, 0)),
            pl.BlockSpec(coords.shape, lambda i: (0, 0)),
            pl.BlockSpec((TI, 2), lambda i: (first + i, 0)),
        ]
        + [ANY] * len(deps),
        out_specs=[
            pl.BlockSpec((16, 64), lambda i: (0, 0)),
            pl.BlockSpec((1, 16, wide), lambda i: (i, 0, 0)),
        ],
        out_shape=[
            jax.ShapeDtypeStruct((16, 64), jnp.float32),
            jax.ShapeDtypeStruct((steps, 16, near_width("enc", TI, key_rows)), jnp.float32),
        ],
        scratch_shapes=[
            pltpu.VMEM((TI // 16, 256, span), jnp.bfloat16),
            pltpu.VMEM((TI // 16, 256, span), jnp.float32),
            pltpu.VMEM((2, TI, span) if kind == "enc" else (1, 8, LANES), jnp.float32),
        ],
        compiler_params=pltpu.CompilerParams(vmem_limit_bytes=VMEM_LIMIT),
        cost_estimate=cost(
            flops=rows * span * 40000, bytes_accessed=2 * heads * rows * span, transcendentals=0
        ),
        name="table_sums_" + kind,
    )(low, coords, coords.T, *deps)
    return tab, diag


def table_grads(kind, tabs, diags, rows, quests, heads):
    steps = diags[0].shape[0]
    starts = [step * TI for step in range(4 * steps)]
    diag = jnp.concatenate(diags, axis=0)
    if kind == "dec":
        span = rows // quests
        near = diag_sums(kind, diag[:, :, :span], [start % span for start in starts])[:, :heads]
        blank = jnp.zeros_like(near)
        return jnp.stack([blank, blank, blank, near])
    tab = sum(tabs)
    near = diag_sums(kind, diag, starts)[:, :heads]
    return jnp.stack([near, tab[:heads, :32].T, tab[:heads, 32:].T, jnp.zeros_like(near)])


def weight_copies(core, pieces, wi_ref, wd_ref, sems):
    in_own, in_far, in_near, down_own, down_far, down_near = pieces
    own = in_own.shape[1]
    block = own // 2
    rows_in, rows_down = in_far.shape[0], down_far.shape[0]
    far_in = pl.ds(pl.multiple_of(core * rows_in, rows_in), rows_in)
    near_in = pl.ds(pl.multiple_of((1 - core) * rows_in, rows_in), rows_in)
    far_down = pl.ds(pl.multiple_of(own + core * rows_down, rows_down), rows_down)
    near_down = pl.ds(pl.multiple_of(own + (1 - core) * rows_down, rows_down), rows_down)
    moves = []
    for b in range(2):
        part = slice(b * block, (b + 1) * block)
        moves.append((in_own.at[:, part], wi_ref.at[:, part]))
        moves.append((down_own.at[part, :], wd_ref.at[part, :]))
    other = slice(own, 2 * own)
    moves.append((in_far, wi_ref.at[far_in, other]))
    moves.append((in_near, wi_ref.at[near_in, other]))
    moves.append((down_far, wd_ref.at[far_down, :]))
    moves.append((down_near, wd_ref.at[near_down, :]))
    return [pltpu.make_async_copy(src, dst, sems.at[i]) for i, (src, dst) in enumerate(moves)]


def ffn_kernel(mode, part, flag_ref, *refs):
    pieces, refs = refs[:6], refs[6:]
    refs, (wi_ref, wd_ref, sems) = refs[:-3], refs[-3:]
    copies = weight_copies(flag_ref[0], pieces, wi_ref, wd_ref, sems)
    first_step = pl.program_id(0) == 0

    @pl.when(first_step)
    def _():
        for copy in copies:
            copy.start()
        for copy in copies:
            copy.wait()

    gain_ref, wa_ref = refs[:2]
    gain = gain_ref[0:1, :]
    if mode == "back":
        middle_ref, second_ref, own_ref, arrived_ref, more_ref, first_ref = refs[2:8]
        dx_ref, hn_ref, gl_ref, ml_ref, act_ref, dzo_ref, do_ref, dgain_ref, z_ref, du_ref = refs[-10:]
        on_encoder = flag_ref[2] == 0
        x = jnp.where(on_encoder, middle_ref[...], second_ref[...])
    else:
        base_ref, att_ref = refs[2:4]
        x = base_ref[...].astype(jnp.float32) + dot(att_ref[...], wa_ref[...])
        if mode == "fwd":
            out_ref, mid_ref, z_ref, u_ref = refs[4:]
        else:
            own_ref, arrived_ref, out_ref, mid_ref, dx_ref, low_ref, do_ref, z_ref, u_ref, du_ref, dz_ref = refs[4:]
        mid_ref[...] = x
    rows, width = x.shape
    hidden = wi_ref.shape[1]
    block, chunk = hidden // FFN_BLOCKS, 32
    if mode != "fwd":
        half = part if mode == "back" else lax.div(2 * pl.program_id(0), pl.num_programs(0))
        grad_low = jnp.where(half == flag_ref[1], own_ref[...], arrived_ref[...])
        grad = grad_low.astype(jnp.float32)
    scale = lax.rsqrt(jnp.mean(x * x, axis=1, keepdims=True) + EPSILON)
    normed_full = x * scale * gain
    normed = normed_full.astype(jnp.bfloat16)
    if mode == "back":
        grad = grad + more_ref[...].astype(jnp.float32)
        grad_low = grad.astype(jnp.bfloat16)
        hn_ref[...] = jnp.transpose(normed_full).astype(jnp.bfloat16)
        gl_ref[...] = jnp.transpose(grad).astype(jnp.bfloat16)
    total = jnp.zeros((rows, width), jnp.float32)
    back = jnp.zeros((rows, width), jnp.float32)
    for index in range(FFN_BLOCKS + 1):
        if index < FFN_BLOCKS:
            cols = slice(index * block, (index + 1) * block)
            z_ref[index % 2] = dot(normed, wi_ref[:, cols])
            if mode != "fwd":
                du_ref[index % 2] = dot(grad_low, wd_ref[cols, :], NT)
        if index == 0:
            continue
        slot = (index - 1) % 2
        cols = slice((index - 1) * block, index * block)
        for r in range(0, rows, chunk):
            lines = slice(r, r + chunk)
            z = z_ref[slot, lines, :]
            square = z * z
            tanh = jnp.tanh(z * (GELU_SCALE + GELU_SCALE * GELU_CUBE * square))
            half = 0.5 + 0.5 * tanh
            act = (z * half).astype(jnp.bfloat16)
            if mode == "back":
                act_ref[lines, cols] = act
            else:
                u_ref[slot, lines, :] = act
            if mode != "fwd":
                slope = half + z * (0.5 - 0.5 * tanh * tanh) * (GELU_SCALE + 3.0 * GELU_SCALE * GELU_CUBE * square)
                d_hidden = (du_ref[slot, lines, :] * slope).astype(jnp.bfloat16)
                if mode == "back":
                    dzo_ref[lines, cols] = d_hidden
                else:
                    dz_ref[slot, lines, :] = d_hidden
        if mode != "back":
            total = total + dot(u_ref[slot], wd_ref[cols, :])
        if mode == "back":
            back = back + dot(dzo_ref[:, cols], wi_ref[:, cols], NT)
        elif mode == "both":
            back = back + dot(dz_ref[slot], wi_ref[:, cols], NT)
    if mode != "back":
        out_ref[...] = (x + total).astype(jnp.bfloat16)
    if mode != "fwd":
        scaled = back * gain
        mean = jnp.mean(scaled * x, axis=1, keepdims=True)
        grad = grad + scale * scaled - x * (scale * scale * scale * mean)
        if mode == "back":
            grad = jnp.where(on_encoder, grad, first_ref[...])
            ml_ref[...] = jnp.transpose(grad).astype(jnp.bfloat16)
            gain_part = jnp.sum((back * x * scale).reshape(rows // 8, 8, width), axis=0)
            dgain_ref[...] = jnp.where(first_step, gain_part, dgain_ref[...] + gain_part)
        else:
            low_ref[...] = grad.astype(jnp.bfloat16)
        dx_ref[...] = grad
        do_ref[...] = dot(grad.astype(jnp.bfloat16), wa_ref[...], NT).astype(jnp.bfloat16)


def feed_forward(mode, part, rows, flags, pieces, gain, w_att, rows_in, held=(), deps=()):
    width = w_att.shape[0]
    hidden = 2 * pieces[0].shape[1]
    steps = rows // TR
    row_block = pl.BlockSpec((TR, width), lambda i: (i, 0))
    turned_block = pl.BlockSpec((width, TR), lambda i: (0, part * steps + i))
    hidden_block = pl.BlockSpec((TR, hidden), lambda i: (part * steps + i, 0))
    low = jax.ShapeDtypeStruct((rows, width), jnp.bfloat16)
    full = jax.ShapeDtypeStruct((rows, width), jnp.float32)
    turned = jax.ShapeDtypeStruct((width, 2 * rows), jnp.bfloat16)
    wide = jax.ShapeDtypeStruct((2 * rows, hidden), jnp.bfloat16)
    small = jax.ShapeDtypeStruct((8, width), jnp.float32)
    outs = {
        "fwd": ([row_block] * 2, [low, full]),
        "both": ([row_block] * 5, [low, full, full, low, low]),
        "back": (
            [row_block]
            + [turned_block] * 3
            + [hidden_block] * 2
            + [row_block, pl.BlockSpec((8, width), lambda i: (0, 0))],
            [full, turned, turned, turned, wide, wide, low, small],
        ),
    }[mode]
    slab = (2, TR, hidden // FFN_BLOCKS)
    slab32, slab16 = pltpu.VMEM(slab, jnp.float32), pltpu.VMEM(slab, jnp.bfloat16)
    scratch = {"fwd": [slab32, slab16], "both": [slab32, slab16, slab32, slab16], "back": [slab32, slab32]}[mode]
    matmuls = {"fwd": 2, "both": 4, "back": 3}[mode]
    inputs = 9 + len(rows_in)
    return pl.pallas_call(
        without(partial(ffn_kernel, mode, part), inputs, len(held) + len(deps)),
        grid=(steps,),
        in_specs=[pl.BlockSpec(memory_space=pltpu.SMEM)]
        + [ANY] * 6
        + [pl.BlockSpec((8, width), lambda i: (0, 0)), pl.BlockSpec(w_att.shape, lambda i: (0, 0))]
        + [pl.BlockSpec((TR, width), lambda i, at=at, turn=turn: (at + i % turn, 0)) for _, at, turn in rows_in]
        + [ANY] * (len(held) + len(deps)),
        out_specs=outs[0],
        out_shape=outs[1],
        scratch_shapes=scratch
        + [
            pltpu.VMEM((width, hidden), jnp.bfloat16),
            pltpu.VMEM((hidden, width), jnp.bfloat16),
            pltpu.SemaphoreType.DMA((8,)),
        ],
        input_output_aliases={inputs + index: 1 + index for index in range(len(held))},
        compiler_params=pltpu.CompilerParams(vmem_limit_bytes=VMEM_LIMIT),
        cost_estimate=cost(
            flops=4 * matmuls * rows * width * hidden,
            bytes_accessed=4 * width * hidden + 8 * rows * width,
            transcendentals=rows * hidden,
        ),
        name="feed_forward_" + mode,
    )(flags, *pieces, jnp.broadcast_to(gain[None], (8, width)), w_att, *(x for x, _, _ in rows_in), *held, *deps)


def product_kernel(left_of, parts_of, slices, which, core_ref, *refs):
    left_count, count = max(left_of) + 1, sum(parts_of)
    lefts, rights = refs[:left_count], refs[left_count : left_count + count]
    outs, held_ref = refs[left_count + count : -1], refs[-1]
    step = pl.program_id(0)
    rows, span = lefts[0].shape
    size = rows // slices
    half = rows // 2

    @pl.when(step == 0)
    def _():
        for index, left in enumerate(lefts):
            if len(outs) == 1:
                held_ref[index] = left[...]
                continue
            for first, core in ((0, 1 - core_ref[0]), (half, core_ref[0])):
                for part in range(slices // 2):
                    source = pl.ds(pl.multiple_of((2 * part + core) * size, 16), size)
                    held_ref[index, first + part * size : first + (part + 1) * size, :] = left[source, :]

    def product(index, lines):
        parts = rights[sum(parts_of[:index]) : sum(parts_of[: index + 1])]
        length = span // len(parts)
        return sum(
            dot(held_ref[left_of[index], lines, part * length : (part + 1) * length], right[...])
            for part, right in enumerate(parts)
        ).astype(jnp.bfloat16)

    for index in range(len(parts_of)):
        steps = [s for s, owner in enumerate(which) if owner == index]
        chosen = functools.reduce(lambda a, b: a | b, [step == s for s in steps])

        @pl.when(chosen)
        def _(index=index):
            if len(outs) == 1:
                outs[0][...] = product(index, slice(0, rows))
            else:
                outs[0][...] = product(index, slice(0, half))
                outs[1][...] = product(index, slice(half, rows))


def products(lefts, left_of, rights, block, slices, core, deps=()):
    rows, span = lefts[0].shape
    parts_of = [len(right) for right in rights]
    counts = [right[0].shape[1] // (2 * block) for right in rights]
    which, place = [], []
    for half in range(2):
        for index, number in enumerate(counts):
            for b in range(number):
                which.append(index)
                place.append(half * number + b)
    maps = []
    for index, right in enumerate(rights):
        held, column_of = 0, []
        for s, owner in enumerate(which):
            if owner == index:
                held = place[s]
            column_of.append(held)
        maps += [column_of] * len(right)
    steps = len(which)
    total = steps * block

    def right_map(column_of):
        def index_map(s):
            value = 0
            for position in range(steps):
                if column_of[position]:
                    value = value + jnp.where(s == position, column_of[position], 0)
            return (0, value)

        return index_map

    size = rows // slices
    apart = size % 16 == 0
    out_rows = rows // 2 if apart else rows
    out = jax.ShapeDtypeStruct((out_rows, total), jnp.bfloat16)
    flat = [part for right in rights for part in right]
    results = pl.pallas_call(
        without(
            partial(product_kernel, left_of, parts_of, slices, which), 1 + len(lefts) + len(flat), len(deps)
        ),
        grid=(steps,),
        in_specs=[pl.BlockSpec(memory_space=pltpu.SMEM)]
        + [pl.BlockSpec((rows, span), lambda s: (0, 0)) for _ in lefts]
        + [pl.BlockSpec((part.shape[0], block), right_map(column_of)) for part, column_of in zip(flat, maps)]
        + [ANY] * len(deps),
        out_specs=[pl.BlockSpec((out_rows, block), lambda s: (0, s))] * (2 if apart else 1),
        out_shape=[out] * (2 if apart else 1),
        scratch_shapes=[pltpu.VMEM((len(lefts), rows, span), jnp.bfloat16)],
        compiler_params=pltpu.CompilerParams(vmem_limit_bytes=VMEM_LIMIT),
        cost_estimate=cost(
            flops=2 * span * rows * total, bytes_accessed=2 * (span + rows) * total, transcendentals=0
        ),
        name="weight_products",
    )(core.reshape(1), *lefts, *flat, *deps)
    if apart:
        return results
    cut = results[0].reshape(slices // 2, 2, size, total)
    return pick(cut, 1 - core, 1).reshape(-1, total), pick(cut, core, 1).reshape(-1, total)


def nothing(shapes):
    return pl.pallas_call(
        lambda *refs: None, out_shape=shapes, out_specs=[ANY] * len(shapes), name="nothing"
    )()


def input_kernel(gain_ref, w_ref, x_ref, first_ref, second_ref, dk_ref, dv_ref, grad_ref, out_ref, dgain_ref):
    step = pl.program_id(0)
    gain = gain_ref[0:1, :]
    rows, width = x_ref.shape
    d_query = jnp.where(2 * step < pl.num_programs(0), first_ref[...], second_ref[...])
    back = dot(d_query, w_ref[:, :width], NT)
    back = back + dot(dk_ref[...], w_ref[:, width : 2 * width], NT)
    back = back + dot(dv_ref[...], w_ref[:, 2 * width :], NT)
    x = x_ref[...].astype(jnp.float32)
    scale = lax.rsqrt(jnp.mean(x * x, axis=1, keepdims=True) + EPSILON)
    scaled = back * gain
    mean = jnp.mean(scaled * x, axis=1, keepdims=True)
    out_ref[...] = grad_ref[...] + scale * scaled - x * (scale * scale * scale * mean)
    gain_part = jnp.sum((back * x * scale).reshape(rows // 8, 8, width), axis=0)
    dgain_ref[...] = jnp.where(step == 0, gain_part, dgain_ref[...] + gain_part)


def input_gradient(x, gain, w_qkv, query_grads, key_grad, value_grad, grad, deps):
    rows, width = x.shape
    steps = rows // TR
    row_block = pl.BlockSpec((TR, width), lambda i: (i, 0))
    half_block = pl.BlockSpec((TR, width), lambda i: (i % (steps // 2), 0))
    fixed = pl.BlockSpec((8, width), lambda i: (0, 0))
    out, dgain = pl.pallas_call(
        without(input_kernel, 8, len(deps)),
        grid=(steps,),
        in_specs=[fixed, pl.BlockSpec(w_qkv.shape, lambda i: (0, 0)), row_block, half_block, half_block]
        + [row_block] * 3
        + [ANY] * len(deps),
        out_specs=[row_block, fixed],
        out_shape=[jax.ShapeDtypeStruct((rows, width), jnp.float32), jax.ShapeDtypeStruct((8, width), jnp.float32)],
        compiler_params=pltpu.CompilerParams(vmem_limit_bytes=VMEM_LIMIT),
        cost_estimate=cost(
            flops=6 * rows * width * width, bytes_accessed=16 * rows * width, transcendentals=0
        ),
        name="input_gradient",
    )(jnp.broadcast_to(gain[None], (8, width)), w_qkv, x, *query_grads, key_grad, value_grad, grad, *deps)
    return out, jnp.sum(dgain, axis=0)


def sum_kernel(rounds, x_ref, out_ref, *refs):
    slots, send_sems, recv_sems = refs[: len(rounds)], refs[len(rounds)], refs[len(rounds) + 1]
    barrier = pltpu.get_barrier_semaphore()
    places, peers = [], []
    for axes in rounds:
        place, count = 0, 1
        for axis in axes:
            place = place * lax.axis_size(axis) + lax.axis_index(axis)
            count = count * lax.axis_size(axis)
        found = []
        for step in range(1, count):
            rest, device = lax.rem(place + step, count), {}
            for axis in reversed(axes):
                device[axis] = lax.rem(rest, lax.axis_size(axis))
                rest = lax.div(rest, lax.axis_size(axis))
            found.append(device)
        places.append(place)
        peers.append(found)
    for device in peers[0] + peers[1]:
        pl.semaphore_signal(barrier, inc=1, device_id=device, device_id_type=pl.DeviceIdType.MESH)
    pl.semaphore_wait(barrier, len(peers[0]) + len(peers[1]))
    value = x_ref[...]
    first = 0
    for slot, place, found in zip(slots, places, peers):
        slot[place] = value
        copies = []
        for step, device in enumerate(found):
            copies.append(
                pltpu.make_async_remote_copy(
                    src_ref=slot.at[place],
                    dst_ref=slot.at[place],
                    send_sem=send_sems.at[first + step],
                    recv_sem=recv_sems.at[first + step],
                    device_id=device,
                    device_id_type=pl.DeviceIdType.MESH,
                )
            )
        for copy in copies:
            copy.start()
        for copy in copies:
            copy.wait()
        first += len(found)
        value = slot[0]
        for index in range(1, len(found) + 1):
            value = value + slot[index]
    out_ref[...] = value


def sum_everywhere(x):
    rounds = (("dp",), ("section", "mp"))
    counts = [math.prod(lax.axis_size(axis) for axis in axes) for axes in rounds]
    copies = sum(counts) - len(counts)
    return pl.pallas_call(
        partial(sum_kernel, rounds),
        out_shape=jax.ShapeDtypeStruct(x.shape, x.dtype),
        in_specs=[pl.BlockSpec(memory_space=pltpu.VMEM)],
        out_specs=pl.BlockSpec(memory_space=pltpu.VMEM),
        scratch_shapes=[pltpu.VMEM((count,) + x.shape, x.dtype) for count in counts]
        + [pltpu.SemaphoreType.DMA((copies,)), pltpu.SemaphoreType.DMA((copies,))],
        compiler_params=pltpu.CompilerParams(collective_id=0, has_side_effects=True),
        name="sum_everywhere",
    )(x)


def pair_permute(x, axis, bit):
    pairs = [(i, i ^ (1 << bit)) for i in range(lax.axis_size(axis))]
    return lax.ppermute(x, axis, pairs)


def shifted(x, axis, by):
    peers = lax.axis_size(axis)
    pairs = [(i, i + by) for i in range(peers) if 0 <= i + by < peers]
    return lax.ppermute(x, axis, pairs)


def in_order(flag, first, second, axis):
    return jnp.where(
        flag == 0,
        jnp.concatenate([first, second], axis=axis),
        jnp.concatenate([second, first], axis=axis),
    )


def pick(x, index, axis):
    return lax.dynamic_index_in_dim(x, index, axis, False)


def after(values, *others):
    return lax.optimization_barrier((values, others))[0]


def exchange_rows(block, where_mp):
    return pick(block, where_mp, 0), pair_permute(pick(block, 1 - where_mp, 0), "mp", 0)


def scatter_rows(rows, where_mp):
    half = rows.shape[0] // 2
    send = lax.dynamic_slice_in_dim(rows, (1 - where_mp) * half, half, 0).astype(jnp.bfloat16)
    return lax.dynamic_slice_in_dim(rows, where_mp * half, half, 0), pair_permute(send, "mp", 0)


def fetch_far(shard, core):
    half = shard.shape[0] // 2
    return pair_permute(lax.dynamic_slice_in_dim(shard, core * half, half, 0), "mp", 0)


def fetch_near(far):
    return pair_permute(far, "dp", 0)


def fetch_other(shard, dp_index):
    quarter = shard.shape[0] // 4
    far = pair_permute(lax.dynamic_slice_in_dim(shard, (dp_index & 3) * quarter, quarter, 0), "mp", 0)
    half = in_order(dp_index & 1, far, pair_permute(far, "dp", 0), 0)
    return in_order((dp_index >> 1) & 1, half, pair_permute(half, "dp", 1), 0), far


class Reduction:
    def __init__(self, send, keep, dp_index, section=None):
        self.total, self.arrived = keep, pair_permute(send, "dp", 0)
        self.dp_index = dp_index
        bits = lax.axis_size("dp").bit_length() - 1
        self.left = ([("section", section)] if section is not None else []) + [("mp", None)]
        self.left += [("dp", bit) for bit in range(1, bits)]

    def joined(self, cut):
        return cut(self.total).astype(jnp.float32) + cut(self.arrived).astype(jnp.float32)

    def hop(self, *ties):
        brought = self.arrived
        self.arrived = after(self.arrived, *ties)
        axis, which = self.left.pop(0)
        rows, width = self.total.shape
        if axis == "section":
            send = self.joined(lambda x: x[: rows // 2]).astype(jnp.bfloat16)
            keep = jnp.where(which == 0, 0.0, self.joined(lambda x: x[rows // 2 :]))
            self.total, self.arrived = keep, shifted(send, "section", -1)
        elif axis == "mp":
            send = self.joined(lambda x: x[:, width // 2 :]).astype(jnp.bfloat16)
            self.total, self.arrived = self.joined(lambda x: x[:, : width // 2]), pair_permute(send, "mp", 0)
        else:
            mark = (self.dp_index >> which) & 1
            halves = (lax.axis_size("dp") >> (which + 1), 2, -1, width)
            send = self.joined(lambda x: pick(x.reshape(halves), 1 - mark, 1)).astype(jnp.bfloat16)
            keep = self.joined(lambda x: pick(x.reshape(halves), mark, 1))
            self.total = keep.reshape(-1, width)
            self.arrived = pair_permute(send.reshape(-1, width), "dp", which)
        return brought

    def finish(self, *ties):
        while self.left:
            self.hop()
        self.arrived = after(self.arrived, *ties)
        return self.joined(lambda x: x)


def rms_norm(inputs, gain_row):
    return (
        inputs * lax.rsqrt(jnp.mean(inputs * inputs, axis=-1, keepdims=True) + EPSILON) * gain_row
    )


def norm_back(rows, gain_row, grad_normed):
    return jax.vjp(rms_norm, rows, gain_row)[1](grad_normed)


def low(x):
    return x.astype(jnp.bfloat16)


def local(
    block_input,
    out_cotangent,
    doc_lengths,
    question_lengths,
    coordinates,
    gains,
    bias_tables,
    self_qkv,
    self_out,
    ffn_in,
    ffn_out,
    cross_q,
    cross_kv,
    cross_out,
):
    section = lax.axis_index("section")
    on_encoder = section == 0
    dp_index = lax.axis_index("dp")
    core = dp_index & 1
    where_mp = lax.axis_index("mp")
    width = block_input.shape[4]
    quests = question_lengths.shape[2]
    own = self_qkv.shape[3]
    pairs = 2 * own // LANES
    heads = 2 * pairs
    parts = lax.axis_size("dp")
    flags = jnp.stack([core, where_mp, section]).astype(jnp.int32)

    rows_low = in_order(where_mp, *exchange_rows(block_input[0, :, 0], where_mp), 0)
    qkv_own = self_qkv[0].reshape(width, -1)
    qkv_other, qkv_far = fetch_other(qkv_own, dp_index)
    w_qkv = jnp.concatenate(
        [x[:, t * own : (t + 1) * own] for t in range(3) for x in (qkv_own, qkv_other)], axis=1
    )
    owned = after((ffn_in[0], ffn_out[0], self_out[0]), rows_low, qkv_far)
    fars = [fetch_far(x, core) for x in owned]

    lens = jnp.concatenate(
        [pick(doc_lengths, where_mp, 0), pick(question_lengths, where_mp, 0)[0]]
    ).astype(jnp.int32)
    coords = pick(coordinates, where_mp, 0)[0]
    tables = jnp.where(where_mp == 0, bias_tables, jnp.roll(bias_tables, heads // 2, axis=2))

    rows = rows_low.astype(jnp.float32)
    span = rows.shape[0]
    half = span // 2
    turn = half // TR
    halves = (slice(0, half), slice(half, span))
    gain_self = jnp.where(on_encoder, gains[0], gains[2])
    normed_self = low(rms_norm(rows, gain_self))
    projected = low(dot(normed_self, w_qkv))
    merged, probs, middles, memories, arrivals = [], [], [], [], []
    for part in range(2):
        deps = memories[:1]

        def forward(kind, chosen):
            return attend_forward(
                kind, part, half, lens, chosen, coords, projected, 0, [projected], 1, 2, pairs, quests, deps
            )

        out, prob = lax.cond(on_encoder, lambda: forward("enc", tables[:3]), lambda: forward("dec", tables[3:]))
        if not part:
            fars = after(fars, out)
            nears = [fetch_near(x) for x in fars]
            w_out = jnp.concatenate([self_out[0], in_order(core, fars[2], nears[2], 0)], axis=0)
            pieces = (ffn_in[0], fars[0], nears[0], ffn_out[0], fars[1], nears[1])
            cross_owned = after(
                (jnp.concatenate([cross_q, cross_kv.reshape(width, -1)], axis=1), cross_out, out_cotangent[0, :, 0]), fars
            )
            cross_fars = [fetch_far(x, core) for x in cross_owned[:2]]
            cot = exchange_rows(cross_owned[2], where_mp)
        else:
            cross_fars = after(cross_fars, out)
        memory, middle = feed_forward(
            "fwd", part, half, flags, pieces, gains[1], w_out, [(rows_low, part * turn, turn), (out, 0, turn)]
        )
        arrivals.append(shifted(memory, "section", 1))
        merged.append(out)
        probs.append(prob)
        middles.append(middle)
        memories.append(memory)
    query_other, cross_other = (in_order(core, far, fetch_near(far), 0) for far in cross_fars)
    w_query = jnp.concatenate([cross_q, query_other[:, :own]], axis=1)
    w_pair = jnp.concatenate(
        [x for t in range(2) for x in (cross_kv[:, t], query_other[:, (t + 1) * own : (t + 2) * own])], axis=1
    )
    w_cross = jnp.concatenate([cross_out, cross_other], axis=0)
    middle = jnp.concatenate(middles, axis=0)

    normed_cross = low(rms_norm(middle, gains[3]))
    queries = low(dot(normed_cross, w_query))
    first_pair = low(dot(arrivals[0], w_pair))
    arrivals[1] = after(arrivals[1], queries, first_pair)
    pair_rows = [first_pair, low(dot(arrivals[1], w_pair))]
    cross_merged, cross_prob = attend_forward(
        "cross", 0, span, lens, None, coords, queries, 0, pair_rows, 0, 1, pairs, quests
    )
    output_low, second, grad_second, second_low, cross_grad = feed_forward(
        "both",
        0,
        span,
        flags,
        pieces,
        gains[4],
        w_cross,
        [(middle, 0, 2 * turn), (cross_merged, 0, 2 * turn), (cot[0], 0, turn), (cot[1], 0, turn)],
    )
    output_own, output_arrived = scatter_rows(
        jnp.where(on_encoder, jnp.concatenate(memories, axis=0), output_low), where_mp
    )
    returns, returned, carry = [], [], ()
    for part in range(2):
        query_grad, key_grad, value_grad, _ = attend_backward(
            "cross",
            part,
            cross_prob,
            cross_grad,
            cross_merged,
            queries,
            0,
            pair_rows[part],
            0,
            1,
            pairs,
            quests,
            carry,
            [returns[0], output_arrived] if part else [],
        )
        carry = (query_grad, key_grad, value_grad)
        returns.append(
            low(
                dot(key_grad[halves[part]], w_pair[:, : 2 * own], NT)
                + dot(value_grad[halves[part]], w_pair[:, 2 * own :], NT)
            )
        )
        returned.append(shifted(returns[part], "section", -1))
    query_cross = after(query_grad, returns[1])

    def cross_norm():
        input_part, gain_part = norm_back(middle, gains[3], dot(query_cross, w_query, NT))
        return grad_second + input_part, gain_part

    def no_norm():
        return tuple(
            nothing([jax.ShapeDtypeStruct((span, width), jnp.float32), jax.ShapeDtypeStruct((width,), jnp.float32)])
        )

    grad_first, gain_cross = lax.cond(on_encoder, no_norm, cross_norm)

    gain_ffn = jnp.where(on_encoder, gains[1], gains[4])
    held, gain_ffn_grad, grads_middle, merged_grads = [], 0.0, [], []
    for part in range(2):
        if part:
            returned[1] = after(returned[1], grads_middle[0])
        grad_middle, *held, merged_grad, gain_part = feed_forward(
            "back",
            part,
            half,
            flags,
            pieces,
            gain_ffn,
            w_out,
            [
                (middles[part], 0, turn),
                (second, part * turn, turn),
                (cot[0], 0, turn),
                (cot[1], 0, turn),
                (returned[part], 0, turn),
                (grad_first, part * turn, turn),
            ],
            held,
        )
        gain_ffn_grad = gain_ffn_grad + jnp.sum(gain_part, axis=0)
        grads_middle.append(grad_middle)
        merged_grads.append(merged_grad)
    hn_turned, gl_turned, ml_turned, activated, hidden_grad = held
    in_send, in_keep = products([hn_turned], [0], [[hidden_grad]], 2 * own, parts, core)
    down_send, down_keep = products([gl_turned], [0], [[activated]], 2 * own, parts, core, [in_send])
    in_steps = Reduction(in_send, in_keep, dp_index)
    down_steps = Reduction(down_send, down_keep, dp_index)

    def cross_products():
        return tuple(
            products(
                [normed_cross.T, jnp.concatenate(arrivals, axis=0).T, second_low.T],
                [0, 1, 1, 2],
                [[query_cross], [key_grad], [value_grad], [cross_merged]],
                own,
                2 * parts,
                core,
                [down_send],
            )
        )

    def no_products():
        blank = jax.ShapeDtypeStruct((width // 2, 8 * own), jnp.bfloat16)
        return tuple(nothing([blank, blank]))

    cross_send, cross_keep = lax.cond(on_encoder, no_products, cross_products)
    cross_steps = Reduction(cross_send, cross_keep, dp_index, section)
    scores, query_grads, carry = [], [], ()
    for part in range(2):
        if part:
            deps = (in_steps.hop(), down_steps.arrived, cross_steps.hop())
        else:
            deps = (down_send, cross_send, in_steps.hop())

        def backward(kind):
            return attend_backward(
                kind, part, probs[part], merged_grads[part], merged[part], projected, 0, projected, 1, 2, pairs, quests,
                carry, deps
            )

        query_grad, key_grad, value_grad, score = lax.cond(
            on_encoder, lambda: backward("enc"), lambda: backward("dec")
        )
        carry = (key_grad, value_grad)
        query_grads.append(query_grad)
        scores.append(score)
    self_send, self_keep = products(
        [normed_self.T, ml_turned],
        [0, 0, 0, 1],
        [query_grads, [key_grad], [value_grad], merged],
        own,
        parts,
        core,
    )
    down_steps.hop(scores[1])
    self_steps = Reduction(self_send, self_keep, dp_index)
    input_grad, gain_self_grad = input_gradient(
        rows_low,
        gain_self,
        w_qkv,
        query_grads,
        key_grad,
        value_grad,
        jnp.concatenate(grads_middle, axis=0),
        [self_send],
    )
    grad_own, grad_arrived = scatter_rows(input_grad, where_mp)

    tabs, diags = [], []
    deps = (self_send, input_grad, in_steps.hop(scores[1]), cross_steps.hop(self_send))
    for part in range(2):
        for quarter in range(2):
            tab, diag = lax.cond(
                on_encoder,
                lambda: table_sums("enc", part, quarter, coords, scores[part], quests, deps),
                lambda: table_sums("dec", part, quarter, coords, scores[part], quests, deps),
            )
            tabs.append(tab)
            diags.append(diag)
            if len(tabs) == 1:
                deps = (tab, self_steps.hop(tab), in_steps.arrived, down_steps.hop(tab))
            elif len(tabs) == 2:
                deps = (tab, cross_steps.hop(tab), grad_arrived)
            elif len(tabs) == 3:
                deps = (tab, self_steps.hop(tab), cross_steps.hop(tab), down_steps.hop(tab))
    table_grad = lax.cond(
        on_encoder,
        lambda: table_grads("enc", tabs, diags, span, quests, heads),
        lambda: table_grads("dec", tabs, diags, span, quests, heads),
    )
    table_grad = jnp.where(where_mp == 0, table_grad, jnp.roll(table_grad, heads // 2, axis=2))
    blank = jnp.zeros((width,), jnp.float32)
    gain_grad = jnp.where(
        on_encoder,
        jnp.stack([gain_self_grad, gain_ffn_grad, blank, blank, blank]),
        jnp.stack([blank, blank, gain_self_grad, gain_cross, gain_ffn_grad]),
    )
    small = jnp.concatenate([gain_grad.reshape(-1, LANES), table_grad.reshape(-1, LANES)], axis=0)
    count = small.shape[0]
    small = jnp.pad(small, ((0, -count % 8), (0, 0)))
    cross_shard, in_shard, down_shard = (x.finish(tabs[3]) for x in (cross_steps, in_steps, down_steps))
    small = sum_everywhere(after(small, self_steps.hop(tab), down_steps.arrived))
    gain_count = gain_grad.size // LANES
    gain_sum = small[:gain_count].reshape(gain_grad.shape)
    table_sum = small[gain_count:count].reshape(table_grad.shape)
    self_shard = self_steps.finish(table_grad)
    output_rows, grad_rows = (
        in_order(where_mp, own_rows[None], after(arrived, tabs[2]).astype(own_rows.dtype)[None], 0)
        for own_rows, arrived in ((output_own, output_arrived), (grad_own, grad_arrived))
    )
    return (
        output_rows[None, :, None],
        grad_rows[None, :, None],
        gain_sum[:4],
        gain_sum[4],
        table_sum,
        self_shard[:, : 3 * own].reshape(-1, 3, own)[None],
        self_shard[:, 3 * own :].T[None],
        in_shard[None],
        down_shard.T[None],
        cross_shard[:, :own],
        cross_shard[:, own : 3 * own].reshape(-1, 2, own),
        cross_shard[:, 3 * own :].T,
    )


def solution(mesh):
    return jax.shard_map(
        local,
        mesh=mesh,
        in_specs=(
            P("section", None, "dp", "mp", None),
            P("section", None, "dp", "mp", None),
            P(None, "dp"),
            P(None, "dp", None),
            P(None, "dp", None, None),
            P(),
            P(),
            P("section", None, None, "mp"),
            P("section", "mp", None),
            P("section", None, "mp"),
            P("section", "mp", None),
            P(None, "mp"),
            P(None, None, "mp"),
            P("mp", None),
        ),
        out_specs=(
            P("section", None, "dp", "mp", None),
            P("section", None, "dp", "mp", None),
            P(),
            P(),
            P(),
            P("section", "dp", None, "mp"),
            P("section", "mp", "dp"),
            P("section", "dp", "mp"),
            P("section", "mp", "dp"),
            P(("section", "dp"), "mp"),
            P(("section", "dp"), None, "mp"),
            P("mp", ("section", "dp")),
        ),
        check_vma=False,
    )
```

```python
import functools
from functools import partial
import math

import jax
import jax.numpy as jnp
from jax import lax
from jax.experimental import pallas as pl
from jax.experimental.pallas import tpu as pltpu
from jax.sharding import PartitionSpec as P

HEAD = 64
LANES = 128
NEGATIVE = -1e30
EPSILON = 1e-06
GELU_SCALE = math.sqrt(2 / math.pi)
GELU_CUBE = 0.044715
TI = 64
FFN_BLOCKS = 4
TR = 256
VMEM_LIMIT = 56 * 1024 * 1024
NT = (((1,), (1,)), ((), ()))
NN = (((1,), (0,)), ((), ()))


def edge_list(exact_span, bucket_count, far_reach):
    log_edges = [
        int(
            math.ceil(
                exact_span * (far_reach / exact_span) ** (power_index / (bucket_count - exact_span))
            )
        )
        for power_index in range(1, bucket_count - exact_span)
    ]
    return list(range(1, exact_span + 1)) + log_edges


def magnitude(distance, exact_span, bucket_count, far_reach):
    bucket = jnp.minimum(distance, exact_span)
    for threshold in edge_list(exact_span, bucket_count, far_reach)[exact_span:]:
        bucket = bucket + (distance >= threshold).astype(jnp.int32)
    return bucket


def two_sided(relative, far_reach):
    return magnitude(jnp.abs(relative), 8, 16, far_reach) + jnp.where(relative > 0, 16, 0)


def one_sided(relative):
    return magnitude(jnp.maximum(-relative, 0), 16, 32, 128)


def half_lanes(block, head):
    lane = lax.broadcasted_iota(jnp.int32, block.shape, 1)
    keep = lane < HEAD if head == 0 else lane >= HEAD
    return jnp.where(keep, block, jnp.zeros_like(block))


def dot(a, b, dims=NN):
    return lax.dot_general(a, b, dims, preferred_element_type=jnp.float32)


def pick_lanes(row, index):
    return jnp.take_along_axis(jnp.broadcast_to(row, index.shape), index, axis=1)


def pick_sublanes(table_ref, head, low, odd, upper):
    parts = [
        jnp.take_along_axis(table_ref[head, 8 * part : 8 * part + 8, :], low, axis=0)
        for part in range(4)
    ]
    return jnp.where(upper, jnp.where(odd, parts[3], parts[2]), jnp.where(odd, parts[1], parts[0]))


def fwd_kernel(kind, part, tq, span, heads, len_ref, tabn_ref, tabx_ref, taby_ref, crow_ref, ccol_ref, q_ref, *refs):
    count = (len(refs) - 7) // 2
    k_refs, v_refs = refs[:count], refs[count : 2 * count]
    o_ref, p_ref, s_ref, idx_ref, mask_ref, near_ref, bias_ref = refs[-7:]
    length = span // count
    pair = pl.program_id(0)
    first_block = 0 if kind == "dec" else part * tq // LANES
    chunk = 16

    @pl.when(pair == 0)
    def _():
        key = lax.broadcasted_iota(jnp.int32, (8, span), 1)
        limit = len_ref[1 + part] if kind == "dec" else len_ref[0]
        mask_ref[...] = jnp.where(key < limit, 0.0, NEGATIVE)
        if kind != "cross":
            def near_rows(r, carry):
                rows = pl.ds(pl.multiple_of(r * 8, 8), 8)
                query = r * 8 + lax.broadcasted_iota(jnp.int32, (8, LANES), 0)
                for d in range(-2, 3):
                    key = d * LANES + lax.broadcasted_iota(jnp.int32, (8, LANES), 1)
                    bucket = one_sided(key - query) if kind == "dec" else two_sided(key - query, 128)
                    for head in range(heads):
                        value = pick_lanes(tabn_ref[head : head + 1, :], bucket)
                        if kind == "dec":
                            value = jnp.where(key <= query, value, NEGATIVE)
                        near_ref[head, rows, (d + 2) * LANES : (d + 3) * LANES] = value
                return carry

            lax.fori_loop(0, LANES // 8, near_rows, 0)
        if kind == "enc":

            def bucket_rows(r, carry):
                rows = pl.ds(pl.multiple_of(r * chunk, chunk), chunk)
                for axis in range(2):
                    far = crow_ref[axis : axis + 1, :] - ccol_ref[rows, axis : axis + 1]
                    idx_ref[axis, rows, :] = two_sided(far, 500)
                return carry

            lax.fori_loop(0, tq // chunk, bucket_rows, 0)

            def bias_rows(r, carry):
                rows = pl.ds(pl.multiple_of(r * 8, 8), 8)
                for c in range(0, span, LANES):
                    lanes = slice(c, c + LANES)
                    across = idx_ref[0, rows, lanes]
                    upward = idx_ref[1, rows, lanes]
                    low, odd, upper = upward & 7, (upward & 8) != 0, upward >= 16
                    for head in range(heads):
                        bias_ref[head, rows, lanes] = pick_lanes(
                            tabx_ref[head : head + 1, :], across
                        ) + pick_sublanes(taby_ref, head, low, odd, upper)
                return carry

            lax.fori_loop(0, tq // 8, bias_rows, 0, unroll=2)

    for head in range(2):
        query = half_lanes(q_ref[...], head)
        for index, k_ref in enumerate(k_refs):
            s_ref[head, :, index * length : (index + 1) * length] = dot(query, k_ref[...], NT)
        for r in range(0, tq, chunk):
            rows = slice(r, r + chunk)
            pieces = []
            for c in range(0, span, LANES):
                lanes = slice(c, c + LANES)
                piece = s_ref[head, rows, lanes] + mask_ref[0:1, lanes]
                if kind != "cross":
                    apart = min(max(c // LANES - (first_block + r // LANES), -2), 2) + 2
                    near = slice(apart * LANES, (apart + 1) * LANES)
                    piece = piece + near_ref[2 * pair + head, r % LANES : r % LANES + chunk, near]
                if kind == "enc":
                    piece = piece + bias_ref[2 * pair + head, rows, lanes]
                pieces.append(piece)
            score = jnp.concatenate(pieces, axis=1)
            score = jnp.exp(score - jnp.max(score, axis=1, keepdims=True))
            score = score * (1.0 / jnp.sum(score, axis=1, keepdims=True))
            p_ref[head, rows, :] = score.astype(jnp.bfloat16)
    first, second = (
        sum(
            dot(p_ref[head, :, index * length : (index + 1) * length], v_ref[...])
            for index, v_ref in enumerate(v_refs)
        )
        for head in range(2)
    )
    lane = lax.broadcasted_iota(jnp.int32, first.shape, 1)
    o_ref[...] = jnp.where(lane < HEAD, first, second).astype(jnp.bfloat16)


def bwd_kernel(kind, part, rows, span, p_ref, do_ref, o_ref, q_ref, k_ref, v_ref, *refs):
    carry = refs[: 2 if kind != "cross" else 3] if part else ()
    outs = refs[len(carry) :]
    dq_ref, dk_ref, dv_ref = outs[:3]
    low_ref, dp_ref = outs[3:]
    chunk = 16
    q_t = jnp.transpose(q_ref[...].astype(jnp.float32)).astype(jnp.bfloat16)
    do_t = jnp.transpose(do_ref[...].astype(jnp.float32)).astype(jnp.bfloat16)
    grads, key_grads, value_grads = [], [], []
    for head in range(2):
        d_out = half_lanes(do_ref[...], head)
        delta = jnp.sum(d_out.astype(jnp.float32) * o_ref[...].astype(jnp.float32), axis=1, keepdims=True)
        dp_ref[head] = dot(d_out, v_ref[...], NT)
        for r in range(0, rows, chunk):
            part_rows = slice(r, r + chunk)
            prob = p_ref[head, part_rows, :].astype(jnp.float32)
            low_ref[head, part_rows, :] = (
                prob * (dp_ref[head, part_rows, :] - delta[part_rows, :])
            ).astype(jnp.bfloat16)
        grads.append(dot(low_ref[head], k_ref[...]))
        half = slice(head * HEAD, (head + 1) * HEAD)
        key_grads.append(dot(q_t[half], low_ref[head]))
        value_grads.append(dot(do_t[half], p_ref[head]))
    lane = lax.broadcasted_iota(jnp.int32, grads[0].shape, 1)
    query_grad = jnp.where(lane < HEAD, grads[0], grads[1])
    if kind == "cross" and part:
        query_grad = query_grad + carry[0][...]
    dq_ref[...] = query_grad.astype(dq_ref.dtype)
    for index, (out_ref, pieces) in enumerate(((dk_ref, key_grads), (dv_ref, value_grads))):
        grad = jnp.transpose(jnp.concatenate(pieces, axis=0))
        if kind == "enc" and part:
            grad = grad + carry[index][...]
        if kind == "dec":
            if part:
                out_ref[0:span, :] = carry[index][0:span, :].astype(out_ref.dtype)
            out_ref[part * span : (part + 1) * span, :] = grad.astype(out_ref.dtype)
        else:
            out_ref[...] = grad.astype(out_ref.dtype)


def table_kernel(kind, ti, span, heads, low_ref, crow_ref, ccol_ref, tab_ref, diag_ref, row_ref, wide_ref, idx_ref):
    step = pl.program_id(0)
    group = 16
    wide = diag_ref.shape[2]
    pad = wide - span

    @pl.when(step == 0)
    def _():
        tab_ref[...] = jnp.zeros_like(tab_ref)

    if kind == "enc":
        for r in range(0, ti, 16):
            for axis in range(2):
                far = crow_ref[axis : axis + 1, :] - ccol_ref[r : r + 16, axis : axis + 1]
                idx_ref[axis, r : r + 16, :] = two_sided(far, 500).astype(jnp.float32)
    out_row = lax.broadcasted_iota(jnp.int32, (256, 256), 0)
    in_row = lax.broadcasted_iota(jnp.int32, (256, 256), 1)
    swap = (lax.div(out_row, 16) == lax.rem(in_row, 16)) & (lax.rem(out_row, 16) == lax.div(in_row, 16))
    swap = jnp.where(swap, 1.0, 0.0).astype(jnp.bfloat16)
    blank = jnp.zeros(((16 - heads) * 16, span), jnp.bfloat16)
    which = lax.broadcasted_iota(jnp.int32, (32, span), 0).astype(jnp.bfloat16)

    tab = jnp.zeros(tab_ref.shape, jnp.float32)
    diag = jnp.zeros((16, wide), jnp.float32)
    for g in range(ti // group):
        first = g * group
        block = jnp.concatenate([low_ref[h, first : first + group, :] for h in range(heads)] + [blank], axis=0)
        wide_ref[g] = dot(swap, block)
        if kind == "enc":
            row_ref[g] = wide_ref[g].astype(jnp.bfloat16)
        for j in range(group):
            lines = slice(16 * j, 16 * j + 16)
            if kind == "enc":
                hot = []
                for axis in range(2):
                    bucket = idx_ref[axis, first + j : first + j + 1, :]
                    bucket = jnp.broadcast_to(bucket, (32, span)).astype(jnp.bfloat16)
                    hot.append(jnp.where(bucket == which, jnp.bfloat16(1), jnp.bfloat16(0)))
                tab = tab + dot(row_ref[g, lines, :], jnp.concatenate(hot, axis=0), NT)
            line = wide_ref[g, lines, :]
            if pad:
                line = jnp.concatenate([line, jnp.zeros((16, pad), jnp.float32)], axis=1)
            diag = diag + pltpu.roll(line, (wide - (first + j)) % wide, 1)
    tab_ref[...] += tab
    diag_ref[0] = diag


ANY = pl.BlockSpec(memory_space=pl.ANY)


def cost(flops, bytes_accessed, transcendentals):
    return pl.CostEstimate(flops=flops // 10, bytes_accessed=bytes_accessed // 10, transcendentals=transcendentals // 10)


def without(kernel, first, count):
    return lambda *refs: kernel(*refs[:first], *refs[first + count :])


def near_width(kind, ti, span):
    return span + ti if kind == "enc" else span


def diag_sums(kind, diag, starts):
    wide = diag.shape[2]
    column = lax.broadcasted_iota(jnp.int32, (len(starts), wide), 1)
    start = jnp.array(starts, jnp.int32)[:, None]
    if kind == "dec":
        bucket = one_sided(jnp.where(column > start, column - wide, column) - start)
    else:
        bucket = two_sided(jnp.where(column > wide - TI, column - wide, column) - start, 128)
    hot = (bucket[..., None] == lax.iota(jnp.int32, 32)).astype(jnp.float32)
    return jnp.einsum("swb,shw->bh", hot, diag, precision=lax.Precision.HIGHEST)


def attend_forward(kind, part, tq, lens, tables, coords, q_src, q_col, kv_srcs, k_col, v_col, pairs, quests, deps=()):
    heads = 2 * pairs
    key_rows = sum(kv_src.shape[0] for kv_src in kv_srcs)
    span = key_rows // quests if kind == "dec" else key_rows
    key_block = part if kind == "dec" else 0
    count = len(kv_srcs)
    flops = tq * span * (60000 if kind == "enc" else 25000)
    tab_n = tab_x = jnp.zeros((16, LANES), jnp.float32)
    tab_y = jnp.zeros((1, 8, LANES), jnp.float32)
    if kind != "cross":
        tab_n = jnp.pad(tables[0].T, ((0, 16 - heads), (0, LANES - 32)))
    if kind == "enc":
        tab_x = jnp.pad(tables[1].T, ((0, 16 - heads), (0, LANES - 32)))
        tab_y = jnp.broadcast_to(tables[2].T[:, :, None], (heads, 32, LANES))
    return pl.pallas_call(
        without(partial(fwd_kernel, kind, part, tq, span, heads), 7 + 2 * count, len(deps)),
        grid=(pairs,),
        in_specs=[
            pl.BlockSpec(memory_space=pltpu.SMEM),
            pl.BlockSpec(tab_n.shape, lambda h: (0, 0)),
            pl.BlockSpec(tab_x.shape, lambda h: (0, 0)),
            pl.BlockSpec(tab_y.shape, lambda h: (0, 0, 0)),
            pl.BlockSpec(coords.shape, lambda h: (0, 0)),
            pl.BlockSpec((tq, 2), lambda h: (part, 0)),
            pl.BlockSpec((tq, LANES), lambda h: (part, q_col * pairs + h)),
        ]
        + [pl.BlockSpec((span // count, LANES), lambda h: (key_block, k_col * pairs + h))] * count
        + [pl.BlockSpec((span // count, LANES), lambda h: (key_block, v_col * pairs + h))] * count
        + [ANY] * len(deps),
        out_specs=[
            pl.BlockSpec((tq, LANES), lambda h: (0, h)),
            pl.BlockSpec((2, tq, span), lambda h: (h, 0, 0)),
        ],
        out_shape=[
            jax.ShapeDtypeStruct((tq, pairs * LANES), jnp.bfloat16),
            jax.ShapeDtypeStruct((heads, tq, key_rows), jnp.bfloat16),
        ],
        scratch_shapes=[
            pltpu.VMEM((2, tq, span), jnp.float32),
            pltpu.VMEM((2, tq, span) if kind == "enc" else (1, 8, LANES), jnp.int32),
            pltpu.VMEM((8, span), jnp.float32),
            pltpu.VMEM((1, 8, LANES) if kind == "cross" else (heads, LANES, 5 * LANES), jnp.float32),
            pltpu.VMEM((heads, tq, span) if kind == "enc" else (1, 8, LANES), jnp.float32),
        ],
        compiler_params=pltpu.CompilerParams(vmem_limit_bytes=VMEM_LIMIT),
        cost_estimate=cost(
            flops=flops, bytes_accessed=4 * tq * span * pairs, transcendentals=2 * tq * span * pairs
        ),
        name="attend_forward_" + kind,
    )(lens, tab_n, tab_x, tab_y, coords, coords.T, q_src, *kv_srcs, *kv_srcs, *deps)


def attend_backward(kind, part, prob, grad_out, out, q_src, q_col, kv_src, k_col, v_col, pairs, quests, carry=(), deps=()):
    rows = grad_out.shape[0]
    key_rows = 2 * kv_src.shape[0] if kind == "cross" else kv_src.shape[0]
    width = pairs * LANES
    span = key_rows if kind == "enc" else key_rows // 2
    key_block = part if kind == "dec" else 0
    query_block = 0 if kind == "cross" else part
    score_block = part if kind == "cross" else 0
    if kind == "cross":
        carried = [pl.BlockSpec((rows, LANES), lambda h: (0, h))] + [pl.BlockSpec(memory_space=pl.ANY)] * 2
        key_out = pl.BlockSpec((span, LANES), lambda h: (part, h))
        aliases = {7: 1, 8: 2} if part else {}
    else:
        carried = [pl.BlockSpec((key_rows, LANES), lambda h: (0, h))] * 2
        key_out = pl.BlockSpec((key_rows, LANES), lambda h: (0, h))
        aliases = {}
    query_type = jnp.float32 if kind == "cross" and not part else jnp.bfloat16
    key_type = jnp.bfloat16 if kind == "cross" or part else jnp.float32
    low_block = pl.BlockSpec((2, rows, span), (lambda h: (0, 0, 0)) if kind == "cross" else (lambda h: (h, 0, 0)))
    low_shape = (2, rows, span) if kind == "cross" else (2 * pairs, rows, key_rows)
    return pl.pallas_call(
        without(partial(bwd_kernel, kind, part, rows, span), 6 + len(carry), len(deps)),
        grid=(pairs,),
        in_specs=[
            pl.BlockSpec((2, rows, span), lambda h: (h, 0, score_block)),
            pl.BlockSpec((rows, LANES), lambda h: (0, h)),
            pl.BlockSpec((rows, LANES), lambda h: (0, h)),
            pl.BlockSpec((rows, LANES), lambda h: (query_block, q_col * pairs + h)),
            pl.BlockSpec((span, LANES), lambda h: (key_block, k_col * pairs + h)),
            pl.BlockSpec((span, LANES), lambda h: (key_block, v_col * pairs + h)),
        ]
        + carried[: len(carry)]
        + [ANY] * len(deps),
        out_specs=[
            pl.BlockSpec((rows, LANES), lambda h: (0, h)),
            key_out,
            key_out,
            low_block,
        ],
        out_shape=[
            jax.ShapeDtypeStruct((rows, width), query_type),
            jax.ShapeDtypeStruct((key_rows, width), key_type),
            jax.ShapeDtypeStruct((key_rows, width), key_type),
            jax.ShapeDtypeStruct(low_shape, jnp.bfloat16),
        ],
        scratch_shapes=[pltpu.VMEM((2, rows, span), jnp.float32)],
        input_output_aliases=aliases,
        compiler_params=pltpu.CompilerParams(vmem_limit_bytes=VMEM_LIMIT),
        cost_estimate=cost(
            flops=rows * span * 28000, bytes_accessed=4 * rows * span * pairs, transcendentals=0
        ),
        name="attend_backward_" + kind,
    )(prob, grad_out, out, q_src, kv_src, kv_src, *carry, *deps)


def table_sums(kind, part, offset, rows, coords, low, quests, deps=()):
    heads, half, key_rows = low.shape
    span = key_rows // quests if kind == "dec" else key_rows
    steps = rows // TI
    wide = near_width(kind, TI, span)
    first = (part * half + offset) // TI
    tab, diag = pl.pallas_call(
        without(partial(table_kernel, kind, TI, span, heads), 3, len(deps)),
        grid=(steps,),
        in_specs=[
            pl.BlockSpec((heads, TI, span), lambda i: (0, offset // TI + i, 0)),
            pl.BlockSpec(coords.shape, lambda i: (0, 0)),
            pl.BlockSpec((TI, 2), lambda i: (first + i, 0)),
        ]
        + [ANY] * len(deps),
        out_specs=[
            pl.BlockSpec((16, 64), lambda i: (0, 0)),
            pl.BlockSpec((1, 16, wide), lambda i: (i, 0, 0)),
        ],
        out_shape=[
            jax.ShapeDtypeStruct((16, 64), jnp.float32),
            jax.ShapeDtypeStruct((steps, 16, near_width("enc", TI, key_rows)), jnp.float32),
        ],
        scratch_shapes=[
            pltpu.VMEM((TI // 16, 256, span), jnp.bfloat16),
            pltpu.VMEM((TI // 16, 256, span), jnp.float32),
            pltpu.VMEM((2, TI, span) if kind == "enc" else (1, 8, LANES), jnp.float32),
        ],
        compiler_params=pltpu.CompilerParams(vmem_limit_bytes=VMEM_LIMIT),
        cost_estimate=cost(
            flops=rows * span * 40000, bytes_accessed=2 * heads * rows * span, transcendentals=0
        ),
        name="table_sums_" + kind,
    )(low, coords, coords.T, *deps)
    return tab, diag


def table_grads(kind, tabs, diags, rows, quests, heads):
    starts = list(range(0, rows, TI))
    diag = jnp.concatenate(diags, axis=0)
    if kind == "dec":
        span = rows // quests
        near = diag_sums(kind, diag[:, :, :span], [start % span for start in starts])[:, :heads]
        blank = jnp.zeros_like(near)
        return jnp.stack([blank, blank, blank, near])
    tab = sum(tabs)
    near = diag_sums(kind, diag, starts)[:, :heads]
    return jnp.stack([near, tab[:heads, :32].T, tab[:heads, 32:].T, jnp.zeros_like(near)])


def weight_copies(core, pieces, wi_ref, wd_ref, sems):
    in_own, in_far, in_near, down_own, down_far, down_near = pieces
    own = in_own.shape[1]
    block = own // 2
    rows_in, rows_down = in_far.shape[0], down_far.shape[0]
    far_in = pl.ds(pl.multiple_of(core * rows_in, rows_in), rows_in)
    near_in = pl.ds(pl.multiple_of((1 - core) * rows_in, rows_in), rows_in)
    far_down = pl.ds(pl.multiple_of(own + core * rows_down, rows_down), rows_down)
    near_down = pl.ds(pl.multiple_of(own + (1 - core) * rows_down, rows_down), rows_down)
    moves = []
    for b in range(2):
        part = slice(b * block, (b + 1) * block)
        moves.append((in_own.at[:, part], wi_ref.at[:, part]))
        moves.append((down_own.at[part, :], wd_ref.at[part, :]))
    other = slice(own, 2 * own)
    moves.append((in_far, wi_ref.at[far_in, other]))
    moves.append((in_near, wi_ref.at[near_in, other]))
    moves.append((down_far, wd_ref.at[far_down, :]))
    moves.append((down_near, wd_ref.at[near_down, :]))
    return [pltpu.make_async_copy(src, dst, sems.at[i]) for i, (src, dst) in enumerate(moves)]


def ffn_kernel(mode, part, flag_ref, *refs):
    pieces, refs = refs[:6], refs[6:]
    refs, (wi_ref, wd_ref, sems) = refs[:-3], refs[-3:]
    copies = weight_copies(flag_ref[0], pieces, wi_ref, wd_ref, sems)
    first_step = pl.program_id(0) == 0

    @pl.when(first_step)
    def _():
        for copy in copies:
            copy.start()
        for copy in copies:
            copy.wait()

    gain_ref, wa_ref = refs[:2]
    gain = gain_ref[0:1, :]
    if mode == "back":
        middle_ref, second_ref, own_ref, arrived_ref, more_ref, first_ref = refs[2:8]
        dx_ref, hn_ref, gl_ref, ml_ref, act_ref, dzo_ref, do_ref, dgain_ref, z_ref, du_ref = refs[-10:]
        on_encoder = flag_ref[2] == 0
        x = jnp.where(on_encoder, middle_ref[...], second_ref[...])
    else:
        base_ref, att_ref = refs[2:4]
        x = base_ref[...].astype(jnp.float32) + dot(att_ref[...], wa_ref[...])
        if mode == "fwd":
            out_ref, mid_ref, z_ref, u_ref = refs[4:]
        else:
            own_ref, arrived_ref, out_ref, mid_ref, dx_ref, low_ref, do_ref, z_ref, u_ref, du_ref, dz_ref = refs[4:]
        mid_ref[...] = x
    rows, width = x.shape
    hidden = wi_ref.shape[1]
    block, chunk = hidden // FFN_BLOCKS, 32
    if mode != "fwd":
        half = part if mode == "back" else lax.div(2 * pl.program_id(0), pl.num_programs(0))
        grad_low = jnp.where(half == flag_ref[1], own_ref[...], arrived_ref[...])
        grad = grad_low.astype(jnp.float32)
    scale = lax.rsqrt(jnp.mean(x * x, axis=1, keepdims=True) + EPSILON)
    normed_full = x * scale * gain
    normed = normed_full.astype(jnp.bfloat16)
    if mode == "back":
        grad = grad + more_ref[...].astype(jnp.float32)
        grad_low = grad.astype(jnp.bfloat16)
        hn_ref[...] = jnp.transpose(normed_full).astype(jnp.bfloat16)
        gl_ref[...] = jnp.transpose(grad).astype(jnp.bfloat16)
    total = jnp.zeros((rows, width), jnp.float32)
    back = jnp.zeros((rows, width), jnp.float32)
    for index in range(FFN_BLOCKS + 1):
        if index < FFN_BLOCKS:
            cols = slice(index * block, (index + 1) * block)
            z_ref[index % 2] = dot(normed, wi_ref[:, cols])
            if mode != "fwd":
                du_ref[index % 2] = dot(grad_low, wd_ref[cols, :], NT)
        if index == 0:
            continue
        slot = (index - 1) % 2
        cols = slice((index - 1) * block, index * block)
        for r in range(0, rows, chunk):
            lines = slice(r, r + chunk)
            z = z_ref[slot, lines, :]
            square = z * z
            tanh = jnp.tanh(z * (GELU_SCALE + GELU_SCALE * GELU_CUBE * square))
            half = 0.5 + 0.5 * tanh
            act = (z * half).astype(jnp.bfloat16)
            if mode == "back":
                act_ref[lines, cols] = act
            else:
                u_ref[slot, lines, :] = act
            if mode != "fwd":
                slope = half + z * (0.5 - 0.5 * tanh * tanh) * (GELU_SCALE + 3.0 * GELU_SCALE * GELU_CUBE * square)
                d_hidden = (du_ref[slot, lines, :] * slope).astype(jnp.bfloat16)
                if mode == "back":
                    dzo_ref[lines, cols] = d_hidden
                else:
                    dz_ref[slot, lines, :] = d_hidden
        if mode != "back":
            total = total + dot(u_ref[slot], wd_ref[cols, :])
        if mode == "back":
            back = back + dot(dzo_ref[:, cols], wi_ref[:, cols], NT)
        elif mode == "both":
            back = back + dot(dz_ref[slot], wi_ref[:, cols], NT)
    if mode != "back":
        out_ref[...] = (x + total).astype(jnp.bfloat16)
    if mode != "fwd":
        scaled = back * gain
        mean = jnp.mean(scaled * x, axis=1, keepdims=True)
        grad = grad + scale * scaled - x * (scale * scale * scale * mean)
        if mode == "back":
            grad = jnp.where(on_encoder, grad, first_ref[...])
            ml_ref[...] = jnp.transpose(grad).astype(jnp.bfloat16)
            gain_part = jnp.sum((back * x * scale).reshape(rows // 8, 8, width), axis=0)
            dgain_ref[...] = jnp.where(first_step, gain_part, dgain_ref[...] + gain_part)
        else:
            low_ref[...] = grad.astype(jnp.bfloat16)
        dx_ref[...] = grad
        do_ref[...] = dot(grad.astype(jnp.bfloat16), wa_ref[...], NT).astype(jnp.bfloat16)


def feed_forward(mode, part, rows, flags, pieces, gain, w_att, rows_in, held=(), deps=()):
    width = w_att.shape[0]
    hidden = 2 * pieces[0].shape[1]
    steps = rows // TR
    row_block = pl.BlockSpec((TR, width), lambda i: (i, 0))
    turned_block = pl.BlockSpec((width, TR), lambda i: (0, part * steps + i))
    hidden_block = pl.BlockSpec((TR, hidden), lambda i: (part * steps + i, 0))
    low = jax.ShapeDtypeStruct((rows, width), jnp.bfloat16)
    full = jax.ShapeDtypeStruct((rows, width), jnp.float32)
    turned = jax.ShapeDtypeStruct((width, 2 * rows), jnp.bfloat16)
    wide = jax.ShapeDtypeStruct((2 * rows, hidden), jnp.bfloat16)
    small = jax.ShapeDtypeStruct((8, width), jnp.float32)
    outs = {
        "fwd": ([row_block] * 2, [low, full]),
        "both": ([row_block] * 5, [low, full, full, low, low]),
        "back": (
            [row_block]
            + [turned_block] * 3
            + [hidden_block] * 2
            + [row_block, pl.BlockSpec((8, width), lambda i: (0, 0))],
            [full, turned, turned, turned, wide, wide, low, small],
        ),
    }[mode]
    slab = (2, TR, hidden // FFN_BLOCKS)
    slab32, slab16 = pltpu.VMEM(slab, jnp.float32), pltpu.VMEM(slab, jnp.bfloat16)
    scratch = {"fwd": [slab32, slab16], "both": [slab32, slab16, slab32, slab16], "back": [slab32, slab32]}[mode]
    matmuls = {"fwd": 2, "both": 4, "back": 3}[mode]
    inputs = 9 + len(rows_in)
    return pl.pallas_call(
        without(partial(ffn_kernel, mode, part), inputs, len(held) + len(deps)),
        grid=(steps,),
        in_specs=[pl.BlockSpec(memory_space=pltpu.SMEM)]
        + [ANY] * 6
        + [pl.BlockSpec((8, width), lambda i: (0, 0)), pl.BlockSpec(w_att.shape, lambda i: (0, 0))]
        + [pl.BlockSpec((TR, width), lambda i, at=at, turn=turn: (at + i % turn, 0)) for _, at, turn in rows_in]
        + [ANY] * (len(held) + len(deps)),
        out_specs=outs[0],
        out_shape=outs[1],
        scratch_shapes=scratch
        + [
            pltpu.VMEM((width, hidden), jnp.bfloat16),
            pltpu.VMEM((hidden, width), jnp.bfloat16),
            pltpu.SemaphoreType.DMA((8,)),
        ],
        input_output_aliases={inputs + index: 1 + index for index in range(len(held))},
        compiler_params=pltpu.CompilerParams(vmem_limit_bytes=VMEM_LIMIT),
        cost_estimate=cost(
            flops=4 * matmuls * rows * width * hidden,
            bytes_accessed=4 * width * hidden + 8 * rows * width,
            transcendentals=rows * hidden,
        ),
        name="feed_forward_" + mode,
    )(flags, *pieces, jnp.broadcast_to(gain[None], (8, width)), w_att, *(x for x, _, _ in rows_in), *held, *deps)


def product_kernel(left_of, parts_of, slices, which, core_ref, *refs):
    left_count, count = max(left_of) + 1, sum(parts_of)
    lefts, rights = refs[:left_count], refs[left_count : left_count + count]
    outs, held_ref = refs[left_count + count : -1], refs[-1]
    step = pl.program_id(0)
    rows, span = lefts[0].shape
    size = rows // slices
    half = rows // 2

    @pl.when(step == 0)
    def _():
        for index, left in enumerate(lefts):
            if len(outs) == 1:
                held_ref[index] = left[...]
                continue
            for first, core in ((0, 1 - core_ref[0]), (half, core_ref[0])):
                for part in range(slices // 2):
                    source = pl.ds(pl.multiple_of((2 * part + core) * size, 16), size)
                    held_ref[index, first + part * size : first + (part + 1) * size, :] = left[source, :]

    def product(index, lines):
        parts = rights[sum(parts_of[:index]) : sum(parts_of[: index + 1])]
        length = span // len(parts)
        return sum(
            dot(held_ref[left_of[index], lines, part * length : (part + 1) * length], right[...])
            for part, right in enumerate(parts)
        ).astype(jnp.bfloat16)

    for index in range(len(parts_of)):
        steps = [s for s, owner in enumerate(which) if owner == index]
        chosen = functools.reduce(lambda a, b: a | b, [step == s for s in steps])

        @pl.when(chosen)
        def _(index=index):
            if len(outs) == 1:
                outs[0][...] = product(index, slice(0, rows))
            else:
                outs[0][...] = product(index, slice(0, half))
                outs[1][...] = product(index, slice(half, rows))


def products(lefts, left_of, rights, block, slices, core, deps=()):
    rows, span = lefts[0].shape
    parts_of = [len(right) for right in rights]
    counts = [right[0].shape[1] // (2 * block) for right in rights]
    which, place = [], []
    for half in range(2):
        for index, number in enumerate(counts):
            for b in range(number):
                which.append(index)
                place.append(half * number + b)
    maps = []
    for index, right in enumerate(rights):
        held, column_of = 0, []
        for s, owner in enumerate(which):
            if owner == index:
                held = place[s]
            column_of.append(held)
        maps += [column_of] * len(right)
    steps = len(which)
    total = steps * block

    def right_map(column_of):
        def index_map(s):
            value = 0
            for position in range(steps):
                if column_of[position]:
                    value = value + jnp.where(s == position, column_of[position], 0)
            return (0, value)

        return index_map

    size = rows // slices
    apart = size % 16 == 0
    out_rows = rows // 2 if apart else rows
    out = jax.ShapeDtypeStruct((out_rows, total), jnp.bfloat16)
    flat = [part for right in rights for part in right]
    results = pl.pallas_call(
        without(
            partial(product_kernel, left_of, parts_of, slices, which), 1 + len(lefts) + len(flat), len(deps)
        ),
        grid=(steps,),
        in_specs=[pl.BlockSpec(memory_space=pltpu.SMEM)]
        + [pl.BlockSpec((rows, span), lambda s: (0, 0)) for _ in lefts]
        + [pl.BlockSpec((part.shape[0], block), right_map(column_of)) for part, column_of in zip(flat, maps)]
        + [ANY] * len(deps),
        out_specs=[pl.BlockSpec((out_rows, block), lambda s: (0, s))] * (2 if apart else 1),
        out_shape=[out] * (2 if apart else 1),
        scratch_shapes=[pltpu.VMEM((len(lefts), rows, span), jnp.bfloat16)],
        compiler_params=pltpu.CompilerParams(vmem_limit_bytes=VMEM_LIMIT),
        cost_estimate=cost(
            flops=2 * span * rows * total, bytes_accessed=2 * (span + rows) * total, transcendentals=0
        ),
        name="weight_products",
    )(core.reshape(1), *lefts, *flat, *deps)
    if apart:
        return results
    cut = results[0].reshape(slices // 2, 2, size, total)
    return pick(cut, 1 - core, 1).reshape(-1, total), pick(cut, core, 1).reshape(-1, total)


def split_kernel(flag_ref, send_total, send_arrived, keep_total, keep_arrived, send_ref, keep_ref):
    send_ref[...] = (send_total[...].astype(jnp.float32) + send_arrived[...].astype(jnp.float32)).astype(jnp.bfloat16)
    keep = keep_total[...].astype(jnp.float32) + keep_arrived[...].astype(jnp.float32)
    keep_ref[...] = jnp.where(flag_ref[1] == 1, 0.0, keep)


def split_sum(total, arrived, size, mark, by_columns, blank):
    rows, width = total.shape
    if by_columns:
        half = width // 2
        send_block = pl.BlockSpec((size, half), lambda i, flag: (i, 1))
        keep_block = pl.BlockSpec((size, half), lambda i, flag: (i, 0))
        out_rows = rows
    else:
        half = width
        send_block = pl.BlockSpec((size, half), lambda i, flag: (2 * i + 1 - flag[0], 0))
        keep_block = pl.BlockSpec((size, half), lambda i, flag: (2 * i + flag[0], 0))
        out_rows = rows // 2
    out_block = pl.BlockSpec((size, half), lambda i, flag: (i, 0))
    return pl.pallas_call(
        split_kernel,
        grid_spec=pltpu.PrefetchScalarGridSpec(
            num_scalar_prefetch=1,
            grid=(out_rows // size,),
            in_specs=[send_block, send_block, keep_block, keep_block],
            out_specs=[out_block, out_block],
        ),
        out_shape=[
            jax.ShapeDtypeStruct((out_rows, half), jnp.bfloat16),
            jax.ShapeDtypeStruct((out_rows, half), jnp.float32),
        ],
        compiler_params=pltpu.CompilerParams(vmem_limit_bytes=VMEM_LIMIT),
        cost_estimate=cost(2 * rows * width, 8 * rows * width, 0),
        name="split_sum",
    )(jnp.stack([mark, blank]).astype(jnp.int32), total, arrived, total, arrived)


def nothing(shapes):
    return pl.pallas_call(
        lambda *refs: None, out_shape=shapes, out_specs=[ANY] * len(shapes), name="nothing"
    )()


def input_kernel(gain_ref, w_ref, x_ref, first_ref, second_ref, dk_ref, dv_ref, grad_ref, out_ref, dgain_ref):
    step = pl.program_id(0)
    gain = gain_ref[0:1, :]
    rows, width = x_ref.shape
    d_query = jnp.where(2 * step < pl.num_programs(0), first_ref[...], second_ref[...])
    back = dot(d_query, w_ref[:, :width], NT)
    back = back + dot(dk_ref[...], w_ref[:, width : 2 * width], NT)
    back = back + dot(dv_ref[...], w_ref[:, 2 * width :], NT)
    x = x_ref[...].astype(jnp.float32)
    scale = lax.rsqrt(jnp.mean(x * x, axis=1, keepdims=True) + EPSILON)
    scaled = back * gain
    mean = jnp.mean(scaled * x, axis=1, keepdims=True)
    out_ref[...] = grad_ref[...] + scale * scaled - x * (scale * scale * scale * mean)
    gain_part = jnp.sum((back * x * scale).reshape(rows // 8, 8, width), axis=0)
    dgain_ref[...] = jnp.where(step == 0, gain_part, dgain_ref[...] + gain_part)


def input_gradient(x, gain, w_qkv, query_grads, key_grad, value_grad, grad, deps):
    rows, width = x.shape
    steps = rows // TR
    row_block = pl.BlockSpec((TR, width), lambda i: (i, 0))
    half_block = pl.BlockSpec((TR, width), lambda i: (i % (steps // 2), 0))
    fixed = pl.BlockSpec((8, width), lambda i: (0, 0))
    out, dgain = pl.pallas_call(
        without(input_kernel, 8, len(deps)),
        grid=(steps,),
        in_specs=[fixed, pl.BlockSpec(w_qkv.shape, lambda i: (0, 0)), row_block, half_block, half_block]
        + [row_block] * 3
        + [ANY] * len(deps),
        out_specs=[row_block, fixed],
        out_shape=[jax.ShapeDtypeStruct((rows, width), jnp.float32), jax.ShapeDtypeStruct((8, width), jnp.float32)],
        compiler_params=pltpu.CompilerParams(vmem_limit_bytes=VMEM_LIMIT),
        cost_estimate=cost(
            flops=6 * rows * width * width, bytes_accessed=16 * rows * width, transcendentals=0
        ),
        name="input_gradient",
    )(jnp.broadcast_to(gain[None], (8, width)), w_qkv, x, *query_grads, key_grad, value_grad, grad, *deps)
    return out, jnp.sum(dgain, axis=0)


def sum_kernel(rounds, x_ref, out_ref, *refs):
    slots, send_sems, recv_sems = refs[: len(rounds)], refs[len(rounds)], refs[len(rounds) + 1]
    barrier = pltpu.get_barrier_semaphore()
    places, peers = [], []
    for axes in rounds:
        place, count = 0, 1
        for axis in axes:
            place = place * lax.axis_size(axis) + lax.axis_index(axis)
            count = count * lax.axis_size(axis)
        found = []
        for step in range(1, count):
            rest, device = lax.rem(place + step, count), {}
            for axis in reversed(axes):
                device[axis] = lax.rem(rest, lax.axis_size(axis))
                rest = lax.div(rest, lax.axis_size(axis))
            found.append(device)
        places.append(place)
        peers.append(found)
    for device in peers[0] + peers[1]:
        pl.semaphore_signal(barrier, inc=1, device_id=device, device_id_type=pl.DeviceIdType.MESH)
    pl.semaphore_wait(barrier, len(peers[0]) + len(peers[1]))
    value = x_ref[...]
    first = 0
    for slot, place, found in zip(slots, places, peers):
        slot[place] = value
        copies = []
        for step, device in enumerate(found):
            copies.append(
                pltpu.make_async_remote_copy(
                    src_ref=slot.at[place],
                    dst_ref=slot.at[place],
                    send_sem=send_sems.at[first + step],
                    recv_sem=recv_sems.at[first + step],
                    device_id=device,
                    device_id_type=pl.DeviceIdType.MESH,
                )
            )
        for copy in copies:
            copy.start()
        for copy in copies:
            copy.wait()
        first += len(found)
        value = slot[0]
        for index in range(1, len(found) + 1):
            value = value + slot[index]
    out_ref[...] = value


def sum_everywhere(x):
    rounds = (("dp",), ("section", "mp"))
    counts = [math.prod(lax.axis_size(axis) for axis in axes) for axes in rounds]
    copies = sum(counts) - len(counts)
    return pl.pallas_call(
        partial(sum_kernel, rounds),
        out_shape=jax.ShapeDtypeStruct(x.shape, x.dtype),
        in_specs=[pl.BlockSpec(memory_space=pltpu.VMEM)],
        out_specs=pl.BlockSpec(memory_space=pltpu.VMEM),
        scratch_shapes=[pltpu.VMEM((count,) + x.shape, x.dtype) for count in counts]
        + [pltpu.SemaphoreType.DMA((copies,)), pltpu.SemaphoreType.DMA((copies,))],
        compiler_params=pltpu.CompilerParams(collective_id=0, has_side_effects=True),
        name="sum_everywhere",
    )(x)


def pair_permute(x, axis, bit):
    pairs = [(i, i ^ (1 << bit)) for i in range(lax.axis_size(axis))]
    return lax.ppermute(x, axis, pairs)


def shifted(x, axis, by):
    peers = lax.axis_size(axis)
    pairs = [(i, i + by) for i in range(peers) if 0 <= i + by < peers]
    return lax.ppermute(x, axis, pairs)


def in_order(flag, first, second, axis):
    return jnp.where(
        flag == 0,
        jnp.concatenate([first, second], axis=axis),
        jnp.concatenate([second, first], axis=axis),
    )


def pick(x, index, axis):
    return lax.dynamic_index_in_dim(x, index, axis, False)


def after(values, *others):
    return lax.optimization_barrier((values, others))[0]


def exchange_rows(block, where_mp):
    return pick(block, where_mp, 0), pair_permute(pick(block, 1 - where_mp, 0), "mp", 0)


def scatter_rows(rows, where_mp):
    half = rows.shape[0] // 2
    send = lax.dynamic_slice_in_dim(rows, (1 - where_mp) * half, half, 0).astype(jnp.bfloat16)
    return lax.dynamic_slice_in_dim(rows, where_mp * half, half, 0), pair_permute(send, "mp", 0)


def core_half(shard, core):
    half = shard.shape[0] // 2
    return lax.dynamic_slice_in_dim(shard, core * half, half, 0)


def fetch_far(shard, core):
    return pair_permute(core_half(shard, core), "mp", 0)


def fetch_near(far):
    return pair_permute(far, "dp", 0)


def fetch_other(shard, dp_index):
    quarter = shard.shape[0] // 4
    far = pair_permute(lax.dynamic_slice_in_dim(shard, (dp_index & 3) * quarter, quarter, 0), "mp", 0)
    half = in_order(dp_index & 1, far, pair_permute(far, "dp", 0), 0)
    return in_order((dp_index >> 1) & 1, half, pair_permute(half, "dp", 1), 0), far


class Reduction:
    def __init__(self, send, keep, dp_index, section=None):
        self.total, self.arrived = keep, pair_permute(send, "dp", 0)
        self.dp_index = dp_index
        bits = lax.axis_size("dp").bit_length() - 1
        self.left = ([("section", section)] if section is not None else []) + [("mp", None)]
        self.left += [("dp", bit) for bit in range(1, bits)]

    def joined(self, cut):
        return cut(self.total).astype(jnp.float32) + cut(self.arrived).astype(jnp.float32)

    def hop(self, *ties):
        brought = self.arrived
        self.arrived = after(self.arrived, *ties)
        axis, which = self.left.pop(0)
        rows, width = self.total.shape
        parts = lax.axis_size("dp")
        never, kept = jnp.int32(0), jnp.int32(1)
        if axis == "section":
            size = rows // 2
            send, self.total = split_sum(self.total, self.arrived, size, kept, False, (which == 0).astype(jnp.int32))
            self.arrived = shifted(send, "section", -1)
        elif axis == "mp":
            send, self.total = split_sum(self.total, self.arrived, rows // 4, never, True, never)
            self.arrived = pair_permute(send, "mp", 0)
        else:
            mark = (self.dp_index >> which) & 1
            halves = (parts >> (which + 1), 2, -1, width)
            size = rows // (2 * halves[0])
            if size % 16 == 0:
                send, self.total = split_sum(self.total, self.arrived, size, mark, False, never)
            else:
                send = self.joined(lambda x: pick(x.reshape(halves), 1 - mark, 1)).astype(jnp.bfloat16)
                send = send.reshape(-1, width)
                self.total = self.joined(lambda x: pick(x.reshape(halves), mark, 1)).reshape(-1, width)
            self.arrived = pair_permute(send, "dp", which)
        return brought

    def finish(self, *ties):
        while self.left:
            self.hop()
        self.arrived = after(self.arrived, *ties)
        return self.joined(lambda x: x)


def rms_norm(inputs, gain_row):
    return (
        inputs * lax.rsqrt(jnp.mean(inputs * inputs, axis=-1, keepdims=True) + EPSILON) * gain_row
    )


def norm_back(rows, gain_row, grad_normed):
    return jax.vjp(rms_norm, rows, gain_row)[1](grad_normed)


def low(x):
    return x.astype(jnp.bfloat16)


def local(
    block_input,
    out_cotangent,
    doc_lengths,
    question_lengths,
    coordinates,
    gains,
    bias_tables,
    self_qkv,
    self_out,
    ffn_in,
    ffn_out,
    cross_q,
    cross_kv,
    cross_out,
):
    section = lax.axis_index("section")
    on_encoder = section == 0
    dp_index = lax.axis_index("dp")
    core = dp_index & 1
    where_mp = lax.axis_index("mp")
    width = block_input.shape[4]
    quests = question_lengths.shape[2]
    own = self_qkv.shape[3]
    pairs = 2 * own // LANES
    heads = 2 * pairs
    parts = lax.axis_size("dp")
    flags = jnp.stack([core, where_mp, section]).astype(jnp.int32)

    rows_low = in_order(where_mp, *exchange_rows(block_input[0, :, 0], where_mp), 0)
    qkv_own = self_qkv[0].reshape(width, -1)
    qkv_other, qkv_far = fetch_other(qkv_own, dp_index)
    w_qkv = jnp.concatenate(
        [x[:, t * own : (t + 1) * own] for t in range(3) for x in (qkv_own, qkv_other)], axis=1
    )
    owned = after((ffn_in[0], ffn_out[0], self_out[0]), rows_low, qkv_far)
    fars = [fetch_far(x, core) for x in owned]
    cross_pieces = [
        core_half(jnp.concatenate([cross_q, cross_kv.reshape(width, -1)], axis=1), core),
        core_half(cross_out, core),
        pick(out_cotangent[0, :, 0], 1 - where_mp, 0),
    ]

    lens = jnp.concatenate(
        [pick(doc_lengths, where_mp, 0), pick(question_lengths, where_mp, 0)[0]]
    ).astype(jnp.int32)
    coords = pick(coordinates, where_mp, 0)[0]
    tables = jnp.where(where_mp == 0, bias_tables, jnp.roll(bias_tables, heads // 2, axis=2))

    rows = rows_low.astype(jnp.float32)
    span = rows.shape[0]
    half = span // 2
    turn = half // TR
    halves = (slice(0, half), slice(half, span))
    gain_self = jnp.where(on_encoder, gains[0], gains[2])
    normed_self = low(rms_norm(rows, gain_self))
    projected = low(dot(normed_self, w_qkv))
    merged, probs, middles, memories, arrivals = [], [], [], [], []
    for part in range(2):
        deps = memories[:1] if part else cross_pieces

        def forward(kind, chosen):
            return attend_forward(
                kind, part, half, lens, chosen, coords, projected, 0, [projected], 1, 2, pairs, quests, deps
            )

        out, prob = lax.cond(on_encoder, lambda: forward("enc", tables[:3]), lambda: forward("dec", tables[3:]))
        if not part:
            fars = after(fars, out)
            nears = [fetch_near(x) for x in fars]
            w_out = jnp.concatenate([self_out[0], in_order(core, fars[2], nears[2], 0)], axis=0)
            pieces = (ffn_in[0], fars[0], nears[0], ffn_out[0], fars[1], nears[1])
            cross_pieces = after(cross_pieces, fars)
            cross_fars = [pair_permute(x, "mp", 0) for x in cross_pieces[:2]]
            cot = (pick(out_cotangent[0, :, 0], where_mp, 0), pair_permute(cross_pieces[2], "mp", 0))
        else:
            cross_fars = after(cross_fars, out)
        memory, middle = feed_forward(
            "fwd", part, half, flags, pieces, gains[1], w_out, [(rows_low, part * turn, turn), (out, 0, turn)]
        )
        arrivals.append(shifted(memory, "section", 1))
        merged.append(out)
        probs.append(prob)
        middles.append(middle)
        memories.append(memory)
    query_other, cross_other = (in_order(core, far, fetch_near(far), 0) for far in cross_fars)
    w_query = jnp.concatenate([cross_q, query_other[:, :own]], axis=1)
    w_pair = jnp.concatenate(
        [x for t in range(2) for x in (cross_kv[:, t], query_other[:, (t + 1) * own : (t + 2) * own])], axis=1
    )
    w_cross = jnp.concatenate([cross_out, cross_other], axis=0)
    middle = jnp.concatenate(middles, axis=0)

    normed_cross = low(rms_norm(middle, gains[3]))
    queries = low(dot(normed_cross, w_query))
    first_pair = low(dot(arrivals[0], w_pair))
    arrivals[1] = after(arrivals[1], queries, first_pair)
    pair_rows = [first_pair, low(dot(arrivals[1], w_pair))]
    cross_merged, cross_prob = attend_forward(
        "cross", 0, span, lens, None, coords, queries, 0, pair_rows, 0, 1, pairs, quests
    )
    output_low, second, grad_second, second_low, cross_grad = feed_forward(
        "both",
        0,
        span,
        flags,
        pieces,
        gains[4],
        w_cross,
        [(middle, 0, 2 * turn), (cross_merged, 0, 2 * turn), (cot[0], 0, turn), (cot[1], 0, turn)],
    )
    output_own, output_arrived = scatter_rows(
        jnp.where(on_encoder, jnp.concatenate(memories, axis=0), output_low), where_mp
    )
    returns, returned, carry = [], [], ()
    for part in range(2):
        query_grad, key_grad, value_grad, _ = attend_backward(
            "cross",
            part,
            cross_prob,
            cross_grad,
            cross_merged,
            queries,
            0,
            pair_rows[part],
            0,
            1,
            pairs,
            quests,
            carry,
            [returns[0], output_arrived] if part else [],
        )
        carry = (query_grad, key_grad, value_grad)
        returns.append(
            low(
                dot(key_grad[halves[part]], w_pair[:, : 2 * own], NT)
                + dot(value_grad[halves[part]], w_pair[:, 2 * own :], NT)
            )
        )
        returned.append(shifted(returns[part], "section", -1))
    query_cross = after(query_grad, returns[1])

    def cross_norm():
        input_part, gain_part = norm_back(middle, gains[3], dot(query_cross, w_query, NT))
        return grad_second + input_part, gain_part

    def no_norm():
        return tuple(
            nothing([jax.ShapeDtypeStruct((span, width), jnp.float32), jax.ShapeDtypeStruct((width,), jnp.float32)])
        )

    grad_first, gain_cross = lax.cond(on_encoder, no_norm, cross_norm)

    gain_ffn = jnp.where(on_encoder, gains[1], gains[4])
    held, gain_ffn_grad, grads_middle, merged_grads = [], 0.0, [], []
    for part in range(2):
        if part:
            returned[1] = after(returned[1], grads_middle[0])
        grad_middle, *held, merged_grad, gain_part = feed_forward(
            "back",
            part,
            half,
            flags,
            pieces,
            gain_ffn,
            w_out,
            [
                (middles[part], 0, turn),
                (second, part * turn, turn),
                (cot[0], 0, turn),
                (cot[1], 0, turn),
                (returned[part], 0, turn),
                (grad_first, part * turn, turn),
            ],
            held,
        )
        gain_ffn_grad = gain_ffn_grad + jnp.sum(gain_part, axis=0)
        grads_middle.append(grad_middle)
        merged_grads.append(merged_grad)
    hn_turned, gl_turned, ml_turned, activated, hidden_grad = held
    in_send, in_keep = products([hn_turned], [0], [[hidden_grad]], 2 * own, parts, core)
    down_send, down_keep = products([gl_turned], [0], [[activated]], 2 * own, parts, core, [in_send])
    in_steps = Reduction(in_send, in_keep, dp_index)
    down_steps = Reduction(down_send, down_keep, dp_index)

    def cross_products():
        return tuple(
            products(
                [normed_cross.T, jnp.concatenate(arrivals, axis=0).T, second_low.T],
                [0, 1, 1, 2],
                [[query_cross], [key_grad], [value_grad], [cross_merged]],
                own,
                2 * parts,
                core,
                [down_send],
            )
        )

    def no_products():
        blank = jax.ShapeDtypeStruct((width // 2, 8 * own), jnp.bfloat16)
        return tuple(nothing([blank, blank]))

    cross_send, cross_keep = lax.cond(on_encoder, no_products, cross_products)
    cross_steps = Reduction(cross_send, cross_keep, dp_index, section)
    scores, query_grads, carry = [], [], ()
    for part in range(2):
        if part:
            deps = (in_steps.hop(), down_steps.arrived, cross_steps.hop())
        else:
            deps = (down_send, cross_send, in_steps.hop())

        def backward(kind):
            return attend_backward(
                kind, part, probs[part], merged_grads[part], merged[part], projected, 0, projected, 1, 2, pairs, quests,
                carry, deps
            )

        query_grad, key_grad, value_grad, score = lax.cond(
            on_encoder, lambda: backward("enc"), lambda: backward("dec")
        )
        carry = (key_grad, value_grad)
        query_grads.append(query_grad)
        scores.append(score)
    self_send, self_keep = products(
        [normed_self.T, ml_turned],
        [0, 0, 0, 1],
        [query_grads, [key_grad], [value_grad], merged],
        own,
        parts,
        core,
    )
    down_steps.hop(scores[1])
    self_steps = Reduction(self_send, self_keep, dp_index)
    input_grad, gain_self_grad = input_gradient(
        rows_low,
        gain_self,
        w_qkv,
        query_grads,
        key_grad,
        value_grad,
        jnp.concatenate(grads_middle, axis=0),
        [self_send],
    )
    grad_own, grad_arrived = scatter_rows(input_grad, where_mp)

    tabs, diags = [], []
    deps = (self_send, input_grad, in_steps.hop(scores[1]), cross_steps.hop(self_send))
    quarter = half // 2
    slots = [(0, 0, quarter), (0, quarter, quarter), (1, 0, quarter), (1, quarter, quarter)]
    for part, offset, count in slots:
        tab, diag = lax.cond(
            on_encoder,
            lambda: table_sums("enc", part, offset, count, coords, scores[part], quests, deps),
            lambda: table_sums("dec", part, offset, count, coords, scores[part], quests, deps),
        )
        tabs.append(tab)
        diags.append(diag)
        if len(tabs) == 1:
            deps = (tab, self_steps.hop(tab), down_steps.hop(tab))
        elif len(tabs) == 2:
            deps = (tab, cross_steps.hop(tab), grad_arrived, in_steps.arrived)
        elif len(tabs) == 3:
            deps = (tab, self_steps.hop(tab), cross_steps.hop(tab), down_steps.hop(tab))
    table_grad = lax.cond(
        on_encoder,
        lambda: table_grads("enc", tabs, diags, span, quests, heads),
        lambda: table_grads("dec", tabs, diags, span, quests, heads),
    )
    table_grad = jnp.where(where_mp == 0, table_grad, jnp.roll(table_grad, heads // 2, axis=2))
    blank = jnp.zeros((width,), jnp.float32)
    gain_grad = jnp.where(
        on_encoder,
        jnp.stack([gain_self_grad, gain_ffn_grad, blank, blank, blank]),
        jnp.stack([blank, blank, gain_self_grad, gain_cross, gain_ffn_grad]),
    )
    small = jnp.concatenate([gain_grad.reshape(-1, LANES), table_grad.reshape(-1, LANES)], axis=0)
    count = small.shape[0]
    small = jnp.pad(small, ((0, -count % 8), (0, 0)))
    cross_shard, in_shard, down_shard = (x.finish(tabs[3]) for x in (cross_steps, in_steps, down_steps))
    small = sum_everywhere(after(small, self_steps.hop(tab), down_steps.arrived))
    gain_count = gain_grad.size // LANES
    gain_sum = small[:gain_count].reshape(gain_grad.shape)
    table_sum = small[gain_count:count].reshape(table_grad.shape)
    self_shard = self_steps.finish(table_grad)
    output_rows, grad_rows = (
        in_order(where_mp, own_rows[None], after(arrived, tabs[2]).astype(own_rows.dtype)[None], 0)
        for own_rows, arrived in ((output_own, output_arrived), (grad_own, grad_arrived))
    )
    return (
        output_rows[None, :, None],
        grad_rows[None, :, None],
        gain_sum[:4],
        gain_sum[4],
        table_sum,
        self_shard[:, : 3 * own].reshape(-1, 3, own)[None],
        self_shard[:, 3 * own :].T[None],
        in_shard[None],
        down_shard.T[None],
        cross_shard[:, :own],
        cross_shard[:, own : 3 * own].reshape(-1, 2, own),
        cross_shard[:, 3 * own :].T,
    )


def solution(mesh):
    return jax.shard_map(
        local,
        mesh=mesh,
        in_specs=(
            P("section", None, "dp", "mp", None),
            P("section", None, "dp", "mp", None),
            P(None, "dp"),
            P(None, "dp", None),
            P(None, "dp", None, None),
            P(),
            P(),
            P("section", None, None, "mp"),
            P("section", "mp", None),
            P("section", None, "mp"),
            P("section", "mp", None),
            P(None, "mp"),
            P(None, None, "mp"),
            P("mp", None),
        ),
        out_specs=(
            P("section", None, "dp", "mp", None),
            P("section", None, "dp", "mp", None),
            P(),
            P(),
            P(),
            P("section", "dp", None, "mp"),
            P("section", "mp", "dp"),
            P("section", "dp", "mp"),
            P("section", "mp", "dp"),
            P(("section", "dp"), "mp"),
            P(("section", "dp"), None, "mp"),
            P("mp", ("section", "dp")),
        ),
        check_vma=False,
    )
```

```python
import functools
from functools import partial
import math

import jax
import jax.numpy as jnp
from jax import lax
from jax.experimental import pallas as pl
from jax.experimental.pallas import tpu as pltpu
from jax.sharding import PartitionSpec as P

HEAD = 64
LANES = 128
NEGATIVE = -1e30
EPSILON = 1e-06
GELU_SCALE = math.sqrt(2 / math.pi)
GELU_CUBE = 0.044715
TI = 64
FFN_BLOCKS = 4
TR = 256
VMEM_LIMIT = 34 * 1024 * 1024
NT = (((1,), (1,)), ((), ()))
NN = (((1,), (0,)), ((), ()))


def edge_list(exact_span, bucket_count, far_reach):
    log_edges = [
        int(
            math.ceil(
                exact_span * (far_reach / exact_span) ** (power_index / (bucket_count - exact_span))
            )
        )
        for power_index in range(1, bucket_count - exact_span)
    ]
    return list(range(1, exact_span + 1)) + log_edges


def magnitude(distance, exact_span, bucket_count, far_reach):
    bucket = jnp.minimum(distance, exact_span)
    for threshold in edge_list(exact_span, bucket_count, far_reach)[exact_span:]:
        bucket = bucket + (distance >= threshold).astype(jnp.int32)
    return bucket


def two_sided(relative, far_reach):
    return magnitude(jnp.abs(relative), 8, 16, far_reach) + jnp.where(relative > 0, 16, 0)


def one_sided(relative):
    return magnitude(jnp.maximum(-relative, 0), 16, 32, 128)


def half_lanes(block, head):
    lane = lax.broadcasted_iota(jnp.int32, block.shape, 1)
    keep = lane < HEAD if head == 0 else lane >= HEAD
    return jnp.where(keep, block, jnp.zeros_like(block))


def dot(a, b, dims=NN):
    return lax.dot_general(a, b, dims, preferred_element_type=jnp.float32)


def pick_lanes(row, index):
    return jnp.take_along_axis(jnp.broadcast_to(row, index.shape), index, axis=1)


def pick_sublanes(table_ref, head, low, odd, upper):
    parts = [
        jnp.take_along_axis(table_ref[head, 8 * part : 8 * part + 8, :], low, axis=0)
        for part in range(4)
    ]
    return jnp.where(upper, jnp.where(odd, parts[3], parts[2]), jnp.where(odd, parts[1], parts[0]))


def fwd_kernel(kind, part, tq, span, heads, len_ref, tabn_ref, tabx_ref, taby_ref, crow_ref, ccol_ref, q_ref, *refs):
    count = (len(refs) - 7) // 2
    k_refs, v_refs = refs[:count], refs[count : 2 * count]
    o_ref, p_ref, s_ref, idx_ref, mask_ref, near_ref, bias_ref = refs[-7:]
    length = span // count
    pair = pl.program_id(0)
    first_block = 0 if kind == "dec" else part * tq // LANES
    chunk = 32

    @pl.when(pair == 0)
    def _():
        key = lax.broadcasted_iota(jnp.int32, (8, span), 1)
        limit = len_ref[1 + part] if kind == "dec" else len_ref[0]
        mask_ref[...] = jnp.where(key < limit, 0.0, NEGATIVE)
        if kind != "cross":
            def near_rows(r, carry):
                rows = pl.ds(pl.multiple_of(r * 8, 8), 8)
                query = r * 8 + lax.broadcasted_iota(jnp.int32, (8, LANES), 0)
                for d in range(-2, 3):
                    key = d * LANES + lax.broadcasted_iota(jnp.int32, (8, LANES), 1)
                    bucket = one_sided(key - query) if kind == "dec" else two_sided(key - query, 128)
                    for head in range(heads):
                        value = pick_lanes(tabn_ref[head : head + 1, :], bucket)
                        if kind == "dec":
                            value = jnp.where(key <= query, value, NEGATIVE)
                        near_ref[head, rows, (d + 2) * LANES : (d + 3) * LANES] = value
                return carry

            lax.fori_loop(0, LANES // 8, near_rows, 0)
        if kind == "enc":

            def bucket_rows(r, carry):
                rows = pl.ds(pl.multiple_of(r * chunk, chunk), chunk)
                for axis in range(2):
                    far = crow_ref[axis : axis + 1, :] - ccol_ref[rows, axis : axis + 1]
                    idx_ref[axis, rows, :] = two_sided(far, 500)
                return carry

            lax.fori_loop(0, tq // chunk, bucket_rows, 0)

            def bias_rows(r, carry):
                rows = pl.ds(pl.multiple_of(r * 8, 8), 8)
                for c in range(0, span, LANES):
                    lanes = slice(c, c + LANES)
                    across = idx_ref[0, rows, lanes]
                    upward = idx_ref[1, rows, lanes]
                    low, odd, upper = upward & 7, (upward & 8) != 0, upward >= 16
                    for head in range(heads):
                        bias_ref[head, rows, lanes] = pick_lanes(
                            tabx_ref[head : head + 1, :], across
                        ) + pick_sublanes(taby_ref, head, low, odd, upper)
                return carry

            lax.fori_loop(0, tq // 8, bias_rows, 0, unroll=4)

    for head in range(2):
        query = half_lanes(q_ref[...], head)
        for index, k_ref in enumerate(k_refs):
            s_ref[head, :, index * length : (index + 1) * length] = dot(query, k_ref[...], NT)
        for r in range(0, tq, chunk):
            rows = slice(r, r + chunk)
            pieces = []
            for c in range(0, span, LANES):
                lanes = slice(c, c + LANES)
                piece = s_ref[head, rows, lanes] + mask_ref[0:1, lanes]
                if kind != "cross":
                    apart = min(max(c // LANES - (first_block + r // LANES), -2), 2) + 2
                    near = slice(apart * LANES, (apart + 1) * LANES)
                    piece = piece + near_ref[2 * pair + head, r % LANES : r % LANES + chunk, near]
                if kind == "enc":
                    piece = piece + bias_ref[2 * pair + head, rows, lanes]
                pieces.append(piece)
            score = jnp.concatenate(pieces, axis=1)
            score = jnp.exp(score - jnp.max(score, axis=1, keepdims=True))
            score = score * (1.0 / jnp.sum(score, axis=1, keepdims=True))
            p_ref[head, rows, :] = score.astype(jnp.bfloat16)
    first, second = (
        sum(
            dot(p_ref[head, :, index * length : (index + 1) * length], v_ref[...])
            for index, v_ref in enumerate(v_refs)
        )
        for head in range(2)
    )
    lane = lax.broadcasted_iota(jnp.int32, first.shape, 1)
    o_ref[...] = jnp.where(lane < HEAD, first, second).astype(jnp.bfloat16)


def bwd_kernel(kind, part, rows, span, p_ref, do_ref, o_ref, q_ref, k_ref, v_ref, *refs):
    carry = refs[: 2 if kind != "cross" else 3] if part else ()
    outs = refs[len(carry) :]
    dq_ref, dk_ref, dv_ref = outs[:3]
    low_ref, dp_ref = outs[3:]
    chunk = 16
    q_t = jnp.transpose(q_ref[...].astype(jnp.float32)).astype(jnp.bfloat16)
    do_t = jnp.transpose(do_ref[...].astype(jnp.float32)).astype(jnp.bfloat16)
    grads, key_grads, value_grads = [], [], []
    for head in range(2):
        d_out = half_lanes(do_ref[...], head)
        delta = jnp.sum(d_out.astype(jnp.float32) * o_ref[...].astype(jnp.float32), axis=1, keepdims=True)
        dp_ref[head] = dot(d_out, v_ref[...], NT)
        for r in range(0, rows, chunk):
            part_rows = slice(r, r + chunk)
            prob = p_ref[head, part_rows, :].astype(jnp.float32)
            low_ref[head, part_rows, :] = (
                prob * (dp_ref[head, part_rows, :] - delta[part_rows, :])
            ).astype(jnp.bfloat16)
        grads.append(dot(low_ref[head], k_ref[...]))
        half = slice(head * HEAD, (head + 1) * HEAD)
        key_grads.append(dot(q_t[half], low_ref[head]))
        value_grads.append(dot(do_t[half], p_ref[head]))
    lane = lax.broadcasted_iota(jnp.int32, grads[0].shape, 1)
    query_grad = jnp.where(lane < HEAD, grads[0], grads[1])
    if kind == "cross" and part:
        query_grad = query_grad + carry[0][...]
    dq_ref[...] = query_grad.astype(dq_ref.dtype)
    for index, (out_ref, pieces) in enumerate(((dk_ref, key_grads), (dv_ref, value_grads))):
        grad = jnp.transpose(jnp.concatenate(pieces, axis=0))
        if kind == "enc" and part:
            grad = grad + carry[index][...]
        if kind == "dec":
            if part:
                out_ref[0:span, :] = carry[index][0:span, :].astype(out_ref.dtype)
            out_ref[part * span : (part + 1) * span, :] = grad.astype(out_ref.dtype)
        else:
            out_ref[...] = grad.astype(out_ref.dtype)


def table_kernel(kind, ti, span, heads, low_ref, crow_ref, ccol_ref, tab_ref, diag_ref, row_ref, wide_ref, idx_ref):
    step = pl.program_id(0)
    group = 16
    wide = diag_ref.shape[2]
    pad = wide - span

    @pl.when(step == 0)
    def _():
        tab_ref[...] = jnp.zeros_like(tab_ref)

    if kind == "enc":
        for r in range(0, ti, 16):
            for axis in range(2):
                far = crow_ref[axis : axis + 1, :] - ccol_ref[r : r + 16, axis : axis + 1]
                idx_ref[axis, r : r + 16, :] = two_sided(far, 500).astype(jnp.float32)
    out_row = lax.broadcasted_iota(jnp.int32, (256, 256), 0)
    in_row = lax.broadcasted_iota(jnp.int32, (256, 256), 1)
    swap = (lax.div(out_row, 16) == lax.rem(in_row, 16)) & (lax.rem(out_row, 16) == lax.div(in_row, 16))
    swap = jnp.where(swap, 1.0, 0.0).astype(jnp.bfloat16)
    blank = jnp.zeros(((16 - heads) * 16, span), jnp.bfloat16)
    which = lax.broadcasted_iota(jnp.int32, (32, span), 0).astype(jnp.bfloat16)

    tab = jnp.zeros(tab_ref.shape, jnp.float32)
    diag = jnp.zeros((16, wide), jnp.float32)
    for g in range(ti // group):
        first = g * group
        block = jnp.concatenate([low_ref[h, first : first + group, :] for h in range(heads)] + [blank], axis=0)
        wide_ref[g] = dot(swap, block)
        if kind == "enc":
            row_ref[g] = wide_ref[g].astype(jnp.bfloat16)
        for j in range(group):
            lines = slice(16 * j, 16 * j + 16)
            if kind == "enc":
                hot = []
                for axis in range(2):
                    bucket = idx_ref[axis, first + j : first + j + 1, :]
                    bucket = jnp.broadcast_to(bucket, (32, span)).astype(jnp.bfloat16)
                    hot.append(jnp.where(bucket == which, jnp.bfloat16(1), jnp.bfloat16(0)))
                tab = tab + dot(row_ref[g, lines, :], jnp.concatenate(hot, axis=0), NT)
            line = wide_ref[g, lines, :]
            if pad:
                line = jnp.concatenate([line, jnp.zeros((16, pad), jnp.float32)], axis=1)
            diag = diag + pltpu.roll(line, (wide - (first + j)) % wide, 1)
    tab_ref[...] += tab
    diag_ref[0] = diag


ANY = pl.BlockSpec(memory_space=pl.ANY)


def cost(flops, bytes_accessed, transcendentals):
    return pl.CostEstimate(flops=flops // 10, bytes_accessed=bytes_accessed // 10, transcendentals=transcendentals // 10)


def without(kernel, first, count):
    return lambda *refs: kernel(*refs[:first], *refs[first + count :])


def near_width(kind, ti, span):
    return span + ti if kind == "enc" else span


def diag_sums(kind, diag, starts):
    wide = diag.shape[2]
    column = lax.broadcasted_iota(jnp.int32, (len(starts), wide), 1)
    start = jnp.array(starts, jnp.int32)[:, None]
    if kind == "dec":
        bucket = one_sided(jnp.where(column > start, column - wide, column) - start)
    else:
        bucket = two_sided(jnp.where(column > wide - TI, column - wide, column) - start, 128)
    hot = (bucket[..., None] == lax.iota(jnp.int32, 32)).astype(jnp.float32)
    return jnp.einsum("swb,shw->bh", hot, diag, precision=lax.Precision.HIGHEST)


def attend_forward(kind, part, tq, lens, tables, coords, q_src, q_col, kv_srcs, k_col, v_col, pairs, quests, deps=()):
    heads = 2 * pairs
    key_rows = sum(kv_src.shape[0] for kv_src in kv_srcs)
    span = key_rows // quests if kind == "dec" else key_rows
    key_block = part if kind == "dec" else 0
    count = len(kv_srcs)
    flops = tq * span * (60000 if kind == "enc" else 25000)
    tab_n = tab_x = jnp.zeros((16, LANES), jnp.float32)
    tab_y = jnp.zeros((1, 8, LANES), jnp.float32)
    if kind != "cross":
        tab_n = jnp.pad(tables[0].T, ((0, 16 - heads), (0, LANES - 32)))
    if kind == "enc":
        tab_x = jnp.pad(tables[1].T, ((0, 16 - heads), (0, LANES - 32)))
        tab_y = jnp.broadcast_to(tables[2].T[:, :, None], (heads, 32, LANES))
    return pl.pallas_call(
        without(partial(fwd_kernel, kind, part, tq, span, heads), 7 + 2 * count, len(deps)),
        grid=(pairs,),
        in_specs=[
            pl.BlockSpec(memory_space=pltpu.SMEM),
            pl.BlockSpec(tab_n.shape, lambda h: (0, 0)),
            pl.BlockSpec(tab_x.shape, lambda h: (0, 0)),
            pl.BlockSpec(tab_y.shape, lambda h: (0, 0, 0)),
            pl.BlockSpec(coords.shape, lambda h: (0, 0)),
            pl.BlockSpec((tq, 2), lambda h: (part, 0)),
            pl.BlockSpec((tq, LANES), lambda h: (part, q_col * pairs + h)),
        ]
        + [pl.BlockSpec((span // count, LANES), lambda h: (key_block, k_col * pairs + h))] * count
        + [pl.BlockSpec((span // count, LANES), lambda h: (key_block, v_col * pairs + h))] * count
        + [ANY] * len(deps),
        out_specs=[
            pl.BlockSpec((tq, LANES), lambda h: (0, h)),
            pl.BlockSpec((2, tq, span), lambda h: (h, 0, 0)),
        ],
        out_shape=[
            jax.ShapeDtypeStruct((tq, pairs * LANES), jnp.bfloat16),
            jax.ShapeDtypeStruct((heads, tq, key_rows), jnp.bfloat16),
        ],
        scratch_shapes=[
            pltpu.VMEM((2, tq, span), jnp.float32),
            pltpu.VMEM((2, tq, span) if kind == "enc" else (1, 8, LANES), jnp.int32),
            pltpu.VMEM((8, span), jnp.float32),
            pltpu.VMEM((1, 8, LANES) if kind == "cross" else (heads, LANES, 5 * LANES), jnp.float32),
            pltpu.VMEM((heads, tq, span) if kind == "enc" else (1, 8, LANES), jnp.float32),
        ],
        compiler_params=pltpu.CompilerParams(vmem_limit_bytes=(52 if kind == "enc" else 34) * 1024 * 1024),
        cost_estimate=cost(
            flops=flops, bytes_accessed=4 * tq * span * pairs, transcendentals=2 * tq * span * pairs
        ),
        name="attend_forward_" + kind,
    )(lens, tab_n, tab_x, tab_y, coords, coords.T, q_src, *kv_srcs, *kv_srcs, *deps)


def attend_backward(kind, part, prob, grad_out, out, q_src, q_col, kv_src, k_col, v_col, pairs, quests, carry=(), deps=()):
    rows = grad_out.shape[0]
    key_rows = 2 * kv_src.shape[0] if kind == "cross" else kv_src.shape[0]
    width = pairs * LANES
    span = key_rows if kind == "enc" else key_rows // 2
    key_block = part if kind == "dec" else 0
    query_block = 0 if kind == "cross" else part
    score_block = part if kind == "cross" else 0
    if kind == "cross":
        carried = [pl.BlockSpec((rows, LANES), lambda h: (0, h))] + [pl.BlockSpec(memory_space=pl.ANY)] * 2
        key_out = pl.BlockSpec((span, LANES), lambda h: (part, h))
        aliases = {7: 1, 8: 2} if part else {}
    else:
        carried = [pl.BlockSpec((key_rows, LANES), lambda h: (0, h))] * 2
        key_out = pl.BlockSpec((key_rows, LANES), lambda h: (0, h))
        aliases = {}
    query_type = jnp.float32 if kind == "cross" and not part else jnp.bfloat16
    key_type = jnp.bfloat16 if kind == "cross" or part else jnp.float32
    low_block = pl.BlockSpec((2, rows, span), (lambda h: (0, 0, 0)) if kind == "cross" else (lambda h: (h, 0, 0)))
    low_shape = (2, rows, span) if kind == "cross" else (2 * pairs, rows, key_rows)
    return pl.pallas_call(
        without(partial(bwd_kernel, kind, part, rows, span), 6 + len(carry), len(deps)),
        grid=(pairs,),
        in_specs=[
            pl.BlockSpec((2, rows, span), lambda h: (h, 0, score_block)),
            pl.BlockSpec((rows, LANES), lambda h: (0, h)),
            pl.BlockSpec((rows, LANES), lambda h: (0, h)),
            pl.BlockSpec((rows, LANES), lambda h: (query_block, q_col * pairs + h)),
            pl.BlockSpec((span, LANES), lambda h: (key_block, k_col * pairs + h)),
            pl.BlockSpec((span, LANES), lambda h: (key_block, v_col * pairs + h)),
        ]
        + carried[: len(carry)]
        + [ANY] * len(deps),
        out_specs=[
            pl.BlockSpec((rows, LANES), lambda h: (0, h)),
            key_out,
            key_out,
            low_block,
        ],
        out_shape=[
            jax.ShapeDtypeStruct((rows, width), query_type),
            jax.ShapeDtypeStruct((key_rows, width), key_type),
            jax.ShapeDtypeStruct((key_rows, width), key_type),
            jax.ShapeDtypeStruct(low_shape, jnp.bfloat16),
        ],
        scratch_shapes=[pltpu.VMEM((2, rows, span), jnp.float32)],
        input_output_aliases=aliases,
        compiler_params=pltpu.CompilerParams(vmem_limit_bytes=VMEM_LIMIT),
        cost_estimate=cost(
            flops=rows * span * 28000, bytes_accessed=4 * rows * span * pairs, transcendentals=0
        ),
        name="attend_backward_" + kind,
    )(prob, grad_out, out, q_src, kv_src, kv_src, *carry, *deps)


def table_sums(kind, part, quarter, coords, low, quests, deps=()):
    heads, rows, key_rows = low.shape
    rows = rows // 2
    span = key_rows // quests if kind == "dec" else key_rows
    steps = rows // TI
    wide = near_width(kind, TI, span)
    first = (2 * part + quarter) * steps
    tab, diag = pl.pallas_call(
        without(partial(table_kernel, kind, TI, span, heads), 3, len(deps)),
        grid=(steps,),
        in_specs=[
            pl.BlockSpec((heads, TI, span), lambda i: (0, quarter * steps + i, 0)),
            pl.BlockSpec(coords.shape, lambda i: (0, 0)),
            pl.BlockSpec((TI, 2), lambda i: (first + i, 0)),
        ]
        + [ANY] * len(deps),
        out_specs=[
            pl.BlockSpec((16, 64), lambda i: (0, 0)),
            pl.BlockSpec((1, 16, wide), lambda i: (i, 0, 0)),
        ],
        out_shape=[
            jax.ShapeDtypeStruct((16, 64), jnp.float32),
            jax.ShapeDtypeStruct((steps, 16, near_width("enc", TI, key_rows)), jnp.float32),
        ],
        scratch_shapes=[
            pltpu.VMEM((TI // 16, 256, span), jnp.bfloat16),
            pltpu.VMEM((TI // 16, 256, span), jnp.float32),
            pltpu.VMEM((2, TI, span) if kind == "enc" else (1, 8, LANES), jnp.float32),
        ],
        compiler_params=pltpu.CompilerParams(vmem_limit_bytes=VMEM_LIMIT),
        cost_estimate=cost(
            flops=rows * span * 40000, bytes_accessed=2 * heads * rows * span, transcendentals=0
        ),
        name="table_sums_" + kind,
    )(low, coords, coords.T, *deps)
    return tab, diag


def table_grads(kind, tabs, diags, rows, quests, heads):
    steps = diags[0].shape[0]
    starts = [step * TI for step in range(4 * steps)]
    diag = jnp.concatenate(diags, axis=0)
    if kind == "dec":
        span = rows // quests
        near = diag_sums(kind, diag[:, :, :span], [start % span for start in starts])[:, :heads]
        blank = jnp.zeros_like(near)
        return jnp.stack([blank, blank, blank, near])
    tab = sum(tabs)
    near = diag_sums(kind, diag, starts)[:, :heads]
    return jnp.stack([near, tab[:heads, :32].T, tab[:heads, 32:].T, jnp.zeros_like(near)])


def weight_copies(core, pieces, wi_ref, wd_ref, sems):
    in_own, in_far, in_near, down_own, down_far, down_near = pieces
    own = in_own.shape[1]
    block = own // 2
    rows_in, rows_down = in_far.shape[0], down_far.shape[0]
    far_in = pl.ds(pl.multiple_of(core * rows_in, rows_in), rows_in)
    near_in = pl.ds(pl.multiple_of((1 - core) * rows_in, rows_in), rows_in)
    far_down = pl.ds(pl.multiple_of(own + core * rows_down, rows_down), rows_down)
    near_down = pl.ds(pl.multiple_of(own + (1 - core) * rows_down, rows_down), rows_down)
    moves = []
    for b in range(2):
        part = slice(b * block, (b + 1) * block)
        moves.append((in_own.at[:, part], wi_ref.at[:, part]))
        moves.append((down_own.at[part, :], wd_ref.at[part, :]))
    other = slice(own, 2 * own)
    moves.append((in_far, wi_ref.at[far_in, other]))
    moves.append((in_near, wi_ref.at[near_in, other]))
    moves.append((down_far, wd_ref.at[far_down, :]))
    moves.append((down_near, wd_ref.at[near_down, :]))
    return [pltpu.make_async_copy(src, dst, sems.at[i]) for i, (src, dst) in enumerate(moves)]


def ffn_kernel(mode, part, flag_ref, *refs):
    pieces, refs = refs[:6], refs[6:]
    refs, (wi_ref, wd_ref, sems) = refs[:-3], refs[-3:]
    copies = weight_copies(flag_ref[0], pieces, wi_ref, wd_ref, sems)
    first_step = pl.program_id(0) == 0

    @pl.when(first_step)
    def _():
        for copy in copies:
            copy.start()
        for copy in copies:
            copy.wait()

    gain_ref, wa_ref = refs[:2]
    gain = gain_ref[0:1, :]
    if mode == "back":
        middle_ref, second_ref, own_ref, arrived_ref, more_ref, first_ref = refs[2:8]
        dx_ref, hn_ref, gl_ref, ml_ref, act_ref, dzo_ref, do_ref, dgain_ref, z_ref, du_ref = refs[-10:]
        on_encoder = flag_ref[2] == 0
        x = jnp.where(on_encoder, middle_ref[...], second_ref[...])
    else:
        base_ref, att_ref = refs[2:4]
        x = base_ref[...].astype(jnp.float32) + dot(att_ref[...], wa_ref[...])
        if mode == "fwd":
            out_ref, mid_ref, z_ref, u_ref = refs[4:]
        else:
            own_ref, arrived_ref, out_ref, mid_ref, dx_ref, low_ref, do_ref, z_ref, u_ref, du_ref, dz_ref = refs[4:]
        mid_ref[...] = x
    rows, width = x.shape
    hidden = wi_ref.shape[1]
    block, chunk = hidden // FFN_BLOCKS, 32
    if mode != "fwd":
        half = part if mode == "back" else lax.div(2 * pl.program_id(0), pl.num_programs(0))
        grad_low = jnp.where(half == flag_ref[1], own_ref[...], arrived_ref[...])
        grad = grad_low.astype(jnp.float32)
    scale = lax.rsqrt(jnp.mean(x * x, axis=1, keepdims=True) + EPSILON)
    normed_full = x * scale * gain
    normed = normed_full.astype(jnp.bfloat16)
    if mode == "back":
        grad = grad + more_ref[...].astype(jnp.float32)
        grad_low = grad.astype(jnp.bfloat16)
        hn_ref[...] = jnp.transpose(normed_full).astype(jnp.bfloat16)
        gl_ref[...] = jnp.transpose(grad).astype(jnp.bfloat16)
    total = jnp.zeros((rows, width), jnp.float32)
    back = jnp.zeros((rows, width), jnp.float32)
    for index in range(FFN_BLOCKS + 1):
        if index < FFN_BLOCKS:
            cols = slice(index * block, (index + 1) * block)
            z_ref[index % 2] = dot(normed, wi_ref[:, cols])
            if mode != "fwd":
                du_ref[index % 2] = dot(grad_low, wd_ref[cols, :], NT)
        if index == 0:
            continue
        slot = (index - 1) % 2
        cols = slice((index - 1) * block, index * block)
        for r in range(0, rows, chunk):
            lines = slice(r, r + chunk)
            z = z_ref[slot, lines, :]
            square = z * z
            tanh = jnp.tanh(z * (GELU_SCALE + GELU_SCALE * GELU_CUBE * square))
            half = 0.5 + 0.5 * tanh
            act = (z * half).astype(jnp.bfloat16)
            if mode == "back":
                act_ref[lines, cols] = act
            else:
                u_ref[slot, lines, :] = act
            if mode != "fwd":
                slope = half + z * (0.5 - 0.5 * tanh * tanh) * (GELU_SCALE + 3.0 * GELU_SCALE * GELU_CUBE * square)
                d_hidden = (du_ref[slot, lines, :] * slope).astype(jnp.bfloat16)
                if mode == "back":
                    dzo_ref[lines, cols] = d_hidden
                else:
                    dz_ref[slot, lines, :] = d_hidden
        if mode != "back":
            total = total + dot(u_ref[slot], wd_ref[cols, :])
        if mode == "back":
            back = back + dot(dzo_ref[:, cols], wi_ref[:, cols], NT)
        elif mode == "both":
            back = back + dot(dz_ref[slot], wi_ref[:, cols], NT)
    if mode != "back":
        out_ref[...] = (x + total).astype(jnp.bfloat16)
    if mode != "fwd":
        scaled = back * gain
        mean = jnp.mean(scaled * x, axis=1, keepdims=True)
        grad = grad + scale * scaled - x * (scale * scale * scale * mean)
        if mode == "back":
            grad = jnp.where(on_encoder, grad, first_ref[...])
            ml_ref[...] = jnp.transpose(grad).astype(jnp.bfloat16)
            gain_part = jnp.sum((back * x * scale).reshape(rows // 8, 8, width), axis=0)
            dgain_ref[...] = jnp.where(first_step, gain_part, dgain_ref[...] + gain_part)
        else:
            low_ref[...] = grad.astype(jnp.bfloat16)
        dx_ref[...] = grad
        do_ref[...] = dot(grad.astype(jnp.bfloat16), wa_ref[...], NT).astype(jnp.bfloat16)


def feed_forward(mode, part, rows, flags, pieces, gain, w_att, rows_in, held=(), deps=()):
    width = w_att.shape[0]
    hidden = 2 * pieces[0].shape[1]
    steps = rows // TR
    row_block = pl.BlockSpec((TR, width), lambda i: (i, 0))
    turned_block = pl.BlockSpec((width, TR), lambda i: (0, part * steps + i))
    hidden_block = pl.BlockSpec((TR, hidden), lambda i: (part * steps + i, 0))
    low = jax.ShapeDtypeStruct((rows, width), jnp.bfloat16)
    full = jax.ShapeDtypeStruct((rows, width), jnp.float32)
    turned = jax.ShapeDtypeStruct((width, 2 * rows), jnp.bfloat16)
    wide = jax.ShapeDtypeStruct((2 * rows, hidden), jnp.bfloat16)
    small = jax.ShapeDtypeStruct((8, width), jnp.float32)
    outs = {
        "fwd": ([row_block] * 2, [low, full]),
        "both": ([row_block] * 5, [low, full, full, low, low]),
        "back": (
            [row_block]
            + [turned_block] * 3
            + [hidden_block] * 2
            + [row_block, pl.BlockSpec((8, width), lambda i: (0, 0))],
            [full, turned, turned, turned, wide, wide, low, small],
        ),
    }[mode]
    slab = (2, TR, hidden // FFN_BLOCKS)
    slab32, slab16 = pltpu.VMEM(slab, jnp.float32), pltpu.VMEM(slab, jnp.bfloat16)
    scratch = {"fwd": [slab32, slab16], "both": [slab32, slab16, slab32, slab16], "back": [slab32, slab32]}[mode]
    matmuls = {"fwd": 2, "both": 4, "back": 3}[mode]
    inputs = 9 + len(rows_in)
    return pl.pallas_call(
        without(partial(ffn_kernel, mode, part), inputs, len(held) + len(deps)),
        grid=(steps,),
        in_specs=[pl.BlockSpec(memory_space=pltpu.SMEM)]
        + [ANY] * 6
        + [pl.BlockSpec((8, width), lambda i: (0, 0)), pl.BlockSpec(w_att.shape, lambda i: (0, 0))]
        + [pl.BlockSpec((TR, width), lambda i, at=at, turn=turn: (at + i % turn, 0)) for _, at, turn in rows_in]
        + [ANY] * (len(held) + len(deps)),
        out_specs=outs[0],
        out_shape=outs[1],
        scratch_shapes=scratch
        + [
            pltpu.VMEM((width, hidden), jnp.bfloat16),
            pltpu.VMEM((hidden, width), jnp.bfloat16),
            pltpu.SemaphoreType.DMA((8,)),
        ],
        input_output_aliases={inputs + index: 1 + index for index in range(len(held))},
        compiler_params=pltpu.CompilerParams(vmem_limit_bytes=VMEM_LIMIT),
        cost_estimate=cost(
            flops=4 * matmuls * rows * width * hidden,
            bytes_accessed=4 * width * hidden + 8 * rows * width,
            transcendentals=rows * hidden,
        ),
        name="feed_forward_" + mode,
    )(flags, *pieces, jnp.broadcast_to(gain[None], (8, width)), w_att, *(x for x, _, _ in rows_in), *held, *deps)


def product_kernel(left_of, parts_of, slices, which, core_ref, *refs):
    left_count, count = max(left_of) + 1, sum(parts_of)
    lefts, rights = refs[:left_count], refs[left_count : left_count + count]
    outs, held_ref = refs[left_count + count : -1], refs[-1]
    step = pl.program_id(0)
    rows, span = lefts[0].shape
    size = rows // slices
    half = rows // 2

    @pl.when(step == 0)
    def _():
        for index, left in enumerate(lefts):
            if len(outs) == 1:
                held_ref[index] = left[...]
                continue
            for first, core in ((0, 1 - core_ref[0]), (half, core_ref[0])):
                for part in range(slices // 2):
                    source = pl.ds(pl.multiple_of((2 * part + core) * size, 16), size)
                    held_ref[index, first + part * size : first + (part + 1) * size, :] = left[source, :]

    def product(index, lines):
        parts = rights[sum(parts_of[:index]) : sum(parts_of[: index + 1])]
        length = span // len(parts)
        return sum(
            dot(held_ref[left_of[index], lines, part * length : (part + 1) * length], right[...])
            for part, right in enumerate(parts)
        ).astype(jnp.bfloat16)

    for index in range(len(parts_of)):
        steps = [s for s, owner in enumerate(which) if owner == index]
        chosen = functools.reduce(lambda a, b: a | b, [step == s for s in steps])

        @pl.when(chosen)
        def _(index=index):
            if len(outs) == 1:
                outs[0][...] = product(index, slice(0, rows))
            else:
                outs[0][...] = product(index, slice(0, half))
                outs[1][...] = product(index, slice(half, rows))


def products(lefts, left_of, rights, block, slices, core, deps=()):
    rows, span = lefts[0].shape
    parts_of = [len(right) for right in rights]
    counts = [right[0].shape[1] // (2 * block) for right in rights]
    which, place = [], []
    for half in range(2):
        for index, number in enumerate(counts):
            for b in range(number):
                which.append(index)
                place.append(half * number + b)
    maps = []
    for index, right in enumerate(rights):
        held, column_of = 0, []
        for s, owner in enumerate(which):
            if owner == index:
                held = place[s]
            column_of.append(held)
        maps += [column_of] * len(right)
    steps = len(which)
    total = steps * block

    def right_map(column_of):
        def index_map(s):
            value = 0
            for position in range(steps):
                if column_of[position]:
                    value = value + jnp.where(s == position, column_of[position], 0)
            return (0, value)

        return index_map

    size = rows // slices
    apart = size % 16 == 0
    out_rows = rows // 2 if apart else rows
    out = jax.ShapeDtypeStruct((out_rows, total), jnp.bfloat16)
    flat = [part for right in rights for part in right]
    results = pl.pallas_call(
        without(
            partial(product_kernel, left_of, parts_of, slices, which), 1 + len(lefts) + len(flat), len(deps)
        ),
        grid=(steps,),
        in_specs=[pl.BlockSpec(memory_space=pltpu.SMEM)]
        + [pl.BlockSpec((rows, span), lambda s: (0, 0)) for _ in lefts]
        + [pl.BlockSpec((part.shape[0], block), right_map(column_of)) for part, column_of in zip(flat, maps)]
        + [ANY] * len(deps),
        out_specs=[pl.BlockSpec((out_rows, block), lambda s: (0, s))] * (2 if apart else 1),
        out_shape=[out] * (2 if apart else 1),
        scratch_shapes=[pltpu.VMEM((len(lefts), rows, span), jnp.bfloat16)],
        compiler_params=pltpu.CompilerParams(vmem_limit_bytes=VMEM_LIMIT),
        cost_estimate=cost(
            flops=2 * span * rows * total, bytes_accessed=2 * (span + rows) * total, transcendentals=0
        ),
        name="weight_products",
    )(core.reshape(1), *lefts, *flat, *deps)
    if apart:
        return results
    cut = results[0].reshape(slices // 2, 2, size, total)
    return pick(cut, 1 - core, 1).reshape(-1, total), pick(cut, core, 1).reshape(-1, total)


def nothing(shapes):
    return pl.pallas_call(
        lambda *refs: None, out_shape=shapes, out_specs=[ANY] * len(shapes), name="nothing"
    )()


def input_kernel(gain_ref, w_ref, x_ref, first_ref, second_ref, dk_ref, dv_ref, grad_ref, out_ref, dgain_ref):
    step = pl.program_id(0)
    gain = gain_ref[0:1, :]
    rows, width = x_ref.shape
    d_query = jnp.where(2 * step < pl.num_programs(0), first_ref[...], second_ref[...])
    back = dot(d_query, w_ref[:, :width], NT)
    back = back + dot(dk_ref[...], w_ref[:, width : 2 * width], NT)
    back = back + dot(dv_ref[...], w_ref[:, 2 * width :], NT)
    x = x_ref[...].astype(jnp.float32)
    scale = lax.rsqrt(jnp.mean(x * x, axis=1, keepdims=True) + EPSILON)
    scaled = back * gain
    mean = jnp.mean(scaled * x, axis=1, keepdims=True)
    out_ref[...] = grad_ref[...] + scale * scaled - x * (scale * scale * scale * mean)
    gain_part = jnp.sum((back * x * scale).reshape(rows // 8, 8, width), axis=0)
    dgain_ref[...] = jnp.where(step == 0, gain_part, dgain_ref[...] + gain_part)


def input_gradient(x, gain, w_qkv, query_grads, key_grad, value_grad, grad, deps):
    rows, width = x.shape
    steps = rows // TR
    row_block = pl.BlockSpec((TR, width), lambda i: (i, 0))
    half_block = pl.BlockSpec((TR, width), lambda i: (i % (steps // 2), 0))
    fixed = pl.BlockSpec((8, width), lambda i: (0, 0))
    out, dgain = pl.pallas_call(
        without(input_kernel, 8, len(deps)),
        grid=(steps,),
        in_specs=[fixed, pl.BlockSpec(w_qkv.shape, lambda i: (0, 0)), row_block, half_block, half_block]
        + [row_block] * 3
        + [ANY] * len(deps),
        out_specs=[row_block, fixed],
        out_shape=[jax.ShapeDtypeStruct((rows, width), jnp.float32), jax.ShapeDtypeStruct((8, width), jnp.float32)],
        compiler_params=pltpu.CompilerParams(vmem_limit_bytes=VMEM_LIMIT),
        cost_estimate=cost(
            flops=6 * rows * width * width, bytes_accessed=16 * rows * width, transcendentals=0
        ),
        name="input_gradient",
    )(jnp.broadcast_to(gain[None], (8, width)), w_qkv, x, *query_grads, key_grad, value_grad, grad, *deps)
    return out, jnp.sum(dgain, axis=0)


def sum_kernel(rounds, x_ref, out_ref, *refs):
    slots, send_sems, recv_sems = refs[: len(rounds)], refs[len(rounds)], refs[len(rounds) + 1]
    barrier = pltpu.get_barrier_semaphore()
    places, peers = [], []
    for axes in rounds:
        place, count = 0, 1
        for axis in axes:
            place = place * lax.axis_size(axis) + lax.axis_index(axis)
            count = count * lax.axis_size(axis)
        found = []
        for step in range(1, count):
            rest, device = lax.rem(place + step, count), {}
            for axis in reversed(axes):
                device[axis] = lax.rem(rest, lax.axis_size(axis))
                rest = lax.div(rest, lax.axis_size(axis))
            found.append(device)
        places.append(place)
        peers.append(found)
    for device in peers[0] + peers[1]:
        pl.semaphore_signal(barrier, inc=1, device_id=device, device_id_type=pl.DeviceIdType.MESH)
    pl.semaphore_wait(barrier, len(peers[0]) + len(peers[1]))
    value = x_ref[...]
    first = 0
    for slot, place, found in zip(slots, places, peers):
        slot[place] = value
        copies = []
        for step, device in enumerate(found):
            copies.append(
                pltpu.make_async_remote_copy(
                    src_ref=slot.at[place],
                    dst_ref=slot.at[place],
                    send_sem=send_sems.at[first + step],
                    recv_sem=recv_sems.at[first + step],
                    device_id=device,
                    device_id_type=pl.DeviceIdType.MESH,
                )
            )
        for copy in copies:
            copy.start()
        for copy in copies:
            copy.wait()
        first += len(found)
        value = slot[0]
        for index in range(1, len(found) + 1):
            value = value + slot[index]
    out_ref[...] = value


def sum_everywhere(x):
    rounds = (("dp",), ("section", "mp"))
    counts = [math.prod(lax.axis_size(axis) for axis in axes) for axes in rounds]
    copies = sum(counts) - len(counts)
    return pl.pallas_call(
        partial(sum_kernel, rounds),
        out_shape=jax.ShapeDtypeStruct(x.shape, x.dtype),
        in_specs=[pl.BlockSpec(memory_space=pltpu.VMEM)],
        out_specs=pl.BlockSpec(memory_space=pltpu.VMEM),
        scratch_shapes=[pltpu.VMEM((count,) + x.shape, x.dtype) for count in counts]
        + [pltpu.SemaphoreType.DMA((copies,)), pltpu.SemaphoreType.DMA((copies,))],
        compiler_params=pltpu.CompilerParams(collective_id=0, has_side_effects=True),
        name="sum_everywhere",
    )(x)


def pair_permute(x, axis, bit):
    pairs = [(i, i ^ (1 << bit)) for i in range(lax.axis_size(axis))]
    return lax.ppermute(x, axis, pairs)


def shifted(x, axis, by):
    peers = lax.axis_size(axis)
    pairs = [(i, i + by) for i in range(peers) if 0 <= i + by < peers]
    return lax.ppermute(x, axis, pairs)


def in_order(flag, first, second, axis):
    return jnp.where(
        flag == 0,
        jnp.concatenate([first, second], axis=axis),
        jnp.concatenate([second, first], axis=axis),
    )


def pick(x, index, axis):
    return lax.dynamic_index_in_dim(x, index, axis, False)


def after(values, *others):
    return lax.optimization_barrier((values, others))[0]


def exchange_rows(block, where_mp):
    return pick(block, where_mp, 0), pair_permute(pick(block, 1 - where_mp, 0), "mp", 0)


def scatter_rows(rows, where_mp):
    half = rows.shape[0] // 2
    send = lax.dynamic_slice_in_dim(rows, (1 - where_mp) * half, half, 0).astype(jnp.bfloat16)
    return lax.dynamic_slice_in_dim(rows, where_mp * half, half, 0), pair_permute(send, "mp", 0)


def fetch_far(shard, core):
    half = shard.shape[0] // 2
    return pair_permute(lax.dynamic_slice_in_dim(shard, core * half, half, 0), "mp", 0)


def fetch_near(far):
    return pair_permute(far, "dp", 0)


def fetch_other(shard, dp_index):
    quarter = shard.shape[0] // 4
    far = pair_permute(lax.dynamic_slice_in_dim(shard, (dp_index & 3) * quarter, quarter, 0), "mp", 0)
    half = in_order(dp_index & 1, far, pair_permute(far, "dp", 0), 0)
    return in_order((dp_index >> 1) & 1, half, pair_permute(half, "dp", 1), 0), far


class Reduction:
    def __init__(self, send, keep, dp_index, section=None):
        self.total, self.arrived = keep, pair_permute(send, "dp", 0)
        self.dp_index = dp_index
        bits = lax.axis_size("dp").bit_length() - 1
        self.left = ([("section", section)] if section is not None else []) + [("mp", None)]
        self.left += [("dp", bit) for bit in range(1, bits)]

    def joined(self, cut):
        return cut(self.total).astype(jnp.float32) + cut(self.arrived).astype(jnp.float32)

    def hop(self, *ties):
        brought = self.arrived
        self.arrived = after(self.arrived, *ties)
        axis, which = self.left.pop(0)
        rows, width = self.total.shape
        if axis == "section":
            send = self.joined(lambda x: x[: rows // 2]).astype(jnp.bfloat16)
            keep = jnp.where(which == 0, 0.0, self.joined(lambda x: x[rows // 2 :]))
            self.total, self.arrived = keep, shifted(send, "section", -1)
        elif axis == "mp":
            send = self.joined(lambda x: x[:, width // 2 :]).astype(jnp.bfloat16)
            self.total, self.arrived = self.joined(lambda x: x[:, : width // 2]), pair_permute(send, "mp", 0)
        else:
            mark = (self.dp_index >> which) & 1
            halves = (lax.axis_size("dp") >> (which + 1), 2, -1, width)
            send = self.joined(lambda x: pick(x.reshape(halves), 1 - mark, 1)).astype(jnp.bfloat16)
            keep = self.joined(lambda x: pick(x.reshape(halves), mark, 1))
            self.total = keep.reshape(-1, width)
            self.arrived = pair_permute(send.reshape(-1, width), "dp", which)
        return brought

    def finish(self, *ties):
        while self.left:
            self.hop()
        self.arrived = after(self.arrived, *ties)
        return self.joined(lambda x: x)


def rms_norm(inputs, gain_row):
    return (
        inputs * lax.rsqrt(jnp.mean(inputs * inputs, axis=-1, keepdims=True) + EPSILON) * gain_row
    )


def norm_back(rows, gain_row, grad_normed):
    return jax.vjp(rms_norm, rows, gain_row)[1](grad_normed)


def low(x):
    return x.astype(jnp.bfloat16)


def local(
    block_input,
    out_cotangent,
    doc_lengths,
    question_lengths,
    coordinates,
    gains,
    bias_tables,
    self_qkv,
    self_out,
    ffn_in,
    ffn_out,
    cross_q,
    cross_kv,
    cross_out,
):
    section = lax.axis_index("section")
    on_encoder = section == 0
    dp_index = lax.axis_index("dp")
    core = dp_index & 1
    where_mp = lax.axis_index("mp")
    width = block_input.shape[4]
    quests = question_lengths.shape[2]
    own = self_qkv.shape[3]
    pairs = 2 * own // LANES
    heads = 2 * pairs
    parts = lax.axis_size("dp")
    flags = jnp.stack([core, where_mp, section]).astype(jnp.int32)

    rows_low = in_order(where_mp, *exchange_rows(block_input[0, :, 0], where_mp), 0)
    qkv_own = self_qkv[0].reshape(width, -1)
    qkv_other, qkv_far = fetch_other(qkv_own, dp_index)
    w_qkv = jnp.concatenate(
        [x[:, t * own : (t + 1) * own] for t in range(3) for x in (qkv_own, qkv_other)], axis=1
    )
    owned = after((ffn_in[0], ffn_out[0], self_out[0]), rows_low, qkv_far)
    fars = [fetch_far(x, core) for x in owned]

    lens = jnp.concatenate(
        [pick(doc_lengths, where_mp, 0), pick(question_lengths, where_mp, 0)[0]]
    ).astype(jnp.int32)
    coords = pick(coordinates, where_mp, 0)[0]
    tables = jnp.where(where_mp == 0, bias_tables, jnp.roll(bias_tables, heads // 2, axis=2))

    rows = rows_low.astype(jnp.float32)
    span = rows.shape[0]
    half = span // 2
    turn = half // TR
    halves = (slice(0, half), slice(half, span))
    gain_self = jnp.where(on_encoder, gains[0], gains[2])
    normed_self = low(rms_norm(rows, gain_self))
    projected = low(dot(normed_self, w_qkv))
    merged, probs, middles, memories, arrivals = [], [], [], [], []
    for part in range(2):
        deps = memories[:1]

        def forward(kind, chosen):
            return attend_forward(
                kind, part, half, lens, chosen, coords, projected, 0, [projected], 1, 2, pairs, quests, deps
            )

        out, prob = lax.cond(on_encoder, lambda: forward("enc", tables[:3]), lambda: forward("dec", tables[3:]))
        if not part:
            fars = after(fars, out)
            nears = [fetch_near(x) for x in fars]
            w_out = jnp.concatenate([self_out[0], in_order(core, fars[2], nears[2], 0)], axis=0)
            pieces = (ffn_in[0], fars[0], nears[0], ffn_out[0], fars[1], nears[1])
            cross_owned = after(
                (jnp.concatenate([cross_q, cross_kv.reshape(width, -1)], axis=1), cross_out, out_cotangent[0, :, 0]), fars
            )
            cross_fars = [fetch_far(x, core) for x in cross_owned[:2]]
            cot = exchange_rows(cross_owned[2], where_mp)
        else:
            cross_fars = after(cross_fars, out)
        memory, middle = feed_forward(
            "fwd", part, half, flags, pieces, gains[1], w_out, [(rows_low, part * turn, turn), (out, 0, turn)]
        )
        arrivals.append(shifted(memory, "section", 1))
        merged.append(out)
        probs.append(prob)
        middles.append(middle)
        memories.append(memory)
    query_other, cross_other = (in_order(core, far, fetch_near(far), 0) for far in cross_fars)
    w_query = jnp.concatenate([cross_q, query_other[:, :own]], axis=1)
    w_pair = jnp.concatenate(
        [x for t in range(2) for x in (cross_kv[:, t], query_other[:, (t + 1) * own : (t + 2) * own])], axis=1
    )
    w_cross = jnp.concatenate([cross_out, cross_other], axis=0)
    middle = jnp.concatenate(middles, axis=0)

    normed_cross = low(rms_norm(middle, gains[3]))
    queries = low(dot(normed_cross, w_query))
    first_pair = low(dot(arrivals[0], w_pair))
    arrivals[1] = after(arrivals[1], queries, first_pair)
    pair_rows = [first_pair, low(dot(arrivals[1], w_pair))]
    cross_merged, cross_prob = attend_forward(
        "cross", 0, span, lens, None, coords, queries, 0, pair_rows, 0, 1, pairs, quests
    )
    output_low, second, grad_second, second_low, cross_grad = feed_forward(
        "both",
        0,
        span,
        flags,
        pieces,
        gains[4],
        w_cross,
        [(middle, 0, 2 * turn), (cross_merged, 0, 2 * turn), (cot[0], 0, turn), (cot[1], 0, turn)],
    )
    output_own, output_arrived = scatter_rows(
        jnp.where(on_encoder, jnp.concatenate(memories, axis=0), output_low), where_mp
    )
    returns, returned, carry = [], [], ()
    for part in range(2):
        query_grad, key_grad, value_grad, _ = attend_backward(
            "cross",
            part,
            cross_prob,
            cross_grad,
            cross_merged,
            queries,
            0,
            pair_rows[part],
            0,
            1,
            pairs,
            quests,
            carry,
            [returns[0], output_arrived] if part else [],
        )
        carry = (query_grad, key_grad, value_grad)
        returns.append(
            low(
                dot(key_grad[halves[part]], w_pair[:, : 2 * own], NT)
                + dot(value_grad[halves[part]], w_pair[:, 2 * own :], NT)
            )
        )
        returned.append(shifted(returns[part], "section", -1))
    query_cross = after(query_grad, returns[1])

    def cross_norm():
        input_part, gain_part = norm_back(middle, gains[3], dot(query_cross, w_query, NT))
        return grad_second + input_part, gain_part

    def no_norm():
        return tuple(
            nothing([jax.ShapeDtypeStruct((span, width), jnp.float32), jax.ShapeDtypeStruct((width,), jnp.float32)])
        )

    grad_first, gain_cross = lax.cond(on_encoder, no_norm, cross_norm)

    gain_ffn = jnp.where(on_encoder, gains[1], gains[4])
    held, gain_ffn_grad, grads_middle, merged_grads = [], 0.0, [], []
    for part in range(2):
        if part:
            returned[1] = after(returned[1], grads_middle[0])
        grad_middle, *held, merged_grad, gain_part = feed_forward(
            "back",
            part,
            half,
            flags,
            pieces,
            gain_ffn,
            w_out,
            [
                (middles[part], 0, turn),
                (second, part * turn, turn),
                (cot[0], 0, turn),
                (cot[1], 0, turn),
                (returned[part], 0, turn),
                (grad_first, part * turn, turn),
            ],
            held,
        )
        gain_ffn_grad = gain_ffn_grad + jnp.sum(gain_part, axis=0)
        grads_middle.append(grad_middle)
        merged_grads.append(merged_grad)
    hn_turned, gl_turned, ml_turned, activated, hidden_grad = held
    in_send, in_keep = products([hn_turned], [0], [[hidden_grad]], 2 * own, parts, core)
    down_send, down_keep = products([gl_turned], [0], [[activated]], 2 * own, parts, core, [in_send])
    in_steps = Reduction(in_send, in_keep, dp_index)
    down_steps = Reduction(down_send, down_keep, dp_index)

    def cross_products():
        return tuple(
            products(
                [normed_cross.T, jnp.concatenate(arrivals, axis=0).T, second_low.T],
                [0, 1, 1, 2],
                [[query_cross], [key_grad], [value_grad], [cross_merged]],
                own,
                2 * parts,
                core,
                [down_send],
            )
        )

    def no_products():
        blank = jax.ShapeDtypeStruct((width // 2, 8 * own), jnp.bfloat16)
        return tuple(nothing([blank, blank]))

    cross_send, cross_keep = lax.cond(on_encoder, no_products, cross_products)
    cross_steps = Reduction(cross_send, cross_keep, dp_index, section)
    scores, query_grads, carry = [], [], ()
    for part in range(2):
        if part:
            deps = (in_steps.hop(), down_steps.arrived, cross_steps.hop())
        else:
            deps = (down_send, cross_send, in_steps.hop())

        def backward(kind):
            return attend_backward(
                kind, part, probs[part], merged_grads[part], merged[part], projected, 0, projected, 1, 2, pairs, quests,
                carry, deps
            )

        query_grad, key_grad, value_grad, score = lax.cond(
            on_encoder, lambda: backward("enc"), lambda: backward("dec")
        )
        carry = (key_grad, value_grad)
        query_grads.append(query_grad)
        scores.append(score)
    self_send, self_keep = products(
        [normed_self.T, ml_turned],
        [0, 0, 0, 1],
        [query_grads, [key_grad], [value_grad], merged],
        own,
        parts,
        core,
    )
    down_steps.hop(scores[1])
    self_steps = Reduction(self_send, self_keep, dp_index)
    input_grad, gain_self_grad = input_gradient(
        rows_low,
        gain_self,
        w_qkv,
        query_grads,
        key_grad,
        value_grad,
        jnp.concatenate(grads_middle, axis=0),
        [self_send],
    )
    grad_own, grad_arrived = scatter_rows(input_grad, where_mp)

    tabs, diags = [], []
    deps = (self_send, input_grad, in_steps.hop(scores[1]), cross_steps.hop(self_send))
    for part in range(2):
        for quarter in range(2):
            tab, diag = lax.cond(
                on_encoder,
                lambda: table_sums("enc", part, quarter, coords, scores[part], quests, deps),
                lambda: table_sums("dec", part, quarter, coords, scores[part], quests, deps),
            )
            tabs.append(tab)
            diags.append(diag)
            if len(tabs) == 1:
                deps = (tab, self_steps.hop(tab), in_steps.arrived, down_steps.hop(tab))
            elif len(tabs) == 2:
                deps = (tab, cross_steps.hop(tab), grad_arrived)
            elif len(tabs) == 3:
                deps = (tab, self_steps.hop(tab), cross_steps.hop(tab), down_steps.hop(tab))
    table_grad = lax.cond(
        on_encoder,
        lambda: table_grads("enc", tabs, diags, span, quests, heads),
        lambda: table_grads("dec", tabs, diags, span, quests, heads),
    )
    table_grad = jnp.where(where_mp == 0, table_grad, jnp.roll(table_grad, heads // 2, axis=2))
    blank = jnp.zeros((width,), jnp.float32)
    gain_grad = jnp.where(
        on_encoder,
        jnp.stack([gain_self_grad, gain_ffn_grad, blank, blank, blank]),
        jnp.stack([blank, blank, gain_self_grad, gain_cross, gain_ffn_grad]),
    )
    small = jnp.concatenate([gain_grad.reshape(-1, LANES), table_grad.reshape(-1, LANES)], axis=0)
    count = small.shape[0]
    small = jnp.pad(small, ((0, -count % 8), (0, 0)))
    cross_shard, in_shard, down_shard = (x.finish(tabs[3]) for x in (cross_steps, in_steps, down_steps))
    small = sum_everywhere(after(small, self_steps.hop(tab), down_steps.arrived))
    gain_count = gain_grad.size // LANES
    gain_sum = small[:gain_count].reshape(gain_grad.shape)
    table_sum = small[gain_count:count].reshape(table_grad.shape)
    self_shard = self_steps.finish(table_grad)
    output_rows, grad_rows = (
        in_order(where_mp, own_rows[None], after(arrived, tabs[2]).astype(own_rows.dtype)[None], 0)
        for own_rows, arrived in ((output_own, output_arrived), (grad_own, grad_arrived))
    )
    return (
        output_rows[None, :, None],
        grad_rows[None, :, None],
        gain_sum[:4],
        gain_sum[4],
        table_sum,
        self_shard[:, : 3 * own].reshape(-1, 3, own)[None],
        self_shard[:, 3 * own :].T[None],
        in_shard[None],
        down_shard.T[None],
        cross_shard[:, :own],
        cross_shard[:, own : 3 * own].reshape(-1, 2, own),
        cross_shard[:, 3 * own :].T,
    )


def solution(mesh):
    return jax.shard_map(
        local,
        mesh=mesh,
        in_specs=(
            P("section", None, "dp", "mp", None),
            P("section", None, "dp", "mp", None),
            P(None, "dp"),
            P(None, "dp", None),
            P(None, "dp", None, None),
            P(),
            P(),
            P("section", None, None, "mp"),
            P("section", "mp", None),
            P("section", None, "mp"),
            P("section", "mp", None),
            P(None, "mp"),
            P(None, None, "mp"),
            P("mp", None),
        ),
        out_specs=(
            P("section", None, "dp", "mp", None),
            P("section", None, "dp", "mp", None),
            P(),
            P(),
            P(),
            P("section", "dp", None, "mp"),
            P("section", "mp", "dp"),
            P("section", "dp", "mp"),
            P("section", "mp", "dp"),
            P(("section", "dp"), "mp"),
            P(("section", "dp"), None, "mp"),
            P("mp", ("section", "dp")),
        ),
        check_vma=False,
    )
```

```python
import functools
from functools import partial
import math

import jax
import jax.numpy as jnp
from jax import lax
from jax.experimental import pallas as pl
from jax.experimental.pallas import tpu as pltpu
from jax.sharding import PartitionSpec as P

HEAD = 64
LANES = 128
NEGATIVE = -1e30
EPSILON = 1e-06
GELU_SCALE = math.sqrt(2 / math.pi)
GELU_CUBE = 0.044715
TI = 64
FFN_BLOCKS = 4
TR = 256
VMEM_LIMIT = 34 * 1024 * 1024
NT = (((1,), (1,)), ((), ()))
NN = (((1,), (0,)), ((), ()))


def edge_list(exact_span, bucket_count, far_reach):
    log_edges = [
        int(
            math.ceil(
                exact_span * (far_reach / exact_span) ** (power_index / (bucket_count - exact_span))
            )
        )
        for power_index in range(1, bucket_count - exact_span)
    ]
    return list(range(1, exact_span + 1)) + log_edges


def magnitude(distance, exact_span, bucket_count, far_reach):
    bucket = jnp.minimum(distance, exact_span)
    for threshold in edge_list(exact_span, bucket_count, far_reach)[exact_span:]:
        bucket = bucket + (distance >= threshold).astype(jnp.int32)
    return bucket


def two_sided(relative, far_reach):
    return magnitude(jnp.abs(relative), 8, 16, far_reach) + jnp.where(relative > 0, 16, 0)


def one_sided(relative):
    return magnitude(jnp.maximum(-relative, 0), 16, 32, 128)


def half_lanes(block, head):
    lane = lax.broadcasted_iota(jnp.int32, block.shape, 1)
    keep = lane < HEAD if head == 0 else lane >= HEAD
    return jnp.where(keep, block, jnp.zeros_like(block))


def dot(a, b, dims=NN):
    return lax.dot_general(a, b, dims, preferred_element_type=jnp.float32)


def pick_lanes(row, index):
    return jnp.take_along_axis(jnp.broadcast_to(row, index.shape), index, axis=1)


def pick_sublanes(table_ref, head, low, odd, upper):
    parts = [
        jnp.take_along_axis(table_ref[head, 8 * part : 8 * part + 8, :], low, axis=0)
        for part in range(4)
    ]
    return jnp.where(upper, jnp.where(odd, parts[3], parts[2]), jnp.where(odd, parts[1], parts[0]))


def fwd_kernel(kind, part, tq, span, heads, len_ref, tabn_ref, tabx_ref, taby_ref, crow_ref, ccol_ref, q_ref, *refs):
    count = (len(refs) - 7) // 2
    k_refs, v_refs = refs[:count], refs[count : 2 * count]
    o_ref, p_ref, s_ref, idx_ref, mask_ref, near_ref, bias_ref = refs[-7:]
    length = span // count
    pair = pl.program_id(0)
    first_block = 0 if kind == "dec" else part * tq // LANES
    chunk = 32

    @pl.when(pair == 0)
    def _():
        key = lax.broadcasted_iota(jnp.int32, (8, span), 1)
        limit = len_ref[1 + part] if kind == "dec" else len_ref[0]
        mask_ref[...] = jnp.where(key < limit, 0.0, NEGATIVE)
        if kind != "cross":
            def near_rows(r, carry):
                rows = pl.ds(pl.multiple_of(r * 8, 8), 8)
                query = r * 8 + lax.broadcasted_iota(jnp.int32, (8, LANES), 0)
                for d in range(-2, 3):
                    key = d * LANES + lax.broadcasted_iota(jnp.int32, (8, LANES), 1)
                    bucket = one_sided(key - query) if kind == "dec" else two_sided(key - query, 128)
                    for head in range(heads):
                        value = pick_lanes(tabn_ref[head : head + 1, :], bucket)
                        if kind == "dec":
                            value = jnp.where(key <= query, value, NEGATIVE)
                        near_ref[head, rows, (d + 2) * LANES : (d + 3) * LANES] = value
                return carry

            lax.fori_loop(0, LANES // 8, near_rows, 0)
        if kind == "enc":

            def bucket_rows(r, carry):
                rows = pl.ds(pl.multiple_of(r * chunk, chunk), chunk)
                for axis in range(2):
                    far = crow_ref[axis : axis + 1, :] - ccol_ref[rows, axis : axis + 1]
                    idx_ref[axis, rows, :] = two_sided(far, 500)
                return carry

            lax.fori_loop(0, tq // chunk, bucket_rows, 0)

            def bias_rows(r, carry):
                rows = pl.ds(pl.multiple_of(r * 8, 8), 8)
                for c in range(0, span, LANES):
                    lanes = slice(c, c + LANES)
                    across = idx_ref[0, rows, lanes]
                    upward = idx_ref[1, rows, lanes]
                    low, odd, upper = upward & 7, (upward & 8) != 0, upward >= 16
                    for head in range(heads):
                        bias_ref[head, rows, lanes] = pick_lanes(
                            tabx_ref[head : head + 1, :], across
                        ) + pick_sublanes(taby_ref, head, low, odd, upper)
                return carry

            lax.fori_loop(0, tq // 8, bias_rows, 0, unroll=4)

    for head in range(2):
        query = half_lanes(q_ref[...], head)
        for index, k_ref in enumerate(k_refs):
            s_ref[head, :, index * length : (index + 1) * length] = dot(query, k_ref[...], NT)
        for r in range(0, tq, chunk):
            rows = slice(r, r + chunk)
            pieces = []
            for c in range(0, span, LANES):
                lanes = slice(c, c + LANES)
                piece = s_ref[head, rows, lanes] + mask_ref[0:1, lanes]
                if kind != "cross":
                    apart = min(max(c // LANES - (first_block + r // LANES), -2), 2) + 2
                    near = slice(apart * LANES, (apart + 1) * LANES)
                    piece = piece + near_ref[2 * pair + head, r % LANES : r % LANES + chunk, near]
                if kind == "enc":
                    piece = piece + bias_ref[2 * pair + head, rows, lanes]
                pieces.append(piece)
            score = jnp.concatenate(pieces, axis=1)
            score = jnp.exp(score - jnp.max(score, axis=1, keepdims=True))
            score = score * (1.0 / jnp.sum(score, axis=1, keepdims=True))
            p_ref[head, rows, :] = score.astype(jnp.bfloat16)
    first, second = (
        sum(
            dot(p_ref[head, :, index * length : (index + 1) * length], v_ref[...])
            for index, v_ref in enumerate(v_refs)
        )
        for head in range(2)
    )
    lane = lax.broadcasted_iota(jnp.int32, first.shape, 1)
    o_ref[...] = jnp.where(lane < HEAD, first, second).astype(jnp.bfloat16)


def bwd_kernel(kind, part, rows, span, p_ref, do_ref, o_ref, q_ref, k_ref, v_ref, *refs):
    carry = refs[: 2 if kind != "cross" else 3] if part else ()
    outs = refs[len(carry) :]
    dq_ref, dk_ref, dv_ref = outs[:3]
    low_ref, dp_ref = outs[3:]
    chunk = 16
    q_t = jnp.transpose(q_ref[...].astype(jnp.float32)).astype(jnp.bfloat16)
    do_t = jnp.transpose(do_ref[...].astype(jnp.float32)).astype(jnp.bfloat16)
    grads, key_grads, value_grads = [], [], []
    for head in range(2):
        d_out = half_lanes(do_ref[...], head)
        delta = jnp.sum(d_out.astype(jnp.float32) * o_ref[...].astype(jnp.float32), axis=1, keepdims=True)
        dp_ref[head] = dot(d_out, v_ref[...], NT)
        for r in range(0, rows, chunk):
            part_rows = slice(r, r + chunk)
            prob = p_ref[head, part_rows, :].astype(jnp.float32)
            low_ref[head, part_rows, :] = (
                prob * (dp_ref[head, part_rows, :] - delta[part_rows, :])
            ).astype(jnp.bfloat16)
        grads.append(dot(low_ref[head], k_ref[...]))
        half = slice(head * HEAD, (head + 1) * HEAD)
        key_grads.append(dot(q_t[half], low_ref[head]))
        value_grads.append(dot(do_t[half], p_ref[head]))
    lane = lax.broadcasted_iota(jnp.int32, grads[0].shape, 1)
    query_grad = jnp.where(lane < HEAD, grads[0], grads[1])
    if kind == "cross" and part:
        query_grad = query_grad + carry[0][...]
    dq_ref[...] = query_grad.astype(dq_ref.dtype)
    for index, (out_ref, pieces) in enumerate(((dk_ref, key_grads), (dv_ref, value_grads))):
        grad = jnp.transpose(jnp.concatenate(pieces, axis=0))
        if kind == "enc" and part:
            grad = grad + carry[index][...]
        if kind == "dec":
            if part:
                out_ref[0:span, :] = carry[index][0:span, :].astype(out_ref.dtype)
            out_ref[part * span : (part + 1) * span, :] = grad.astype(out_ref.dtype)
        else:
            out_ref[...] = grad.astype(out_ref.dtype)


def table_kernel(kind, ti, span, heads, low_ref, crow_ref, ccol_ref, tab_ref, diag_ref, row_ref, wide_ref, idx_ref):
    step = pl.program_id(0)
    group = 16
    wide = diag_ref.shape[2]
    pad = wide - span

    @pl.when(step == 0)
    def _():
        tab_ref[...] = jnp.zeros_like(tab_ref)

    if kind == "enc":
        for r in range(0, ti, 16):
            for axis in range(2):
                far = crow_ref[axis : axis + 1, :] - ccol_ref[r : r + 16, axis : axis + 1]
                idx_ref[axis, r : r + 16, :] = two_sided(far, 500).astype(jnp.float32)
    out_row = lax.broadcasted_iota(jnp.int32, (256, 256), 0)
    in_row = lax.broadcasted_iota(jnp.int32, (256, 256), 1)
    swap = (lax.div(out_row, 16) == lax.rem(in_row, 16)) & (lax.rem(out_row, 16) == lax.div(in_row, 16))
    swap = jnp.where(swap, 1.0, 0.0).astype(jnp.bfloat16)
    blank = jnp.zeros(((16 - heads) * 16, span), jnp.bfloat16)
    which = lax.broadcasted_iota(jnp.int32, (32, span), 0).astype(jnp.bfloat16)

    tab = jnp.zeros(tab_ref.shape, jnp.float32)
    diag = jnp.zeros((16, wide), jnp.float32)
    for g in range(ti // group):
        first = g * group
        block = jnp.concatenate([low_ref[h, first : first + group, :] for h in range(heads)] + [blank], axis=0)
        wide_ref[g] = dot(swap, block)
        if kind == "enc":
            row_ref[g] = wide_ref[g].astype(jnp.bfloat16)
        for j in range(group):
            lines = slice(16 * j, 16 * j + 16)
            if kind == "enc":
                hot = []
                for axis in range(2):
                    bucket = idx_ref[axis, first + j : first + j + 1, :]
                    bucket = jnp.broadcast_to(bucket, (32, span)).astype(jnp.bfloat16)
                    hot.append(jnp.where(bucket == which, jnp.bfloat16(1), jnp.bfloat16(0)))
                tab = tab + dot(row_ref[g, lines, :], jnp.concatenate(hot, axis=0), NT)
            line = wide_ref[g, lines, :]
            if pad:
                line = jnp.concatenate([line, jnp.zeros((16, pad), jnp.float32)], axis=1)
            diag = diag + pltpu.roll(line, (wide - (first + j)) % wide, 1)
    tab_ref[...] += tab
    diag_ref[0] = diag


ANY = pl.BlockSpec(memory_space=pl.ANY)


def cost(flops, bytes_accessed, transcendentals):
    return pl.CostEstimate(flops=flops // 10, bytes_accessed=bytes_accessed // 10, transcendentals=transcendentals // 10)


def without(kernel, first, count):
    return lambda *refs: kernel(*refs[:first], *refs[first + count :])


def near_width(kind, ti, span):
    return span + ti if kind == "enc" else span


def diag_sums(kind, diag, starts):
    wide = diag.shape[2]
    column = lax.broadcasted_iota(jnp.int32, (len(starts), wide), 1)
    start = jnp.array(starts, jnp.int32)[:, None]
    if kind == "dec":
        bucket = one_sided(jnp.where(column > start, column - wide, column) - start)
    else:
        bucket = two_sided(jnp.where(column > wide - TI, column - wide, column) - start, 128)
    hot = (bucket[..., None] == lax.iota(jnp.int32, 32)).astype(jnp.float32)
    return jnp.einsum("swb,shw->bh", hot, diag, precision=lax.Precision.HIGHEST)


def forward_tables(kind, tables, heads):
    tab_n = tab_x = jnp.zeros((16, LANES), jnp.float32)
    tab_y = jnp.zeros((1, 8, LANES), jnp.float32)
    if kind != "cross":
        tab_n = jnp.pad(tables[0].T, ((0, 16 - heads), (0, LANES - 32)))
    if kind == "enc":
        tab_x = jnp.pad(tables[1].T, ((0, 16 - heads), (0, LANES - 32)))
        tab_y = jnp.broadcast_to(tables[2].T[:, :, None], (heads, 32, LANES))
    return tab_n, tab_x, tab_y


def attend_forward(kind, part, tq, lens, tables, coords, q_src, q_col, kv_srcs, k_col, v_col, pairs, quests, deps=()):
    heads = 2 * pairs
    key_rows = sum(kv_src.shape[0] for kv_src in kv_srcs)
    span = key_rows // quests if kind == "dec" else key_rows
    key_block = part if kind == "dec" else 0
    count = len(kv_srcs)
    flops = tq * span * (60000 if kind == "enc" else 25000)
    tab_n, tab_x, tab_y = tables
    coords, coords_t = coords
    return pl.pallas_call(
        without(partial(fwd_kernel, kind, part, tq, span, heads), 7 + 2 * count, len(deps)),
        grid=(pairs,),
        in_specs=[
            pl.BlockSpec(memory_space=pltpu.SMEM),
            pl.BlockSpec(tab_n.shape, lambda h: (0, 0)),
            pl.BlockSpec(tab_x.shape, lambda h: (0, 0)),
            pl.BlockSpec(tab_y.shape, lambda h: (0, 0, 0)),
            pl.BlockSpec(coords.shape, lambda h: (0, 0)),
            pl.BlockSpec((tq, 2), lambda h: (part, 0)),
            pl.BlockSpec((tq, LANES), lambda h: (part, q_col * pairs + h)),
        ]
        + [pl.BlockSpec((span // count, LANES), lambda h: (key_block, k_col * pairs + h))] * count
        + [pl.BlockSpec((span // count, LANES), lambda h: (key_block, v_col * pairs + h))] * count
        + [ANY] * len(deps),
        out_specs=[
            pl.BlockSpec((tq, LANES), lambda h: (0, h)),
            pl.BlockSpec((2, tq, span), lambda h: (h, 0, 0)),
        ],
        out_shape=[
            jax.ShapeDtypeStruct((tq, pairs * LANES), jnp.bfloat16),
            jax.ShapeDtypeStruct((heads, tq, key_rows), jnp.bfloat16),
        ],
        scratch_shapes=[
            pltpu.VMEM((2, tq, span), jnp.float32),
            pltpu.VMEM((2, tq, span) if kind == "enc" else (1, 8, LANES), jnp.int32),
            pltpu.VMEM((8, span), jnp.float32),
            pltpu.VMEM((1, 8, LANES) if kind == "cross" else (heads, LANES, 5 * LANES), jnp.float32),
            pltpu.VMEM((heads, tq, span) if kind == "enc" else (1, 8, LANES), jnp.float32),
        ],
        compiler_params=pltpu.CompilerParams(vmem_limit_bytes=(52 if kind == "enc" else 34) * 1024 * 1024),
        cost_estimate=cost(
            flops=flops, bytes_accessed=4 * tq * span * pairs, transcendentals=2 * tq * span * pairs
        ),
        name="attend_forward_" + kind,
    )(lens, tab_n, tab_x, tab_y, coords, coords_t, q_src, *kv_srcs, *kv_srcs, *deps)


def attend_backward(kind, part, prob, grad_out, out, q_src, q_col, kv_src, k_col, v_col, pairs, quests, carry=(), deps=()):
    rows = grad_out.shape[0]
    key_rows = 2 * kv_src.shape[0] if kind == "cross" else kv_src.shape[0]
    width = pairs * LANES
    span = key_rows if kind == "enc" else key_rows // 2
    key_block = part if kind == "dec" else 0
    query_block = 0 if kind == "cross" else part
    score_block = part if kind == "cross" else 0
    if kind == "cross":
        carried = [pl.BlockSpec((rows, LANES), lambda h: (0, h))] + [pl.BlockSpec(memory_space=pl.ANY)] * 2
        key_out = pl.BlockSpec((span, LANES), lambda h: (part, h))
        aliases = {7: 1, 8: 2} if part else {}
    else:
        carried = [pl.BlockSpec((key_rows, LANES), lambda h: (0, h))] * 2
        key_out = pl.BlockSpec((key_rows, LANES), lambda h: (0, h))
        aliases = {}
    query_type = jnp.float32 if kind == "cross" and not part else jnp.bfloat16
    key_type = jnp.bfloat16 if kind == "cross" or part else jnp.float32
    low_block = pl.BlockSpec((2, rows, span), (lambda h: (0, 0, 0)) if kind == "cross" else (lambda h: (h, 0, 0)))
    low_shape = (2, rows, span) if kind == "cross" else (2 * pairs, rows, key_rows)
    return pl.pallas_call(
        without(partial(bwd_kernel, kind, part, rows, span), 6 + len(carry), len(deps)),
        grid=(pairs,),
        in_specs=[
            pl.BlockSpec((2, rows, span), lambda h: (h, 0, score_block)),
            pl.BlockSpec((rows, LANES), lambda h: (0, h)),
            pl.BlockSpec((rows, LANES), lambda h: (0, h)),
            pl.BlockSpec((rows, LANES), lambda h: (query_block, q_col * pairs + h)),
            pl.BlockSpec((span, LANES), lambda h: (key_block, k_col * pairs + h)),
            pl.BlockSpec((span, LANES), lambda h: (key_block, v_col * pairs + h)),
        ]
        + carried[: len(carry)]
        + [ANY] * len(deps),
        out_specs=[
            pl.BlockSpec((rows, LANES), lambda h: (0, h)),
            key_out,
            key_out,
            low_block,
        ],
        out_shape=[
            jax.ShapeDtypeStruct((rows, width), query_type),
            jax.ShapeDtypeStruct((key_rows, width), key_type),
            jax.ShapeDtypeStruct((key_rows, width), key_type),
            jax.ShapeDtypeStruct(low_shape, jnp.bfloat16),
        ],
        scratch_shapes=[pltpu.VMEM((2, rows, span), jnp.float32)],
        input_output_aliases=aliases,
        compiler_params=pltpu.CompilerParams(vmem_limit_bytes=VMEM_LIMIT),
        cost_estimate=cost(
            flops=rows * span * 28000, bytes_accessed=4 * rows * span * pairs, transcendentals=0
        ),
        name="attend_backward_" + kind,
    )(prob, grad_out, out, q_src, kv_src, kv_src, *carry, *deps)


def table_sums(kind, part, quarter, coords, low, quests, deps=()):
    heads, rows, key_rows = low.shape
    rows = rows // 2
    span = key_rows // quests if kind == "dec" else key_rows
    steps = rows // TI
    wide = near_width(kind, TI, span)
    first = (2 * part + quarter) * steps
    tab, diag = pl.pallas_call(
        without(partial(table_kernel, kind, TI, span, heads), 3, len(deps)),
        grid=(steps,),
        in_specs=[
            pl.BlockSpec((heads, TI, span), lambda i: (0, quarter * steps + i, 0)),
            pl.BlockSpec(coords.shape, lambda i: (0, 0)),
            pl.BlockSpec((TI, 2), lambda i: (first + i, 0)),
        ]
        + [ANY] * len(deps),
        out_specs=[
            pl.BlockSpec((16, 64), lambda i: (0, 0)),
            pl.BlockSpec((1, 16, wide), lambda i: (i, 0, 0)),
        ],
        out_shape=[
            jax.ShapeDtypeStruct((16, 64), jnp.float32),
            jax.ShapeDtypeStruct((steps, 16, near_width("enc", TI, key_rows)), jnp.float32),
        ],
        scratch_shapes=[
            pltpu.VMEM((TI // 16, 256, span), jnp.bfloat16),
            pltpu.VMEM((TI // 16, 256, span), jnp.float32),
            pltpu.VMEM((2, TI, span) if kind == "enc" else (1, 8, LANES), jnp.float32),
        ],
        compiler_params=pltpu.CompilerParams(vmem_limit_bytes=VMEM_LIMIT),
        cost_estimate=cost(
            flops=rows * span * 40000, bytes_accessed=2 * heads * rows * span, transcendentals=0
        ),
        name="table_sums_" + kind,
    )(low, coords, coords.T, *deps)
    return tab, diag


def table_grads(kind, tabs, diags, rows, quests, heads):
    steps = diags[0].shape[0]
    starts = [step * TI for step in range(4 * steps)]
    diag = jnp.concatenate(diags, axis=0)
    if kind == "dec":
        span = rows // quests
        near = diag_sums(kind, diag[:, :, :span], [start % span for start in starts])[:, :heads]
        blank = jnp.zeros_like(near)
        return jnp.stack([blank, blank, blank, near])
    tab = sum(tabs)
    near = diag_sums(kind, diag, starts)[:, :heads]
    return jnp.stack([near, tab[:heads, :32].T, tab[:heads, 32:].T, jnp.zeros_like(near)])


def weight_copies(core, pieces, wi_ref, wd_ref, sems):
    in_own, in_far, in_near, down_own, down_far, down_near = pieces
    own = in_own.shape[1]
    block = own // 2
    rows_in, rows_down = in_far.shape[0], down_far.shape[0]
    far_in = pl.ds(pl.multiple_of(core * rows_in, rows_in), rows_in)
    near_in = pl.ds(pl.multiple_of((1 - core) * rows_in, rows_in), rows_in)
    far_down = pl.ds(pl.multiple_of(own + core * rows_down, rows_down), rows_down)
    near_down = pl.ds(pl.multiple_of(own + (1 - core) * rows_down, rows_down), rows_down)
    moves = []
    for b in range(2):
        part = slice(b * block, (b + 1) * block)
        moves.append((in_own.at[:, part], wi_ref.at[:, part]))
        moves.append((down_own.at[part, :], wd_ref.at[part, :]))
    other = slice(own, 2 * own)
    moves.append((in_far, wi_ref.at[far_in, other]))
    moves.append((in_near, wi_ref.at[near_in, other]))
    moves.append((down_far, wd_ref.at[far_down, :]))
    moves.append((down_near, wd_ref.at[near_down, :]))
    return [pltpu.make_async_copy(src, dst, sems.at[i]) for i, (src, dst) in enumerate(moves)]


def ffn_kernel(mode, part, flag_ref, *refs):
    pieces, refs = refs[:6], refs[6:]
    refs, (wi_ref, wd_ref, sems) = refs[:-3], refs[-3:]
    copies = weight_copies(flag_ref[0], pieces, wi_ref, wd_ref, sems)
    first_step = pl.program_id(0) == 0

    @pl.when(first_step)
    def _():
        for copy in copies:
            copy.start()
        for copy in copies:
            copy.wait()

    gain_ref, wa_ref = refs[:2]
    gain = gain_ref[0:1, :]
    if mode == "back":
        middle_ref, second_ref, own_ref, arrived_ref, more_ref, first_ref = refs[2:8]
        dx_ref, hn_ref, gl_ref, ml_ref, act_ref, dzo_ref, do_ref, dgain_ref, z_ref, du_ref = refs[-10:]
        on_encoder = flag_ref[2] == 0
        x = jnp.where(on_encoder, middle_ref[...], second_ref[...])
    else:
        base_ref, att_ref = refs[2:4]
        x = base_ref[...].astype(jnp.float32) + dot(att_ref[...], wa_ref[...])
        if mode == "fwd":
            out_ref, mid_ref, z_ref, u_ref = refs[4:]
        else:
            own_ref, arrived_ref, out_ref, mid_ref, dx_ref, low_ref, do_ref, z_ref, u_ref, du_ref, dz_ref = refs[4:]
        mid_ref[...] = x
    rows, width = x.shape
    hidden = wi_ref.shape[1]
    block, chunk = hidden // FFN_BLOCKS, 32
    if mode != "fwd":
        half = part if mode == "back" else lax.div(2 * pl.program_id(0), pl.num_programs(0))
        grad_low = jnp.where(half == flag_ref[1], own_ref[...], arrived_ref[...])
        grad = grad_low.astype(jnp.float32)
    scale = lax.rsqrt(jnp.mean(x * x, axis=1, keepdims=True) + EPSILON)
    normed_full = x * scale * gain
    normed = normed_full.astype(jnp.bfloat16)
    if mode == "back":
        grad = grad + more_ref[...].astype(jnp.float32)
        grad_low = grad.astype(jnp.bfloat16)
        hn_ref[...] = jnp.transpose(normed_full).astype(jnp.bfloat16)
        gl_ref[...] = jnp.transpose(grad).astype(jnp.bfloat16)
    total = jnp.zeros((rows, width), jnp.float32)
    back = jnp.zeros((rows, width), jnp.float32)
    for index in range(FFN_BLOCKS + 1):
        if index < FFN_BLOCKS:
            cols = slice(index * block, (index + 1) * block)
            z_ref[index % 2] = dot(normed, wi_ref[:, cols])
            if mode != "fwd":
                du_ref[index % 2] = dot(grad_low, wd_ref[cols, :], NT)
        if index == 0:
            continue
        slot = (index - 1) % 2
        cols = slice((index - 1) * block, index * block)
        for r in range(0, rows, chunk):
            lines = slice(r, r + chunk)
            z = z_ref[slot, lines, :]
            square = z * z
            tanh = jnp.tanh(z * (GELU_SCALE + GELU_SCALE * GELU_CUBE * square))
            half = 0.5 + 0.5 * tanh
            act = (z * half).astype(jnp.bfloat16)
            if mode == "back":
                act_ref[lines, cols] = act
            else:
                u_ref[slot, lines, :] = act
            if mode != "fwd":
                slope = half + z * (0.5 - 0.5 * tanh * tanh) * (GELU_SCALE + 3.0 * GELU_SCALE * GELU_CUBE * square)
                d_hidden = (du_ref[slot, lines, :] * slope).astype(jnp.bfloat16)
                if mode == "back":
                    dzo_ref[lines, cols] = d_hidden
                else:
                    dz_ref[slot, lines, :] = d_hidden
        if mode != "back":
            total = total + dot(u_ref[slot], wd_ref[cols, :])
        if mode == "back":
            back = back + dot(dzo_ref[:, cols], wi_ref[:, cols], NT)
        elif mode == "both":
            back = back + dot(dz_ref[slot], wi_ref[:, cols], NT)
    if mode != "back":
        out_ref[...] = (x + total).astype(jnp.bfloat16)
    if mode != "fwd":
        scaled = back * gain
        mean = jnp.mean(scaled * x, axis=1, keepdims=True)
        grad = grad + scale * scaled - x * (scale * scale * scale * mean)
        if mode == "back":
            grad = jnp.where(on_encoder, grad, first_ref[...])
            ml_ref[...] = jnp.transpose(grad).astype(jnp.bfloat16)
            gain_part = jnp.sum((back * x * scale).reshape(rows // 8, 8, width), axis=0)
            dgain_ref[...] = jnp.where(first_step, gain_part, dgain_ref[...] + gain_part)
        else:
            low_ref[...] = grad.astype(jnp.bfloat16)
        dx_ref[...] = grad
        do_ref[...] = dot(grad.astype(jnp.bfloat16), wa_ref[...], NT).astype(jnp.bfloat16)


def feed_forward(mode, part, rows, flags, pieces, gain, w_att, rows_in, held=(), deps=()):
    width = w_att.shape[0]
    hidden = 2 * pieces[0].shape[1]
    steps = rows // TR
    row_block = pl.BlockSpec((TR, width), lambda i: (i, 0))
    turned_block = pl.BlockSpec((width, TR), lambda i: (0, part * steps + i))
    hidden_block = pl.BlockSpec((TR, hidden), lambda i: (part * steps + i, 0))
    low = jax.ShapeDtypeStruct((rows, width), jnp.bfloat16)
    full = jax.ShapeDtypeStruct((rows, width), jnp.float32)
    turned = jax.ShapeDtypeStruct((width, 2 * rows), jnp.bfloat16)
    wide = jax.ShapeDtypeStruct((2 * rows, hidden), jnp.bfloat16)
    small = jax.ShapeDtypeStruct((8, width), jnp.float32)
    outs = {
        "fwd": ([row_block] * 2, [low, full]),
        "both": ([row_block] * 5, [low, full, full, low, low]),
        "back": (
            [row_block]
            + [turned_block] * 3
            + [hidden_block] * 2
            + [row_block, pl.BlockSpec((8, width), lambda i: (0, 0))],
            [full, turned, turned, turned, wide, wide, low, small],
        ),
    }[mode]
    slab = (2, TR, hidden // FFN_BLOCKS)
    slab32, slab16 = pltpu.VMEM(slab, jnp.float32), pltpu.VMEM(slab, jnp.bfloat16)
    scratch = {"fwd": [slab32, slab16], "both": [slab32, slab16, slab32, slab16], "back": [slab32, slab32]}[mode]
    matmuls = {"fwd": 2, "both": 4, "back": 3}[mode]
    inputs = 9 + len(rows_in)
    return pl.pallas_call(
        without(partial(ffn_kernel, mode, part), inputs, len(held) + len(deps)),
        grid=(steps,),
        in_specs=[pl.BlockSpec(memory_space=pltpu.SMEM)]
        + [ANY] * 6
        + [pl.BlockSpec((8, width), lambda i: (0, 0)), pl.BlockSpec(w_att.shape, lambda i: (0, 0))]
        + [pl.BlockSpec((TR, width), lambda i, at=at, turn=turn: (at + i % turn, 0)) for _, at, turn in rows_in]
        + [ANY] * (len(held) + len(deps)),
        out_specs=outs[0],
        out_shape=outs[1],
        scratch_shapes=scratch
        + [
            pltpu.VMEM((width, hidden), jnp.bfloat16),
            pltpu.VMEM((hidden, width), jnp.bfloat16),
            pltpu.SemaphoreType.DMA((8,)),
        ],
        input_output_aliases={inputs + index: 1 + index for index in range(len(held))},
        compiler_params=pltpu.CompilerParams(vmem_limit_bytes=VMEM_LIMIT),
        cost_estimate=cost(
            flops=4 * matmuls * rows * width * hidden,
            bytes_accessed=4 * width * hidden + 8 * rows * width,
            transcendentals=rows * hidden,
        ),
        name="feed_forward_" + mode,
    )(flags, *pieces, jnp.broadcast_to(gain[None], (8, width)), w_att, *(x for x, _, _ in rows_in), *held, *deps)


def product_kernel(left_of, parts_of, slices, which, core_ref, *refs):
    left_count, count = max(left_of) + 1, sum(parts_of)
    lefts, rights = refs[:left_count], refs[left_count : left_count + count]
    outs, held_ref = refs[left_count + count : -1], refs[-1]
    step = pl.program_id(0)
    rows, span = lefts[0].shape
    size = rows // slices
    half = rows // 2

    @pl.when(step == 0)
    def _():
        for index, left in enumerate(lefts):
            if len(outs) == 1:
                held_ref[index] = left[...]
                continue
            for first, core in ((0, 1 - core_ref[0]), (half, core_ref[0])):
                for part in range(slices // 2):
                    source = pl.ds(pl.multiple_of((2 * part + core) * size, 16), size)
                    held_ref[index, first + part * size : first + (part + 1) * size, :] = left[source, :]

    def product(index, lines):
        parts = rights[sum(parts_of[:index]) : sum(parts_of[: index + 1])]
        length = span // len(parts)
        return sum(
            dot(held_ref[left_of[index], lines, part * length : (part + 1) * length], right[...])
            for part, right in enumerate(parts)
        ).astype(jnp.bfloat16)

    for index in range(len(parts_of)):
        steps = [s for s, owner in enumerate(which) if owner == index]
        chosen = functools.reduce(lambda a, b: a | b, [step == s for s in steps])

        @pl.when(chosen)
        def _(index=index):
            if len(outs) == 1:
                outs[0][...] = product(index, slice(0, rows))
            else:
                outs[0][...] = product(index, slice(0, half))
                outs[1][...] = product(index, slice(half, rows))


def products(lefts, left_of, rights, block, slices, core, deps=()):
    rows, span = lefts[0].shape
    parts_of = [len(right) for right in rights]
    counts = [right[0].shape[1] // (2 * block) for right in rights]
    which, place = [], []
    for half in range(2):
        for index, number in enumerate(counts):
            for b in range(number):
                which.append(index)
                place.append(half * number + b)
    maps = []
    for index, right in enumerate(rights):
        held, column_of = 0, []
        for s, owner in enumerate(which):
            if owner == index:
                held = place[s]
            column_of.append(held)
        maps += [column_of] * len(right)
    steps = len(which)
    total = steps * block

    def right_map(column_of):
        def index_map(s):
            value = 0
            for position in range(steps):
                if column_of[position]:
                    value = value + jnp.where(s == position, column_of[position], 0)
            return (0, value)

        return index_map

    size = rows // slices
    apart = size % 16 == 0
    out_rows = rows // 2 if apart else rows
    out = jax.ShapeDtypeStruct((out_rows, total), jnp.bfloat16)
    flat = [part for right in rights for part in right]
    results = pl.pallas_call(
        without(
            partial(product_kernel, left_of, parts_of, slices, which), 1 + len(lefts) + len(flat), len(deps)
        ),
        grid=(steps,),
        in_specs=[pl.BlockSpec(memory_space=pltpu.SMEM)]
        + [pl.BlockSpec((rows, span), lambda s: (0, 0)) for _ in lefts]
        + [pl.BlockSpec((part.shape[0], block), right_map(column_of)) for part, column_of in zip(flat, maps)]
        + [ANY] * len(deps),
        out_specs=[pl.BlockSpec((out_rows, block), lambda s: (0, s))] * (2 if apart else 1),
        out_shape=[out] * (2 if apart else 1),
        scratch_shapes=[pltpu.VMEM((len(lefts), rows, span), jnp.bfloat16)],
        compiler_params=pltpu.CompilerParams(vmem_limit_bytes=VMEM_LIMIT),
        cost_estimate=cost(
            flops=2 * span * rows * total, bytes_accessed=2 * (span + rows) * total, transcendentals=0
        ),
        name="weight_products",
    )(core.reshape(1), *lefts, *flat, *deps)
    if apart:
        return results
    cut = results[0].reshape(slices // 2, 2, size, total)
    return pick(cut, 1 - core, 1).reshape(-1, total), pick(cut, core, 1).reshape(-1, total)


def nothing(shapes):
    return pl.pallas_call(
        lambda *refs: None, out_shape=shapes, out_specs=[ANY] * len(shapes), name="nothing"
    )()


def input_kernel(gain_ref, w_ref, x_ref, first_ref, second_ref, dk_ref, dv_ref, ahead_ref, behind_ref, out_ref, dgain_ref):
    step = pl.program_id(0)
    gain = gain_ref[0:1, :]
    rows, width = x_ref.shape
    in_first = 2 * step < pl.num_programs(0)
    d_query = jnp.where(in_first, first_ref[...], second_ref[...])
    back = dot(d_query, w_ref[:, :width], NT)
    back = back + dot(dk_ref[...], w_ref[:, width : 2 * width], NT)
    back = back + dot(dv_ref[...], w_ref[:, 2 * width :], NT)
    x = x_ref[...].astype(jnp.float32)
    scale = lax.rsqrt(jnp.mean(x * x, axis=1, keepdims=True) + EPSILON)
    scaled = back * gain
    mean = jnp.mean(scaled * x, axis=1, keepdims=True)
    grad = jnp.where(in_first, ahead_ref[...], behind_ref[...])
    out_ref[...] = grad + scale * scaled - x * (scale * scale * scale * mean)
    gain_part = jnp.sum((back * x * scale).reshape(rows // 8, 8, width), axis=0)
    dgain_ref[...] = jnp.where(step == 0, gain_part, dgain_ref[...] + gain_part)


def input_gradient(x, gain, w_qkv, query_grads, key_grad, value_grad, grads, deps):
    rows, width = x.shape
    steps = rows // TR
    row_block = pl.BlockSpec((TR, width), lambda i: (i, 0))
    half_block = pl.BlockSpec((TR, width), lambda i: (i % (steps // 2), 0))
    fixed = pl.BlockSpec((8, width), lambda i: (0, 0))
    out, dgain = pl.pallas_call(
        without(input_kernel, 9, len(deps)),
        grid=(steps,),
        in_specs=[fixed, pl.BlockSpec(w_qkv.shape, lambda i: (0, 0)), row_block, half_block, half_block]
        + [row_block] * 2
        + [half_block] * 2
        + [ANY] * len(deps),
        out_specs=[row_block, fixed],
        out_shape=[jax.ShapeDtypeStruct((rows, width), jnp.float32), jax.ShapeDtypeStruct((8, width), jnp.float32)],
        compiler_params=pltpu.CompilerParams(vmem_limit_bytes=VMEM_LIMIT),
        cost_estimate=cost(
            flops=6 * rows * width * width, bytes_accessed=16 * rows * width, transcendentals=0
        ),
        name="input_gradient",
    )(jnp.broadcast_to(gain[None], (8, width)), w_qkv, x, *query_grads, key_grad, value_grad, *grads, *deps)
    return out, jnp.sum(dgain, axis=0)


def sum_kernel(rounds, x_ref, out_ref, *refs):
    slots, send_sems, recv_sems = refs[: len(rounds)], refs[len(rounds)], refs[len(rounds) + 1]
    barrier = pltpu.get_barrier_semaphore()
    places, peers = [], []
    for axes in rounds:
        place, count = 0, 1
        for axis in axes:
            place = place * lax.axis_size(axis) + lax.axis_index(axis)
            count = count * lax.axis_size(axis)
        found = []
        for step in range(1, count):
            rest, device = lax.rem(place + step, count), {}
            for axis in reversed(axes):
                device[axis] = lax.rem(rest, lax.axis_size(axis))
                rest = lax.div(rest, lax.axis_size(axis))
            found.append(device)
        places.append(place)
        peers.append(found)
    for device in peers[0] + peers[1]:
        pl.semaphore_signal(barrier, inc=1, device_id=device, device_id_type=pl.DeviceIdType.MESH)
    pl.semaphore_wait(barrier, len(peers[0]) + len(peers[1]))
    value = x_ref[...]
    first = 0
    for slot, place, found in zip(slots, places, peers):
        slot[place] = value
        copies = []
        for step, device in enumerate(found):
            copies.append(
                pltpu.make_async_remote_copy(
                    src_ref=slot.at[place],
                    dst_ref=slot.at[place],
                    send_sem=send_sems.at[first + step],
                    recv_sem=recv_sems.at[first + step],
                    device_id=device,
                    device_id_type=pl.DeviceIdType.MESH,
                )
            )
        for copy in copies:
            copy.start()
        for copy in copies:
            copy.wait()
        first += len(found)
        value = slot[0]
        for index in range(1, len(found) + 1):
            value = value + slot[index]
    out_ref[...] = value


def sum_everywhere(x):
    rounds = (("dp",), ("section", "mp"))
    counts = [math.prod(lax.axis_size(axis) for axis in axes) for axes in rounds]
    copies = sum(counts) - len(counts)
    return pl.pallas_call(
        partial(sum_kernel, rounds),
        out_shape=jax.ShapeDtypeStruct(x.shape, x.dtype),
        in_specs=[pl.BlockSpec(memory_space=pltpu.VMEM)],
        out_specs=pl.BlockSpec(memory_space=pltpu.VMEM),
        scratch_shapes=[pltpu.VMEM((count,) + x.shape, x.dtype) for count in counts]
        + [pltpu.SemaphoreType.DMA((copies,)), pltpu.SemaphoreType.DMA((copies,))],
        compiler_params=pltpu.CompilerParams(collective_id=0, has_side_effects=True),
        name="sum_everywhere",
    )(x)


def pair_permute(x, axis, bit):
    pairs = [(i, i ^ (1 << bit)) for i in range(lax.axis_size(axis))]
    return lax.ppermute(x, axis, pairs)


def shifted(x, axis, by):
    peers = lax.axis_size(axis)
    pairs = [(i, i + by) for i in range(peers) if 0 <= i + by < peers]
    return lax.ppermute(x, axis, pairs)


def in_order(flag, first, second, axis):
    return jnp.where(
        flag == 0,
        jnp.concatenate([first, second], axis=axis),
        jnp.concatenate([second, first], axis=axis),
    )


def pick(x, index, axis):
    return lax.dynamic_index_in_dim(x, index, axis, False)


def after(values, *others):
    return lax.optimization_barrier((values, others))[0]


def exchange_rows(block, where_mp):
    return pick(block, where_mp, 0), pair_permute(pick(block, 1 - where_mp, 0), "mp", 0)


def scatter_rows(rows, where_mp):
    half = rows.shape[0] // 2
    send = lax.dynamic_slice_in_dim(rows, (1 - where_mp) * half, half, 0).astype(jnp.bfloat16)
    return lax.dynamic_slice_in_dim(rows, where_mp * half, half, 0), pair_permute(send, "mp", 0)


def fetch_far(shard, core):
    half = shard.shape[0] // 2
    return pair_permute(lax.dynamic_slice_in_dim(shard, core * half, half, 0), "mp", 0)


def fetch_near(far):
    return pair_permute(far, "dp", 0)


def fetch_other(shard, dp_index):
    quarter = shard.shape[0] // 4
    far = pair_permute(lax.dynamic_slice_in_dim(shard, (dp_index & 3) * quarter, quarter, 0), "mp", 0)
    half = in_order(dp_index & 1, far, pair_permute(far, "dp", 0), 0)
    return in_order((dp_index >> 1) & 1, half, pair_permute(half, "dp", 1), 0), far


class Reduction:
    def __init__(self, send, keep, dp_index, section=None):
        self.total, self.arrived = keep, pair_permute(send, "dp", 0)
        self.dp_index = dp_index
        bits = lax.axis_size("dp").bit_length() - 1
        self.left = ([("section", section)] if section is not None else []) + [("mp", None)]
        self.left += [("dp", bit) for bit in range(1, bits)]

    def joined(self, cut):
        return cut(self.total).astype(jnp.float32) + cut(self.arrived).astype(jnp.float32)

    def hop(self, *ties):
        brought = self.arrived
        self.arrived = after(self.arrived, *ties)
        axis, which = self.left.pop(0)
        rows, width = self.total.shape
        if axis == "section":
            send = self.joined(lambda x: x[: rows // 2]).astype(jnp.bfloat16)
            keep = jnp.where(which == 0, 0.0, self.joined(lambda x: x[rows // 2 :]))
            self.total, self.arrived = keep, shifted(send, "section", -1)
        elif axis == "mp":
            send = self.joined(lambda x: x[:, width // 2 :]).astype(jnp.bfloat16)
            self.total, self.arrived = self.joined(lambda x: x[:, : width // 2]), pair_permute(send, "mp", 0)
        else:
            mark = (self.dp_index >> which) & 1
            halves = (lax.axis_size("dp") >> (which + 1), 2, -1, width)
            send = self.joined(lambda x: pick(x.reshape(halves), 1 - mark, 1)).astype(jnp.bfloat16)
            keep = self.joined(lambda x: pick(x.reshape(halves), mark, 1))
            self.total = keep.reshape(-1, width)
            self.arrived = pair_permute(send.reshape(-1, width), "dp", which)
        return brought

    def finish(self, *ties):
        while self.left:
            self.hop()
        self.arrived = after(self.arrived, *ties)
        return self.joined(lambda x: x)


def rms_norm(inputs, gain_row):
    return (
        inputs * lax.rsqrt(jnp.mean(inputs * inputs, axis=-1, keepdims=True) + EPSILON) * gain_row
    )


def norm_back(rows, gain_row, grad_normed):
    return jax.vjp(rms_norm, rows, gain_row)[1](grad_normed)


def low(x):
    return x.astype(jnp.bfloat16)


def local(
    block_input,
    out_cotangent,
    doc_lengths,
    question_lengths,
    coordinates,
    gains,
    bias_tables,
    self_qkv,
    self_out,
    ffn_in,
    ffn_out,
    cross_q,
    cross_kv,
    cross_out,
):
    section = lax.axis_index("section")
    on_encoder = section == 0
    dp_index = lax.axis_index("dp")
    core = dp_index & 1
    where_mp = lax.axis_index("mp")
    width = block_input.shape[4]
    quests = question_lengths.shape[2]
    own = self_qkv.shape[3]
    pairs = 2 * own // LANES
    heads = 2 * pairs
    parts = lax.axis_size("dp")
    flags = jnp.stack([core, where_mp, section]).astype(jnp.int32)

    rows_low = in_order(where_mp, *exchange_rows(block_input[0, :, 0], where_mp), 0)
    qkv_own = self_qkv[0].reshape(width, -1)
    qkv_other, qkv_far = fetch_other(qkv_own, dp_index)
    w_qkv = jnp.concatenate(
        [x[:, t * own : (t + 1) * own] for t in range(3) for x in (qkv_own, qkv_other)], axis=1
    )
    owned = after((ffn_in[0], ffn_out[0], self_out[0]), rows_low, qkv_far)
    fars = [fetch_far(x, core) for x in owned]

    lens = jnp.concatenate(
        [pick(doc_lengths, where_mp, 0), pick(question_lengths, where_mp, 0)[0]]
    ).astype(jnp.int32)
    coords = pick(coordinates, where_mp, 0)[0]
    tables = jnp.where(where_mp == 0, bias_tables, jnp.roll(bias_tables, heads // 2, axis=2))

    enc_tables, dec_tables = forward_tables("enc", tables[:3], heads), forward_tables("dec", tables[3:], heads)
    coords_both = (coords, coords.T)

    rows = rows_low.astype(jnp.float32)
    span = rows.shape[0]
    half = span // 2
    turn = half // TR
    halves = (slice(0, half), slice(half, span))
    gain_self = jnp.where(on_encoder, gains[0], gains[2])
    normed_self = low(rms_norm(rows, gain_self))
    projected = low(dot(normed_self, w_qkv))
    merged, probs, middles, memories, arrivals = [], [], [], [], []
    for part in range(2):
        deps = memories[:1]

        def forward(kind, chosen):
            return attend_forward(
                kind, part, half, lens, chosen, coords_both, projected, 0, [projected], 1, 2, pairs, quests, deps
            )

        out, prob = lax.cond(on_encoder, lambda: forward("enc", enc_tables), lambda: forward("dec", dec_tables))
        if not part:
            fars = after(fars, out)
            nears = [fetch_near(x) for x in fars]
            w_out = jnp.concatenate([self_out[0], in_order(core, fars[2], nears[2], 0)], axis=0)
            pieces = (ffn_in[0], fars[0], nears[0], ffn_out[0], fars[1], nears[1])
            cross_owned = after(
                (jnp.concatenate([cross_q, cross_kv.reshape(width, -1)], axis=1), cross_out, out_cotangent[0, :, 0]), fars
            )
            cross_fars = [fetch_far(x, core) for x in cross_owned[:2]]
            cot = exchange_rows(cross_owned[2], where_mp)
        else:
            cross_fars = after(cross_fars, out)
        memory, middle = feed_forward(
            "fwd", part, half, flags, pieces, gains[1], w_out, [(rows_low, part * turn, turn), (out, 0, turn)]
        )
        arrivals.append(shifted(memory, "section", 1))
        merged.append(out)
        probs.append(prob)
        middles.append(middle)
        memories.append(memory)
    query_other, cross_other = (in_order(core, far, fetch_near(far), 0) for far in cross_fars)
    w_query = jnp.concatenate([cross_q, query_other[:, :own]], axis=1)
    w_pair = jnp.concatenate(
        [x for t in range(2) for x in (cross_kv[:, t], query_other[:, (t + 1) * own : (t + 2) * own])], axis=1
    )
    w_cross = jnp.concatenate([cross_out, cross_other], axis=0)
    middle = jnp.concatenate(middles, axis=0)

    normed_cross = low(rms_norm(middle, gains[3]))
    queries = low(dot(normed_cross, w_query))
    first_pair = low(dot(arrivals[0], w_pair))
    arrivals[1] = after(arrivals[1], queries, first_pair)
    pair_rows = [first_pair, low(dot(arrivals[1], w_pair))]
    cross_merged, cross_prob = attend_forward(
        "cross", 0, span, lens, forward_tables("cross", None, heads), coords_both, queries, 0, pair_rows, 0, 1, pairs, quests
    )
    output_low, second, grad_second, second_low, cross_grad = feed_forward(
        "both",
        0,
        span,
        flags,
        pieces,
        gains[4],
        w_cross,
        [(middle, 0, 2 * turn), (cross_merged, 0, 2 * turn), (cot[0], 0, turn), (cot[1], 0, turn)],
    )
    output_own, output_arrived = scatter_rows(
        jnp.where(on_encoder, jnp.concatenate(memories, axis=0), output_low), where_mp
    )
    returns, returned, carry = [], [], ()
    for part in range(2):
        query_grad, key_grad, value_grad, _ = attend_backward(
            "cross",
            part,
            cross_prob,
            cross_grad,
            cross_merged,
            queries,
            0,
            pair_rows[part],
            0,
            1,
            pairs,
            quests,
            carry,
            [returns[0], output_arrived] if part else [],
        )
        carry = (query_grad, key_grad, value_grad)
        returns.append(
            low(
                dot(key_grad[halves[part]], w_pair[:, : 2 * own], NT)
                + dot(value_grad[halves[part]], w_pair[:, 2 * own :], NT)
            )
        )
        returned.append(shifted(returns[part], "section", -1))
    query_cross = after(query_grad, returns[1])

    def cross_norm():
        input_part, gain_part = norm_back(middle, gains[3], dot(query_cross, w_query, NT))
        return grad_second + input_part, gain_part

    def no_norm():
        return tuple(
            nothing([jax.ShapeDtypeStruct((span, width), jnp.float32), jax.ShapeDtypeStruct((width,), jnp.float32)])
        )

    grad_first, gain_cross = lax.cond(on_encoder, no_norm, cross_norm)

    gain_ffn = jnp.where(on_encoder, gains[1], gains[4])
    held, gain_ffn_grad, grads_middle, merged_grads = [], 0.0, [], []
    for part in range(2):
        if part:
            returned[1] = after(returned[1], grads_middle[0])
        grad_middle, *held, merged_grad, gain_part = feed_forward(
            "back",
            part,
            half,
            flags,
            pieces,
            gain_ffn,
            w_out,
            [
                (middles[part], 0, turn),
                (second, part * turn, turn),
                (cot[0], 0, turn),
                (cot[1], 0, turn),
                (returned[part], 0, turn),
                (grad_first, part * turn, turn),
            ],
            held,
        )
        gain_ffn_grad = gain_ffn_grad + jnp.sum(gain_part, axis=0)
        grads_middle.append(grad_middle)
        merged_grads.append(merged_grad)
    hn_turned, gl_turned, ml_turned, activated, hidden_grad = held
    in_send, in_keep = products([hn_turned], [0], [[hidden_grad]], 2 * own, parts, core)
    down_send, down_keep = products([gl_turned], [0], [[activated]], 2 * own, parts, core, [in_send])
    in_steps = Reduction(in_send, in_keep, dp_index)
    down_steps = Reduction(down_send, down_keep, dp_index)

    def cross_products():
        return tuple(
            products(
                [normed_cross.T, jnp.concatenate(arrivals, axis=0).T, second_low.T],
                [0, 1, 1, 2],
                [[query_cross], [key_grad], [value_grad], [cross_merged]],
                own,
                2 * parts,
                core,
                [down_send],
            )
        )

    def no_products():
        blank = jax.ShapeDtypeStruct((width // 2, 8 * own), jnp.bfloat16)
        return tuple(nothing([blank, blank]))

    cross_send, cross_keep = lax.cond(on_encoder, no_products, cross_products)
    cross_steps = Reduction(cross_send, cross_keep, dp_index, section)
    scores, query_grads, carry = [], [], ()
    for part in range(2):
        if part:
            deps = (in_steps.hop(), down_steps.arrived, cross_steps.hop())
        else:
            deps = (down_send, cross_send, in_steps.hop())

        def backward(kind):
            return attend_backward(
                kind, part, probs[part], merged_grads[part], merged[part], projected, 0, projected, 1, 2, pairs, quests,
                carry, deps
            )

        query_grad, key_grad, value_grad, score = lax.cond(
            on_encoder, lambda: backward("enc"), lambda: backward("dec")
        )
        carry = (key_grad, value_grad)
        query_grads.append(query_grad)
        scores.append(score)
    self_send, self_keep = products(
        [normed_self.T, ml_turned],
        [0, 0, 0, 1],
        [query_grads, [key_grad], [value_grad], merged],
        own,
        parts,
        core,
    )
    down_steps.hop(scores[1])
    self_steps = Reduction(self_send, self_keep, dp_index)
    input_grad, gain_self_grad = input_gradient(
        rows_low,
        gain_self,
        w_qkv,
        query_grads,
        key_grad,
        value_grad,
        grads_middle,
        [self_send],
    )
    grad_own, grad_arrived = scatter_rows(input_grad, where_mp)

    tabs, diags = [], []
    deps = (self_send, input_grad, in_steps.hop(scores[1]), cross_steps.hop(self_send))
    for part in range(2):
        for quarter in range(2):
            tab, diag = lax.cond(
                on_encoder,
                lambda: table_sums("enc", part, quarter, coords, scores[part], quests, deps),
                lambda: table_sums("dec", part, quarter, coords, scores[part], quests, deps),
            )
            tabs.append(tab)
            diags.append(diag)
            if len(tabs) == 1:
                deps = (tab, self_steps.hop(tab), in_steps.arrived, down_steps.hop(tab))
            elif len(tabs) == 2:
                deps = (tab, cross_steps.hop(tab), grad_arrived)
            elif len(tabs) == 3:
                deps = (tab, self_steps.hop(tab), cross_steps.hop(tab), down_steps.hop(tab))
    table_grad = lax.cond(
        on_encoder,
        lambda: table_grads("enc", tabs, diags, span, quests, heads),
        lambda: table_grads("dec", tabs, diags, span, quests, heads),
    )
    table_grad = jnp.where(where_mp == 0, table_grad, jnp.roll(table_grad, heads // 2, axis=2))
    blank = jnp.zeros((width,), jnp.float32)
    gain_grad = jnp.where(
        on_encoder,
        jnp.stack([gain_self_grad, gain_ffn_grad, blank, blank, blank]),
        jnp.stack([blank, blank, gain_self_grad, gain_cross, gain_ffn_grad]),
    )
    small = jnp.concatenate([gain_grad.reshape(-1, LANES), table_grad.reshape(-1, LANES)], axis=0)
    count = small.shape[0]
    small = jnp.pad(small, ((0, -count % 8), (0, 0)))
    cross_shard, in_shard, down_shard = (x.finish(tabs[3]) for x in (cross_steps, in_steps, down_steps))
    small = sum_everywhere(after(small, self_steps.hop(tab), down_steps.arrived))
    gain_count = gain_grad.size // LANES
    gain_sum = small[:gain_count].reshape(gain_grad.shape)
    table_sum = small[gain_count:count].reshape(table_grad.shape)
    self_shard = self_steps.finish(table_grad)
    output_rows, grad_rows = (
        in_order(where_mp, own_rows[None], after(arrived, tabs[2]).astype(own_rows.dtype)[None], 0)
        for own_rows, arrived in ((output_own, output_arrived), (grad_own, grad_arrived))
    )
    return (
        output_rows[None, :, None],
        grad_rows[None, :, None],
        gain_sum[:4],
        gain_sum[4],
        table_sum,
        self_shard[:, : 3 * own].reshape(-1, 3, own)[None],
        self_shard[:, 3 * own :].T[None],
        in_shard[None],
        down_shard.T[None],
        cross_shard[:, :own],
        cross_shard[:, own : 3 * own].reshape(-1, 2, own),
        cross_shard[:, 3 * own :].T,
    )


def solution(mesh):
    return jax.shard_map(
        local,
        mesh=mesh,
        in_specs=(
            P("section", None, "dp", "mp", None),
            P("section", None, "dp", "mp", None),
            P(None, "dp"),
            P(None, "dp", None),
            P(None, "dp", None, None),
            P(),
            P(),
            P("section", None, None, "mp"),
            P("section", "mp", None),
            P("section", None, "mp"),
            P("section", "mp", None),
            P(None, "mp"),
            P(None, None, "mp"),
            P("mp", None),
        ),
        out_specs=(
            P("section", None, "dp", "mp", None),
            P("section", None, "dp", "mp", None),
            P(),
            P(),
            P(),
            P("section", "dp", None, "mp"),
            P("section", "mp", "dp"),
            P("section", "dp", "mp"),
            P("section", "mp", "dp"),
            P(("section", "dp"), "mp"),
            P(("section", "dp"), None, "mp"),
            P("mp", ("section", "dp")),
        ),
        check_vma=False,
    )
```

```python
import functools
from functools import partial
import math

import jax
import jax.numpy as jnp
from jax import lax
from jax.experimental import pallas as pl
from jax.experimental.pallas import tpu as pltpu
from jax.sharding import PartitionSpec as P

HEAD = 64
LANES = 128
NEGATIVE = -1e30
EPSILON = 1e-06
GELU_SCALE = math.sqrt(2 / math.pi)
GELU_CUBE = 0.044715
TI = 64
FFN_BLOCKS = 4
TR = 256
VMEM_LIMIT = 28 * 1024 * 1024
NT = (((1,), (1,)), ((), ()))
NN = (((1,), (0,)), ((), ()))


def edge_list(exact_span, bucket_count, far_reach):
    log_edges = [
        int(
            math.ceil(
                exact_span * (far_reach / exact_span) ** (power_index / (bucket_count - exact_span))
            )
        )
        for power_index in range(1, bucket_count - exact_span)
    ]
    return list(range(1, exact_span + 1)) + log_edges


def magnitude(distance, exact_span, bucket_count, far_reach):
    bucket = jnp.minimum(distance, exact_span)
    for threshold in edge_list(exact_span, bucket_count, far_reach)[exact_span:]:
        bucket = bucket + (distance >= threshold).astype(jnp.int32)
    return bucket


def two_sided(relative, far_reach):
    return magnitude(jnp.abs(relative), 8, 16, far_reach) + jnp.where(relative > 0, 16, 0)


def one_sided(relative):
    return magnitude(jnp.maximum(-relative, 0), 16, 32, 128)


def half_lanes(block, head):
    lane = lax.broadcasted_iota(jnp.int32, block.shape, 1)
    keep = lane < HEAD if head == 0 else lane >= HEAD
    return jnp.where(keep, block, jnp.zeros_like(block))


def dot(a, b, dims=NN):
    return lax.dot_general(a, b, dims, preferred_element_type=jnp.float32)


def pick_lanes(row, index):
    return jnp.take_along_axis(jnp.broadcast_to(row, index.shape), index, axis=1)


def pick_sublanes(table_ref, head, low, odd, upper):
    parts = [
        jnp.take_along_axis(table_ref[head, 8 * part : 8 * part + 8, :], low, axis=0)
        for part in range(4)
    ]
    return jnp.where(upper, jnp.where(odd, parts[3], parts[2]), jnp.where(odd, parts[1], parts[0]))


def fwd_kernel(kind, part, tq, span, heads, len_ref, tabn_ref, tabx_ref, taby_ref, crow_ref, ccol_ref, q_ref, *refs):
    count = (len(refs) - 7) // 2
    k_refs, v_refs = refs[:count], refs[count : 2 * count]
    o_ref, p_ref, s_ref, idx_ref, mask_ref, near_ref, bias_ref = refs[-7:]
    length = span // count
    pair = pl.program_id(0)
    first_block = 0 if kind == "dec" else part * tq // LANES
    chunk = 32

    @pl.when(pair == 0)
    def _():
        key = lax.broadcasted_iota(jnp.int32, (8, span), 1)
        limit = len_ref[1 + part] if kind == "dec" else len_ref[0]
        mask_ref[...] = jnp.where(key < limit, 0.0, NEGATIVE)
        if kind != "cross":
            def near_rows(r, carry):
                rows = pl.ds(pl.multiple_of(r * 8, 8), 8)
                query = r * 8 + lax.broadcasted_iota(jnp.int32, (8, LANES), 0)
                for d in range(-2, 3):
                    key = d * LANES + lax.broadcasted_iota(jnp.int32, (8, LANES), 1)
                    bucket = one_sided(key - query) if kind == "dec" else two_sided(key - query, 128)
                    for head in range(heads):
                        value = pick_lanes(tabn_ref[head : head + 1, :], bucket)
                        if kind == "dec":
                            value = jnp.where(key <= query, value, NEGATIVE)
                        near_ref[head, rows, (d + 2) * LANES : (d + 3) * LANES] = value
                return carry

            lax.fori_loop(0, LANES // 8, near_rows, 0)
        if kind == "enc":

            def bucket_rows(r, carry):
                rows = pl.ds(pl.multiple_of(r * chunk, chunk), chunk)
                for axis in range(2):
                    far = crow_ref[axis : axis + 1, :] - ccol_ref[rows, axis : axis + 1]
                    idx_ref[axis, rows, :] = two_sided(far, 500)
                return carry

            lax.fori_loop(0, tq // chunk, bucket_rows, 0)

            def bias_rows(r, carry):
                rows = pl.ds(pl.multiple_of(r * 8, 8), 8)
                for c in range(0, span, LANES):
                    lanes = slice(c, c + LANES)
                    across = idx_ref[0, rows, lanes]
                    upward = idx_ref[1, rows, lanes]
                    low, odd, upper = upward & 7, (upward & 8) != 0, upward >= 16
                    for head in range(heads):
                        bias_ref[head, rows, lanes] = pick_lanes(
                            tabx_ref[head : head + 1, :], across
                        ) + pick_sublanes(taby_ref, head, low, odd, upper)
                return carry

            lax.fori_loop(0, tq // 8, bias_rows, 0, unroll=4)

    for head in range(2):
        query = half_lanes(q_ref[...], head)
        for index, k_ref in enumerate(k_refs):
            s_ref[head, :, index * length : (index + 1) * length] = dot(query, k_ref[...], NT)
        for r in range(0, tq, chunk):
            rows = slice(r, r + chunk)
            pieces = []
            for c in range(0, span, LANES):
                lanes = slice(c, c + LANES)
                piece = s_ref[head, rows, lanes] + mask_ref[0:1, lanes]
                if kind != "cross":
                    apart = min(max(c // LANES - (first_block + r // LANES), -2), 2) + 2
                    near = slice(apart * LANES, (apart + 1) * LANES)
                    piece = piece + near_ref[2 * pair + head, r % LANES : r % LANES + chunk, near]
                if kind == "enc":
                    piece = piece + bias_ref[2 * pair + head, rows, lanes]
                pieces.append(piece)
            score = jnp.concatenate(pieces, axis=1)
            score = jnp.exp(score - jnp.max(score, axis=1, keepdims=True))
            score = score * (1.0 / jnp.sum(score, axis=1, keepdims=True))
            p_ref[head, rows, :] = score.astype(jnp.bfloat16)
    first, second = (
        sum(
            dot(p_ref[head, :, index * length : (index + 1) * length], v_ref[...])
            for index, v_ref in enumerate(v_refs)
        )
        for head in range(2)
    )
    lane = lax.broadcasted_iota(jnp.int32, first.shape, 1)
    o_ref[...] = jnp.where(lane < HEAD, first, second).astype(jnp.bfloat16)


def bwd_kernel(kind, part, rows, span, p_ref, do_ref, o_ref, q_ref, k_ref, v_ref, *refs):
    carry = refs[: 2 if kind != "cross" else 3] if part else ()
    outs = refs[len(carry) :]
    dq_ref, dk_ref, dv_ref = outs[:3]
    low_ref, dp_ref = outs[3:]
    chunk = 16
    q_t = jnp.transpose(q_ref[...].astype(jnp.float32)).astype(jnp.bfloat16)
    do_t = jnp.transpose(do_ref[...].astype(jnp.float32)).astype(jnp.bfloat16)
    grads, key_grads, value_grads = [], [], []
    for head in range(2):
        d_out = half_lanes(do_ref[...], head)
        delta = jnp.sum(d_out.astype(jnp.float32) * o_ref[...].astype(jnp.float32), axis=1, keepdims=True)
        dp_ref[head] = dot(d_out, v_ref[...], NT)
        for r in range(0, rows, chunk):
            part_rows = slice(r, r + chunk)
            prob = p_ref[head, part_rows, :].astype(jnp.float32)
            low_ref[head, part_rows, :] = (
                prob * (dp_ref[head, part_rows, :] - delta[part_rows, :])
            ).astype(jnp.bfloat16)
        grads.append(dot(low_ref[head], k_ref[...]))
        half = slice(head * HEAD, (head + 1) * HEAD)
        key_grads.append(dot(q_t[half], low_ref[head]))
        value_grads.append(dot(do_t[half], p_ref[head]))
    lane = lax.broadcasted_iota(jnp.int32, grads[0].shape, 1)
    query_grad = jnp.where(lane < HEAD, grads[0], grads[1])
    if kind == "cross" and part:
        query_grad = query_grad + carry[0][...]
    dq_ref[...] = query_grad.astype(dq_ref.dtype)
    for index, (out_ref, pieces) in enumerate(((dk_ref, key_grads), (dv_ref, value_grads))):
        grad = jnp.transpose(jnp.concatenate(pieces, axis=0))
        if kind == "enc" and part:
            grad = grad + carry[index][...]
        if kind == "dec":
            if part:
                out_ref[0:span, :] = carry[index][0:span, :].astype(out_ref.dtype)
            out_ref[part * span : (part + 1) * span, :] = grad.astype(out_ref.dtype)
        else:
            out_ref[...] = grad.astype(out_ref.dtype)


def table_kernel(kind, ti, span, heads, low_ref, crow_ref, ccol_ref, tab_ref, diag_ref, row_ref, wide_ref, idx_ref):
    step = pl.program_id(0)
    group = 16
    wide = diag_ref.shape[2]
    pad = wide - span

    @pl.when(step == 0)
    def _():
        tab_ref[...] = jnp.zeros_like(tab_ref)

    if kind == "enc":
        for r in range(0, ti, 16):
            for axis in range(2):
                far = crow_ref[axis : axis + 1, :] - ccol_ref[r : r + 16, axis : axis + 1]
                idx_ref[axis, r : r + 16, :] = two_sided(far, 500).astype(jnp.float32)
    out_row = lax.broadcasted_iota(jnp.int32, (256, 256), 0)
    in_row = lax.broadcasted_iota(jnp.int32, (256, 256), 1)
    swap = (lax.div(out_row, 16) == lax.rem(in_row, 16)) & (lax.rem(out_row, 16) == lax.div(in_row, 16))
    swap = jnp.where(swap, 1.0, 0.0).astype(jnp.bfloat16)
    blank = jnp.zeros(((16 - heads) * 16, span), jnp.bfloat16)
    which = lax.broadcasted_iota(jnp.int32, (32, span), 0).astype(jnp.bfloat16)

    tab = jnp.zeros(tab_ref.shape, jnp.float32)
    diag = jnp.zeros((16, wide), jnp.float32)
    for g in range(ti // group):
        first = g * group
        block = jnp.concatenate([low_ref[h, first : first + group, :] for h in range(heads)] + [blank], axis=0)
        wide_ref[g] = dot(swap, block)
        if kind == "enc":
            row_ref[g] = wide_ref[g].astype(jnp.bfloat16)
        for j in range(group):
            lines = slice(16 * j, 16 * j + 16)
            if kind == "enc":
                hot = []
                for axis in range(2):
                    bucket = idx_ref[axis, first + j : first + j + 1, :]
                    bucket = jnp.broadcast_to(bucket, (32, span)).astype(jnp.bfloat16)
                    hot.append(jnp.where(bucket == which, jnp.bfloat16(1), jnp.bfloat16(0)))
                tab = tab + dot(row_ref[g, lines, :], jnp.concatenate(hot, axis=0), NT)
            line = wide_ref[g, lines, :]
            if pad:
                line = jnp.concatenate([line, jnp.zeros((16, pad), jnp.float32)], axis=1)
            diag = diag + pltpu.roll(line, (wide - (first + j)) % wide, 1)
    tab_ref[...] += tab
    diag_ref[0] = diag


ANY = pl.BlockSpec(memory_space=pl.ANY)


def cost(flops, bytes_accessed, transcendentals):
    return pl.CostEstimate(flops=flops // 10, bytes_accessed=bytes_accessed // 10, transcendentals=transcendentals // 10)


def without(kernel, first, count):
    return lambda *refs: kernel(*refs[:first], *refs[first + count :])


def near_width(kind, ti, span):
    return span + ti if kind == "enc" else span


def diag_sums(kind, diag, starts):
    wide = diag.shape[2]
    column = lax.broadcasted_iota(jnp.int32, (len(starts), wide), 1)
    start = jnp.array(starts, jnp.int32)[:, None]
    if kind == "dec":
        bucket = one_sided(jnp.where(column > start, column - wide, column) - start)
    else:
        bucket = two_sided(jnp.where(column > wide - TI, column - wide, column) - start, 128)
    hot = (bucket[..., None] == lax.iota(jnp.int32, 32)).astype(jnp.float32)
    return jnp.einsum("swb,shw->bh", hot, diag, precision=lax.Precision.HIGHEST)


def forward_tables(kind, tables, heads):
    tab_n = tab_x = jnp.zeros((16, LANES), jnp.float32)
    tab_y = jnp.zeros((1, 8, LANES), jnp.float32)
    if kind != "cross":
        tab_n = jnp.pad(tables[0].T, ((0, 16 - heads), (0, LANES - 32)))
    if kind == "enc":
        tab_x = jnp.pad(tables[1].T, ((0, 16 - heads), (0, LANES - 32)))
        tab_y = jnp.broadcast_to(tables[2].T[:, :, None], (heads, 32, LANES))
    return tab_n, tab_x, tab_y


def attend_forward(kind, part, tq, lens, tables, coords, q_src, q_col, kv_srcs, k_col, v_col, pairs, quests, deps=()):
    heads = 2 * pairs
    key_rows = sum(kv_src.shape[0] for kv_src in kv_srcs)
    span = key_rows // quests if kind == "dec" else key_rows
    key_block = part if kind == "dec" else 0
    count = len(kv_srcs)
    flops = tq * span * (60000 if kind == "enc" else 25000)
    tab_n, tab_x, tab_y = tables
    coords, coords_t = coords
    return pl.pallas_call(
        without(partial(fwd_kernel, kind, part, tq, span, heads), 7 + 2 * count, len(deps)),
        grid=(pairs,),
        in_specs=[
            pl.BlockSpec(memory_space=pltpu.SMEM),
            pl.BlockSpec(tab_n.shape, lambda h: (0, 0)),
            pl.BlockSpec(tab_x.shape, lambda h: (0, 0)),
            pl.BlockSpec(tab_y.shape, lambda h: (0, 0, 0)),
            pl.BlockSpec(coords.shape, lambda h: (0, 0)),
            pl.BlockSpec((tq, 2), lambda h: (part, 0)),
            pl.BlockSpec((tq, LANES), lambda h: (part, q_col * pairs + h)),
        ]
        + [pl.BlockSpec((span // count, LANES), lambda h: (key_block, k_col * pairs + h))] * count
        + [pl.BlockSpec((span // count, LANES), lambda h: (key_block, v_col * pairs + h))] * count
        + [ANY] * len(deps),
        out_specs=[
            pl.BlockSpec((tq, LANES), lambda h: (0, h)),
            pl.BlockSpec((2, tq, span), lambda h: (h, 0, 0)),
        ],
        out_shape=[
            jax.ShapeDtypeStruct((tq, pairs * LANES), jnp.bfloat16),
            jax.ShapeDtypeStruct((heads, tq, key_rows), jnp.bfloat16),
        ],
        scratch_shapes=[
            pltpu.VMEM((2, tq, span), jnp.float32),
            pltpu.VMEM((2, tq, span) if kind == "enc" else (1, 8, LANES), jnp.int32),
            pltpu.VMEM((8, span), jnp.float32),
            pltpu.VMEM((1, 8, LANES) if kind == "cross" else (heads, LANES, 5 * LANES), jnp.float32),
            pltpu.VMEM((heads, tq, span) if kind == "enc" else (1, 8, LANES), jnp.float32),
        ],
        compiler_params=pltpu.CompilerParams(vmem_limit_bytes=(48 if kind == "enc" else 28) * 1024 * 1024),
        cost_estimate=cost(
            flops=flops, bytes_accessed=4 * tq * span * pairs, transcendentals=2 * tq * span * pairs
        ),
        name="attend_forward_" + kind,
    )(lens, tab_n, tab_x, tab_y, coords, coords_t, q_src, *kv_srcs, *kv_srcs, *deps)


def attend_backward(kind, part, prob, grad_out, out, q_src, q_col, kv_src, k_col, v_col, pairs, quests, carry=(), deps=()):
    rows = grad_out.shape[0]
    key_rows = 2 * kv_src.shape[0] if kind == "cross" else kv_src.shape[0]
    width = pairs * LANES
    span = key_rows if kind == "enc" else key_rows // 2
    key_block = part if kind == "dec" else 0
    query_block = 0 if kind == "cross" else part
    score_block = part if kind == "cross" else 0
    if kind == "cross":
        carried = [pl.BlockSpec((rows, LANES), lambda h: (0, h))] + [pl.BlockSpec(memory_space=pl.ANY)] * 2
        key_out = pl.BlockSpec((span, LANES), lambda h: (part, h))
        aliases = {7: 1, 8: 2} if part else {}
    else:
        carried = [pl.BlockSpec((key_rows, LANES), lambda h: (0, h))] * 2
        key_out = pl.BlockSpec((key_rows, LANES), lambda h: (0, h))
        aliases = {}
    query_type = jnp.float32 if kind == "cross" and not part else jnp.bfloat16
    key_type = jnp.bfloat16 if kind == "cross" or part else jnp.float32
    low_block = pl.BlockSpec((2, rows, span), (lambda h: (0, 0, 0)) if kind == "cross" else (lambda h: (h, 0, 0)))
    low_shape = (2, rows, span) if kind == "cross" else (2 * pairs, rows, key_rows)
    return pl.pallas_call(
        without(partial(bwd_kernel, kind, part, rows, span), 6 + len(carry), len(deps)),
        grid=(pairs,),
        in_specs=[
            pl.BlockSpec((2, rows, span), lambda h: (h, 0, score_block)),
            pl.BlockSpec((rows, LANES), lambda h: (0, h)),
            pl.BlockSpec((rows, LANES), lambda h: (0, h)),
            pl.BlockSpec((rows, LANES), lambda h: (query_block, q_col * pairs + h)),
            pl.BlockSpec((span, LANES), lambda h: (key_block, k_col * pairs + h)),
            pl.BlockSpec((span, LANES), lambda h: (key_block, v_col * pairs + h)),
        ]
        + carried[: len(carry)]
        + [ANY] * len(deps),
        out_specs=[
            pl.BlockSpec((rows, LANES), lambda h: (0, h)),
            key_out,
            key_out,
            low_block,
        ],
        out_shape=[
            jax.ShapeDtypeStruct((rows, width), query_type),
            jax.ShapeDtypeStruct((key_rows, width), key_type),
            jax.ShapeDtypeStruct((key_rows, width), key_type),
            jax.ShapeDtypeStruct(low_shape, jnp.bfloat16),
        ],
        scratch_shapes=[pltpu.VMEM((2, rows, span), jnp.float32)],
        input_output_aliases=aliases,
        compiler_params=pltpu.CompilerParams(vmem_limit_bytes=VMEM_LIMIT),
        cost_estimate=cost(
            flops=rows * span * 28000, bytes_accessed=4 * rows * span * pairs, transcendentals=0
        ),
        name="attend_backward_" + kind,
    )(prob, grad_out, out, q_src, kv_src, kv_src, *carry, *deps)


def table_sums(kind, part, quarter, coords, low, quests, deps=()):
    heads, rows, key_rows = low.shape
    rows = rows // 2
    span = key_rows // quests if kind == "dec" else key_rows
    steps = rows // TI
    wide = near_width(kind, TI, span)
    first = (2 * part + quarter) * steps
    tab, diag = pl.pallas_call(
        without(partial(table_kernel, kind, TI, span, heads), 3, len(deps)),
        grid=(steps,),
        in_specs=[
            pl.BlockSpec((heads, TI, span), lambda i: (0, quarter * steps + i, 0)),
            pl.BlockSpec(coords.shape, lambda i: (0, 0)),
            pl.BlockSpec((TI, 2), lambda i: (first + i, 0)),
        ]
        + [ANY] * len(deps),
        out_specs=[
            pl.BlockSpec((16, 64), lambda i: (0, 0)),
            pl.BlockSpec((1, 16, wide), lambda i: (i, 0, 0)),
        ],
        out_shape=[
            jax.ShapeDtypeStruct((16, 64), jnp.float32),
            jax.ShapeDtypeStruct((steps, 16, near_width("enc", TI, key_rows)), jnp.float32),
        ],
        scratch_shapes=[
            pltpu.VMEM((TI // 16, 256, span), jnp.bfloat16),
            pltpu.VMEM((TI // 16, 256, span), jnp.float32),
            pltpu.VMEM((2, TI, span) if kind == "enc" else (1, 8, LANES), jnp.float32),
        ],
        compiler_params=pltpu.CompilerParams(vmem_limit_bytes=VMEM_LIMIT),
        cost_estimate=cost(
            flops=rows * span * 40000, bytes_accessed=2 * heads * rows * span, transcendentals=0
        ),
        name="table_sums_" + kind,
    )(low, coords, coords.T, *deps)
    return tab, diag


def table_grads(kind, tabs, diags, rows, quests, heads):
    steps = diags[0].shape[0]
    starts = [step * TI for step in range(4 * steps)]
    diag = jnp.concatenate(diags, axis=0)
    if kind == "dec":
        span = rows // quests
        near = diag_sums(kind, diag[:, :, :span], [start % span for start in starts])[:, :heads]
        blank = jnp.zeros_like(near)
        return jnp.stack([blank, blank, blank, near])
    tab = sum(tabs)
    near = diag_sums(kind, diag, starts)[:, :heads]
    return jnp.stack([near, tab[:heads, :32].T, tab[:heads, 32:].T, jnp.zeros_like(near)])


def weight_copies(core, pieces, wi_ref, wd_ref, sems):
    in_own, in_far, in_near, down_own, down_far, down_near = pieces
    own = in_own.shape[1]
    block = own // 2
    rows_in, rows_down = in_far.shape[0], down_far.shape[0]
    far_in = pl.ds(pl.multiple_of(core * rows_in, rows_in), rows_in)
    near_in = pl.ds(pl.multiple_of((1 - core) * rows_in, rows_in), rows_in)
    far_down = pl.ds(pl.multiple_of(own + core * rows_down, rows_down), rows_down)
    near_down = pl.ds(pl.multiple_of(own + (1 - core) * rows_down, rows_down), rows_down)
    moves = []
    for b in range(2):
        part = slice(b * block, (b + 1) * block)
        moves.append((in_own.at[:, part], wi_ref.at[:, part]))
        moves.append((down_own.at[part, :], wd_ref.at[part, :]))
    other = slice(own, 2 * own)
    moves.append((in_far, wi_ref.at[far_in, other]))
    moves.append((in_near, wi_ref.at[near_in, other]))
    moves.append((down_far, wd_ref.at[far_down, :]))
    moves.append((down_near, wd_ref.at[near_down, :]))
    return [pltpu.make_async_copy(src, dst, sems.at[i]) for i, (src, dst) in enumerate(moves)]


def ffn_kernel(mode, part, flag_ref, *refs):
    pieces, refs = refs[:6], refs[6:]
    refs, (wi_ref, wd_ref, sems) = refs[:-3], refs[-3:]
    copies = weight_copies(flag_ref[0], pieces, wi_ref, wd_ref, sems)
    first_step = pl.program_id(0) == 0

    @pl.when(first_step)
    def _():
        for copy in copies:
            copy.start()
        for copy in copies:
            copy.wait()

    gain_ref, wa_ref = refs[:2]
    gain = gain_ref[0:1, :]
    if mode == "back":
        middle_ref, second_ref, own_ref, arrived_ref, more_ref, first_ref = refs[2:8]
        dx_ref, hn_ref, gl_ref, ml_ref, act_ref, dzo_ref, do_ref, dgain_ref, z_ref, du_ref = refs[-10:]
        on_encoder = flag_ref[2] == 0
        x = jnp.where(on_encoder, middle_ref[...], second_ref[...])
    else:
        base_ref, att_ref = refs[2:4]
        x = base_ref[...].astype(jnp.float32) + dot(att_ref[...], wa_ref[...])
        if mode == "fwd":
            out_ref, mid_ref, z_ref, u_ref = refs[4:]
        else:
            own_ref, arrived_ref, out_ref, mid_ref, dx_ref, low_ref, do_ref, z_ref, u_ref, du_ref, dz_ref = refs[4:]
        mid_ref[...] = x
    rows, width = x.shape
    hidden = wi_ref.shape[1]
    block, chunk = hidden // FFN_BLOCKS, 32
    if mode != "fwd":
        half = part if mode == "back" else lax.div(2 * pl.program_id(0), pl.num_programs(0))
        grad_low = jnp.where(half == flag_ref[1], own_ref[...], arrived_ref[...])
        grad = grad_low.astype(jnp.float32)
    scale = lax.rsqrt(jnp.mean(x * x, axis=1, keepdims=True) + EPSILON)
    normed_full = x * scale * gain
    normed = normed_full.astype(jnp.bfloat16)
    if mode == "back":
        grad = grad + more_ref[...].astype(jnp.float32)
        grad_low = grad.astype(jnp.bfloat16)
        hn_ref[...] = jnp.transpose(normed_full).astype(jnp.bfloat16)
        gl_ref[...] = jnp.transpose(grad).astype(jnp.bfloat16)
    total = jnp.zeros((rows, width), jnp.float32)
    back = jnp.zeros((rows, width), jnp.float32)
    for index in range(FFN_BLOCKS + 1):
        if index < FFN_BLOCKS:
            cols = slice(index * block, (index + 1) * block)
            z_ref[index % 2] = dot(normed, wi_ref[:, cols])
            if mode != "fwd":
                du_ref[index % 2] = dot(grad_low, wd_ref[cols, :], NT)
        if index == 0:
            continue
        slot = (index - 1) % 2
        cols = slice((index - 1) * block, index * block)
        for r in range(0, rows, chunk):
            lines = slice(r, r + chunk)
            z = z_ref[slot, lines, :]
            square = z * z
            tanh = jnp.tanh(z * (GELU_SCALE + GELU_SCALE * GELU_CUBE * square))
            half = 0.5 + 0.5 * tanh
            act = (z * half).astype(jnp.bfloat16)
            if mode == "back":
                act_ref[lines, cols] = act
            else:
                u_ref[slot, lines, :] = act
            if mode != "fwd":
                slope = half + z * (0.5 - 0.5 * tanh * tanh) * (GELU_SCALE + 3.0 * GELU_SCALE * GELU_CUBE * square)
                d_hidden = (du_ref[slot, lines, :] * slope).astype(jnp.bfloat16)
                if mode == "back":
                    dzo_ref[lines, cols] = d_hidden
                else:
                    dz_ref[slot, lines, :] = d_hidden
        if mode != "back":
            total = total + dot(u_ref[slot], wd_ref[cols, :])
        if mode == "back":
            back = back + dot(dzo_ref[:, cols], wi_ref[:, cols], NT)
        elif mode == "both":
            back = back + dot(dz_ref[slot], wi_ref[:, cols], NT)
    if mode != "back":
        out_ref[...] = (x + total).astype(jnp.bfloat16)
    if mode != "fwd":
        scaled = back * gain
        mean = jnp.mean(scaled * x, axis=1, keepdims=True)
        grad = grad + scale * scaled - x * (scale * scale * scale * mean)
        if mode == "back":
            grad = jnp.where(on_encoder, grad, first_ref[...])
            ml_ref[...] = jnp.transpose(grad).astype(jnp.bfloat16)
            gain_part = jnp.sum((back * x * scale).reshape(rows // 8, 8, width), axis=0)
            dgain_ref[...] = jnp.where(first_step, gain_part, dgain_ref[...] + gain_part)
        else:
            low_ref[...] = grad.astype(jnp.bfloat16)
        dx_ref[...] = grad
        do_ref[...] = dot(grad.astype(jnp.bfloat16), wa_ref[...], NT).astype(jnp.bfloat16)


def feed_forward(mode, part, rows, flags, pieces, gain, w_att, rows_in, held=(), deps=()):
    width = w_att.shape[0]
    hidden = 2 * pieces[0].shape[1]
    steps = rows // TR
    row_block = pl.BlockSpec((TR, width), lambda i: (i, 0))
    turned_block = pl.BlockSpec((width, TR), lambda i: (0, part * steps + i))
    hidden_block = pl.BlockSpec((TR, hidden), lambda i: (part * steps + i, 0))
    low = jax.ShapeDtypeStruct((rows, width), jnp.bfloat16)
    full = jax.ShapeDtypeStruct((rows, width), jnp.float32)
    turned = jax.ShapeDtypeStruct((width, 2 * rows), jnp.bfloat16)
    wide = jax.ShapeDtypeStruct((2 * rows, hidden), jnp.bfloat16)
    small = jax.ShapeDtypeStruct((8, width), jnp.float32)
    outs = {
        "fwd": ([row_block] * 2, [low, full]),
        "both": ([row_block] * 5, [low, full, full, low, low]),
        "back": (
            [row_block]
            + [turned_block] * 3
            + [hidden_block] * 2
            + [row_block, pl.BlockSpec((8, width), lambda i: (0, 0))],
            [full, turned, turned, turned, wide, wide, low, small],
        ),
    }[mode]
    slab = (2, TR, hidden // FFN_BLOCKS)
    slab32, slab16 = pltpu.VMEM(slab, jnp.float32), pltpu.VMEM(slab, jnp.bfloat16)
    scratch = {"fwd": [slab32, slab16], "both": [slab32, slab16, slab32, slab16], "back": [slab32, slab32]}[mode]
    matmuls = {"fwd": 2, "both": 4, "back": 3}[mode]
    inputs = 9 + len(rows_in)
    return pl.pallas_call(
        without(partial(ffn_kernel, mode, part), inputs, len(held) + len(deps)),
        grid=(steps,),
        in_specs=[pl.BlockSpec(memory_space=pltpu.SMEM)]
        + [ANY] * 6
        + [pl.BlockSpec((8, width), lambda i: (0, 0)), pl.BlockSpec(w_att.shape, lambda i: (0, 0))]
        + [pl.BlockSpec((TR, width), lambda i, at=at, turn=turn: (at + i % turn, 0)) for _, at, turn in rows_in]
        + [ANY] * (len(held) + len(deps)),
        out_specs=outs[0],
        out_shape=outs[1],
        scratch_shapes=scratch
        + [
            pltpu.VMEM((width, hidden), jnp.bfloat16),
            pltpu.VMEM((hidden, width), jnp.bfloat16),
            pltpu.SemaphoreType.DMA((8,)),
        ],
        input_output_aliases={inputs + index: 1 + index for index in range(len(held))},
        compiler_params=pltpu.CompilerParams(vmem_limit_bytes=VMEM_LIMIT),
        cost_estimate=cost(
            flops=4 * matmuls * rows * width * hidden,
            bytes_accessed=4 * width * hidden + 8 * rows * width,
            transcendentals=rows * hidden,
        ),
        name="feed_forward_" + mode,
    )(flags, *pieces, jnp.broadcast_to(gain[None], (8, width)), w_att, *(x for x, _, _ in rows_in), *held, *deps)


def product_kernel(left_of, parts_of, slices, which, core_ref, *refs):
    left_count, count = max(left_of) + 1, sum(parts_of)
    lefts, rights = refs[:left_count], refs[left_count : left_count + count]
    outs, held_ref = refs[left_count + count : -1], refs[-1]
    step = pl.program_id(0)
    rows, span = lefts[0].shape
    size = rows // slices
    half = rows // 2

    @pl.when(step == 0)
    def _():
        for index, left in enumerate(lefts):
            if len(outs) == 1:
                held_ref[index] = left[...]
                continue
            for first, core in ((0, 1 - core_ref[0]), (half, core_ref[0])):
                for part in range(slices // 2):
                    source = pl.ds(pl.multiple_of((2 * part + core) * size, 16), size)
                    held_ref[index, first + part * size : first + (part + 1) * size, :] = left[source, :]

    def product(index, lines):
        parts = rights[sum(parts_of[:index]) : sum(parts_of[: index + 1])]
        length = span // len(parts)
        return sum(
            dot(held_ref[left_of[index], lines, part * length : (part + 1) * length], right[...])
            for part, right in enumerate(parts)
        ).astype(jnp.bfloat16)

    for index in range(len(parts_of)):
        steps = [s for s, owner in enumerate(which) if owner == index]
        chosen = functools.reduce(lambda a, b: a | b, [step == s for s in steps])

        @pl.when(chosen)
        def _(index=index):
            if len(outs) == 1:
                outs[0][...] = product(index, slice(0, rows))
            else:
                outs[0][...] = product(index, slice(0, half))
                outs[1][...] = product(index, slice(half, rows))


def products(lefts, left_of, rights, block, slices, core, deps=()):
    rows, span = lefts[0].shape
    parts_of = [len(right) for right in rights]
    counts = [right[0].shape[1] // (2 * block) for right in rights]
    which, place = [], []
    for half in range(2):
        for index, number in enumerate(counts):
            for b in range(number):
                which.append(index)
                place.append(half * number + b)
    maps = []
    for index, right in enumerate(rights):
        held, column_of = 0, []
        for s, owner in enumerate(which):
            if owner == index:
                held = place[s]
            column_of.append(held)
        maps += [column_of] * len(right)
    steps = len(which)
    total = steps * block

    def right_map(column_of):
        def index_map(s):
            value = 0
            for position in range(steps):
                if column_of[position]:
                    value = value + jnp.where(s == position, column_of[position], 0)
            return (0, value)

        return index_map

    size = rows // slices
    apart = size % 16 == 0
    out_rows = rows // 2 if apart else rows
    out = jax.ShapeDtypeStruct((out_rows, total), jnp.bfloat16)
    flat = [part for right in rights for part in right]
    results = pl.pallas_call(
        without(
            partial(product_kernel, left_of, parts_of, slices, which), 1 + len(lefts) + len(flat), len(deps)
        ),
        grid=(steps,),
        in_specs=[pl.BlockSpec(memory_space=pltpu.SMEM)]
        + [pl.BlockSpec((rows, span), lambda s: (0, 0)) for _ in lefts]
        + [pl.BlockSpec((part.shape[0], block), right_map(column_of)) for part, column_of in zip(flat, maps)]
        + [ANY] * len(deps),
        out_specs=[pl.BlockSpec((out_rows, block), lambda s: (0, s))] * (2 if apart else 1),
        out_shape=[out] * (2 if apart else 1),
        scratch_shapes=[pltpu.VMEM((len(lefts), rows, span), jnp.bfloat16)],
        compiler_params=pltpu.CompilerParams(vmem_limit_bytes=VMEM_LIMIT),
        cost_estimate=cost(
            flops=2 * span * rows * total, bytes_accessed=2 * (span + rows) * total, transcendentals=0
        ),
        name="weight_products",
    )(core.reshape(1), *lefts, *flat, *deps)
    if apart:
        return results
    cut = results[0].reshape(slices // 2, 2, size, total)
    return pick(cut, 1 - core, 1).reshape(-1, total), pick(cut, core, 1).reshape(-1, total)


def nothing(shapes):
    return pl.pallas_call(
        lambda *refs: None, out_shape=shapes, out_specs=[ANY] * len(shapes), name="nothing"
    )()


def input_kernel(gain_ref, w_ref, x_ref, first_ref, second_ref, dk_ref, dv_ref, ahead_ref, behind_ref, out_ref, dgain_ref):
    step = pl.program_id(0)
    gain = gain_ref[0:1, :]
    rows, width = x_ref.shape
    in_first = 2 * step < pl.num_programs(0)
    d_query = jnp.where(in_first, first_ref[...], second_ref[...])
    back = dot(d_query, w_ref[:, :width], NT)
    back = back + dot(dk_ref[...], w_ref[:, width : 2 * width], NT)
    back = back + dot(dv_ref[...], w_ref[:, 2 * width :], NT)
    x = x_ref[...].astype(jnp.float32)
    scale = lax.rsqrt(jnp.mean(x * x, axis=1, keepdims=True) + EPSILON)
    scaled = back * gain
    mean = jnp.mean(scaled * x, axis=1, keepdims=True)
    grad = jnp.where(in_first, ahead_ref[...], behind_ref[...])
    out_ref[...] = grad + scale * scaled - x * (scale * scale * scale * mean)
    gain_part = jnp.sum((back * x * scale).reshape(rows // 8, 8, width), axis=0)
    dgain_ref[...] = jnp.where(step == 0, gain_part, dgain_ref[...] + gain_part)


def input_gradient(x, gain, w_qkv, query_grads, key_grad, value_grad, grads, deps):
    rows, width = x.shape
    steps = rows // TR
    row_block = pl.BlockSpec((TR, width), lambda i: (i, 0))
    half_block = pl.BlockSpec((TR, width), lambda i: (i % (steps // 2), 0))
    fixed = pl.BlockSpec((8, width), lambda i: (0, 0))
    out, dgain = pl.pallas_call(
        without(input_kernel, 9, len(deps)),
        grid=(steps,),
        in_specs=[fixed, pl.BlockSpec(w_qkv.shape, lambda i: (0, 0)), row_block, half_block, half_block]
        + [row_block] * 2
        + [half_block] * 2
        + [ANY] * len(deps),
        out_specs=[row_block, fixed],
        out_shape=[jax.ShapeDtypeStruct((rows, width), jnp.float32), jax.ShapeDtypeStruct((8, width), jnp.float32)],
        compiler_params=pltpu.CompilerParams(vmem_limit_bytes=VMEM_LIMIT),
        cost_estimate=cost(
            flops=6 * rows * width * width, bytes_accessed=16 * rows * width, transcendentals=0
        ),
        name="input_gradient",
    )(jnp.broadcast_to(gain[None], (8, width)), w_qkv, x, *query_grads, key_grad, value_grad, *grads, *deps)
    return out, jnp.sum(dgain, axis=0)


def sum_kernel(rounds, x_ref, out_ref, *refs):
    slots, send_sems, recv_sems = refs[: len(rounds)], refs[len(rounds)], refs[len(rounds) + 1]
    barrier = pltpu.get_barrier_semaphore()
    places, peers = [], []
    for axes in rounds:
        place, count = 0, 1
        for axis in axes:
            place = place * lax.axis_size(axis) + lax.axis_index(axis)
            count = count * lax.axis_size(axis)
        found = []
        for step in range(1, count):
            rest, device = lax.rem(place + step, count), {}
            for axis in reversed(axes):
                device[axis] = lax.rem(rest, lax.axis_size(axis))
                rest = lax.div(rest, lax.axis_size(axis))
            found.append(device)
        places.append(place)
        peers.append(found)
    for device in peers[0] + peers[1]:
        pl.semaphore_signal(barrier, inc=1, device_id=device, device_id_type=pl.DeviceIdType.MESH)
    pl.semaphore_wait(barrier, len(peers[0]) + len(peers[1]))
    value = x_ref[...]
    first = 0
    for slot, place, found in zip(slots, places, peers):
        slot[place] = value
        copies = []
        for step, device in enumerate(found):
            copies.append(
                pltpu.make_async_remote_copy(
                    src_ref=slot.at[place],
                    dst_ref=slot.at[place],
                    send_sem=send_sems.at[first + step],
                    recv_sem=recv_sems.at[first + step],
                    device_id=device,
                    device_id_type=pl.DeviceIdType.MESH,
                )
            )
        for copy in copies:
            copy.start()
        for copy in copies:
            copy.wait()
        first += len(found)
        value = slot[0]
        for index in range(1, len(found) + 1):
            value = value + slot[index]
    out_ref[...] = value


def sum_everywhere(x):
    rounds = (("dp",), ("section", "mp"))
    counts = [math.prod(lax.axis_size(axis) for axis in axes) for axes in rounds]
    copies = sum(counts) - len(counts)
    return pl.pallas_call(
        partial(sum_kernel, rounds),
        out_shape=jax.ShapeDtypeStruct(x.shape, x.dtype),
        in_specs=[pl.BlockSpec(memory_space=pltpu.VMEM)],
        out_specs=pl.BlockSpec(memory_space=pltpu.VMEM),
        scratch_shapes=[pltpu.VMEM((count,) + x.shape, x.dtype) for count in counts]
        + [pltpu.SemaphoreType.DMA((copies,)), pltpu.SemaphoreType.DMA((copies,))],
        compiler_params=pltpu.CompilerParams(collective_id=0, has_side_effects=True),
        name="sum_everywhere",
    )(x)


def pair_permute(x, axis, bit):
    pairs = [(i, i ^ (1 << bit)) for i in range(lax.axis_size(axis))]
    return lax.ppermute(x, axis, pairs)


def shifted(x, axis, by):
    peers = lax.axis_size(axis)
    pairs = [(i, i + by) for i in range(peers) if 0 <= i + by < peers]
    return lax.ppermute(x, axis, pairs)


def in_order(flag, first, second, axis):
    return jnp.where(
        flag == 0,
        jnp.concatenate([first, second], axis=axis),
        jnp.concatenate([second, first], axis=axis),
    )


def pick(x, index, axis):
    return lax.dynamic_index_in_dim(x, index, axis, False)


def after(values, *others):
    return lax.optimization_barrier((values, others))[0]


def exchange_rows(block, where_mp):
    return pick(block, where_mp, 0), pair_permute(pick(block, 1 - where_mp, 0), "mp", 0)


def scatter_rows(rows, where_mp):
    half = rows.shape[0] // 2
    send = lax.dynamic_slice_in_dim(rows, (1 - where_mp) * half, half, 0).astype(jnp.bfloat16)
    return lax.dynamic_slice_in_dim(rows, where_mp * half, half, 0), pair_permute(send, "mp", 0)


def fetch_far(shard, core):
    half = shard.shape[0] // 2
    return pair_permute(lax.dynamic_slice_in_dim(shard, core * half, half, 0), "mp", 0)


def fetch_near(far):
    return pair_permute(far, "dp", 0)


def fetch_other(shard, dp_index):
    quarter = shard.shape[0] // 4
    far = pair_permute(lax.dynamic_slice_in_dim(shard, (dp_index & 3) * quarter, quarter, 0), "mp", 0)
    half = in_order(dp_index & 1, far, pair_permute(far, "dp", 0), 0)
    return in_order((dp_index >> 1) & 1, half, pair_permute(half, "dp", 1), 0), far


class Reduction:
    def __init__(self, send, keep, dp_index, section=None):
        self.total, self.arrived = keep, pair_permute(send, "dp", 0)
        self.dp_index = dp_index
        bits = lax.axis_size("dp").bit_length() - 1
        self.left = ([("section", section)] if section is not None else []) + [("mp", None)]
        self.left += [("dp", bit) for bit in range(1, bits)]

    def joined(self, cut):
        return cut(self.total).astype(jnp.float32) + cut(self.arrived).astype(jnp.float32)

    def hop(self, *ties):
        brought = self.arrived
        self.arrived = after(self.arrived, *ties)
        axis, which = self.left.pop(0)
        rows, width = self.total.shape
        if axis == "section":
            send = self.joined(lambda x: x[: rows // 2]).astype(jnp.bfloat16)
            keep = jnp.where(which == 0, 0.0, self.joined(lambda x: x[rows // 2 :]))
            self.total, self.arrived = keep, shifted(send, "section", -1)
        elif axis == "mp":
            send = self.joined(lambda x: x[:, width // 2 :]).astype(jnp.bfloat16)
            self.total, self.arrived = self.joined(lambda x: x[:, : width // 2]), pair_permute(send, "mp", 0)
        else:
            mark = (self.dp_index >> which) & 1
            halves = (lax.axis_size("dp") >> (which + 1), 2, -1, width)
            send = self.joined(lambda x: pick(x.reshape(halves), 1 - mark, 1)).astype(jnp.bfloat16)
            keep = self.joined(lambda x: pick(x.reshape(halves), mark, 1))
            self.total = keep.reshape(-1, width)
            self.arrived = pair_permute(send.reshape(-1, width), "dp", which)
        return brought

    def finish(self, *ties):
        while self.left:
            self.hop()
        self.arrived = after(self.arrived, *ties)
        return self.joined(lambda x: x)


def rms_norm(inputs, gain_row):
    return (
        inputs * lax.rsqrt(jnp.mean(inputs * inputs, axis=-1, keepdims=True) + EPSILON) * gain_row
    )


def norm_back(rows, gain_row, grad_normed):
    return jax.vjp(rms_norm, rows, gain_row)[1](grad_normed)


def low(x):
    return x.astype(jnp.bfloat16)


def local(
    block_input,
    out_cotangent,
    doc_lengths,
    question_lengths,
    coordinates,
    gains,
    bias_tables,
    self_qkv,
    self_out,
    ffn_in,
    ffn_out,
    cross_q,
    cross_kv,
    cross_out,
):
    section = lax.axis_index("section")
    on_encoder = section == 0
    dp_index = lax.axis_index("dp")
    core = dp_index & 1
    where_mp = lax.axis_index("mp")
    width = block_input.shape[4]
    quests = question_lengths.shape[2]
    own = self_qkv.shape[3]
    pairs = 2 * own // LANES
    heads = 2 * pairs
    parts = lax.axis_size("dp")
    flags = jnp.stack([core, where_mp, section]).astype(jnp.int32)

    rows_low = in_order(where_mp, *exchange_rows(block_input[0, :, 0], where_mp), 0)
    qkv_own = self_qkv[0].reshape(width, -1)
    qkv_other, qkv_far = fetch_other(qkv_own, dp_index)
    w_qkv = jnp.concatenate(
        [x[:, t * own : (t + 1) * own] for t in range(3) for x in (qkv_own, qkv_other)], axis=1
    )
    owned = after((ffn_in[0], ffn_out[0], self_out[0]), rows_low, qkv_far)
    fars = [fetch_far(x, core) for x in owned]

    lens = jnp.concatenate(
        [pick(doc_lengths, where_mp, 0), pick(question_lengths, where_mp, 0)[0]]
    ).astype(jnp.int32)
    coords = pick(coordinates, where_mp, 0)[0]
    tables = jnp.where(where_mp == 0, bias_tables, jnp.roll(bias_tables, heads // 2, axis=2))

    enc_tables, dec_tables = forward_tables("enc", tables[:3], heads), forward_tables("dec", tables[3:], heads)
    coords_both = (coords, coords.T)

    rows = rows_low.astype(jnp.float32)
    span = rows.shape[0]
    half = span // 2
    turn = half // TR
    halves = (slice(0, half), slice(half, span))
    gain_self = jnp.where(on_encoder, gains[0], gains[2])
    normed_self = low(rms_norm(rows, gain_self))
    projected = low(dot(normed_self, w_qkv))
    merged, probs, middles, memories, arrivals = [], [], [], [], []
    for part in range(2):
        deps = memories[:1]

        def forward(kind, chosen):
            return attend_forward(
                kind, part, half, lens, chosen, coords_both, projected, 0, [projected], 1, 2, pairs, quests, deps
            )

        out, prob = lax.cond(on_encoder, lambda: forward("enc", enc_tables), lambda: forward("dec", dec_tables))
        if not part:
            fars = after(fars, out)
            nears = [fetch_near(x) for x in fars]
            w_out = jnp.concatenate([self_out[0], in_order(core, fars[2], nears[2], 0)], axis=0)
            pieces = (ffn_in[0], fars[0], nears[0], ffn_out[0], fars[1], nears[1])
            cross_owned = after(
                (jnp.concatenate([cross_q, cross_kv.reshape(width, -1)], axis=1), cross_out, out_cotangent[0, :, 0]), fars
            )
            cross_fars = [fetch_far(x, core) for x in cross_owned[:2]]
            cot = exchange_rows(cross_owned[2], where_mp)
        else:
            cross_fars = after(cross_fars, out)
        memory, middle = feed_forward(
            "fwd", part, half, flags, pieces, gains[1], w_out, [(rows_low, part * turn, turn), (out, 0, turn)]
        )
        arrivals.append(shifted(memory, "section", 1))
        merged.append(out)
        probs.append(prob)
        middles.append(middle)
        memories.append(memory)
    query_other, cross_other = (in_order(core, far, fetch_near(far), 0) for far in cross_fars)
    w_query = jnp.concatenate([cross_q, query_other[:, :own]], axis=1)
    w_pair = jnp.concatenate(
        [x for t in range(2) for x in (cross_kv[:, t], query_other[:, (t + 1) * own : (t + 2) * own])], axis=1
    )
    w_cross = jnp.concatenate([cross_out, cross_other], axis=0)
    middle = jnp.concatenate(middles, axis=0)

    normed_cross = low(rms_norm(middle, gains[3]))
    queries = low(dot(normed_cross, w_query))
    first_pair = low(dot(arrivals[0], w_pair))
    arrivals[1] = after(arrivals[1], queries, first_pair)
    pair_rows = [first_pair, low(dot(arrivals[1], w_pair))]
    cross_merged, cross_prob = attend_forward(
        "cross", 0, span, lens, forward_tables("cross", None, heads), coords_both, queries, 0, pair_rows, 0, 1, pairs, quests
    )
    output_low, second, grad_second, second_low, cross_grad = feed_forward(
        "both",
        0,
        span,
        flags,
        pieces,
        gains[4],
        w_cross,
        [(middle, 0, 2 * turn), (cross_merged, 0, 2 * turn), (cot[0], 0, turn), (cot[1], 0, turn)],
    )
    output_own, output_arrived = scatter_rows(
        jnp.where(on_encoder, jnp.concatenate(memories, axis=0), output_low), where_mp
    )
    returns, returned, carry = [], [], ()
    for part in range(2):
        query_grad, key_grad, value_grad, _ = attend_backward(
            "cross",
            part,
            cross_prob,
            cross_grad,
            cross_merged,
            queries,
            0,
            pair_rows[part],
            0,
            1,
            pairs,
            quests,
            carry,
            [returns[0], output_arrived] if part else [],
        )
        carry = (query_grad, key_grad, value_grad)
        returns.append(
            low(
                dot(key_grad[halves[part]], w_pair[:, : 2 * own], NT)
                + dot(value_grad[halves[part]], w_pair[:, 2 * own :], NT)
            )
        )
        returned.append(shifted(returns[part], "section", -1))
    query_cross = after(query_grad, returns[1])

    def cross_norm():
        input_part, gain_part = norm_back(middle, gains[3], dot(query_cross, w_query, NT))
        return grad_second + input_part, gain_part

    def no_norm():
        return tuple(
            nothing([jax.ShapeDtypeStruct((span, width), jnp.float32), jax.ShapeDtypeStruct((width,), jnp.float32)])
        )

    grad_first, gain_cross = lax.cond(on_encoder, no_norm, cross_norm)

    gain_ffn = jnp.where(on_encoder, gains[1], gains[4])
    held, gain_ffn_grad, grads_middle, merged_grads = [], 0.0, [], []
    for part in range(2):
        if part:
            returned[1] = after(returned[1], grads_middle[0])
        grad_middle, *held, merged_grad, gain_part = feed_forward(
            "back",
            part,
            half,
            flags,
            pieces,
            gain_ffn,
            w_out,
            [
                (middles[part], 0, turn),
                (second, part * turn, turn),
                (cot[0], 0, turn),
                (cot[1], 0, turn),
                (returned[part], 0, turn),
                (grad_first, part * turn, turn),
            ],
            held,
        )
        gain_ffn_grad = gain_ffn_grad + jnp.sum(gain_part, axis=0)
        grads_middle.append(grad_middle)
        merged_grads.append(merged_grad)
    hn_turned, gl_turned, ml_turned, activated, hidden_grad = held
    in_send, in_keep = products([hn_turned], [0], [[hidden_grad]], 2 * own, parts, core)
    down_send, down_keep = products([gl_turned], [0], [[activated]], 2 * own, parts, core, [in_send])
    in_steps = Reduction(in_send, in_keep, dp_index)
    down_steps = Reduction(down_send, down_keep, dp_index)

    def cross_products():
        return tuple(
            products(
                [normed_cross.T, jnp.concatenate(arrivals, axis=0).T, second_low.T],
                [0, 1, 1, 2],
                [[query_cross], [key_grad], [value_grad], [cross_merged]],
                own,
                2 * parts,
                core,
                [down_send],
            )
        )

    def no_products():
        blank = jax.ShapeDtypeStruct((width // 2, 8 * own), jnp.bfloat16)
        return tuple(nothing([blank, blank]))

    cross_send, cross_keep = lax.cond(on_encoder, no_products, cross_products)
    cross_steps = Reduction(cross_send, cross_keep, dp_index, section)
    scores, query_grads, carry = [], [], ()
    for part in range(2):
        if part:
            deps = (in_steps.hop(), down_steps.arrived, cross_steps.hop())
        else:
            deps = (down_send, cross_send, in_steps.hop())

        def backward(kind):
            return attend_backward(
                kind, part, probs[part], merged_grads[part], merged[part], projected, 0, projected, 1, 2, pairs, quests,
                carry, deps
            )

        query_grad, key_grad, value_grad, score = lax.cond(
            on_encoder, lambda: backward("enc"), lambda: backward("dec")
        )
        carry = (key_grad, value_grad)
        query_grads.append(query_grad)
        scores.append(score)
    self_send, self_keep = products(
        [normed_self.T, ml_turned],
        [0, 0, 0, 1],
        [query_grads, [key_grad], [value_grad], merged],
        own,
        parts,
        core,
    )
    down_steps.hop(scores[1])
    self_steps = Reduction(self_send, self_keep, dp_index)
    input_grad, gain_self_grad = input_gradient(
        rows_low,
        gain_self,
        w_qkv,
        query_grads,
        key_grad,
        value_grad,
        grads_middle,
        [self_send],
    )
    grad_own, grad_arrived = scatter_rows(input_grad, where_mp)

    tabs, diags = [], []
    deps = (self_send, input_grad, in_steps.hop(scores[1]), cross_steps.hop(self_send))
    for part in range(2):
        for quarter in range(2):
            tab, diag = lax.cond(
                on_encoder,
                lambda: table_sums("enc", part, quarter, coords, scores[part], quests, deps),
                lambda: table_sums("dec", part, quarter, coords, scores[part], quests, deps),
            )
            tabs.append(tab)
            diags.append(diag)
            if len(tabs) == 1:
                deps = (tab, self_steps.hop(tab), in_steps.arrived, down_steps.hop(tab))
            elif len(tabs) == 2:
                deps = (tab, cross_steps.hop(tab), grad_arrived)
            elif len(tabs) == 3:
                deps = (tab, self_steps.hop(tab), cross_steps.hop(tab), down_steps.hop(tab))
    table_grad = lax.cond(
        on_encoder,
        lambda: table_grads("enc", tabs, diags, span, quests, heads),
        lambda: table_grads("dec", tabs, diags, span, quests, heads),
    )
    table_grad = jnp.where(where_mp == 0, table_grad, jnp.roll(table_grad, heads // 2, axis=2))
    blank = jnp.zeros((width,), jnp.float32)
    gain_grad = jnp.where(
        on_encoder,
        jnp.stack([gain_self_grad, gain_ffn_grad, blank, blank, blank]),
        jnp.stack([blank, blank, gain_self_grad, gain_cross, gain_ffn_grad]),
    )
    small = jnp.concatenate([gain_grad.reshape(-1, LANES), table_grad.reshape(-1, LANES)], axis=0)
    count = small.shape[0]
    small = jnp.pad(small, ((0, -count % 8), (0, 0)))
    cross_shard, in_shard, down_shard = (x.finish(tabs[3]) for x in (cross_steps, in_steps, down_steps))
    small = sum_everywhere(after(small, self_steps.hop(tab), down_steps.arrived))
    gain_count = gain_grad.size // LANES
    gain_sum = small[:gain_count].reshape(gain_grad.shape)
    table_sum = small[gain_count:count].reshape(table_grad.shape)
    self_shard = self_steps.finish(table_grad)
    output_rows, grad_rows = (
        in_order(where_mp, own_rows[None], after(arrived, tabs[2]).astype(own_rows.dtype)[None], 0)
        for own_rows, arrived in ((output_own, output_arrived), (grad_own, grad_arrived))
    )
    return (
        output_rows[None, :, None],
        grad_rows[None, :, None],
        gain_sum[:4],
        gain_sum[4],
        table_sum,
        self_shard[:, : 3 * own].reshape(-1, 3, own)[None],
        self_shard[:, 3 * own :].T[None],
        in_shard[None],
        down_shard.T[None],
        cross_shard[:, :own],
        cross_shard[:, own : 3 * own].reshape(-1, 2, own),
        cross_shard[:, 3 * own :].T,
    )


def solution(mesh):
    return jax.shard_map(
        local,
        mesh=mesh,
        in_specs=(
            P("section", None, "dp", "mp", None),
            P("section", None, "dp", "mp", None),
            P(None, "dp"),
            P(None, "dp", None),
            P(None, "dp", None, None),
            P(),
            P(),
            P("section", None, None, "mp"),
            P("section", "mp", None),
            P("section", None, "mp"),
            P("section", "mp", None),
            P(None, "mp"),
            P(None, None, "mp"),
            P("mp", None),
        ),
        out_specs=(
            P("section", None, "dp", "mp", None),
            P("section", None, "dp", "mp", None),
            P(),
            P(),
            P(),
            P("section", "dp", None, "mp"),
            P("section", "mp", "dp"),
            P("section", "dp", "mp"),
            P("section", "mp", "dp"),
            P(("section", "dp"), "mp"),
            P(("section", "dp"), None, "mp"),
            P("mp", ("section", "dp")),
        ),
        check_vma=False,
    )
```
